128 devices in a mesh: group: 16 (over z, x), shard: 8 (over y, core).
Axes of the slice: x: 4, y: 4, z: 4, core: 2. Of those that a mesh axis runs over, the one named last changes fastest.
Arguments:
- replay: float32 [1048576, 42], P(('group', 'shard')), may hold values from -6 to 6
- sample_index: int32 [128, 128, 32], P(('group', 'shard')), may hold values from 0 to 8191
- pair_count: int32 [128, 128], P(('group', 'shard')), may hold values from 0 to 32, as said below
- noise: float32 [128, 128, 32, 6], P(('group', 'shard')), may hold values from -5 to 5
- actor: float32 [71942], replicated
- critic: float32 [2, 72193], replicated
- actor_momentum: float32 [71942], replicated, may hold values from -0.3125 to 0.3125
- critic_momentum: float32 [2, 72193], replicated, may hold values from -0.3125 to 0.3125
- actor_average: float32 [71942], replicated
- critic_average: float32 [2, 72193], replicated
- actor_target: float32 [71942], replicated
- critic_target: float32 [2, 72193], replicated
Outputs:
- loss_parts: float32 [2], replicated
- priority: float32 [128, 128, 32], P(('group', 'shard'))
- actor_new: float32 [71942], replicated
- critic_new: float32 [2, 72193], replicated
- actor_momentum_new: float32 [71942], replicated
- critic_momentum_new: float32 [2, 72193], replicated
- actor_average_new: float32 [71942], replicated
- critic_average_new: float32 [2, 72193], replicated
- actor_target_new: float32 [71942], replicated
- critic_target_new: float32 [2, 72193], replicated
- actor_low: bfloat16 [71942], replicated
- critic_low: bfloat16 [2, 72193], replicated
The draws below stay inside these ranges and needn't reach their ends.
Inputs may be any that keep to these rules, and one draw needn't show every extreme that they name: `pair_count`: at most 32; the last shard fills all 32 slots to the last device.
All inputs are finite; a program needn't handle non-finite values.
Results may differ from the reference program's by a relative error of at most 0.001.
Values sent between devices are 32-bit elements; how exact they have to be, the bound alone decides.
A program may use at most 128 MiB of HBM per device.

```python
import math
import jax
import jax.numpy as jnp
from jax import lax

OBS = 17
ACT = 6
UNITS = 256
CAP = 32
R_DEV = 8192
DEVS = 128
ROW = 42
ROWS = 1048576
PA = 71942
PC = 72193


def net_flat(key, width_in, width_out):
    shapes = [(width_in, UNITS), (UNITS,), (UNITS, UNITS), (UNITS,), (UNITS, width_out), (width_out,)]
    keys = jax.random.split(key, 6)
    pieces = []
    for number in range(6):
        shape = shapes[number]
        base = jax.random.normal(keys[number], shape, jnp.float32)
        if len(shape) == 2:
            base = base * shape[0] ** (-0.5)
        else:
            base = base * 0.1
        pieces.append(base.reshape(-1))
    return jnp.concatenate(pieces)


def critic_pair(key):
    first, second = jax.random.split(key)
    return jnp.stack([net_flat(first, OBS + ACT, 1), net_flat(second, OBS + ACT, 1)])


def draw_actor(key, part):
    key = jax.random.fold_in(key, 1)
    return net_flat(key, OBS, ACT)


def draw_critic(key, part):
    key = jax.random.fold_in(key, 2)
    return critic_pair(key)


def draw_actor_average(key, part):
    key = jax.random.fold_in(key, 3)
    return net_flat(key, OBS, ACT)


def draw_critic_average(key, part):
    key = jax.random.fold_in(key, 4)
    return critic_pair(key)


def draw_actor_target(key, part):
    key = jax.random.fold_in(key, 5)
    return net_flat(key, OBS, ACT)


def draw_critic_target(key, part):
    key = jax.random.fold_in(key, 6)
    return critic_pair(key)


def draw_pair_count(key, part):
    key = jax.random.fold_in(key, 7)
    owner = jnp.arange(DEVS, dtype=jnp.int32)[:, None]
    dest = jnp.arange(DEVS, dtype=jnp.int32)[None, :]
    top = 1 + CAP * (owner + 1) * (dest + DEVS) // (DEVS * DEVS)
    spread = jax.random.randint(key, (DEVS, DEVS), 0, 1 << 20)
    counts = top // 2 + spread % (top - top // 2 + 1)
    counts = jnp.minimum(counts, CAP)
    counts = counts.at[DEVS - 1, DEVS - 1].set(CAP)
    return counts.astype(jnp.int32)


def plant(array, rng, smallest, high):
    longest = array.shape.index(max(array.shape))
    spots = []
    for shift in (0, 1):
        where = [jax.random.randint(jax.random.fold_in(rng, axis), (), 0, length) for axis, length in enumerate(array.shape)]
        where[longest] = (where[longest] + shift) % array.shape[longest]
        spots.append(tuple(where))
    return array.at[spots[0]].set(smallest).at[spots[1]].set(high)


def block_levels(stream_key, extent, cuts, least, high):
    factor_of, own = 1.0, jax.random.fold_in(stream_key, 6)
    for position, parts in cuts:
        draws = jnp.exp(jax.random.uniform(jax.random.fold_in(own, position), (parts,), jnp.float32, least / len(cuts), high / len(cuts)))
        factor_of = factor_of * jnp.repeat(draws, extent[position] // parts).reshape([-1 if axis == position else 1 for axis in range(len(extent))])
    return factor_of


def bell_draw(own_key, extent, scale, bound, cuts=(), held_as=jnp.bfloat16):
    drawn = scale * jax.random.normal(own_key, extent, jnp.float32)
    if cuts:
        drawn = drawn * block_levels(own_key, extent, cuts, -0.22, 0.18)
    return jnp.clip(drawn, -bound, bound).astype(held_as)


def setup_inputs(seed: int = 0) -> dict:
    key_of = jax.random.split(jax.random.key(seed), 13)
    return {
        "replay": bell_draw(key_of[0], (ROWS, ROW), 1.0, 6.0, ((0, 128),), jnp.float32),
        "sample_index": plant(jax.random.randint(key_of[1], (DEVS, DEVS, CAP), 0, R_DEV), jax.random.fold_in(key_of[1], 1), 0, R_DEV - 1).astype(jnp.int32),
        "pair_count": draw_pair_count(jax.random.fold_in(key_of[12], 71), 0),
        "noise": bell_draw(key_of[3], (DEVS, DEVS, CAP, ACT), 1.0, 5.0, ((0, 128),), jnp.float32),
        "actor": draw_actor(jax.random.fold_in(key_of[12], 71), 0),
        "critic": draw_critic(jax.random.fold_in(key_of[12], 71), 0),
        "actor_momentum": bell_draw(key_of[6], (PA,), 0.02, 0.3125, (), jnp.float32),
        "critic_momentum": bell_draw(key_of[7], (2, PC), 0.02, 0.3125, (), jnp.float32),
        "actor_average": draw_actor_average(jax.random.fold_in(key_of[12], 71), 0),
        "critic_average": draw_critic_average(jax.random.fold_in(key_of[12], 71), 0),
        "actor_target": draw_actor_target(jax.random.fold_in(key_of[12], 71), 0),
        "critic_target": draw_critic_target(jax.random.fold_in(key_of[12], 71), 0),
    }


@jax.custom_vjp
def low(v):
    return lax.optimization_barrier(v.astype(jnp.bfloat16)).astype(jnp.float32)

@jax.custom_vjp
def low_back(v):
    return v

def low_keep(v):
    return (low(v), None)

def low_pass(kept, grad):
    return (grad,)

def back_keep(v):
    return (v, None)

def back_low(kept, grad):
    return (low(grad),)
low.defvjp(low_keep, low_pass)
low_back.defvjp(back_keep, back_low)

def matmul(a, b):
    return jnp.dot(a, b, precision=lax.Precision.HIGHEST)

def unpack(flat, width_in, width_out):
    shapes = [(width_in, UNITS), (UNITS,), (UNITS, UNITS), (UNITS,), (UNITS, width_out), (width_out,)]
    pieces = []
    start = 0
    for shape in shapes:
        number = math.prod(shape)
        pieces.append(flat[start:start + number].reshape(shape))
        start = start + number
    return pieces

def network(flat, inputs, width_out):
    w_one, b_one, w_two, b_two, w_three, b_three = unpack(flat, inputs.shape[1], width_out)
    hidden = jax.nn.silu(matmul(inputs, w_one) + b_one)
    hidden = jax.nn.silu(matmul(hidden, w_two) + b_two)
    return matmul(hidden, w_three) + b_three

def bootstrap(actor_target, critic_target, next_state, reward, weight, noise):
    smooth = 0.5 * jnp.tanh(0.4 * noise)
    next_action = jnp.tanh(network(actor_target, next_state, ACT) + smooth)
    joined = jnp.concatenate([next_state, next_action], 1)
    first = network(critic_target[0], joined, 1)[:, 0]
    second = network(critic_target[1], joined, 1)[:, 0]
    return reward + 0.99 * weight * jnp.minimum(first, second)

def numerator(actor, critic, critic_fixed, state, action, target, valid):
    joined = jnp.concatenate([state, action], 1)
    first = network(critic[0], joined, 1)[:, 0]
    second = network(critic[1], joined, 1)[:, 0]
    policy = jnp.tanh(network(actor, state, ACT))
    policy_value = network(critic_fixed[0], jnp.concatenate([state, policy], 1), 1)[:, 0]
    terms = valid * ((first - target) ** 2 + (second - target) ** 2 - policy_value)
    return (jnp.sum(terms), first - target)

def update(weight, grad, momentum, average, target):
    momentum_new = 0.9 * momentum + grad
    weight_new = weight - 0.1 * (grad + 0.9 * momentum_new)
    average_new = 0.99 * average + 0.01 * weight_new
    target_new = 0.005 * weight_new + 0.995 * target
    return (weight_new, momentum_new, average_new, target_new, weight_new.astype(jnp.bfloat16))

def reference(replay, sample_index, pair_count, noise, actor, critic, actor_momentum, critic_momentum, actor_average, critic_average, actor_target, critic_target):
    owners = jnp.arange(DEVS, dtype=jnp.int32)[:, None, None] * R_DEV
    picked = replay[(owners + sample_index).astype(jnp.int32)]
    batch = jnp.transpose(picked, (1, 0, 2, 3)).reshape(DEVS * DEVS * CAP, ROW)
    slots = jnp.arange(CAP, dtype=jnp.int32)[None, None, :]
    valid = (slots < jnp.transpose(pair_count)[:, :, None]).astype(jnp.float32).reshape(-1)
    noise_rows = noise.reshape(DEVS * DEVS * CAP, ACT)
    state = batch[:, :OBS]
    action = batch[:, OBS:OBS + ACT]
    reward = batch[:, OBS + ACT]
    weight = batch[:, OBS + ACT + 1]
    next_state = batch[:, OBS + ACT + 2:]
    target = bootstrap(actor_target, critic_target, next_state, reward, weight, noise_rows)
    count = jnp.sum(valid)

    def scaled(actor_in, critic_in):
        total, delta = numerator(actor_in, critic_in, critic, state, action, target, valid)
        return (total / count, (total, delta))
    value, pull, extra = jax.vjp(scaled, actor, critic, has_aux=True)
    grad_actor, grad_critic = pull(jnp.float32(1.0))
    total, delta = extra
    priority = (valid * jnp.sqrt(delta * delta + 1.0)).reshape(DEVS, DEVS, CAP)
    priority = jnp.transpose(priority, (1, 0, 2))
    actor_out = update(actor, grad_actor, actor_momentum, actor_average, actor_target)
    critic_out = update(critic, grad_critic, critic_momentum, critic_average, critic_target)
    loss_parts = jnp.stack([total, count])
    return (loss_parts, priority, actor_out[0], critic_out[0], actor_out[1], critic_out[1], actor_out[2], critic_out[2], actor_out[3], critic_out[3], actor_out[4], critic_out[4])
```

```python
import functools

import jax
import jax.numpy as jnp
from jax import lax
from jax.experimental import pallas as pl
from jax.experimental.pallas import tpu as pltpu
from jax.sharding import PartitionSpec as P

OBS = 17
ACT = 6
UNITS = 256
CAP = 32
DEVS = 128
R_DEV = 8192
ROW = 42
PA = 71942
PC = 72193
N = DEVS * CAP

bf = jnp.bfloat16
f32 = jnp.float32
MESH = pl.DeviceIdType.MESH
VM = pl.BlockSpec(memory_space=pltpu.VMEM)
SM = pl.BlockSpec(memory_space=pltpu.SMEM)
SDS = jax.ShapeDtypeStruct

SCALE = 2.0**-19
C0, C1, A, AT, T0, T1 = range(6)
FEAT = 48
ONE = 42
NEXT = 25

ROWS_A = 568
STAT = 564
TILES_C = 565
PACK = 1728
HALF = PACK // 2
CHUNK = 16
OWNERS = HALF // CHUNK
CHIPS = DEVS // 2


def dot(a, b):
    return lax.dot_general(a, b, (((1,), (0,)), ((), ())), preferred_element_type=f32)


def dot_nt(a, b):
    return lax.dot_general(a, b, (((1,), (1,)), ((), ())), preferred_element_type=f32)


def dot_exact(a, b, dims):
    return lax.dot_general(a, b, (dims, ((), ())), precision=lax.Precision.HIGHEST, preferred_element_type=f32)


def split(v):
    hi = v.astype(bf)
    return hi, (v - hi.astype(f32)).astype(bf)


def three(v):
    hi, lo = split(v)
    return jnp.concatenate([hi, lo, hi], 0)


def lanes(tile, width):
    return jnp.concatenate([tile] * (width // 128), 1)


def fold(v):
    out = v[:, :128]
    for i in range(1, v.shape[1] // 128):
        out = out + v[:, 128 * i : 128 * (i + 1)]
    return out


def column(row):
    return jnp.transpose(jnp.broadcast_to(row, (128, 128)))


def exchange_start(me, group_size, shard_size, noise_ref, q_ref, nsend, nrecv, send_sem, recv_sem):
    q_ref[...] = jnp.zeros_like(q_ref)
    for j in range(ACT):
        q_ref[pl.ds(j + 1, CAP, stride=8), :] = 0.5 * jnp.tanh(0.4 * noise_ref[j])
    turned = jnp.transpose(q_ref[...])
    nsend[:, 0, :] = turned[:, :128]
    nsend[:, 1, :] = turned[:, 128:]
    nrecv[pl.ds(me, 1)] = nsend[pl.ds(me, 1)]

    def send(k, carry):
        peer = lax.rem(me + k, DEVS)
        pltpu.make_async_remote_copy(
            src_ref=nsend.at[peer],
            dst_ref=nrecv.at[me],
            send_sem=send_sem,
            recv_sem=recv_sem,
            device_id=(peer // shard_size, lax.rem(peer, shard_size)),
            device_id_type=MESH,
        ).start()
        return carry

    lax.fori_loop(1, DEVS, send, 0)


def exchange_wait(nsend, nrecv, send_sem, recv_sem, nz_ref):
    pltpu.make_async_copy(nsend.at[pl.ds(0, DEVS - 1)], nsend.at[pl.ds(0, DEVS - 1)], send_sem).wait()
    pltpu.make_async_copy(nrecv.at[pl.ds(0, DEVS - 1)], nrecv.at[pl.ds(0, DEVS - 1)], recv_sem).wait()
    back = jnp.transpose(jnp.concatenate([nrecv[:, 0, :], nrecv[:, 1, :]], 1))
    for c in range(CAP):
        nz_ref[:, 128 * c : 128 * (c + 1)] = back[8 * c : 8 * (c + 1), :]


def turn_table(table_ref, rows_ref):
    width = 512

    def body(i, carry):
        s = pl.ds(pl.multiple_of(i * width, width), width)
        v = jnp.concatenate([table_ref[:, s], jnp.zeros((128 - ROW, width), f32)], 0)
        rows_ref[s, :] = jnp.transpose(v)
        return carry

    lax.fori_loop(0, R_DEV // width, body, 0)


def pick_rows(index_ref, rows_ref, picked_ref, x_ref):
    ones = lax.broadcasted_iota(jnp.int32, (8, 128), 0) == (ONE - 40)

    def body(c, carry):
        for d in range(DEVS):
            picked_ref[d : d + 1, :] = rows_ref[pl.ds(index_ref[c, d], 1), :]
        turned = jnp.transpose(picked_ref[...])
        s = pl.ds(pl.multiple_of(c * 128, 128), 128)
        x_ref[0:40, s] = turned[0:40]
        x_ref[40:48, s] = jnp.where(ones, 1.0, turned[40:48])
        return carry

    lax.fori_loop(0, CAP, body, 0)


def gather_kernel(
    group_size, shard_size, table_ref, index_ref, noise_ref, x_ref, nz_ref, rows_ref, picked_ref, q_ref, nsend, nrecv, send_sem, recv_sem
):
    me = lax.axis_index("group") * shard_size + lax.axis_index("shard")
    barrier = pltpu.get_barrier_semaphore()

    def greet(k, carry):
        peer = lax.rem(me + k, DEVS)
        pl.semaphore_signal(
            barrier, inc=1, device_id=(peer // shard_size, lax.rem(peer, shard_size)), device_id_type=MESH
        )
        return carry

    lax.fori_loop(1, DEVS, greet, 0)
    turn_table(table_ref, rows_ref)
    pl.semaphore_wait(barrier, DEVS - 1)
    exchange_start(me, group_size, shard_size, noise_ref, q_ref, nsend, nrecv, send_sem, recv_sem)
    pick_rows(index_ref, rows_ref, picked_ref, x_ref)
    exchange_wait(nsend, nrecv, send_sem, recv_sem, nz_ref)


def put_square(net, w2, w2f_ref, w2b_ref):
    w2 = 0.5 * w2
    turned = jnp.transpose(w2)
    hi, lo = split(turned)
    w2f_ref[net] = jnp.concatenate([hi, hi, lo], 1)
    if net in (C0, C1, A):
        hi, lo = split(w2)
        w2b_ref[net] = jnp.concatenate([hi, hi, lo], 1)


def put_first(net, pad_ref, w1_ref):
    w1 = 0.5 * pad_ref[...]
    hi = w1.astype(bf).astype(f32)
    lo = w1 - hi
    stacked = jnp.concatenate([hi, hi, lo, jnp.zeros((256 - 3 * FEAT, 256), f32)], 0)
    w1_ref[net] = jnp.transpose(stacked).astype(bf)


def put_column(ref, net, left, right, factor):
    ref[net] = jnp.concatenate([column(left * factor), column(right * factor)], 0)


def prepare_critics(critic_ref, rows_ref, pad_ref, first, w1_ref, w2f_ref, w2b_ref, b2_ref, w3_ref, b3_ref, w1a_ref):
    for t in range(TILES_C - 1):
        rows_ref[2 * t : 2 * t + 2, :] = critic_ref[:, 128 * t : 128 * (t + 1)]
    for c in range(2):
        net = first + c
        start = NEXT if first == T0 else 0
        pad_ref[...] = jnp.zeros_like(pad_ref)
        for half in range(2):
            s = pl.ds(128 * half, 128)
            pad_ref[pl.ds(start, OBS), s] = rows_ref[pl.ds(c + 2 * half, OBS, stride=4), :]
            pad_ref[pl.ds(OBS, ACT), s] = rows_ref[pl.ds(c + 2 * half + 4 * OBS, ACT, stride=4), :]
            pad_ref[pl.ds(ONE, 1), s] = rows_ref[pl.ds(92 + c + 2 * half, 1), :]
        put_first(net, pad_ref, w1_ref)
        if net == C0:
            hi = pad_ref[16:24, :].astype(bf).astype(f32)
            lo = pad_ref[16:24, :] - hi
            block = jnp.concatenate([hi, hi, lo], 1)
            w1a_ref[...] = jnp.concatenate([block, jnp.zeros_like(block)], 0).astype(bf)
        w2 = jnp.concatenate(
            [rows_ref[pl.ds(96 + c, UNITS, stride=4), :], rows_ref[pl.ds(98 + c, UNITS, stride=4), :]], 1
        )
        put_square(net, w2, w2f_ref, w2b_ref)
        put_column(b2_ref, net, rows_ref[1120 + c : 1121 + c, :], rows_ref[1122 + c : 1123 + c, :], 0.5)
        put_column(w3_ref, net, rows_ref[1124 + c : 1125 + c, :], rows_ref[1126 + c : 1127 + c, :], 1.0)
        b3_ref[net] = jnp.broadcast_to(critic_ref[c : c + 1, PC - 1 : PC], (1, 128))


def head_maps(j):
    k = lax.broadcasted_iota(jnp.int32, (UNITS, 16), 0)
    r = lax.broadcasted_iota(jnp.int32, (UNITS, 16), 1)
    row = ((k * ACT + j) // 128) == r
    k = lax.broadcasted_iota(jnp.int32, (UNITS, 128), 0)
    l = lax.broadcasted_iota(jnp.int32, (UNITS, 128), 1)
    lane = ((k * ACT + j) % 128) == l
    return row.astype(f32), lane


def head_of(flat):
    hi = flat.astype(bf).astype(f32)
    out = []
    for part in (hi, flat - hi):
        part = part.astype(bf)
        spread = []
        for j in range(ACT):
            row, lane = head_maps(j)
            spread.append(jnp.where(lane, dot(row.astype(bf), part), 0.0).astype(bf))
        r = lax.broadcasted_iota(jnp.int32, (16, 128 * ACT), 0)
        l = lax.broadcasted_iota(jnp.int32, (16, 128 * ACT), 1)
        take = ((l // 128) == (r - 1)).astype(f32).astype(bf)
        out.append(dot_nt(take, jnp.concatenate(spread, 1))[:8])
    return out


def head_back(turned):
    out = jnp.zeros((16, 128), f32)
    for j in range(ACT):
        row, lane = head_maps(j)
        picked = jnp.transpose(row) * turned[j + 1 : j + 2, :]
        out = out + dot_exact(picked, lane.astype(f32), ((1,), (0,)))
    return out


def prepare_actor(net, rows_ref, pad_ref, w1_ref, w2f_ref, w2b_ref, b2_ref, w3t_ref, w3b_ref, b3a_ref):
    start = NEXT if net == AT else 0
    pad_ref[...] = jnp.zeros_like(pad_ref)
    for half in range(2):
        s = pl.ds(128 * half, 128)
        pad_ref[pl.ds(start, OBS), s] = rows_ref[pl.ds(half, OBS, stride=2), :]
        pad_ref[pl.ds(ONE, 1), s] = rows_ref[pl.ds(34 + half, 1), :]
    put_first(net, pad_ref, w1_ref)
    w2 = jnp.concatenate([rows_ref[pl.ds(36, UNITS, stride=2), :], rows_ref[pl.ds(37, UNITS, stride=2), :]], 1)
    put_square(net, w2, w2f_ref, w2b_ref)
    put_column(b2_ref, net, rows_ref[548:549, :], rows_ref[549:550, :], 0.5)
    flat = jnp.concatenate([rows_ref[550:562, :], jnp.zeros((4, 128), f32)], 0)
    hi, lo = head_of(flat)
    block = jnp.concatenate([hi, hi, lo], 1)
    w3t_ref[net - A] = jnp.concatenate([block, jnp.zeros_like(block)], 0).astype(bf)
    if net == A:
        stacked = jnp.concatenate([hi, hi, lo, jnp.zeros((104, UNITS), f32)], 0)
        w3b_ref[...] = (0.5 * jnp.transpose(stacked)).astype(bf)
    bias = column(rows_ref[562:563, :])
    b3a_ref[net - A] = jnp.zeros((8, 128), f32)
    b3a_ref[net - A, 1 : 1 + ACT, :] = bias[:ACT]


def act(zh):
    u = jnp.tanh(zh) + 1.0
    return u, zh * u


def slope(u, s):
    return u + s * (2.0 - u)


def train_rows(
    width,
    x_ref,
    nz_ref,
    count_ref,
    w1_ref,
    w2f_ref,
    w2b_ref,
    b2_ref,
    w3_ref,
    b3_ref,
    w3t_ref,
    w3b_ref,
    b3a_ref,
    w1a_ref,
    prio_ref,
    g2_ref,
    g1_ref,
    g3a_ref,
    db2_ref,
    dw3_ref,
    st_ref,
):
    for ref in (g2_ref, g1_ref, g3a_ref, db2_ref, dw3_ref, st_ref):
        ref[...] = jnp.zeros_like(ref)
    rows8 = lax.broadcasted_iota(jnp.int32, (8, width), 0)
    is_action = (rows8 >= 1) & (rows8 <= ACT)

    def body(i, carry):
        s_ = pl.ds(pl.multiple_of(i * width, width), width)
        x = x_ref[:, s_]
        x3 = three(x)
        xhi, xlo = x3[:FEAT], x3[FEAT : 2 * FEAT]
        x_left = jnp.concatenate(
            [jnp.concatenate([xhi, xlo], 0), jnp.concatenate([xhi, jnp.zeros_like(xlo)], 0)], 1
        )

        def with_action(a):
            return three(jnp.concatenate([x[:16], jnp.where(is_action, a, x[16:24]), x[24:]], 0))

        def first(net, xx):
            return act(dot(w1_ref[net, :, : 3 * FEAT], xx))

        def second(net, h3):
            return act(dot(w2f_ref[net], h3) + lanes(b2_ref[net], width))

        def value(net, s):
            return jnp.sum(s * lanes(w3_ref[net], width), 0, keepdims=True) + lanes(b3_ref[net], width)

        def head(net, s3):
            return dot(w3t_ref[net - A], s3)[:8] + lanes(b3a_ref[net - A], width)

        u, s = first(AT, x3)
        u, s = second(AT, three(s))
        next_action = jnp.tanh(head(AT, three(s)) + nz_ref[:, s_])

        u, s = first(A, x3)
        h1a, d1a = three(s), slope(u, s)
        u, s = second(A, h1a)
        h2a, d2a = three(s), slope(u, s)
        policy = jnp.tanh(head(A, h2a))

        kept = []
        for net in (C0, C1):
            u, s = first(net, x3)
            h1, d1 = three(s), slope(u, s)
            u, s = second(net, h1)
            kept.append((h1, d1, s, slope(u, s), value(net, s)))

        xt = with_action(next_action)
        targets = []
        for net in (T0, T1):
            u, s = first(net, xt)
            u, s = second(net, three(s))
            targets.append(value(net, s))

        u, s = first(C0, with_action(policy))
        d1f = slope(u, s)
        u, s = second(C0, three(s))
        d2f, q_policy = slope(u, s), value(C0, s)

        y = x[23:24] + 0.99 * x[24:25] * jnp.minimum(targets[0], targets[1])
        tiles = width // 128
        valid = jnp.concatenate([((i * tiles + t) < count_ref[...]).astype(f32) for t in range(tiles)], 1)
        delta = [k[4] - y for k in kept]
        prio_ref[:, s_] = valid * jnp.sqrt(delta[0] * delta[0] + 1.0)
        st_ref[0:1, :] += fold(valid * (delta[0] * delta[0] + delta[1] * delta[1] - q_policy))
        st_ref[1:2, :] += fold(valid)
        scaled = valid * SCALE

        def back(net, dz2):
            hi, lo = split(dz2)
            return hi, lo, dot(w2b_ref[net], jnp.concatenate([hi, lo, hi], 0))

        def weight_grads(net, h1, hi, lo, dz1):
            left = jnp.concatenate([h1[:UNITS], h1[UNITS : 2 * UNITS], h1[:UNITS]], 1)
            g2_ref[net] += dot_nt(left, jnp.concatenate([hi, hi, lo], 1))
            a, b = split(dz1)
            g1_ref[net] += dot_nt(x_left, jnp.concatenate([a, b], 1))

        for net in (C0, C1):
            h1, d1, s2, d2, _ = kept[net]
            dq = (2.0 * scaled) * delta[net]
            st_ref[2 + net : 3 + net, :] += fold(dq)
            dw3_ref[net] += fold(s2 * dq)
            dz2 = lanes(w3_ref[net], width) * (0.5 * dq) * d2
            db2_ref[net] += fold(dz2)
            hi, lo, dh1 = back(net, dz2)
            weight_grads(net, h1, hi, lo, dh1 * d1)

        dz2 = lanes(w3_ref[C0], width) * (-0.5 * scaled) * d2f
        hi, lo, dh1 = back(C0, dz2)
        da = dot(w1a_ref[...], three(dh1 * d1f))[:8]
        dp = jnp.where(is_action, da * (1.0 - policy * policy), 0.0)
        st_ref[8:16, :] += fold(dp)
        hi = dp.astype(bf).astype(f32)
        lo = dp - hi
        zero = jnp.zeros_like(hi)
        stacked = jnp.concatenate([hi, lo, hi, zero], 0).astype(bf)
        left = jnp.concatenate(
            [jnp.concatenate([hi, lo], 0), jnp.concatenate([hi, zero], 0)], 1
        ).astype(bf)
        g3a_ref[...] += dot_nt(left, jnp.concatenate([h2a[:UNITS], h2a[UNITS : 2 * UNITS]], 1))
        dz2 = dot(w3b_ref[:, :32], stacked) * d2a
        db2_ref[A] += fold(dz2)
        hi, lo, dh1 = back(A, dz2)
        weight_grads(A, h1a, hi, lo, dh1 * d1a)
        return carry

    lax.fori_loop(0, N // width, body, 0)


def lane_sums(tile):
    return dot_exact(jnp.ones((8, 128), f32), tile, ((1,), (1,)))


def pack_grads(pack_ref, g2_ref, g1_ref, g3a_ref, db2_ref, dw3_ref, st_ref):
    lane = lax.broadcasted_iota(jnp.int32, (1, 128), 1)
    sums = jnp.sum(st_ref[...], 1, keepdims=True)

    g1 = g1_ref[A, :FEAT, :] + g1_ref[A, FEAT:, :]
    b2 = lane_sums(db2_ref[A])[0:1]
    for half in range(2):
        s = slice(128 * half, 128 * (half + 1))
        pack_ref[pl.ds(half, OBS, stride=2), :] = g1[:OBS, s]
        pack_ref[34 + half : 35 + half, :] = g1[ONE : ONE + 1, s]
        pack_ref[pl.ds(36 + half, UNITS, stride=2), :] = g2_ref[A, :, s]
        pack_ref[548 + half : 549 + half, :] = b2[:, s]
    pack_ref[550:562, :] = head_back(g3a_ref[:8, :] + g3a_ref[8:, :])[:12]
    e = lax.broadcasted_iota(jnp.int32, (8, 128), 1) == lax.broadcasted_iota(jnp.int32, (8, 128), 0) - 1
    pack_ref[562:563, :] = jnp.sum(jnp.where(e, sums[8:16], 0.0), 0, keepdims=True)
    pack_ref[563:ROWS_A, :] = jnp.zeros((ROWS_A - 563, 128), f32)
    pack_ref[STAT : STAT + 1, :] = jnp.where(lane == 0, sums[0:1], jnp.where(lane == 1, sums[1:2], 0.0))

    for c in range(2):
        base = ROWS_A + c
        g1 = g1_ref[c, :FEAT, :] + g1_ref[c, FEAT:, :]
        b2 = lane_sums(db2_ref[c])[0:1]
        w3 = lane_sums(dw3_ref[c])[0:1]
        for half in range(2):
            s = slice(128 * half, 128 * (half + 1))
            at = base + 2 * half
            pack_ref[pl.ds(at, OBS + ACT, stride=4), :] = g1[: OBS + ACT, s]
            pack_ref[at + 92 : at + 93, :] = g1[ONE : ONE + 1, s]
            pack_ref[pl.ds(at + 96, UNITS, stride=4), :] = g2_ref[c, :, s]
            pack_ref[at + 1120 : at + 1121, :] = b2[:, s]
            pack_ref[at + 1124 : at + 1125, :] = w3[:, s]
        pack_ref[base + 1128 : base + 1129, :] = jnp.where(lane == 0, sums[2 + c : 3 + c], 0.0)
    last = ROWS_A + 2 * TILES_C
    pack_ref[last:PACK, :] = jnp.zeros((PACK - last, 128), f32)


def train_kernel(
    width, x_ref, nz_ref, count_ref, actor_ref, actor_t_ref, critic_ref, critic_t_ref, prio_ref, pack_ref, rows_ref, pad_ref, *scratch
):
    weights, grads = scratch[:10], scratch[10:]
    w1_ref, w2f_ref, w2b_ref, b2_ref, w3_ref, b3_ref, w3t_ref, w3b_ref, b3a_ref, w1a_ref = weights
    for first, ref in ((C0, critic_ref), (T0, critic_t_ref)):
        prepare_critics(
            ref, rows_ref, pad_ref, first, w1_ref, w2f_ref, w2b_ref, b2_ref, w3_ref, b3_ref, w1a_ref
        )
    for net, ref in ((A, actor_ref), (AT, actor_t_ref)):
        prepare_actor(net, ref, pad_ref, w1_ref, w2f_ref, w2b_ref, b2_ref, w3t_ref, w3b_ref, b3a_ref)
    train_rows(width, x_ref, nz_ref, count_ref, *weights, prio_ref, *grads)
    pack_grads(pack_ref, *grads)


WEIGHTS = [
    pltpu.VMEM((6, UNITS, 256), bf),
    pltpu.VMEM((6, UNITS, 3 * UNITS), bf),
    pltpu.VMEM((3, UNITS, 3 * UNITS), bf),
    pltpu.VMEM((6, UNITS, 128), f32),
    pltpu.VMEM((6, UNITS, 128), f32),
    pltpu.VMEM((6, 1, 128), f32),
    pltpu.VMEM((2, 16, 3 * UNITS), bf),
    pltpu.VMEM((UNITS, 128), bf),
    pltpu.VMEM((2, 8, 128), f32),
    pltpu.VMEM((16, 3 * UNITS), bf),
]
GRADS = [
    pltpu.VMEM((3, UNITS, UNITS), f32),
    pltpu.VMEM((3, 2 * FEAT, UNITS), f32),
    pltpu.VMEM((16, UNITS), f32),
    pltpu.VMEM((3, UNITS, 128), f32),
    pltpu.VMEM((2, UNITS, 128), f32),
    pltpu.VMEM((16, 128), f32),
]


def reduce_kernel(shard_size, pack_ref, ga_ref, gc_ref, stat_ref, other, half, parts, mine, gathered, whole, sems):
    group, shard = lax.axis_index("group"), lax.axis_index("shard")
    core = lax.rem(shard, 2)
    per = shard_size // 2
    chip = group * per + shard // 2

    def at(c):
        return (c // per, lax.rem(c, per) * 2 + core)

    sibling = (group, shard + 1 - 2 * core)
    barrier = pltpu.get_barrier_semaphore()
    pl.semaphore_signal(barrier, inc=1, device_id=sibling, device_id_type=MESH)

    def greet(k, carry):
        peer = lax.rem(chip + k, CHIPS)
        pl.semaphore_signal(barrier, inc=1, device_id=at(peer), device_id_type=MESH)
        return carry

    lax.fori_loop(1, CHIPS, greet, 0)
    pl.semaphore_wait(barrier, CHIPS)

    def remote(src, dst, n, to):
        return pltpu.make_async_remote_copy(
            src_ref=src, dst_ref=dst, send_sem=sems.at[2 * n], recv_sem=sems.at[2 * n + 1], device_id=to, device_id_type=MESH
        )

    def drain(ref, n, copies):
        view = ref.at[pl.ds(0, copies)]
        pltpu.make_async_copy(view, view, sems.at[n]).wait()

    keep = pl.multiple_of(core * HALF, HALF)
    give = pl.multiple_of((1 - core) * HALF, HALF)
    swap = remote(pack_ref.at[pl.ds(give, HALF)], other, 0, sibling)
    swap.start()
    swap.wait()
    total = pack_ref[pl.ds(keep, HALF), :] + other[...]
    half[...] = total.reshape(OWNERS, CHUNK, 128)

    def scatter(k, carry):
        peer = lax.rem(chip + k, CHIPS)

        @pl.when(peer < OWNERS)
        def _():
            remote(half.at[peer], parts.at[chip], 1, at(peer)).start()

        return carry

    lax.fori_loop(1, CHIPS, scatter, 0)
    owner = chip < OWNERS

    @pl.when(owner)
    def _():
        drain(half, 2, OWNERS - 1)
        parts[pl.ds(chip, 1)] = half[pl.ds(chip, 1)]
        drain(parts, 3, CHIPS - 1)
        mine[...] = jnp.sum(parts[...], 0)
        gathered[pl.ds(chip, 1)] = mine[...][None]

        def spread(k, carry):
            peer = lax.rem(chip + k, CHIPS)
            remote(mine, gathered.at[chip], 2, at(peer)).start()
            return carry

        lax.fori_loop(1, CHIPS, spread, 0)
        drain(parts, 4, CHIPS - 1)
        drain(gathered, 5, OWNERS - 1)

    @pl.when(jnp.logical_not(owner))
    def _():
        drain(half, 2, OWNERS)
        drain(gathered, 5, OWNERS)

    whole[pl.ds(core, 1)] = gathered[...].reshape(1, HALF, 128)
    back = remote(whole.at[core], whole.at[core], 3, sibling)
    back.start()
    back.wait()

    stat = whole[0, STAT : STAT + 1, :]
    factor = (1.0 / SCALE) / stat[:, 1:2]
    stat_ref[...] = stat
    ga_ref[...] = whole[0, :ROWS_A, :] * factor
    for t in range(TILES_C):
        r = ROWS_A + 2 * t
        h, r = r // HALF, r % HALF
        gc_ref[:, 128 * t : 128 * (t + 1)] = whole[h, r : r + 2, :] * factor


def update(weight, grad, momentum, average, target):
    momentum_new = 0.9 * momentum + grad
    weight_new = weight - 0.1 * (grad + 0.9 * momentum_new)
    average_new = 0.99 * average + 0.01 * weight_new
    target_new = 0.005 * weight_new + 0.995 * target
    return (weight_new, momentum_new, average_new, target_new, weight_new.astype(bf))


def actor_rows(flat):
    return jnp.pad(flat, (0, ROWS_A * 128 - PA)).reshape(ROWS_A, 128)


def local(
    group_size,
    shard_size,
    replay,
    sample_index,
    pair_count,
    noise,
    actor,
    critic,
    actor_momentum,
    critic_momentum,
    actor_average,
    critic_average,
    actor_target,
    critic_target,
):
    table = replay.T
    index = sample_index[0].T
    noise = jnp.transpose(noise[0], (2, 1, 0))
    x, nz = pl.pallas_call(
        functools.partial(gather_kernel, group_size, shard_size),
        out_shape=(SDS((FEAT, N), f32), SDS((8, N), f32)),
        in_specs=[VM, SM, VM],
        out_specs=(VM, VM),
        scratch_shapes=[
            pltpu.VMEM((R_DEV, 128), f32),
            pltpu.VMEM((128, 128), f32),
            pltpu.VMEM((256, 128), f32),
            pltpu.VMEM((DEVS, 2, 128), f32),
            pltpu.VMEM((DEVS, 2, 128), f32),
            pltpu.SemaphoreType.DMA,
            pltpu.SemaphoreType.DMA,
        ],
        compiler_params=pltpu.CompilerParams(
            collective_id=0, has_side_effects=True, vmem_limit_bytes=32 << 20
        ),
        name="gather_rows",
    )(table, index, noise)
    prio, pack = pl.pallas_call(
        functools.partial(train_kernel, 1024),
        out_shape=(SDS((1, N), f32), SDS((PACK, 128), f32)),
        in_specs=[VM] * 7,
        out_specs=(VM, VM),
        scratch_shapes=[pltpu.VMEM((2 * TILES_C + 6, 128), f32), pltpu.VMEM((FEAT, 256), f32)] + WEIGHTS + GRADS,
        compiler_params=pltpu.CompilerParams(vmem_limit_bytes=56 << 20),
        name="train_rows",
    )(x, nz, pair_count, actor_rows(actor), actor_rows(actor_target), critic, critic_target)
    ga, gc, stat = pl.pallas_call(
        functools.partial(reduce_kernel, shard_size),
        out_shape=(SDS((ROWS_A, 128), f32), SDS((2, TILES_C * 128), f32), SDS((1, 128), f32)),
        in_specs=[VM],
        out_specs=(VM, VM, VM),
        scratch_shapes=[
            pltpu.VMEM((HALF, 128), f32),
            pltpu.VMEM((OWNERS, CHUNK, 128), f32),
            pltpu.VMEM((CHIPS, CHUNK, 128), f32),
            pltpu.VMEM((CHUNK, 128), f32),
            pltpu.VMEM((OWNERS, CHUNK, 128), f32),
            pltpu.VMEM((2, HALF, 128), f32),
            pltpu.SemaphoreType.DMA((8,)),
        ],
        compiler_params=pltpu.CompilerParams(
            collective_id=1, has_side_effects=True, vmem_limit_bytes=32 << 20
        ),
        name="sum_grads",
    )(pack)
    actor_out = update(actor, ga.reshape(-1)[:PA], actor_momentum, actor_average, actor_target)
    critic_out = update(critic, gc[:, :PC], critic_momentum, critic_average, critic_target)
    outs = [stat[0, :2], prio.reshape(CAP, DEVS).T[None]]
    for one, two in zip(actor_out, critic_out):
        outs += [one, two]
    return tuple(outs)


def solution(mesh):
    rows = ("group", "shard")
    in_specs = (P(rows, None), P(rows, None, None), P(rows, None), P(rows, None, None, None)) + (P(),) * 8
    out_specs = (P(), P(rows, None, None)) + (P(),) * 10
    body = functools.partial(local, mesh.shape["group"], mesh.shape["shard"])
    return jax.shard_map(body, mesh=mesh, in_specs=in_specs, out_specs=out_specs, check_vma=False)
```

```python
import functools

import jax
import jax.numpy as jnp
from jax import lax
from jax.experimental import pallas as pl
from jax.experimental.pallas import tpu as pltpu
from jax.sharding import PartitionSpec as P

OBS = 17
ACT = 6
UNITS = 256
CAP = 32
DEVS = 128
R_DEV = 8192
ROW = 42
PA = 71942
PC = 72193
N = DEVS * CAP

bf = jnp.bfloat16
f32 = jnp.float32
MESH = pl.DeviceIdType.MESH
VM = pl.BlockSpec(memory_space=pltpu.VMEM)
SDS = jax.ShapeDtypeStruct

SCALE = 2.0**-19
C0, C1, A, AT, T0, T1 = range(6)
FEAT = 48
ONE = 42
NEXT = 25

TILES_C = 565
ROWS_A = 568
AT_ACTOR = 1136
STAT = AT_ACTOR + 564
CHIPS = DEVS // 2
CHUNK = 8
HALF = CHIPS * CHUNK
PACK = 4 * HALF
TURN = 512
WIDTH = 1024


def dot(a, b):
    return lax.dot_general(a, b, (((1,), (0,)), ((), ())), preferred_element_type=f32)


def dot_nt(a, b):
    return lax.dot_general(a, b, (((1,), (1,)), ((), ())), preferred_element_type=f32)


def dot_exact(a, b, dims):
    return lax.dot_general(a, b, (dims, ((), ())), precision=lax.Precision.HIGHEST, preferred_element_type=f32)


def split(v):
    hi = v.astype(bf)
    return hi, (v - hi.astype(f32)).astype(bf)


def three(v):
    hi, lo = split(v)
    return jnp.concatenate([hi, lo, hi], 0)


def lanes(tile, width):
    return jnp.concatenate([tile] * (width // 128), 1)


def fold(v):
    out = v[:, :128]
    for i in range(1, v.shape[1] // 128):
        out = out + v[:, 128 * i : 128 * (i + 1)]
    return out


def column(row):
    return jnp.transpose(jnp.broadcast_to(row, (128, 128)))


def turn_noise(noise_ref, q_ref, nsend):
    q_ref[...] = jnp.zeros_like(q_ref)
    for j in range(ACT):
        q_ref[pl.ds(j + 1, CAP, stride=8), :] = 0.5 * jnp.tanh(0.4 * noise_ref[j])
    turned = jnp.transpose(q_ref[...])
    nsend[:, 0, :] = turned[:, :128]
    nsend[:, 1, :] = turned[:, 128:]


def noise_back(nrecv, nz_ref):
    back = jnp.transpose(jnp.concatenate([nrecv[:, 0, :], nrecv[:, 1, :]], 1))
    for c in range(CAP):
        nz_ref[:, 128 * c : 128 * (c + 1)] = back[8 * c : 8 * (c + 1), :]


def turn_table(i, table_ref, rows_ref):
    s = pl.ds(pl.multiple_of(i * TURN, TURN), TURN)
    v = jnp.concatenate([table_ref[:, s], jnp.zeros((128 - ROW, TURN), f32)], 0)
    rows_ref[s, :] = jnp.transpose(v)


def pick_rows(index_ref, rows_ref, picked_ref, x_ref):
    ones = lax.broadcasted_iota(jnp.int32, (8, 128), 0) == (ONE - 40)

    def body(c, carry):
        for d in range(DEVS):
            picked_ref[d : d + 1, :] = rows_ref[pl.ds(index_ref[c, d], 1), :]
        turned = jnp.transpose(picked_ref[...])
        s = pl.ds(pl.multiple_of(c * 128, 128), 128)
        x_ref[0:40, s] = turned[0:40]
        x_ref[40:48, s] = jnp.where(ones, 1.0, turned[40:48])
        return carry

    lax.fori_loop(0, CAP, body, 0)


def put_square(net, w2, w2f_ref, w2b_ref):
    w2 = 0.5 * w2
    turned = jnp.transpose(w2)
    hi, lo = split(turned)
    w2f_ref[net] = jnp.concatenate([hi, hi, lo], 1)
    if net in (C0, C1, A):
        hi, lo = split(w2)
        w2b_ref[net] = jnp.concatenate([hi, hi, lo], 1)


def put_first(net, pad_ref, w1_ref):
    w1 = 0.5 * pad_ref[...]
    hi = w1.astype(bf).astype(f32)
    lo = w1 - hi
    stacked = jnp.concatenate([hi, hi, lo, jnp.zeros((256 - 3 * FEAT, 256), f32)], 0)
    w1_ref[net] = jnp.transpose(stacked).astype(bf)


def put_column(ref, net, left, right, factor):
    ref[net] = jnp.concatenate([column(left * factor), column(right * factor)], 0)


def prepare_critics(critic_ref, rows_ref, pad_ref, first, w1_ref, w2f_ref, w2b_ref, b2_ref, w3_ref, b3_ref, w1a_ref):
    for t in range(TILES_C - 1):
        rows_ref[2 * t : 2 * t + 2, :] = critic_ref[:, 128 * t : 128 * (t + 1)]
    for c in range(2):
        net = first + c
        start = NEXT if first == T0 else 0
        pad_ref[...] = jnp.zeros_like(pad_ref)
        for half in range(2):
            s = pl.ds(128 * half, 128)
            pad_ref[pl.ds(start, OBS), s] = rows_ref[pl.ds(c + 2 * half, OBS, stride=4), :]
            pad_ref[pl.ds(OBS, ACT), s] = rows_ref[pl.ds(c + 2 * half + 4 * OBS, ACT, stride=4), :]
            pad_ref[pl.ds(ONE, 1), s] = rows_ref[pl.ds(92 + c + 2 * half, 1), :]
        put_first(net, pad_ref, w1_ref)
        if net == C0:
            hi = pad_ref[16:24, :].astype(bf).astype(f32)
            lo = pad_ref[16:24, :] - hi
            block = jnp.concatenate([hi, hi, lo], 1)
            w1a_ref[...] = jnp.concatenate([block, jnp.zeros_like(block)], 0).astype(bf)
        w2 = jnp.concatenate(
            [rows_ref[pl.ds(96 + c, UNITS, stride=4), :], rows_ref[pl.ds(98 + c, UNITS, stride=4), :]], 1
        )
        put_square(net, w2, w2f_ref, w2b_ref)
        put_column(b2_ref, net, rows_ref[1120 + c : 1121 + c, :], rows_ref[1122 + c : 1123 + c, :], 0.5)
        put_column(w3_ref, net, rows_ref[1124 + c : 1125 + c, :], rows_ref[1126 + c : 1127 + c, :], 1.0)
        b3_ref[net] = jnp.broadcast_to(critic_ref[c : c + 1, PC - 1 : PC], (1, 128))


def head_maps(j):
    k = lax.broadcasted_iota(jnp.int32, (UNITS, 16), 0)
    r = lax.broadcasted_iota(jnp.int32, (UNITS, 16), 1)
    row = ((k * ACT + j) // 128) == r
    k = lax.broadcasted_iota(jnp.int32, (UNITS, 128), 0)
    l = lax.broadcasted_iota(jnp.int32, (UNITS, 128), 1)
    lane = ((k * ACT + j) % 128) == l
    return row.astype(f32), lane


def head_of(flat):
    hi = flat.astype(bf).astype(f32)
    out = []
    for part in (hi, flat - hi):
        part = part.astype(bf)
        spread = []
        for j in range(ACT):
            row, lane = head_maps(j)
            spread.append(jnp.where(lane, dot(row.astype(bf), part), 0.0).astype(bf))
        r = lax.broadcasted_iota(jnp.int32, (16, 128 * ACT), 0)
        l = lax.broadcasted_iota(jnp.int32, (16, 128 * ACT), 1)
        take = ((l // 128) == (r - 1)).astype(f32).astype(bf)
        out.append(dot_nt(take, jnp.concatenate(spread, 1))[:8])
    return out


def head_back(turned):
    out = jnp.zeros((16, 128), f32)
    for j in range(ACT):
        row, lane = head_maps(j)
        picked = jnp.transpose(row) * turned[j + 1 : j + 2, :]
        out = out + dot_exact(picked, lane.astype(f32), ((1,), (0,)))
    return out


def prepare_actor(net, actor_ref, rows_ref, pad_ref, w1_ref, w2f_ref, w2b_ref, b2_ref, w3t_ref, w3b_ref, b3a_ref):
    whole = PA // 1024
    for t in range(whole):
        rows_ref[8 * t : 8 * t + 8, :] = actor_ref[pl.ds(1024 * t, 1024)].reshape(8, 128)
    rest = (PA - 1024 * whole) // 128
    rows_ref[8 * whole : 8 * whole + rest, :] = actor_ref[pl.ds(1024 * whole, 128 * rest)].reshape(rest, 128)
    rows_ref[562:563, 0:ACT] = actor_ref[pl.ds(562 * 128, ACT)].reshape(1, ACT)
    start = NEXT if net == AT else 0
    pad_ref[...] = jnp.zeros_like(pad_ref)
    for half in range(2):
        s = pl.ds(128 * half, 128)
        pad_ref[pl.ds(start, OBS), s] = rows_ref[pl.ds(half, OBS, stride=2), :]
        pad_ref[pl.ds(ONE, 1), s] = rows_ref[pl.ds(34 + half, 1), :]
    put_first(net, pad_ref, w1_ref)
    w2 = jnp.concatenate([rows_ref[pl.ds(36, UNITS, stride=2), :], rows_ref[pl.ds(37, UNITS, stride=2), :]], 1)
    put_square(net, w2, w2f_ref, w2b_ref)
    put_column(b2_ref, net, rows_ref[548:549, :], rows_ref[549:550, :], 0.5)
    flat = jnp.concatenate([rows_ref[550:562, :], jnp.zeros((4, 128), f32)], 0)
    hi, lo = head_of(flat)
    block = jnp.concatenate([hi, hi, lo], 1)
    w3t_ref[net - A] = jnp.concatenate([block, jnp.zeros_like(block)], 0).astype(bf)
    if net == A:
        stacked = jnp.concatenate([hi, hi, lo, jnp.zeros((104, UNITS), f32)], 0)
        w3b_ref[...] = (0.5 * jnp.transpose(stacked)).astype(bf)
    bias = column(rows_ref[562:563, :])
    b3a_ref[net - A] = jnp.zeros((8, 128), f32)
    b3a_ref[net - A, 1 : 1 + ACT, :] = bias[:ACT]


def act(zh):
    u = jnp.tanh(zh) + 1.0
    return u, zh * u


def slope(u, s):
    return u + s * (2.0 - u)


class Step:
    def __init__(self, i, width, x_ref, weights):
        (
            self.w1, self.w2f, self.w2b, self.b2, self.w3, self.b3, self.w3t, self.w3b, self.b3a, self.w1a,
        ) = weights
        self.i, self.width = i, width
        self.lanes = pl.ds(pl.multiple_of(i * width, width), width)
        self.x = x_ref[:, self.lanes]
        self.x3 = three(self.x)
        rows8 = lax.broadcasted_iota(jnp.int32, (8, width), 0)
        self.is_action = (rows8 >= 1) & (rows8 <= ACT)

    def with_action(self, a):
        x = self.x
        return three(jnp.concatenate([x[:16], jnp.where(self.is_action, a, x[16:24]), x[24:]], 0))

    def first(self, net, xx):
        return act(dot(self.w1[net, :, : 3 * FEAT], xx))

    def second(self, net, h3):
        return act(dot(self.w2f[net], h3) + lanes(self.b2[net], self.width))

    def value(self, net, s):
        return jnp.sum(s * lanes(self.w3[net], self.width), 0, keepdims=True) + lanes(self.b3[net], self.width)

    def head(self, net, s3):
        return dot(self.w3t[net - A], s3)[:8] + lanes(self.b3a[net - A], self.width)

    def valid(self, count_ref):
        tiles = self.width // 128
        return jnp.concatenate([((self.i * tiles + t) < count_ref[...]).astype(f32) for t in range(tiles)], 1)

    def back(self, net, dz2):
        hi, lo = split(dz2)
        return hi, lo, dot(self.w2b[net], jnp.concatenate([hi, lo, hi], 0))

    def weight_grads(self, net, h1, hi, lo, dz1, g2_ref, g1_ref):
        left = jnp.concatenate([h1[:UNITS], h1[UNITS : 2 * UNITS], h1[:UNITS]], 1)
        g2_ref[net] += dot_nt(left, jnp.concatenate([hi, hi, lo], 1))
        xhi, xlo = self.x3[:FEAT], self.x3[FEAT : 2 * FEAT]
        left = jnp.concatenate(
            [jnp.concatenate([xhi, xlo], 0), jnp.concatenate([xhi, jnp.zeros_like(xlo)], 0)], 1
        )
        a, b = split(dz1)
        g1_ref[net] += dot_nt(left, jnp.concatenate([a, b], 1))


def critic_block(i, width, x_ref, nz_ref, count_ref, weights, prio_ref, grads):
    g2_ref, g1_ref, g3a_ref, db2_ref, dw3_ref, st_ref = grads
    st = Step(i, width, x_ref, weights)
    x, x3 = st.x, st.x3

    u, s = st.first(AT, x3)
    u, s = st.second(AT, three(s))
    next_action = jnp.tanh(st.head(AT, three(s)) + nz_ref[:, st.lanes])

    kept = []
    for net in (C0, C1):
        u, s = st.first(net, x3)
        h1, d1 = three(s), slope(u, s)
        u, s = st.second(net, h1)
        kept.append((h1, d1, s, slope(u, s), st.value(net, s)))

    xt = st.with_action(next_action)
    targets = []
    for net in (T0, T1):
        u, s = st.first(net, xt)
        u, s = st.second(net, three(s))
        targets.append(st.value(net, s))

    y = x[23:24] + 0.99 * x[24:25] * jnp.minimum(targets[0], targets[1])
    valid = st.valid(count_ref)
    delta = [k[4] - y for k in kept]
    prio = valid * jnp.sqrt(delta[0] * delta[0] + 1.0)
    tiles = width // 128
    for t in range(tiles):
        prio_ref[pl.ds(i * tiles + t, 1), :] = prio[:, 128 * t : 128 * (t + 1)]
    st_ref[0:1, :] += fold(valid * (delta[0] * delta[0] + delta[1] * delta[1]))
    st_ref[1:2, :] += fold(valid)
    scaled = valid * SCALE

    for net in (C0, C1):
        h1, d1, s2, d2, _ = kept[net]
        dq = (2.0 * scaled) * delta[net]
        st_ref[2 + net : 3 + net, :] += fold(dq)
        dw3_ref[net] += fold(s2 * dq)
        dz2 = lanes(st.w3[net], width) * (0.5 * dq) * d2
        db2_ref[net] += fold(dz2)
        hi, lo, dh1 = st.back(net, dz2)
        st.weight_grads(net, h1, hi, lo, dh1 * d1, g2_ref, g1_ref)


def actor_block(i, width, x_ref, count_ref, weights, grads):
    g2_ref, g1_ref, g3a_ref, db2_ref, dw3_ref, st_ref = grads
    st = Step(i, width, x_ref, weights)

    u, s = st.first(A, st.x3)
    h1a, d1a = three(s), slope(u, s)
    u, s = st.second(A, h1a)
    h2a, d2a = three(s), slope(u, s)
    policy = jnp.tanh(st.head(A, h2a))

    u, s = st.first(C0, st.with_action(policy))
    d1f = slope(u, s)
    u, s = st.second(C0, three(s))
    d2f, q_policy = slope(u, s), st.value(C0, s)
    valid = st.valid(count_ref)
    st_ref[0:1, :] -= fold(valid * q_policy)

    dz2 = lanes(st.w3[C0], width) * (-0.5 * SCALE * valid) * d2f
    hi, lo, dh1 = st.back(C0, dz2)
    da = dot(st.w1a[...], three(dh1 * d1f))[:8]
    dp = jnp.where(st.is_action, da * (1.0 - policy * policy), 0.0)
    st_ref[8:16, :] += fold(dp)
    hi = dp.astype(bf).astype(f32)
    lo = dp - hi
    zero = jnp.zeros_like(hi)
    stacked = jnp.concatenate([hi, lo, hi, zero], 0).astype(bf)
    left = jnp.concatenate([jnp.concatenate([hi, lo], 0), jnp.concatenate([hi, zero], 0)], 1).astype(bf)
    g3a_ref[...] += dot_nt(left, jnp.concatenate([h2a[:UNITS], h2a[UNITS : 2 * UNITS]], 1))
    dz2 = dot(st.w3b[:, :32], stacked) * d2a
    db2_ref[A] += fold(dz2)
    hi, lo, dh1 = st.back(A, dz2)
    st.weight_grads(A, h1a, hi, lo, dh1 * d1a, g2_ref, g1_ref)


def lane_sums(tile):
    return dot_exact(jnp.ones((8, 128), f32), tile, ((1,), (1,)))


def pack_critics(pack_ref, grads):
    g2_ref, g1_ref, g3a_ref, db2_ref, dw3_ref, st_ref = grads
    lane = lax.broadcasted_iota(jnp.int32, (1, 128), 1)
    sums = jnp.sum(st_ref[...], 1, keepdims=True)
    for c in range(2):
        g1 = g1_ref[c, :FEAT, :] + g1_ref[c, FEAT:, :]
        b2 = lane_sums(db2_ref[c])[0:1]
        w3 = lane_sums(dw3_ref[c])[0:1]
        for half in range(2):
            s = slice(128 * half, 128 * (half + 1))
            at = c + 2 * half
            pack_ref[pl.ds(at, OBS + ACT, stride=4), :] = g1[: OBS + ACT, s]
            pack_ref[at + 92 : at + 93, :] = g1[ONE : ONE + 1, s]
            pack_ref[pl.ds(at + 96, UNITS, stride=4), :] = g2_ref[c, :, s]
            pack_ref[at + 1120 : at + 1121, :] = b2[:, s]
            pack_ref[at + 1124 : at + 1125, :] = w3[:, s]
        pack_ref[c + 1128 : c + 1129, :] = jnp.where(lane == 0, sums[2 + c : 3 + c], 0.0)
    pack_ref[2 * TILES_C : AT_ACTOR, :] = jnp.zeros((AT_ACTOR - 2 * TILES_C, 128), f32)


def pack_actor(pack_ref, grads):
    g2_ref, g1_ref, g3a_ref, db2_ref, dw3_ref, st_ref = grads
    lane = lax.broadcasted_iota(jnp.int32, (1, 128), 1)
    sums = jnp.sum(st_ref[...], 1, keepdims=True)
    g1 = g1_ref[A, :FEAT, :] + g1_ref[A, FEAT:, :]
    b2 = lane_sums(db2_ref[A])[0:1]
    o = AT_ACTOR
    for half in range(2):
        s = slice(128 * half, 128 * (half + 1))
        pack_ref[pl.ds(o + half, OBS, stride=2), :] = g1[:OBS, s]
        pack_ref[o + 34 + half : o + 35 + half, :] = g1[ONE : ONE + 1, s]
        pack_ref[pl.ds(o + 36 + half, UNITS, stride=2), :] = g2_ref[A, :, s]
        pack_ref[o + 548 + half : o + 549 + half, :] = b2[:, s]
    pack_ref[o + 550 : o + 562, :] = head_back(g3a_ref[:8, :] + g3a_ref[8:, :])[:12]
    e = lax.broadcasted_iota(jnp.int32, (8, 128), 1) == lax.broadcasted_iota(jnp.int32, (8, 128), 0) - 1
    pack_ref[o + 562 : o + 563, :] = jnp.sum(jnp.where(e, sums[8:16], 0.0), 0, keepdims=True)
    pack_ref[o + 563 : STAT, :] = jnp.zeros((STAT - o - 563, 128), f32)
    pack_ref[STAT : STAT + 1, :] = jnp.where(lane == 0, sums[0:1], jnp.where(lane == 1, sums[1:2], 0.0))
    pack_ref[STAT + 1 : PACK, :] = jnp.zeros((PACK - STAT - 1, 128), f32)


WEIGHTS = [
    pltpu.VMEM((6, UNITS, 256), bf),
    pltpu.VMEM((6, UNITS, 3 * UNITS), bf),
    pltpu.VMEM((3, UNITS, 3 * UNITS), bf),
    pltpu.VMEM((6, UNITS, 128), f32),
    pltpu.VMEM((6, UNITS, 128), f32),
    pltpu.VMEM((6, 1, 128), f32),
    pltpu.VMEM((2, 16, 3 * UNITS), bf),
    pltpu.VMEM((UNITS, 128), bf),
    pltpu.VMEM((2, 8, 128), f32),
    pltpu.VMEM((16, 3 * UNITS), bf),
]
GRADS = [
    pltpu.VMEM((3, UNITS, UNITS), f32),
    pltpu.VMEM((3, 2 * FEAT, UNITS), f32),
    pltpu.VMEM((16, UNITS), f32),
    pltpu.VMEM((3, UNITS, 128), f32),
    pltpu.VMEM((2, UNITS, 128), f32),
    pltpu.VMEM((16, 128), f32),
]


def drain(ref, sem, copies):
    view = ref.at[pl.ds(0, copies)]
    pltpu.make_async_copy(view, view, sem).wait()


class Sum:
    def __init__(self, g, shard_size, pack_ref, buffers, sems):
        group, shard = lax.axis_index("group"), lax.axis_index("shard")
        self.g, self.per = g, shard_size // 2
        self.core = lax.rem(shard, 2)
        self.chip = group * self.per + shard // 2
        self.sibling = (group, shard + 1 - 2 * self.core)
        self.pack_ref = pack_ref
        self.other, self.half, self.parts, self.mine, self.whole = (b.at[g] for b in buffers)
        self.sems = sems.at[g]

    def remote(self, src, dst, n, to):
        return pltpu.make_async_remote_copy(
            src_ref=src,
            dst_ref=dst,
            send_sem=self.sems.at[2 * n],
            recv_sem=self.sems.at[2 * n + 1],
            device_id=to,
            device_id_type=MESH,
        )

    def to_all(self, src_of, dst, n):
        def send(k, carry):
            peer = lax.rem(self.chip + k, CHIPS)
            to = (peer // self.per, lax.rem(peer, self.per) * 2 + self.core)
            self.remote(src_of(peer), dst, n, to).start()
            return carry

        lax.fori_loop(1, CHIPS, send, 0)

    def swap(self):
        give = pl.multiple_of(self.g * 2 * HALF + (1 - self.core) * HALF, HALF)
        return self.remote(self.pack_ref.at[pl.ds(give, HALF)], self.other, 0, self.sibling)

    def scatter(self):
        keep = pl.multiple_of(self.g * 2 * HALF + self.core * HALF, HALF)
        total = self.pack_ref[pl.ds(keep, HALF), :] + self.other[...]
        self.half[...] = total.reshape(CHIPS, CHUNK, 128)
        self.to_all(lambda peer: self.half.at[peer], self.parts.at[self.chip], 1)

    def spread(self):
        drain(self.half, self.sems.at[2], CHIPS - 1)
        drain(self.parts, self.sems.at[3], CHIPS - 1)
        self.parts[pl.ds(self.chip, 1)] = self.half[pl.ds(self.chip, 1)]
        self.mine[...] = jnp.sum(self.parts[...], 0)
        self.to_all(lambda peer: self.mine, self.whole.at[self.core, self.chip], 2)

    def back(self):
        drain(self.parts, self.sems.at[4], CHIPS - 1)
        drain(self.whole.at[0], self.sems.at[5], CHIPS - 1)
        self.whole[pl.ds(self.core, 1), pl.ds(self.chip, 1)] = self.mine[...][None, None]
        return self.remote(self.whole.at[self.core], self.whole.at[self.core], 3, self.sibling)


def step_kernel(
    group_size,
    shard_size,
    width,
    table_hbm,
    index_hbm,
    noise_hbm,
    count_hbm,
    actor_hbm,
    actor_t_hbm,
    critic_hbm,
    critic_t_hbm,
    prio_ref,
    sum_ref,
    table_ref,
    index_ref,
    noise_ref,
    count_ref,
    actor_ref,
    actor_t_ref,
    critic_ref,
    critic_t_ref,
    in_sems,
    rows_ref,
    picked_ref,
    q_ref,
    nsend,
    nrecv,
    noise_sems,
    x_ref,
    nz_ref,
    flat_ref,
    pad_ref,
    pack_ref,
    other,
    half,
    parts,
    mine,
    whole,
    sems,
    *scratch,
):
    weights, grads = scratch[: len(WEIGHTS)], scratch[len(WEIGHTS) :]
    w1_ref, w2f_ref, w2b_ref, b2_ref, w3_ref, b3_ref, w3t_ref, w3b_ref, b3a_ref, w1a_ref = weights
    me = lax.axis_index("group") * shard_size + lax.axis_index("shard")

    def device(k):
        peer = lax.rem(me + k, DEVS)
        return peer, (peer // shard_size, lax.rem(peer, shard_size))

    loads = [
        pltpu.make_async_copy(src, dst, in_sems.at[n])
        for n, (src, dst) in enumerate(
            (
                (noise_hbm, noise_ref),
                (critic_t_hbm, critic_t_ref),
                (actor_t_hbm, actor_t_ref),
                (critic_hbm, critic_ref),
                (actor_hbm, actor_ref),
                (count_hbm, count_ref),
                (table_hbm, table_ref),
                (index_hbm, index_ref),
            )
        )
    ]
    for load in loads:
        load.start()

    barrier = pltpu.get_barrier_semaphore()

    def greet(k, carry):
        pl.semaphore_signal(barrier, inc=1, device_id=device(k)[1], device_id_type=MESH)
        return carry

    lax.fori_loop(1, DEVS, greet, 0)
    for ref in grads:
        ref[...] = jnp.zeros_like(ref)
    loads[0].wait()
    turn_noise(noise_ref, q_ref, nsend)
    for n, first, ref in ((1, T0, critic_t_ref), (3, C0, critic_ref)):
        loads[n].wait()
        prepare_critics(
            ref, flat_ref, pad_ref, first, w1_ref, w2f_ref, w2b_ref, b2_ref, w3_ref, b3_ref, w1a_ref
        )
    for n, net, ref in ((2, AT, actor_t_ref), (4, A, actor_ref)):
        loads[n].wait()
        prepare_actor(net, ref, flat_ref, pad_ref, w1_ref, w2f_ref, w2b_ref, b2_ref, w3t_ref, w3b_ref, b3a_ref)
    for n in (5, 6, 7):
        loads[n].wait()

    pl.semaphore_wait(barrier, DEVS - 1)

    def send(k):
        peer, to = device(k)
        pltpu.make_async_remote_copy(
            src_ref=nsend.at[peer],
            dst_ref=nrecv.at[me],
            send_sem=noise_sems.at[0],
            recv_sem=noise_sems.at[1],
            device_id=to,
            device_id_type=MESH,
        ).start()

    steps = R_DEV // TURN
    each = DEVS // steps

    def turn(i, carry):
        turn_table(i, table_ref, rows_ref)
        for j in range(each):
            send(1 + i * each + j)
        return carry

    lax.fori_loop(0, steps - 1, turn, 0)
    turn_table(steps - 1, table_ref, rows_ref)
    for j in range(each - 1):
        send(1 + (steps - 1) * each + j)
    pick_rows(index_ref, rows_ref, picked_ref, x_ref)
    drain(nsend, noise_sems.at[0], DEVS - 1)
    drain(nrecv, noise_sems.at[1], DEVS - 1)
    nrecv[pl.ds(me, 1)] = nsend[pl.ds(me, 1)]
    noise_back(nrecv, nz_ref)

    def critics(i, carry):
        critic_block(i, width, x_ref, nz_ref, count_ref, weights, prio_ref, grads)
        return carry

    blocks = N // width
    lax.fori_loop(0, blocks, critics, 0)
    pack_critics(pack_ref, grads)

    buffers = (other, half, parts, mine, whole)
    early = Sum(0, shard_size, pack_ref, buffers, sems)
    late = Sum(1, shard_size, pack_ref, buffers, sems)
    swap = early.swap()
    swap.start()
    back = early.back
    for i in range(blocks):
        actor_block(i, width, x_ref, count_ref, weights, grads)
        if i == 0:
            swap.wait()
            early.scatter()
        elif i == 1:
            early.spread()
        elif i == 2:
            back = early.back()
            back.start()
    pack_actor(pack_ref, grads)
    swap = late.swap()
    swap.start()
    back.wait()
    swap.wait()
    late.scatter()
    sum_ref[: 2 * HALF, :] = whole[0].reshape(2 * HALF, 128)
    late.spread()
    back = late.back()
    back.start()
    back.wait()
    sum_ref[2 * HALF :, :] = whole[1].reshape(2 * HALF, 128)


def update(weight, grad, momentum, average, target):
    momentum_new = 0.9 * momentum + grad
    weight_new = weight - 0.1 * (grad + 0.9 * momentum_new)
    average_new = 0.99 * average + 0.01 * weight_new
    target_new = 0.005 * weight_new + 0.995 * target
    return (weight_new, momentum_new, average_new, target_new, weight_new.astype(bf))


def grads_kernel(sum_ref, prio_in, ga_ref, gc_ref, stat_ref, prio_ref):
    stat = sum_ref[STAT : STAT + 1, :]
    factor = (1.0 / SCALE) / stat[:, 1:2]
    stat_ref[...] = stat
    prio_ref[...] = prio_in[...]
    ga_ref[...] = sum_ref[AT_ACTOR : AT_ACTOR + ROWS_A, :] * factor
    for t in range(TILES_C):
        gc_ref[:, 128 * t : 128 * (t + 1)] = sum_ref[2 * t : 2 * t + 2, :] * factor


def local(
    group_size,
    shard_size,
    replay,
    sample_index,
    pair_count,
    noise,
    actor,
    critic,
    actor_momentum,
    critic_momentum,
    actor_average,
    critic_average,
    actor_target,
    critic_target,
):
    any_ = pl.BlockSpec(memory_space=pl.ANY)
    prio, total = pl.pallas_call(
        functools.partial(step_kernel, group_size, shard_size, WIDTH),
        out_shape=(SDS((CAP, DEVS), f32), SDS((PACK, 128), f32)),
        in_specs=[any_] * 8,
        out_specs=(VM, VM),
        scratch_shapes=[
            pltpu.VMEM((ROW, R_DEV), f32),
            pltpu.SMEM((CAP, DEVS), jnp.int32),
            pltpu.VMEM((ACT, CAP, DEVS), f32),
            pltpu.VMEM((1, DEVS), jnp.int32),
            pltpu.VMEM((PA,), f32),
            pltpu.VMEM((PA,), f32),
            pltpu.VMEM((2, PC), f32),
            pltpu.VMEM((2, PC), f32),
            pltpu.SemaphoreType.DMA((8,)),
            pltpu.VMEM((R_DEV, 128), f32),
            pltpu.VMEM((128, 128), f32),
            pltpu.VMEM((256, 128), f32),
            pltpu.VMEM((DEVS, 2, 128), f32),
            pltpu.VMEM((DEVS, 2, 128), f32),
            pltpu.SemaphoreType.DMA((2,)),
            pltpu.VMEM((FEAT, N), f32),
            pltpu.VMEM((8, N), f32),
            pltpu.VMEM((2 * TILES_C + 6, 128), f32),
            pltpu.VMEM((FEAT, 256), f32),
            pltpu.VMEM((PACK, 128), f32),
            pltpu.VMEM((2, HALF, 128), f32),
            pltpu.VMEM((2, CHIPS, CHUNK, 128), f32),
            pltpu.VMEM((2, CHIPS, CHUNK, 128), f32),
            pltpu.VMEM((2, CHUNK, 128), f32),
            pltpu.VMEM((2, 2, CHIPS, CHUNK, 128), f32),
            pltpu.SemaphoreType.DMA((2, 8)),
        ]
        + WEIGHTS
        + GRADS,
        compiler_params=pltpu.CompilerParams(
            collective_id=0, has_side_effects=True, vmem_limit_bytes=56 << 20
        ),
        name="td3_step",
    )(
        replay.T,
        sample_index[0].T,
        jnp.transpose(noise[0], (2, 1, 0)),
        pair_count,
        actor,
        actor_target,
        critic,
        critic_target,
    )
    ga, gc, stat, prio = pl.pallas_call(
        grads_kernel,
        out_shape=(
            SDS((ROWS_A, 128), f32),
            SDS((2, TILES_C * 128), f32),
            SDS((1, 128), f32),
            SDS((CAP, DEVS), f32),
        ),
        in_specs=[VM, VM],
        out_specs=(VM, VM, VM, VM),
        name="unpack_grads",
    )(total, prio)
    actor_out = update(actor, ga.reshape(-1)[:PA], actor_momentum, actor_average, actor_target)
    critic_out = update(critic, gc[:, :PC], critic_momentum, critic_average, critic_target)
    outs = [stat[0, :2], prio.T[None]]
    for one, two in zip(actor_out, critic_out):
        outs += [one, two]
    return tuple(outs)


def solution(mesh):
    rows = ("group", "shard")
    in_specs = (P(rows, None), P(rows, None, None), P(rows, None), P(rows, None, None, None)) + (P(),) * 8
    out_specs = (P(), P(rows, None, None)) + (P(),) * 10
    body = functools.partial(local, mesh.shape["group"], mesh.shape["shard"])
    return jax.shard_map(body, mesh=mesh, in_specs=in_specs, out_specs=out_specs, check_vma=False)
```

```python
import functools

import jax
import jax.numpy as jnp
from jax import lax
from jax.experimental import pallas as pl
from jax.experimental.pallas import tpu as pltpu
from jax.sharding import PartitionSpec as P

OBS = 17
ACT = 6
UNITS = 256
CAP = 32
DEVS = 128
R_DEV = 8192
ROW = 42
PA = 71942
PC = 72193
N = DEVS * CAP

bf = jnp.bfloat16
f32 = jnp.float32
MESH = pl.DeviceIdType.MESH
VM = pl.BlockSpec(memory_space=pltpu.VMEM)
SDS = jax.ShapeDtypeStruct

SCALE = 2.0**-19
C0, C1, A, AT, T0, T1 = range(6)
FEAT = 48
ONE = 42
NEXT = 25

TILES_C = 565
W2_ROW, W2_END = 96, 1120
REST = 1024
STAT = 1130
AT_ACTOR = 1136
ROWS_A = 563
CHIPS = DEVS // 2
CHUNK = 8
PACK = AT_ACTOR + 2 * CHIPS * CHUNK
GROUPS = ((0, CHIPS, 1), (REST, 7, 9), (AT_ACTOR, CHIPS, 1))
TURN = 512
WIDTH = 1024


def critic_row(r):
    return r - W2_ROW if W2_ROW <= r < W2_END else r + REST if r < W2_ROW else r


def dot(a, b):
    return lax.dot_general(a, b, (((1,), (0,)), ((), ())), preferred_element_type=f32)


def dot_nt(a, b):
    return lax.dot_general(a, b, (((1,), (1,)), ((), ())), preferred_element_type=f32)


def dot_exact(a, b, dims):
    return lax.dot_general(a, b, (dims, ((), ())), precision=lax.Precision.HIGHEST, preferred_element_type=f32)


def split(v):
    hi = v.astype(bf)
    return hi, (v - hi.astype(f32)).astype(bf)


def three(v):
    hi, lo = split(v)
    return jnp.concatenate([hi, lo, hi], 0)


def lanes(tile, width):
    return jnp.concatenate([tile] * (width // 128), 1)


def fold(v):
    out = v[:, :128]
    for i in range(1, v.shape[1] // 128):
        out = out + v[:, 128 * i : 128 * (i + 1)]
    return out


def column(row):
    return jnp.transpose(jnp.broadcast_to(row, (128, 128)))


def turn_noise(noise_ref, q_ref, nsend):
    q_ref[...] = jnp.zeros_like(q_ref)
    for j in range(ACT):
        q_ref[pl.ds(j + 1, CAP, stride=8), :] = 0.5 * jnp.tanh(0.4 * noise_ref[j])
    turned = jnp.transpose(q_ref[...])
    nsend[:, 0, :] = turned[:, :128]
    nsend[:, 1, :] = turned[:, 128:]


def noise_back(nrecv, nz_ref):
    back = jnp.transpose(jnp.concatenate([nrecv[:, 0, :], nrecv[:, 1, :]], 1))
    for c in range(CAP):
        nz_ref[:, 128 * c : 128 * (c + 1)] = back[8 * c : 8 * (c + 1), :]


def turn_table(i, table_ref, rows_ref):
    s = pl.ds(pl.multiple_of(i * TURN, TURN), TURN)
    v = jnp.concatenate([table_ref[:, s], jnp.zeros((128 - ROW, TURN), f32)], 0)
    rows_ref[s, :] = jnp.transpose(v)


def pick_rows(block, width, index_ref, rows_ref, picked_ref, x_ref):
    ones = lax.broadcasted_iota(jnp.int32, (8, 128), 0) == (ONE - 40)
    tiles = width // 128
    for t in range(tiles):
        c = block * tiles + t
        for d in range(DEVS):
            picked_ref[t, d : d + 1, :] = rows_ref[pl.ds(index_ref[c, d], 1), :]
        turned = jnp.transpose(picked_ref[t])
        s = pl.ds(pl.multiple_of(c * 128, 128), 128)
        x_ref[0:40, s] = turned[0:40]
        x_ref[40:48, s] = jnp.where(ones, 1.0, turned[40:48])


def put_square(net, w2, w2f_ref, w2b_ref):
    w2 = 0.5 * w2
    turned = jnp.transpose(w2)
    hi, lo = split(turned)
    w2f_ref[net] = jnp.concatenate([hi, hi, lo], 1)
    if net in (C0, C1, A):
        hi, lo = split(w2)
        w2b_ref[net] = jnp.concatenate([hi, hi, lo], 1)


def put_first(net, pad_ref, w1_ref):
    w1 = 0.5 * pad_ref[...]
    hi = w1.astype(bf).astype(f32)
    lo = w1 - hi
    stacked = jnp.concatenate([hi, hi, lo, jnp.zeros((256 - 3 * FEAT, 256), f32)], 0)
    w1_ref[net] = jnp.transpose(stacked).astype(bf)


def put_column(ref, net, left, right, factor):
    ref[net] = jnp.concatenate([column(left * factor), column(right * factor)], 0)


def prepare_critics(critic_ref, rows_ref, pad_ref, first, w1_ref, w2f_ref, w2b_ref, b2_ref, w3_ref, b3_ref, w1a_ref):
    for t in range(TILES_C - 1):
        rows_ref[2 * t : 2 * t + 2, :] = critic_ref[:, 128 * t : 128 * (t + 1)]
    for c in range(2):
        net = first + c
        start = NEXT if first == T0 else 0
        pad_ref[...] = jnp.zeros_like(pad_ref)
        for half in range(2):
            s = pl.ds(128 * half, 128)
            pad_ref[pl.ds(start, OBS), s] = rows_ref[pl.ds(c + 2 * half, OBS, stride=4), :]
            pad_ref[pl.ds(OBS, ACT), s] = rows_ref[pl.ds(c + 2 * half + 4 * OBS, ACT, stride=4), :]
            pad_ref[pl.ds(ONE, 1), s] = rows_ref[pl.ds(92 + c + 2 * half, 1), :]
        put_first(net, pad_ref, w1_ref)
        if net == C0:
            hi = pad_ref[16:24, :].astype(bf).astype(f32)
            lo = pad_ref[16:24, :] - hi
            block = jnp.concatenate([hi, hi, lo], 1)
            w1a_ref[...] = jnp.concatenate([block, jnp.zeros_like(block)], 0).astype(bf)
        w2 = jnp.concatenate(
            [rows_ref[pl.ds(96 + c, UNITS, stride=4), :], rows_ref[pl.ds(98 + c, UNITS, stride=4), :]], 1
        )
        put_square(net, w2, w2f_ref, w2b_ref)
        put_column(b2_ref, net, rows_ref[1120 + c : 1121 + c, :], rows_ref[1122 + c : 1123 + c, :], 0.5)
        put_column(w3_ref, net, rows_ref[1124 + c : 1125 + c, :], rows_ref[1126 + c : 1127 + c, :], 1.0)
        b3_ref[net] = jnp.broadcast_to(critic_ref[c : c + 1, PC - 1 : PC], (1, 128))


def head_maps(j):
    k = lax.broadcasted_iota(jnp.int32, (UNITS, 16), 0)
    r = lax.broadcasted_iota(jnp.int32, (UNITS, 16), 1)
    row = ((k * ACT + j) // 128) == r
    k = lax.broadcasted_iota(jnp.int32, (UNITS, 128), 0)
    l = lax.broadcasted_iota(jnp.int32, (UNITS, 128), 1)
    lane = ((k * ACT + j) % 128) == l
    return row.astype(f32), lane


def head_of(flat):
    hi = flat.astype(bf).astype(f32)
    out = []
    for part in (hi, flat - hi):
        part = part.astype(bf)
        spread = []
        for j in range(ACT):
            row, lane = head_maps(j)
            spread.append(jnp.where(lane, dot(row.astype(bf), part), 0.0).astype(bf))
        r = lax.broadcasted_iota(jnp.int32, (16, 128 * ACT), 0)
        l = lax.broadcasted_iota(jnp.int32, (16, 128 * ACT), 1)
        take = ((l // 128) == (r - 1)).astype(f32).astype(bf)
        out.append(dot_nt(take, jnp.concatenate(spread, 1))[:8])
    return out


def head_back(turned):
    out = jnp.zeros((16, 128), f32)
    for j in range(ACT):
        row, lane = head_maps(j)
        picked = jnp.transpose(row) * turned[j + 1 : j + 2, :]
        out = out + dot_exact(picked, lane.astype(f32), ((1,), (0,)))
    return out


def prepare_actor(net, actor_ref, rows_ref, pad_ref, w1_ref, w2f_ref, w2b_ref, b2_ref, w3t_ref, w3b_ref, b3a_ref):
    whole = PA // 1024
    for t in range(whole):
        rows_ref[8 * t : 8 * t + 8, :] = actor_ref[pl.ds(1024 * t, 1024)].reshape(8, 128)
    rest = (PA - 1024 * whole) // 128
    rows_ref[8 * whole : 8 * whole + rest, :] = actor_ref[pl.ds(1024 * whole, 128 * rest)].reshape(rest, 128)
    rows_ref[562:563, 0:ACT] = actor_ref[pl.ds(562 * 128, ACT)].reshape(1, ACT)
    start = NEXT if net == AT else 0
    pad_ref[...] = jnp.zeros_like(pad_ref)
    for half in range(2):
        s = pl.ds(128 * half, 128)
        pad_ref[pl.ds(start, OBS), s] = rows_ref[pl.ds(half, OBS, stride=2), :]
        pad_ref[pl.ds(ONE, 1), s] = rows_ref[pl.ds(34 + half, 1), :]
    put_first(net, pad_ref, w1_ref)
    w2 = jnp.concatenate([rows_ref[pl.ds(36, UNITS, stride=2), :], rows_ref[pl.ds(37, UNITS, stride=2), :]], 1)
    put_square(net, w2, w2f_ref, w2b_ref)
    put_column(b2_ref, net, rows_ref[548:549, :], rows_ref[549:550, :], 0.5)
    flat = jnp.concatenate([rows_ref[550:562, :], jnp.zeros((4, 128), f32)], 0)
    hi, lo = head_of(flat)
    block = jnp.concatenate([hi, hi, lo], 1)
    w3t_ref[net - A] = jnp.concatenate([block, jnp.zeros_like(block)], 0).astype(bf)
    if net == A:
        stacked = jnp.concatenate([hi, hi, lo, jnp.zeros((104, UNITS), f32)], 0)
        w3b_ref[...] = (0.5 * jnp.transpose(stacked)).astype(bf)
    bias = column(rows_ref[562:563, :])
    b3a_ref[net - A] = jnp.zeros((8, 128), f32)
    b3a_ref[net - A, 1 : 1 + ACT, :] = bias[:ACT]


def act(zh):
    u = jnp.tanh(zh) + 1.0
    return u, zh * u


def slope(u, s):
    return u + s * (2.0 - u)


class Step:
    def __init__(self, i, width, x_ref, weights):
        (
            self.w1, self.w2f, self.w2b, self.b2, self.w3, self.b3, self.w3t, self.w3b, self.b3a, self.w1a,
        ) = weights
        self.i, self.width = i, width
        self.lanes = pl.ds(pl.multiple_of(i * width, width), width)
        self.x = x_ref[:, self.lanes]
        self.x3 = three(self.x)
        rows8 = lax.broadcasted_iota(jnp.int32, (8, width), 0)
        self.is_action = (rows8 >= 1) & (rows8 <= ACT)

    def with_action(self, a):
        x = self.x
        return three(jnp.concatenate([x[:16], jnp.where(self.is_action, a, x[16:24]), x[24:]], 0))

    def first(self, net, xx):
        return act(dot(self.w1[net, :, : 3 * FEAT], xx))

    def second(self, net, h3):
        return act(dot(self.w2f[net], h3) + lanes(self.b2[net], self.width))

    def value(self, net, s):
        return jnp.sum(s * lanes(self.w3[net], self.width), 0, keepdims=True) + lanes(self.b3[net], self.width)

    def head(self, net, s3):
        return dot(self.w3t[net - A], s3)[:8] + lanes(self.b3a[net - A], self.width)

    def valid(self, count_ref):
        tiles = self.width // 128
        return jnp.concatenate([((self.i * tiles + t) < count_ref[...]).astype(f32) for t in range(tiles)], 1)

    def back(self, net, dz2):
        hi, lo = split(dz2)
        return hi, lo, dot(self.w2b[net], jnp.concatenate([hi, lo, hi], 0))

    def weight_grads(self, net, h1, hi, lo, dz1, g2_ref, g1_ref):
        left = jnp.concatenate([h1[:UNITS], h1[UNITS : 2 * UNITS], h1[:UNITS]], 1)
        g2_ref[net] += dot_nt(left, jnp.concatenate([hi, hi, lo], 1))
        xhi, xlo = self.x3[:FEAT], self.x3[FEAT : 2 * FEAT]
        left = jnp.concatenate(
            [jnp.concatenate([xhi, xlo], 0), jnp.concatenate([xhi, jnp.zeros_like(xlo)], 0)], 1
        )
        a, b = split(dz1)
        g1_ref[net] += dot_nt(left, jnp.concatenate([a, b], 1))


def critic_block(i, width, x_ref, nz_ref, count_ref, weights, prio_ref, grads):
    g2_ref, g1_ref, g3a_ref, db2_ref, dw3_ref, st_ref = grads
    st = Step(i, width, x_ref, weights)
    x, x3 = st.x, st.x3

    u, s = st.first(AT, x3)
    u, s = st.second(AT, three(s))
    next_action = jnp.tanh(st.head(AT, three(s)) + nz_ref[:, st.lanes])

    kept = []
    for net in (C0, C1):
        u, s = st.first(net, x3)
        h1, d1 = three(s), slope(u, s)
        u, s = st.second(net, h1)
        kept.append((h1, d1, s, slope(u, s), st.value(net, s)))

    xt = st.with_action(next_action)
    targets = []
    for net in (T0, T1):
        u, s = st.first(net, xt)
        u, s = st.second(net, three(s))
        targets.append(st.value(net, s))

    y = x[23:24] + 0.99 * x[24:25] * jnp.minimum(targets[0], targets[1])
    valid = st.valid(count_ref)
    delta = [k[4] - y for k in kept]
    prio = valid * jnp.sqrt(delta[0] * delta[0] + 1.0)
    tiles = width // 128
    for t in range(tiles):
        prio_ref[pl.ds(i * tiles + t, 1), :] = prio[:, 128 * t : 128 * (t + 1)]
    st_ref[0:1, :] += fold(valid * (delta[0] * delta[0] + delta[1] * delta[1]))
    st_ref[1:2, :] += fold(valid)
    scaled = valid * SCALE

    for net in (C0, C1):
        h1, d1, s2, d2, _ = kept[net]
        dq = (2.0 * scaled) * delta[net]
        st_ref[2 + net : 3 + net, :] += fold(dq)
        dw3_ref[net] += fold(s2 * dq)
        dz2 = lanes(st.w3[net], width) * (0.5 * dq) * d2
        db2_ref[net] += fold(dz2)
        hi, lo, dh1 = st.back(net, dz2)
        st.weight_grads(net, h1, hi, lo, dh1 * d1, g2_ref, g1_ref)


def actor_block(i, width, x_ref, count_ref, weights, grads):
    g2_ref, g1_ref, g3a_ref, db2_ref, dw3_ref, st_ref = grads
    st = Step(i, width, x_ref, weights)

    u, s = st.first(A, st.x3)
    h1a, d1a = three(s), slope(u, s)
    u, s = st.second(A, h1a)
    h2a, d2a = three(s), slope(u, s)
    policy = jnp.tanh(st.head(A, h2a))

    u, s = st.first(C0, st.with_action(policy))
    d1f = slope(u, s)
    u, s = st.second(C0, three(s))
    d2f, q_policy = slope(u, s), st.value(C0, s)
    valid = st.valid(count_ref)
    st_ref[0:1, :] -= fold(valid * q_policy)

    dz2 = lanes(st.w3[C0], width) * (-0.5 * SCALE * valid) * d2f
    hi, lo, dh1 = st.back(C0, dz2)
    da = dot(st.w1a[...], three(dh1 * d1f))[:8]
    dp = jnp.where(st.is_action, da * (1.0 - policy * policy), 0.0)
    st_ref[8:16, :] += fold(dp)
    hi = dp.astype(bf).astype(f32)
    lo = dp - hi
    zero = jnp.zeros_like(hi)
    stacked = jnp.concatenate([hi, lo, hi, zero], 0).astype(bf)
    left = jnp.concatenate([jnp.concatenate([hi, lo], 0), jnp.concatenate([hi, zero], 0)], 1).astype(bf)
    g3a_ref[...] += dot_nt(left, jnp.concatenate([h2a[:UNITS], h2a[UNITS : 2 * UNITS]], 1))
    dz2 = dot(st.w3b[:, :32], stacked) * d2a
    db2_ref[A] += fold(dz2)
    hi, lo, dh1 = st.back(A, dz2)
    st.weight_grads(A, h1a, hi, lo, dh1 * d1a, g2_ref, g1_ref)


def lane_sums(tile):
    return dot_exact(jnp.ones((8, 128), f32), tile, ((1,), (1,)))


def pack_critics(pack_ref, grads):
    g2_ref, g1_ref, g3a_ref, db2_ref, dw3_ref, st_ref = grads
    lane = lax.broadcasted_iota(jnp.int32, (1, 128), 1)
    sums = jnp.sum(st_ref[...], 1, keepdims=True)
    for c in range(2):
        g1 = g1_ref[c, :FEAT, :] + g1_ref[c, FEAT:, :]
        b2 = lane_sums(db2_ref[c])[0:1]
        w3 = lane_sums(dw3_ref[c])[0:1]
        for half in range(2):
            s = slice(128 * half, 128 * (half + 1))
            at = c + 2 * half
            pack_ref[pl.ds(REST + at, OBS + ACT, stride=4), :] = g1[: OBS + ACT, s]
            pack_ref[REST + at + 92 : REST + at + 93, :] = g1[ONE : ONE + 1, s]
            pack_ref[pl.ds(at, UNITS, stride=4), :] = g2_ref[c, :, s]
            pack_ref[at + 1120 : at + 1121, :] = b2[:, s]
            pack_ref[at + 1124 : at + 1125, :] = w3[:, s]
        pack_ref[c + 1128 : c + 1129, :] = jnp.where(lane == 0, sums[2 + c : 3 + c], 0.0)
    pack_ref[STAT : STAT + 1, :] = jnp.where(lane == 0, sums[0:1], jnp.where(lane == 1, sums[1:2], 0.0))
    pack_ref[STAT + 1 : AT_ACTOR, :] = jnp.zeros((AT_ACTOR - STAT - 1, 128), f32)


def pack_actor(pack_ref, grads):
    g2_ref, g1_ref, g3a_ref, db2_ref, dw3_ref, st_ref = grads
    sums = jnp.sum(st_ref[...], 1, keepdims=True)
    g1 = g1_ref[A, :FEAT, :] + g1_ref[A, FEAT:, :]
    b2 = lane_sums(db2_ref[A])[0:1]
    o = AT_ACTOR
    for half in range(2):
        s = slice(128 * half, 128 * (half + 1))
        pack_ref[pl.ds(o + half, OBS, stride=2), :] = g1[:OBS, s]
        pack_ref[o + 34 + half : o + 35 + half, :] = g1[ONE : ONE + 1, s]
        pack_ref[pl.ds(o + 36 + half, UNITS, stride=2), :] = g2_ref[A, :, s]
        pack_ref[o + 548 + half : o + 549 + half, :] = b2[:, s]
    pack_ref[o + 550 : o + 562, :] = head_back(g3a_ref[:8, :] + g3a_ref[8:, :])[:12]
    e = lax.broadcasted_iota(jnp.int32, (8, 128), 1) == lax.broadcasted_iota(jnp.int32, (8, 128), 0) - 1
    pack_ref[o + 562 : o + 563, :] = jnp.sum(jnp.where(e, sums[8:16], 0.0), 0, keepdims=True)
    pack_ref[o + ROWS_A : PACK, :] = jnp.zeros((PACK - o - ROWS_A, 128), f32)


WEIGHTS = [
    pltpu.VMEM((6, UNITS, 256), bf),
    pltpu.VMEM((6, UNITS, 3 * UNITS), bf),
    pltpu.VMEM((3, UNITS, 3 * UNITS), bf),
    pltpu.VMEM((6, UNITS, 128), f32),
    pltpu.VMEM((6, UNITS, 128), f32),
    pltpu.VMEM((6, 1, 128), f32),
    pltpu.VMEM((2, 16, 3 * UNITS), bf),
    pltpu.VMEM((UNITS, 128), bf),
    pltpu.VMEM((2, 8, 128), f32),
    pltpu.VMEM((16, 3 * UNITS), bf),
]
GRADS = [
    pltpu.VMEM((3, UNITS, UNITS), f32),
    pltpu.VMEM((3, 2 * FEAT, UNITS), f32),
    pltpu.VMEM((16, UNITS), f32),
    pltpu.VMEM((3, UNITS, 128), f32),
    pltpu.VMEM((2, UNITS, 128), f32),
    pltpu.VMEM((16, 128), f32),
]


def drain(ref, sem, copies):
    view = ref.at[pl.ds(0, copies)]
    pltpu.make_async_copy(view, view, sem).wait()


class Sum:
    def __init__(self, g, shard_size, pack_ref, total_ref, buffers, sems):
        group, shard = lax.axis_index("group"), lax.axis_index("shard")
        self.first, self.owners, self.apart = GROUPS[g]
        self.rows = self.owners * CHUNK
        self.per = shard_size // 2
        self.core = lax.rem(shard, 2)
        self.chip = group * self.per + shard // 2
        self.sibling = (group, shard + 1 - 2 * self.core)
        self.pack_ref, self.total_ref = pack_ref, total_ref
        self.other, self.half, self.parts, self.mine, self.whole = buffers
        self.sems = sems.at[g]
        if self.owners == CHIPS:
            self.own, self.owner = self.chip, None
        else:
            self.own = self.chip // self.apart
            self.owner = (lax.rem(self.chip, self.apart) == 0) & (self.own < self.owners)

    def remote(self, src, dst, n, to):
        return pltpu.make_async_remote_copy(
            src_ref=src,
            dst_ref=dst,
            send_sem=self.sems.at[2 * n],
            recv_sem=self.sems.at[2 * n + 1],
            device_id=to,
            device_id_type=MESH,
        )

    def at(self, chip):
        return (chip // self.per, lax.rem(chip, self.per) * 2 + self.core)

    def if_owner(self, yes, no):
        if self.owner is None:
            yes()
        else:
            pl.when(self.owner)(yes)
            pl.when(jnp.logical_not(self.owner))(no)

    def swap(self):
        give = pl.multiple_of(self.first + (1 - self.core) * self.rows, 8)
        return self.remote(self.pack_ref.at[pl.ds(give, self.rows)], self.other, 0, self.sibling)

    def scatter(self):
        keep = pl.multiple_of(self.first + self.core * self.rows, 8)
        total = self.pack_ref[pl.ds(keep, self.rows), :] + self.other[...]
        self.half[...] = total.reshape(self.owners, CHUNK, 128)
        if self.owner is None:

            def send(k, carry):
                peer = lax.rem(self.chip + k, CHIPS)
                self.remote(self.half.at[peer], self.parts.at[self.chip], 1, self.at(peer)).start()
                return carry

            lax.fori_loop(1, CHIPS, send, 0)
        else:
            for k in range(self.owners):

                @pl.when(self.chip != k * self.apart)
                def _():
                    self.remote(self.half.at[k], self.parts.at[self.chip], 1, self.at(k * self.apart)).start()

    def spread(self):
        def yes():
            drain(self.half, self.sems.at[2], self.owners - 1)
            drain(self.parts, self.sems.at[3], CHIPS - 1)
            self.parts[pl.ds(self.chip, 1)] = self.half[pl.ds(self.own, 1)]
            self.mine[...] = jnp.sum(self.parts[...], 0)

            def send(k, carry):
                peer = lax.rem(self.chip + k, CHIPS)
                self.remote(self.mine, self.whole.at[self.core, self.own], 2, self.at(peer)).start()
                return carry

            lax.fori_loop(1, CHIPS, send, 0)

        self.if_owner(yes, lambda: drain(self.half, self.sems.at[2], self.owners))

    def back(self):
        def yes():
            drain(self.parts, self.sems.at[4], CHIPS - 1)
            drain(self.whole.at[0], self.sems.at[5], self.owners - 1)
            self.whole[pl.ds(self.core, 1), pl.ds(self.own, 1)] = self.mine[...][None, None]

        self.if_owner(yes, lambda: drain(self.whole.at[0], self.sems.at[5], self.owners))
        return self.remote(self.whole.at[self.core], self.whole.at[self.core], 3, self.sibling)

    def store(self):
        self.total_ref[self.first : self.first + 2 * self.rows, :] = self.whole[...].reshape(2 * self.rows, 128)


def sum_buffers():
    out = []
    for _, owners, _ in GROUPS:
        out += [
            pltpu.VMEM((owners * CHUNK, 128), f32),
            pltpu.VMEM((owners, CHUNK, 128), f32),
            pltpu.VMEM((CHIPS, CHUNK, 128), f32),
            pltpu.VMEM((CHUNK, 128), f32),
            pltpu.VMEM((2, owners, CHUNK, 128), f32),
        ]
    return out


def step_kernel(
    group_size,
    shard_size,
    width,
    table_hbm,
    index_hbm,
    noise_hbm,
    count_hbm,
    actor_hbm,
    actor_t_hbm,
    critic_hbm,
    critic_t_hbm,
    prio_ref,
    sum_ref,
    table_ref,
    index_ref,
    noise_ref,
    count_ref,
    actor_ref,
    actor_t_ref,
    critic_ref,
    critic_t_ref,
    in_sems,
    rows_ref,
    picked_ref,
    q_ref,
    nsend,
    nrecv,
    noise_sems,
    x_ref,
    nz_ref,
    flat_ref,
    pad_ref,
    pack_ref,
    sems,
    *scratch,
):
    weights, grads = scratch[: len(WEIGHTS)], scratch[len(WEIGHTS) : len(WEIGHTS) + len(GRADS)]
    buffers = scratch[len(WEIGHTS) + len(GRADS) :]
    w1_ref, w2f_ref, w2b_ref, b2_ref, w3_ref, b3_ref, w3t_ref, w3b_ref, b3a_ref, w1a_ref = weights
    blocks = N // width
    me = lax.axis_index("group") * shard_size + lax.axis_index("shard")

    def device(k):
        peer = lax.rem(me + k, DEVS)
        return peer, (peer // shard_size, lax.rem(peer, shard_size))

    loads = [
        pltpu.make_async_copy(src, dst, in_sems.at[n])
        for n, (src, dst) in enumerate(
            (
                (table_hbm, table_ref),
                (index_hbm, index_ref),
                (critic_hbm, critic_ref),
                (actor_hbm, actor_ref),
                (count_hbm, count_ref),
                (noise_hbm, noise_ref),
                (critic_t_hbm, critic_t_ref),
                (actor_t_hbm, actor_t_ref),
            )
        )
    ]
    for load in loads:
        load.start()

    barrier = pltpu.get_barrier_semaphore()

    def greet(k, carry):
        pl.semaphore_signal(barrier, inc=1, device_id=device(k)[1], device_id_type=MESH)
        return carry

    lax.fori_loop(1, DEVS, greet, 0)
    for ref in grads:
        ref[...] = jnp.zeros_like(ref)
    loads[0].wait()

    def turn(i, carry):
        turn_table(i, table_ref, rows_ref)
        return carry

    lax.fori_loop(0, R_DEV // TURN, turn, 0)
    loads[1].wait()
    pick_rows(0, width, index_ref, rows_ref, picked_ref, x_ref)
    loads[2].wait()
    prepare_critics(
        critic_ref, flat_ref, pad_ref, C0, w1_ref, w2f_ref, w2b_ref, b2_ref, w3_ref, b3_ref, w1a_ref
    )
    loads[3].wait()
    prepare_actor(
        A, actor_ref, flat_ref, pad_ref, w1_ref, w2f_ref, w2b_ref, b2_ref, w3t_ref, w3b_ref, b3a_ref
    )
    loads[4].wait()
    loads[5].wait()
    turn_noise(noise_ref, q_ref, nsend)

    def send(k, carry):
        peer, to = device(k)
        pltpu.make_async_remote_copy(
            src_ref=nsend.at[peer],
            dst_ref=nrecv.at[me],
            send_sem=noise_sems.at[0],
            recv_sem=noise_sems.at[1],
            device_id=to,
            device_id_type=MESH,
        ).start()
        return carry

    def actors(i, carry):
        pick_rows(lax.rem(i + 1, blocks), width, index_ref, rows_ref, picked_ref, x_ref)
        actor_block(i, width, x_ref, count_ref, weights, grads)

        @pl.when(i == 0)
        def _():
            pl.semaphore_wait(barrier, DEVS - 1)
            lax.fori_loop(1, DEVS, send, 0)

        return carry

    lax.fori_loop(0, blocks, actors, 0)
    pack_actor(pack_ref, grads)
    wide, rest, early = (
        Sum(g, shard_size, pack_ref, sum_ref, buffers[5 * g : 5 * g + 5], sems) for g in range(3)
    )
    early.swap().start()

    loads[6].wait()
    prepare_critics(
        critic_t_ref, flat_ref, pad_ref, T0, w1_ref, w2f_ref, w2b_ref, b2_ref, w3_ref, b3_ref, w1a_ref
    )
    loads[7].wait()
    prepare_actor(
        AT, actor_t_ref, flat_ref, pad_ref, w1_ref, w2f_ref, w2b_ref, b2_ref, w3t_ref, w3b_ref, b3a_ref
    )
    drain(nsend, noise_sems.at[0], DEVS - 1)
    drain(nrecv, noise_sems.at[1], DEVS - 1)
    nrecv[pl.ds(me, 1)] = nsend[pl.ds(me, 1)]
    noise_back(nrecv, nz_ref)

    def critics(i, carry):
        critic_block(i, width, x_ref, nz_ref, count_ref, weights, prio_ref, grads)

        @pl.when(i == 0)
        def _():
            early.swap().wait()
            early.scatter()

        @pl.when(i == 1)
        def _():
            early.spread()

        @pl.when(i == 2)
        def _():
            early.back().start()

        return carry

    lax.fori_loop(0, blocks, critics, 0)
    pack_critics(pack_ref, grads)
    late = (wide, rest)
    for part in late:
        part.swap().start()
    early.remote(early.whole.at[early.core], early.whole.at[early.core], 3, early.sibling).wait()
    for part in late:
        part.swap().wait()
        part.scatter()
    early.store()
    for part in late:
        part.spread()
    backs = [part.back() for part in late]
    for copy in backs:
        copy.start()
    for copy in backs:
        copy.wait()
    for part in late:
        part.store()


def update(weight, grad, momentum, average, target):
    momentum_new = 0.9 * momentum + grad
    weight_new = weight - 0.1 * (grad + 0.9 * momentum_new)
    average_new = 0.99 * average + 0.01 * weight_new
    target_new = 0.005 * weight_new + 0.995 * target
    return (weight_new, momentum_new, average_new, target_new, weight_new.astype(bf))


def update_kernel(sum_ref, prio_in, *refs):
    ins, (stat_ref, prio_ref), outs, grad_ref = refs[:8], refs[8:10], refs[10:20], refs[20]
    stat = sum_ref[STAT : STAT + 1, :]
    factor = (1.0 / SCALE) / stat[:, 1:2]
    stat_ref[...] = stat
    prio_ref[...] = prio_in[...]
    for t in range(TILES_C):
        r = critic_row(2 * t)
        grad_ref[:, 128 * t : 128 * (t + 1)] = sum_ref[r : r + 2, :] * factor

    def critics(s):
        values = update(ins[1][:, s], grad_ref[:, s], ins[3][:, s], ins[5][:, s], ins[7][:, s])
        for ref, value in zip(outs[1::2], values):
            ref[:, s] = value

    def actor(s, grad):
        values = update(ins[0][s], grad, ins[2][s], ins[4][s], ins[6][s])
        for ref, value in zip(outs[0::2], values):
            ref[s] = value

    step = 1024

    def body(i, carry):
        critics(pl.ds(pl.multiple_of(i * step, step), step))
        r = pl.multiple_of(AT_ACTOR + 8 * i, 8)
        actor(pl.ds(pl.multiple_of(i * step, step), step), (sum_ref[pl.ds(r, 8), :] * factor).reshape(step))
        return carry

    lax.fori_loop(0, PA // step, body, 0)
    done = PA // step * step
    critics(pl.ds(done, PC - done))
    r = AT_ACTOR + done // 128
    more = (PA - done) // 128
    actor(pl.ds(done, 128 * more), (sum_ref[r : r + more, :] * factor).reshape(128 * more))
    done += 128 * more
    actor(pl.ds(done, ACT), (sum_ref[r + more : r + more + 1, :ACT] * factor).reshape(ACT))


def local(
    group_size,
    shard_size,
    replay,
    sample_index,
    pair_count,
    noise,
    actor,
    critic,
    actor_momentum,
    critic_momentum,
    actor_average,
    critic_average,
    actor_target,
    critic_target,
):
    any_ = pl.BlockSpec(memory_space=pl.ANY)
    prio, total = pl.pallas_call(
        functools.partial(step_kernel, group_size, shard_size, WIDTH),
        out_shape=(SDS((CAP, DEVS), f32), SDS((PACK, 128), f32)),
        in_specs=[any_] * 8,
        out_specs=(VM, VM),
        scratch_shapes=[
            pltpu.VMEM((ROW, R_DEV), f32),
            pltpu.SMEM((CAP, DEVS), jnp.int32),
            pltpu.VMEM((ACT, CAP, DEVS), f32),
            pltpu.VMEM((1, DEVS), jnp.int32),
            pltpu.VMEM((PA,), f32),
            pltpu.VMEM((PA,), f32),
            pltpu.VMEM((2, PC), f32),
            pltpu.VMEM((2, PC), f32),
            pltpu.SemaphoreType.DMA((8,)),
            pltpu.VMEM((R_DEV, 128), f32),
            pltpu.VMEM((WIDTH // 128, 128, 128), f32),
            pltpu.VMEM((256, 128), f32),
            pltpu.VMEM((DEVS, 2, 128), f32),
            pltpu.VMEM((DEVS, 2, 128), f32),
            pltpu.SemaphoreType.DMA((2,)),
            pltpu.VMEM((FEAT, N), f32),
            pltpu.VMEM((8, N), f32),
            pltpu.VMEM((2 * TILES_C + 6, 128), f32),
            pltpu.VMEM((FEAT, 256), f32),
            pltpu.VMEM((PACK, 128), f32),
            pltpu.SemaphoreType.DMA((3, 8)),
        ]
        + WEIGHTS
        + GRADS
        + sum_buffers(),
        compiler_params=pltpu.CompilerParams(
            collective_id=0, has_side_effects=True, vmem_limit_bytes=56 << 20
        ),
        name="td3_step",
    )(
        replay.T,
        sample_index[0].T,
        jnp.transpose(noise[0], (2, 1, 0)),
        pair_count,
        actor,
        actor_target,
        critic,
        critic_target,
    )
    shapes = [SDS((1, 128), f32), SDS((CAP, DEVS), f32)]
    for kind in (f32, f32, f32, f32, bf):
        shapes += [SDS((PA,), kind), SDS((2, PC), kind)]
    stat, prio, *outs = pl.pallas_call(
        update_kernel,
        out_shape=tuple(shapes),
        in_specs=[VM] * 10,
        out_specs=(VM,) * 12,
        scratch_shapes=[pltpu.VMEM((2, TILES_C * 128), f32)],
        compiler_params=pltpu.CompilerParams(vmem_limit_bytes=24 << 20),
        name="update",
    )(
        total,
        prio,
        actor,
        critic,
        actor_momentum,
        critic_momentum,
        actor_average,
        critic_average,
        actor_target,
        critic_target,
    )
    return (stat[0, :2], prio.T[None], *outs)


def solution(mesh):
    rows = ("group", "shard")
    in_specs = (P(rows, None), P(rows, None, None), P(rows, None), P(rows, None, None, None)) + (P(),) * 8
    out_specs = (P(), P(rows, None, None)) + (P(),) * 10
    body = functools.partial(local, mesh.shape["group"], mesh.shape["shard"])
    return jax.shard_map(body, mesh=mesh, in_specs=in_specs, out_specs=out_specs, check_vma=False)
```

```python
import functools

import jax
import jax.numpy as jnp
from jax import lax
from jax.experimental import pallas as pl
from jax.experimental.pallas import tpu as pltpu
from jax.sharding import PartitionSpec as P

OBS = 17
ACT = 6
UNITS = 256
CAP = 32
DEVS = 128
R_DEV = 8192
ROW = 42
PA = 71942
PC = 72193
N = DEVS * CAP

bf = jnp.bfloat16
f32 = jnp.float32
MESH = pl.DeviceIdType.MESH
VM = pl.BlockSpec(memory_space=pltpu.VMEM)
SDS = jax.ShapeDtypeStruct

SCALE = 2.0**-19
C0, C1, A, AT, T0, T1 = range(6)
FEAT = 48
ONE = 42
NEXT = 25

TILES_C = 565
STAT = 1130
ROWS_A = 563
CHIPS = DEVS // 2
CHUNKS = (9, 5)
AT_ACTOR = 2 * CHIPS * CHUNKS[0]
PACK = AT_ACTOR + 2 * CHIPS * CHUNKS[1]
TURN = 512
WIDTH = 1024
STEPS = sorted(
    ((z, x, y) for z in range(4) for x in range(4) for y in range(4)),
    key=lambda step: -sum(min(n, 4 - n) for n in step),
)[:-1]


def dot(a, b):
    return lax.dot_general(a, b, (((1,), (0,)), ((), ())), preferred_element_type=f32)


def dot_nt(a, b):
    return lax.dot_general(a, b, (((1,), (1,)), ((), ())), preferred_element_type=f32)


def dot_exact(a, b, dims):
    return lax.dot_general(a, b, (dims, ((), ())), precision=lax.Precision.HIGHEST, preferred_element_type=f32)


def split(v):
    hi = v.astype(bf)
    return hi, (v - hi.astype(f32)).astype(bf)


def three(v):
    hi, lo = split(v)
    return jnp.concatenate([hi, lo, hi], 0)


def lanes(tile, width):
    return jnp.concatenate([tile] * (width // 128), 1)


def fold(v):
    out = v[:, :128]
    for i in range(1, v.shape[1] // 128):
        out = out + v[:, 128 * i : 128 * (i + 1)]
    return out


def column(row):
    return jnp.transpose(jnp.broadcast_to(row, (128, 128)))


def turn_noise(noise_ref, q_ref, nsend):
    q_ref[...] = jnp.zeros_like(q_ref)
    for j in range(ACT):
        q_ref[pl.ds(j + 1, CAP, stride=8), :] = 0.5 * jnp.tanh(0.4 * noise_ref[j])
    turned = jnp.transpose(q_ref[...])
    nsend[:, 0, :] = turned[:, :128]
    nsend[:, 1, :] = turned[:, 128:]


def noise_back(nrecv, nz_ref):
    back = jnp.transpose(jnp.concatenate([nrecv[:, 0, :], nrecv[:, 1, :]], 1))
    for c in range(CAP):
        nz_ref[:, 128 * c : 128 * (c + 1)] = back[8 * c : 8 * (c + 1), :]


def turn_table(i, table_ref, rows_ref):
    s = pl.ds(pl.multiple_of(i * TURN, TURN), TURN)
    v = jnp.concatenate([table_ref[:, s], jnp.zeros((128 - ROW, TURN), f32)], 0)
    rows_ref[s, :] = jnp.transpose(v)


def pick_rows(block, width, index_ref, rows_ref, picked_ref):
    tiles = width // 128
    for t in range(tiles):
        for d in range(DEVS):
            picked_ref[t, d : d + 1, :] = rows_ref[pl.ds(index_ref[block * tiles + t, d], 1), :]


def turn_rows(width, picked_ref):
    parts = [jnp.transpose(picked_ref[t])[:FEAT] for t in range(width // 128)]
    x = jnp.concatenate(parts, 1)
    ones = lax.broadcasted_iota(jnp.int32, (8, width), 0) == (ONE - 40)
    return jnp.concatenate([x[:40], jnp.where(ones, 1.0, x[40:])], 0)


def put_square(net, w2, w2f_ref, w2b_ref):
    w2 = 0.5 * w2
    turned = jnp.transpose(w2)
    hi, lo = split(turned)
    w2f_ref[net] = jnp.concatenate([hi, hi, lo], 1)
    if net in (C0, C1, A):
        hi, lo = split(w2)
        w2b_ref[net] = jnp.concatenate([hi, hi, lo], 1)


def put_first(net, pad_ref, w1_ref):
    w1 = 0.5 * pad_ref[...]
    hi = w1.astype(bf).astype(f32)
    lo = w1 - hi
    stacked = jnp.concatenate([hi, hi, lo, jnp.zeros((256 - 3 * FEAT, 256), f32)], 0)
    w1_ref[net] = jnp.transpose(stacked).astype(bf)


def put_column(ref, net, left, right, factor):
    ref[net] = jnp.concatenate([column(left * factor), column(right * factor)], 0)


def prepare_critics(critic_ref, rows_ref, pad_ref, first, w1_ref, w2f_ref, w2b_ref, b2_ref, w3_ref, b3_ref, w1a_ref):
    for t in range(TILES_C - 1):
        rows_ref[2 * t : 2 * t + 2, :] = critic_ref[:, 128 * t : 128 * (t + 1)]
    for c in range(2):
        net = first + c
        start = NEXT if first == T0 else 0
        pad_ref[...] = jnp.zeros_like(pad_ref)
        for half in range(2):
            s = pl.ds(128 * half, 128)
            pad_ref[pl.ds(start, OBS), s] = rows_ref[pl.ds(c + 2 * half, OBS, stride=4), :]
            pad_ref[pl.ds(OBS, ACT), s] = rows_ref[pl.ds(c + 2 * half + 4 * OBS, ACT, stride=4), :]
            pad_ref[pl.ds(ONE, 1), s] = rows_ref[pl.ds(92 + c + 2 * half, 1), :]
        put_first(net, pad_ref, w1_ref)
        if net == C0:
            hi = pad_ref[16:24, :].astype(bf).astype(f32)
            lo = pad_ref[16:24, :] - hi
            block = jnp.concatenate([hi, hi, lo], 1)
            w1a_ref[...] = jnp.concatenate([block, jnp.zeros_like(block)], 0).astype(bf)
        w2 = jnp.concatenate(
            [rows_ref[pl.ds(96 + c, UNITS, stride=4), :], rows_ref[pl.ds(98 + c, UNITS, stride=4), :]], 1
        )
        put_square(net, w2, w2f_ref, w2b_ref)
        put_column(b2_ref, net, rows_ref[1120 + c : 1121 + c, :], rows_ref[1122 + c : 1123 + c, :], 0.5)
        put_column(w3_ref, net, rows_ref[1124 + c : 1125 + c, :], rows_ref[1126 + c : 1127 + c, :], 1.0)
        b3_ref[net] = jnp.broadcast_to(critic_ref[c : c + 1, PC - 1 : PC], (1, 128))


def head_maps(j):
    k = lax.broadcasted_iota(jnp.int32, (UNITS, 16), 0)
    r = lax.broadcasted_iota(jnp.int32, (UNITS, 16), 1)
    row = ((k * ACT + j) // 128) == r
    k = lax.broadcasted_iota(jnp.int32, (UNITS, 128), 0)
    l = lax.broadcasted_iota(jnp.int32, (UNITS, 128), 1)
    lane = ((k * ACT + j) % 128) == l
    return row.astype(f32), lane


def head_of(flat):
    hi = flat.astype(bf).astype(f32)
    out = []
    for part in (hi, flat - hi):
        part = part.astype(bf)
        spread = []
        for j in range(ACT):
            row, lane = head_maps(j)
            spread.append(jnp.where(lane, dot(row.astype(bf), part), 0.0).astype(bf))
        r = lax.broadcasted_iota(jnp.int32, (16, 128 * ACT), 0)
        l = lax.broadcasted_iota(jnp.int32, (16, 128 * ACT), 1)
        take = ((l // 128) == (r - 1)).astype(f32).astype(bf)
        out.append(dot_nt(take, jnp.concatenate(spread, 1))[:8])
    return out


def head_back(turned):
    out = jnp.zeros((16, 128), f32)
    for j in range(ACT):
        row, lane = head_maps(j)
        picked = jnp.transpose(row) * turned[j + 1 : j + 2, :]
        out = out + dot_exact(picked, lane.astype(f32), ((1,), (0,)))
    return out


def prepare_actor(net, actor_ref, rows_ref, pad_ref, w1_ref, w2f_ref, w2b_ref, b2_ref, w3t_ref, w3b_ref, b3a_ref):
    whole = PA // 1024
    for t in range(whole):
        rows_ref[8 * t : 8 * t + 8, :] = actor_ref[pl.ds(1024 * t, 1024)].reshape(8, 128)
    rest = (PA - 1024 * whole) // 128
    rows_ref[8 * whole : 8 * whole + rest, :] = actor_ref[pl.ds(1024 * whole, 128 * rest)].reshape(rest, 128)
    rows_ref[562:563, 0:ACT] = actor_ref[pl.ds(562 * 128, ACT)].reshape(1, ACT)
    start = NEXT if net == AT else 0
    pad_ref[...] = jnp.zeros_like(pad_ref)
    for half in range(2):
        s = pl.ds(128 * half, 128)
        pad_ref[pl.ds(start, OBS), s] = rows_ref[pl.ds(half, OBS, stride=2), :]
        pad_ref[pl.ds(ONE, 1), s] = rows_ref[pl.ds(34 + half, 1), :]
    put_first(net, pad_ref, w1_ref)
    w2 = jnp.concatenate([rows_ref[pl.ds(36, UNITS, stride=2), :], rows_ref[pl.ds(37, UNITS, stride=2), :]], 1)
    put_square(net, w2, w2f_ref, w2b_ref)
    put_column(b2_ref, net, rows_ref[548:549, :], rows_ref[549:550, :], 0.5)
    flat = jnp.concatenate([rows_ref[550:562, :], jnp.zeros((4, 128), f32)], 0)
    hi, lo = head_of(flat)
    block = jnp.concatenate([hi, hi, lo], 1)
    w3t_ref[net - A] = jnp.concatenate([block, jnp.zeros_like(block)], 0).astype(bf)
    if net == A:
        stacked = jnp.concatenate([hi, hi, lo, jnp.zeros((104, UNITS), f32)], 0)
        w3b_ref[...] = (0.5 * jnp.transpose(stacked)).astype(bf)
    bias = column(rows_ref[562:563, :])
    b3a_ref[net - A] = jnp.zeros((8, 128), f32)
    b3a_ref[net - A, 1 : 1 + ACT, :] = bias[:ACT]


def act(zh):
    u = jnp.tanh(zh) + 1.0
    return u, zh * u


def slope(u, s):
    return u + s * (2.0 - u)


class Step:
    def __init__(self, i, width, x, weights):
        (
            self.w1, self.w2f, self.w2b, self.b2, self.w3, self.b3, self.w3t, self.w3b, self.b3a, self.w1a,
        ) = weights
        self.i, self.width = i, width
        self.lanes = pl.ds(pl.multiple_of(i * width, width), width)
        self.x = x
        self.x3 = three(self.x)
        rows8 = lax.broadcasted_iota(jnp.int32, (8, width), 0)
        self.is_action = (rows8 >= 1) & (rows8 <= ACT)

    def with_action(self, a):
        x = self.x
        return three(jnp.concatenate([x[:16], jnp.where(self.is_action, a, x[16:24]), x[24:]], 0))

    def first(self, net, xx):
        return act(dot(self.w1[net, :, : 3 * FEAT], xx))

    def second(self, net, h3):
        return act(dot(self.w2f[net], h3) + lanes(self.b2[net], self.width))

    def value(self, net, s):
        return jnp.sum(s * lanes(self.w3[net], self.width), 0, keepdims=True) + lanes(self.b3[net], self.width)

    def head(self, net, s3):
        return dot(self.w3t[net - A], s3)[:8] + lanes(self.b3a[net - A], self.width)

    def valid(self, count_ref):
        tiles = self.width // 128
        return jnp.concatenate([((self.i * tiles + t) < count_ref[...]).astype(f32) for t in range(tiles)], 1)

    def back(self, net, dz2):
        hi, lo = split(dz2)
        return hi, lo, dot(self.w2b[net], jnp.concatenate([hi, lo, hi], 0))

    def weight_grads(self, net, h1, hi, lo, dz1, g2_ref, g1_ref):
        left = jnp.concatenate([h1[:UNITS], h1[UNITS : 2 * UNITS], h1[:UNITS]], 1)
        g2_ref[net] += dot_nt(left, jnp.concatenate([hi, hi, lo], 1))
        xhi, xlo = self.x3[:FEAT], self.x3[FEAT : 2 * FEAT]
        left = jnp.concatenate(
            [jnp.concatenate([xhi, xlo], 0), jnp.concatenate([xhi, jnp.zeros_like(xlo)], 0)], 1
        )
        a, b = split(dz1)
        g1_ref[net] += dot_nt(left, jnp.concatenate([a, b], 1))


def critic_block(i, width, x, nz_ref, count_ref, weights, prio_ref, grads):
    g2_ref, g1_ref, g3a_ref, db2_ref, dw3_ref, st_ref = grads
    st = Step(i, width, x, weights)
    x3 = st.x3

    u, s = st.first(AT, x3)
    u, s = st.second(AT, three(s))
    next_action = jnp.tanh(st.head(AT, three(s)) + nz_ref[:, st.lanes])

    kept = []
    for net in (C0, C1):
        u, s = st.first(net, x3)
        h1, d1 = three(s), slope(u, s)
        u, s = st.second(net, h1)
        kept.append((h1, d1, s, slope(u, s), st.value(net, s)))

    xt = st.with_action(next_action)
    targets = []
    for net in (T0, T1):
        u, s = st.first(net, xt)
        u, s = st.second(net, three(s))
        targets.append(st.value(net, s))

    y = x[23:24] + 0.99 * x[24:25] * jnp.minimum(targets[0], targets[1])
    valid = st.valid(count_ref)
    delta = [k[4] - y for k in kept]
    prio = valid * jnp.sqrt(delta[0] * delta[0] + 1.0)
    tiles = width // 128
    for t in range(tiles):
        prio_ref[pl.ds(i * tiles + t, 1), :] = prio[:, 128 * t : 128 * (t + 1)]
    st_ref[0:1, :] += fold(valid * (delta[0] * delta[0] + delta[1] * delta[1]))
    st_ref[1:2, :] += fold(valid)
    scaled = valid * SCALE

    for net in (C0, C1):
        h1, d1, s2, d2, _ = kept[net]
        dq = (2.0 * scaled) * delta[net]
        st_ref[2 + net : 3 + net, :] += fold(dq)
        dw3_ref[net] += fold(s2 * dq)
        dz2 = lanes(st.w3[net], width) * (0.5 * dq) * d2
        db2_ref[net] += fold(dz2)
        hi, lo, dh1 = st.back(net, dz2)
        st.weight_grads(net, h1, hi, lo, dh1 * d1, g2_ref, g1_ref)


def actor_block(i, width, x, count_ref, weights, grads):
    g2_ref, g1_ref, g3a_ref, db2_ref, dw3_ref, st_ref = grads
    st = Step(i, width, x, weights)

    u, s = st.first(A, st.x3)
    h1a, d1a = three(s), slope(u, s)
    u, s = st.second(A, h1a)
    h2a, d2a = three(s), slope(u, s)
    policy = jnp.tanh(st.head(A, h2a))

    u, s = st.first(C0, st.with_action(policy))
    d1f = slope(u, s)
    u, s = st.second(C0, three(s))
    d2f, q_policy = slope(u, s), st.value(C0, s)
    valid = st.valid(count_ref)
    st_ref[0:1, :] -= fold(valid * q_policy)

    dz2 = lanes(st.w3[C0], width) * (-0.5 * SCALE * valid) * d2f
    hi, lo, dh1 = st.back(C0, dz2)
    da = dot(st.w1a[...], three(dh1 * d1f))[:8]
    dp = jnp.where(st.is_action, da * (1.0 - policy * policy), 0.0)
    st_ref[8:16, :] += fold(dp)
    hi = dp.astype(bf).astype(f32)
    lo = dp - hi
    zero = jnp.zeros_like(hi)
    stacked = jnp.concatenate([hi, lo, hi, zero], 0).astype(bf)
    left = jnp.concatenate([jnp.concatenate([hi, lo], 0), jnp.concatenate([hi, zero], 0)], 1).astype(bf)
    g3a_ref[...] += dot_nt(left, jnp.concatenate([h2a[:UNITS], h2a[UNITS : 2 * UNITS]], 1))
    dz2 = dot(st.w3b[:, :32], stacked) * d2a
    db2_ref[A] += fold(dz2)
    hi, lo, dh1 = st.back(A, dz2)
    st.weight_grads(A, h1a, hi, lo, dh1 * d1a, g2_ref, g1_ref)


def lane_sums(tile):
    return dot_exact(jnp.ones((8, 128), f32), tile, ((1,), (1,)))


def pack_critics(pack_ref, grads):
    g2_ref, g1_ref, g3a_ref, db2_ref, dw3_ref, st_ref = grads
    lane = lax.broadcasted_iota(jnp.int32, (1, 128), 1)
    sums = jnp.sum(st_ref[...], 1, keepdims=True)
    for c in range(2):
        g1 = g1_ref[c, :FEAT, :] + g1_ref[c, FEAT:, :]
        b2 = lane_sums(db2_ref[c])[0:1]
        w3 = lane_sums(dw3_ref[c])[0:1]
        for half in range(2):
            s = slice(128 * half, 128 * (half + 1))
            at = c + 2 * half
            pack_ref[pl.ds(at, OBS + ACT, stride=4), :] = g1[: OBS + ACT, s]
            pack_ref[at + 92 : at + 93, :] = g1[ONE : ONE + 1, s]
            pack_ref[pl.ds(at + 96, UNITS, stride=4), :] = g2_ref[c, :, s]
            pack_ref[at + 1120 : at + 1121, :] = b2[:, s]
            pack_ref[at + 1124 : at + 1125, :] = w3[:, s]
        pack_ref[c + 1128 : c + 1129, :] = jnp.where(lane == 0, sums[2 + c : 3 + c], 0.0)
    pack_ref[STAT : STAT + 1, :] = jnp.where(lane == 0, sums[0:1], jnp.where(lane == 1, sums[1:2], 0.0))
    pack_ref[STAT + 1 : AT_ACTOR, :] = jnp.zeros((AT_ACTOR - STAT - 1, 128), f32)


def pack_actor(pack_ref, grads):
    g2_ref, g1_ref, g3a_ref, db2_ref, dw3_ref, st_ref = grads
    sums = jnp.sum(st_ref[...], 1, keepdims=True)
    g1 = g1_ref[A, :FEAT, :] + g1_ref[A, FEAT:, :]
    b2 = lane_sums(db2_ref[A])[0:1]
    o = AT_ACTOR
    for half in range(2):
        s = slice(128 * half, 128 * (half + 1))
        pack_ref[pl.ds(o + half, OBS, stride=2), :] = g1[:OBS, s]
        pack_ref[o + 34 + half : o + 35 + half, :] = g1[ONE : ONE + 1, s]
        pack_ref[pl.ds(o + 36 + half, UNITS, stride=2), :] = g2_ref[A, :, s]
        pack_ref[o + 548 + half : o + 549 + half, :] = b2[:, s]
    pack_ref[o + 550 : o + 562, :] = head_back(g3a_ref[:8, :] + g3a_ref[8:, :])[:12]
    e = lax.broadcasted_iota(jnp.int32, (8, 128), 1) == lax.broadcasted_iota(jnp.int32, (8, 128), 0) - 1
    pack_ref[o + 562 : o + 563, :] = jnp.sum(jnp.where(e, sums[8:16], 0.0), 0, keepdims=True)
    pack_ref[o + ROWS_A : PACK, :] = jnp.zeros((PACK - o - ROWS_A, 128), f32)


WEIGHTS = [
    pltpu.VMEM((6, UNITS, 256), bf),
    pltpu.VMEM((6, UNITS, 3 * UNITS), bf),
    pltpu.VMEM((3, UNITS, 3 * UNITS), bf),
    pltpu.VMEM((6, UNITS, 128), f32),
    pltpu.VMEM((6, UNITS, 128), f32),
    pltpu.VMEM((6, 1, 128), f32),
    pltpu.VMEM((2, 16, 3 * UNITS), bf),
    pltpu.VMEM((UNITS, 128), bf),
    pltpu.VMEM((2, 8, 128), f32),
    pltpu.VMEM((16, 3 * UNITS), bf),
]
GRADS = [
    pltpu.VMEM((3, UNITS, UNITS), f32),
    pltpu.VMEM((3, 2 * FEAT, UNITS), f32),
    pltpu.VMEM((16, UNITS), f32),
    pltpu.VMEM((3, UNITS, 128), f32),
    pltpu.VMEM((2, UNITS, 128), f32),
    pltpu.VMEM((16, 128), f32),
]


def drain(ref, sem, copies):
    view = ref.at[pl.ds(0, copies)]
    pltpu.make_async_copy(view, view, sem).wait()


class Place:
    def __init__(self):
        group, shard = lax.axis_index("group"), lax.axis_index("shard")
        self.core = lax.rem(shard, 2)
        z, x, y = group // 4, lax.rem(group, 4), shard // 2
        self.chip = group * 4 + y
        self.sibling = (group, shard + 1 - 2 * self.core)
        self.sibling_at = group * 8 + shard + 1 - 2 * self.core
        self.me = group * 8 + shard
        self.zs, self.xs, self.ys = ([lax.rem(v + n, 4) for n in range(4)] for v in (z, x, y))

    def others(self, other_core=False):
        core = 1 - self.core if other_core else self.core
        for dz, dx, dy in STEPS:
            group = self.zs[dz] * 4 + self.xs[dx]
            yield group * 4 + self.ys[dy], (group, self.ys[dy] * 2 + core)


class Sum:
    def __init__(self, place, g, pack_ref, total_ref, buffers, sems):
        self.place, self.chunk = place, CHUNKS[g]
        self.first = (0, AT_ACTOR)[g]
        self.rows = CHIPS * self.chunk
        self.pack_ref, self.total_ref = pack_ref, total_ref
        self.other, self.half, self.parts, self.mine, self.whole = buffers
        self.sems = sems.at[g]

    def remote(self, src, dst, n, to):
        return pltpu.make_async_remote_copy(
            src_ref=src,
            dst_ref=dst,
            send_sem=self.sems.at[2 * n],
            recv_sem=self.sems.at[2 * n + 1],
            device_id=to,
            device_id_type=MESH,
        )

    def swap(self):
        give = pl.multiple_of(self.first + (1 - self.place.core) * self.rows, 8)
        return self.remote(self.pack_ref.at[pl.ds(give, self.rows)], self.other, 0, self.place.sibling)

    def scatter(self):
        keep = pl.multiple_of(self.first + self.place.core * self.rows, 8)
        total = self.pack_ref[pl.ds(keep, self.rows), :] + self.other[...]
        for j in range(self.chunk):
            self.half[:, j, :] = total[CHIPS * j : CHIPS * (j + 1)]
        chip = self.place.chip
        for peer, device in self.place.others():
            self.remote(self.half.at[peer], self.parts.at[chip], 1, device).start()

    def spread(self):
        chip = self.place.chip
        drain(self.half, self.sems.at[2], CHIPS - 1)
        drain(self.parts, self.sems.at[3], CHIPS - 1)
        self.parts[pl.ds(chip, 1)] = self.half[pl.ds(chip, 1)]
        self.mine[...] = jnp.sum(self.parts[...], 0)
        for _, device in self.place.others():
            self.remote(self.mine, self.whole.at[self.place.core, chip], 2, device).start()

    def back_copy(self):
        ref = self.whole.at[self.place.core]
        return self.remote(ref, ref, 3, self.place.sibling)

    def back(self):
        drain(self.parts, self.sems.at[4], CHIPS - 1)
        drain(self.whole.at[0], self.sems.at[5], CHIPS - 1)
        self.whole[pl.ds(self.place.core, 1), pl.ds(self.place.chip, 1)] = self.mine[...][None, None]
        self.back_copy().start()

    def store(self):
        self.back_copy().wait()
        for core in range(2):
            for j in range(self.chunk):
                at = self.first + core * self.rows + CHIPS * j
                self.total_ref[at : at + CHIPS, :] = self.whole[core, :, j, :]


def sum_buffers():
    out = []
    for chunk in CHUNKS:
        out += [
            pltpu.VMEM((CHIPS * chunk, 128), f32),
            pltpu.VMEM((CHIPS, chunk, 128), f32),
            pltpu.VMEM((CHIPS, chunk, 128), f32),
            pltpu.VMEM((chunk, 128), f32),
            pltpu.VMEM((2, CHIPS, chunk, 128), f32),
        ]
    return out


def step_kernel(
    width,
    table_hbm,
    index_hbm,
    noise_hbm,
    count_hbm,
    actor_hbm,
    actor_t_hbm,
    critic_hbm,
    critic_t_hbm,
    prio_ref,
    sum_ref,
    table_ref,
    index_ref,
    noise_ref,
    count_ref,
    actor_ref,
    actor_t_ref,
    critic_ref,
    critic_t_ref,
    in_sems,
    rows_ref,
    picked_ref,
    q_ref,
    nsend,
    nrecv,
    noise_sems,
    x_ref,
    nz_ref,
    flat_ref,
    pad_ref,
    pack_ref,
    sems,
    *scratch,
):
    weights, grads = scratch[: len(WEIGHTS)], scratch[len(WEIGHTS) : len(WEIGHTS) + len(GRADS)]
    buffers = scratch[len(WEIGHTS) + len(GRADS) :]
    w1_ref, w2f_ref, w2b_ref, b2_ref, w3_ref, b3_ref, w3t_ref, w3b_ref, b3a_ref, w1a_ref = weights
    blocks = N // width
    place = Place()
    me = place.me

    loads = [
        pltpu.make_async_copy(src, dst, in_sems.at[n])
        for n, (src, dst) in enumerate(
            (
                (table_hbm, table_ref),
                (index_hbm, index_ref),
                (critic_hbm, critic_ref),
                (actor_hbm, actor_ref),
                (count_hbm, count_ref),
                (noise_hbm, noise_ref),
                (critic_t_hbm, critic_t_ref),
                (actor_t_hbm, actor_t_ref),
            )
        )
    ]
    for load in loads:
        load.start()

    barrier = pltpu.get_barrier_semaphore()

    def all_others():
        for other_core in (False, True):
            for _, device in place.others(other_core):
                yield device[0] * 8 + device[1], device
        yield place.sibling_at, place.sibling

    for _, device in all_others():
        pl.semaphore_signal(barrier, inc=1, device_id=device, device_id_type=MESH)
    for ref in grads:
        ref[...] = jnp.zeros_like(ref)
    loads[0].wait()

    def turn(i, carry):
        turn_table(i, table_ref, rows_ref)
        return carry

    lax.fori_loop(0, R_DEV // TURN, turn, 0)
    loads[1].wait()
    pick_rows(0, width, index_ref, rows_ref, picked_ref)
    loads[2].wait()
    prepare_critics(
        critic_ref, flat_ref, pad_ref, C0, w1_ref, w2f_ref, w2b_ref, b2_ref, w3_ref, b3_ref, w1a_ref
    )
    loads[3].wait()
    prepare_actor(
        A, actor_ref, flat_ref, pad_ref, w1_ref, w2f_ref, w2b_ref, b2_ref, w3t_ref, w3b_ref, b3a_ref
    )
    loads[4].wait()
    loads[5].wait()
    turn_noise(noise_ref, q_ref, nsend)

    def send():
        for peer, device in all_others():
            pltpu.make_async_remote_copy(
                src_ref=nsend.at[peer],
                dst_ref=nrecv.at[me],
                send_sem=noise_sems.at[0],
                recv_sem=noise_sems.at[1],
                device_id=device,
                device_id_type=MESH,
            ).start()

    def actors(i, carry):
        x = turn_rows(width, picked_ref)
        x_ref[:, pl.ds(pl.multiple_of(i * width, width), width)] = x
        actor_block(i, width, x, count_ref, weights, grads)
        pick_rows(lax.rem(i + 1, blocks), width, index_ref, rows_ref, picked_ref)

        @pl.when(i == 0)
        def _():
            pl.semaphore_wait(barrier, DEVS - 1)
            send()

        return carry

    lax.fori_loop(0, blocks, actors, 0)
    pack_actor(pack_ref, grads)
    late, early = (Sum(place, g, pack_ref, sum_ref, buffers[5 * g : 5 * g + 5], sems) for g in range(2))
    early.swap().start()

    loads[6].wait()
    prepare_critics(
        critic_t_ref, flat_ref, pad_ref, T0, w1_ref, w2f_ref, w2b_ref, b2_ref, w3_ref, b3_ref, w1a_ref
    )
    loads[7].wait()
    prepare_actor(
        AT, actor_t_ref, flat_ref, pad_ref, w1_ref, w2f_ref, w2b_ref, b2_ref, w3t_ref, w3b_ref, b3a_ref
    )
    drain(nsend, noise_sems.at[0], DEVS - 1)
    drain(nrecv, noise_sems.at[1], DEVS - 1)
    nrecv[pl.ds(me, 1)] = nsend[pl.ds(me, 1)]
    noise_back(nrecv, nz_ref)

    def critics(i, carry):
        x = x_ref[:, pl.ds(pl.multiple_of(i * width, width), width)]
        critic_block(i, width, x, nz_ref, count_ref, weights, prio_ref, grads)

        @pl.when(i == 0)
        def _():
            early.swap().wait()
            early.scatter()

        @pl.when(i == 1)
        def _():
            early.spread()

        @pl.when(i == 2)
        def _():
            early.back()

        return carry

    lax.fori_loop(0, blocks, critics, 0)
    pack_critics(pack_ref, grads)
    late.swap().start()
    early.store()
    late.swap().wait()
    late.scatter()
    late.spread()
    late.back()
    late.store()


def update(weight, grad, momentum, average, target):
    momentum_new = 0.9 * momentum + grad
    weight_new = weight - 0.1 * (grad + 0.9 * momentum_new)
    average_new = 0.99 * average + 0.01 * weight_new
    target_new = 0.005 * weight_new + 0.995 * target
    return (weight_new, momentum_new, average_new, target_new, weight_new.astype(bf))


def update_kernel(sum_hbm, prio_hbm, *refs):
    ins_hbm, stat_ref, prio_out, outs_hbm = refs[:8], refs[8], refs[9], refs[10:20]
    sum_ref, ins, outs, grad_ref, in_sems, out_sems = refs[20], refs[21:29], refs[29:39], refs[39], refs[40], refs[41]
    loads = [pltpu.make_async_copy(sum_hbm, sum_ref, in_sems.at[8])]
    loads += [pltpu.make_async_copy(ins_hbm[n], ins[n], in_sems.at[n]) for n in range(8)]
    for load in [loads[0]] + loads[1::2] + loads[2::2]:
        load.start()
    pass_on = pltpu.make_async_copy(prio_hbm, prio_out, in_sems.at[9])
    pass_on.start()
    loads[0].wait()
    stat = sum_ref[STAT : STAT + 1, :]
    factor = (1.0 / SCALE) / stat[:, 1:2]
    stat_ref[...] = stat
    stores = [pltpu.make_async_copy(outs[n], outs_hbm[n], out_sems.at[n]) for n in range(10)]
    step = 1024

    def actor(s, grad):
        values = update(ins[0][s], grad, ins[2][s], ins[4][s], ins[6][s])
        for ref, value in zip(outs[0::2], values):
            ref[s] = value

    for load in loads[1::2]:
        load.wait()

    def body(i, carry):
        r = pl.multiple_of(AT_ACTOR + 8 * i, 8)
        actor(pl.ds(pl.multiple_of(i * step, step), step), (sum_ref[pl.ds(r, 8), :] * factor).reshape(step))
        return carry

    lax.fori_loop(0, PA // step, body, 0, unroll=5)
    done = PA // step * step
    r = AT_ACTOR + done // 128
    more = (PA - done) // 128
    actor(pl.ds(done, 128 * more), (sum_ref[r : r + more, :] * factor).reshape(128 * more))
    done += 128 * more
    actor(pl.ds(done, ACT), (sum_ref[r + more : r + more + 1, :ACT] * factor).reshape(ACT))
    for store in stores[0::2]:
        store.start()

    def critics(s):
        values = update(ins[1][:, s], grad_ref[:, s], ins[3][:, s], ins[5][:, s], ins[7][:, s])
        for ref, value in zip(outs[1::2], values):
            ref[:, s] = value

    for t in range(TILES_C):
        grad_ref[:, 128 * t : 128 * (t + 1)] = sum_ref[2 * t : 2 * t + 2, :] * factor
    for load in loads[2::2]:
        load.wait()

    def body(i, carry):
        critics(pl.ds(pl.multiple_of(i * step, step), step))
        return carry

    lax.fori_loop(0, PC // step, body, 0, unroll=5)
    done = PC // step * step
    critics(pl.ds(done, PC - done))
    for store in stores[1::2]:
        store.start()
    for store in stores:
        store.wait()
    pass_on.wait()


def local(
    replay,
    sample_index,
    pair_count,
    noise,
    actor,
    critic,
    actor_momentum,
    critic_momentum,
    actor_average,
    critic_average,
    actor_target,
    critic_target,
):
    any_ = pl.BlockSpec(memory_space=pl.ANY)
    prio, total = pl.pallas_call(
        functools.partial(step_kernel, WIDTH),
        out_shape=(SDS((CAP, DEVS), f32), SDS((PACK, 128), f32)),
        in_specs=[any_] * 8,
        out_specs=(VM, VM),
        scratch_shapes=[
            pltpu.VMEM((ROW, R_DEV), f32),
            pltpu.SMEM((CAP, DEVS), jnp.int32),
            pltpu.VMEM((ACT, CAP, DEVS), f32),
            pltpu.VMEM((1, DEVS), jnp.int32),
            pltpu.VMEM((PA,), f32),
            pltpu.VMEM((PA,), f32),
            pltpu.VMEM((2, PC), f32),
            pltpu.VMEM((2, PC), f32),
            pltpu.SemaphoreType.DMA((8,)),
            pltpu.VMEM((R_DEV, 128), f32),
            pltpu.VMEM((WIDTH // 128, 128, 128), f32),
            pltpu.VMEM((256, 128), f32),
            pltpu.VMEM((DEVS, 2, 128), f32),
            pltpu.VMEM((DEVS, 2, 128), f32),
            pltpu.SemaphoreType.DMA((2,)),
            pltpu.VMEM((FEAT, N), f32),
            pltpu.VMEM((8, N), f32),
            pltpu.VMEM((2 * TILES_C + 6, 128), f32),
            pltpu.VMEM((FEAT, 256), f32),
            pltpu.VMEM((PACK, 128), f32),
            pltpu.SemaphoreType.DMA((2, 8)),
        ]
        + WEIGHTS
        + GRADS
        + sum_buffers(),
        compiler_params=pltpu.CompilerParams(
            collective_id=0, has_side_effects=True, vmem_limit_bytes=56 << 20
        ),
        name="td3_step",
    )(
        replay.T,
        sample_index[0].T,
        jnp.transpose(noise[0], (2, 1, 0)),
        pair_count,
        actor,
        actor_target,
        critic,
        critic_target,
    )
    shapes = [SDS((1, 128), f32), SDS((CAP, DEVS), f32)]
    places = [SDS((PA,), f32), SDS((2, PC), f32)] * 4 + [SDS((PA,), bf), SDS((2, PC), bf)]
    stat, prio, *outs = pl.pallas_call(
        update_kernel,
        out_shape=tuple(shapes + places),
        in_specs=[any_] * 10,
        out_specs=(VM,) + (any_,) * 11,
        scratch_shapes=[pltpu.VMEM((PACK, 128), f32)]
        + [pltpu.VMEM(p.shape, p.dtype) for p in places[:8] + places]
        + [pltpu.VMEM((2, TILES_C * 128), f32), pltpu.SemaphoreType.DMA((10,)), pltpu.SemaphoreType.DMA((10,))],
        compiler_params=pltpu.CompilerParams(vmem_limit_bytes=24 << 20),
        name="update",
    )(
        total,
        prio,
        actor,
        critic,
        actor_momentum,
        critic_momentum,
        actor_average,
        critic_average,
        actor_target,
        critic_target,
    )
    return (stat[0, :2], prio.T[None], *outs)


def solution(mesh):
    rows = ("group", "shard")
    in_specs = (P(rows, None), P(rows, None, None), P(rows, None), P(rows, None, None, None)) + (P(),) * 8
    out_specs = (P(), P(rows, None, None)) + (P(),) * 10
    return jax.shard_map(local, mesh=mesh, in_specs=in_specs, out_specs=out_specs, check_vma=False)
```

```python
import functools

import jax
import jax.numpy as jnp
from jax import lax
from jax.experimental import pallas as pl
from jax.experimental.pallas import tpu as pltpu
from jax.sharding import PartitionSpec as P

OBS = 17
ACT = 6
UNITS = 256
CAP = 32
DEVS = 128
R_DEV = 8192
ROW = 42
PA = 71942
PC = 72193
N = DEVS * CAP

bf = jnp.bfloat16
f32 = jnp.float32
MESH = pl.DeviceIdType.MESH
VM = pl.BlockSpec(memory_space=pltpu.VMEM)
SDS = jax.ShapeDtypeStruct

SCALE = 2.0**-19
C0, C1, A, AT, T0, T1 = range(6)
FEAT = 48
ONE = 42
NEXT = 25

TILES_C = 565
STAT = 1130
ROWS_A = 563
CHIPS = DEVS // 2
CHUNKS = (9, 5)
AT_ACTOR = 2 * CHIPS * CHUNKS[0]
PACK = AT_ACTOR + 2 * CHIPS * CHUNKS[1]
TURN = 512
WIDTH = 1024
STEPS = sorted(
    ((z, x, y) for z in range(4) for x in range(4) for y in range(4)),
    key=lambda step: -sum(min(n, 4 - n) for n in step),
)[:-1]


def dot(a, b):
    return lax.dot_general(a, b, (((1,), (0,)), ((), ())), preferred_element_type=f32)


def dot_nt(a, b):
    return lax.dot_general(a, b, (((1,), (1,)), ((), ())), preferred_element_type=f32)


def dot_exact(a, b, dims):
    return lax.dot_general(a, b, (dims, ((), ())), precision=lax.Precision.HIGHEST, preferred_element_type=f32)


def split(v):
    hi = v.astype(bf)
    return hi, (v - hi.astype(f32)).astype(bf)


def three(v):
    hi, lo = split(v)
    return jnp.concatenate([hi, lo, hi], 0)


def lanes(tile, width):
    return jnp.concatenate([tile] * (width // 128), 1)


def fold(v):
    out = v[:, :128]
    for i in range(1, v.shape[1] // 128):
        out = out + v[:, 128 * i : 128 * (i + 1)]
    return out


def column(row):
    return jnp.transpose(jnp.broadcast_to(row, (128, 128)))


def turn_noise(noise_ref, q_ref, nsend):
    q_ref[...] = jnp.zeros_like(q_ref)
    for j in range(ACT):
        q_ref[pl.ds(j + 1, CAP, stride=8), :] = 0.5 * jnp.tanh(0.4 * noise_ref[j])
    turned = jnp.transpose(q_ref[...])
    nsend[:, 0, :] = turned[:, :128]
    nsend[:, 1, :] = turned[:, 128:]


def noise_back(nrecv, nz_ref):
    back = jnp.transpose(jnp.concatenate([nrecv[:, 0, :], nrecv[:, 1, :]], 1))
    for c in range(CAP):
        nz_ref[:, 128 * c : 128 * (c + 1)] = back[8 * c : 8 * (c + 1), :]


def turn_table(i, table_ref, rows_ref):
    s = pl.ds(pl.multiple_of(i * TURN, TURN), TURN)
    v = jnp.concatenate([table_ref[:, s], jnp.zeros((128 - ROW, TURN), f32)], 0)
    rows_ref[s, :] = jnp.transpose(v)


def pick_rows(block, width, index_ref, rows_ref, picked_ref):
    tiles = width // 128
    for t in range(tiles):
        for d in range(DEVS):
            picked_ref[t, d : d + 1, :] = rows_ref[pl.ds(index_ref[block * tiles + t, d], 1), :]


def turn_rows(width, picked_ref):
    parts = [jnp.transpose(picked_ref[t])[:FEAT] for t in range(width // 128)]
    x = jnp.concatenate(parts, 1)
    ones = lax.broadcasted_iota(jnp.int32, (8, width), 0) == (ONE - 40)
    return jnp.concatenate([x[:40], jnp.where(ones, 1.0, x[40:])], 0)


def put_square(net, w2, w2f_ref, w2b_ref):
    w2 = 0.5 * w2
    turned = jnp.transpose(w2)
    hi, lo = split(turned)
    w2f_ref[net] = jnp.concatenate([hi, hi, lo], 1)
    if net in (C0, C1, A):
        hi, lo = split(w2)
        w2b_ref[net] = jnp.concatenate([hi, hi, lo], 1)


def put_first(net, pad_ref, w1_ref):
    w1 = 0.5 * pad_ref[...]
    hi = w1.astype(bf).astype(f32)
    lo = w1 - hi
    stacked = jnp.concatenate([hi, hi, lo, jnp.zeros((256 - 3 * FEAT, 256), f32)], 0)
    w1_ref[net] = jnp.transpose(stacked).astype(bf)


def put_column(ref, net, left, right, factor):
    ref[net] = jnp.concatenate([column(left * factor), column(right * factor)], 0)


def prepare_critics(critic_ref, rows_ref, pad_ref, first, w1_ref, w2f_ref, w2b_ref, b2_ref, w3_ref, b3_ref, w1a_ref):
    for t in range(TILES_C - 1):
        rows_ref[2 * t : 2 * t + 2, :] = critic_ref[:, 128 * t : 128 * (t + 1)]
    for c in range(2):
        net = first + c
        start = NEXT if first == T0 else 0
        pad_ref[...] = jnp.zeros_like(pad_ref)
        for half in range(2):
            s = pl.ds(128 * half, 128)
            pad_ref[pl.ds(start, OBS), s] = rows_ref[pl.ds(c + 2 * half, OBS, stride=4), :]
            pad_ref[pl.ds(OBS, ACT), s] = rows_ref[pl.ds(c + 2 * half + 4 * OBS, ACT, stride=4), :]
            pad_ref[pl.ds(ONE, 1), s] = rows_ref[pl.ds(92 + c + 2 * half, 1), :]
        put_first(net, pad_ref, w1_ref)
        if net == C0:
            hi = pad_ref[16:24, :].astype(bf).astype(f32)
            lo = pad_ref[16:24, :] - hi
            block = jnp.concatenate([hi, hi, lo], 1)
            w1a_ref[...] = jnp.concatenate([block, jnp.zeros_like(block)], 0).astype(bf)
        w2 = jnp.concatenate(
            [rows_ref[pl.ds(96 + c, UNITS, stride=4), :], rows_ref[pl.ds(98 + c, UNITS, stride=4), :]], 1
        )
        put_square(net, w2, w2f_ref, w2b_ref)
        put_column(b2_ref, net, rows_ref[1120 + c : 1121 + c, :], rows_ref[1122 + c : 1123 + c, :], 0.5)
        put_column(w3_ref, net, rows_ref[1124 + c : 1125 + c, :], rows_ref[1126 + c : 1127 + c, :], 1.0)
        b3_ref[net] = jnp.broadcast_to(critic_ref[c : c + 1, PC - 1 : PC], (1, 128))


def head_maps(j):
    k = lax.broadcasted_iota(jnp.int32, (UNITS, 16), 0)
    r = lax.broadcasted_iota(jnp.int32, (UNITS, 16), 1)
    row = ((k * ACT + j) >> 7) == r
    k = lax.broadcasted_iota(jnp.int32, (UNITS, 128), 0)
    l = lax.broadcasted_iota(jnp.int32, (UNITS, 128), 1)
    lane = ((k * ACT + j) & 127) == l
    return row.astype(f32), lane


def head_of(flat):
    hi = flat.astype(bf).astype(f32)
    out = []
    for part in (hi, flat - hi):
        part = part.astype(bf)
        spread = []
        for j in range(ACT):
            row, lane = head_maps(j)
            spread.append(jnp.where(lane, dot(row.astype(bf), part), 0.0).astype(bf))
        r = lax.broadcasted_iota(jnp.int32, (16, 128 * ACT), 0)
        l = lax.broadcasted_iota(jnp.int32, (16, 128 * ACT), 1)
        take = ((l >> 7) == (r - 1)).astype(f32).astype(bf)
        out.append(dot_nt(take, jnp.concatenate(spread, 1))[:8])
    return out


def head_back(turned):
    out = jnp.zeros((16, 128), f32)
    for j in range(ACT):
        row, lane = head_maps(j)
        picked = jnp.transpose(row) * turned[j + 1 : j + 2, :]
        out = out + dot_exact(picked, lane.astype(f32), ((1,), (0,)))
    return out


def prepare_actor(net, actor_ref, rows_ref, pad_ref, w1_ref, w2f_ref, w2b_ref, b2_ref, w3t_ref, w3b_ref, b3a_ref):
    whole = PA // 1024
    for t in range(whole):
        rows_ref[8 * t : 8 * t + 8, :] = actor_ref[pl.ds(1024 * t, 1024)].reshape(8, 128)
    rest = (PA - 1024 * whole) // 128
    rows_ref[8 * whole : 8 * whole + rest, :] = actor_ref[pl.ds(1024 * whole, 128 * rest)].reshape(rest, 128)
    rows_ref[562:563, 0:ACT] = actor_ref[pl.ds(562 * 128, ACT)].reshape(1, ACT)
    start = NEXT if net == AT else 0
    pad_ref[...] = jnp.zeros_like(pad_ref)
    for half in range(2):
        s = pl.ds(128 * half, 128)
        pad_ref[pl.ds(start, OBS), s] = rows_ref[pl.ds(half, OBS, stride=2), :]
        pad_ref[pl.ds(ONE, 1), s] = rows_ref[pl.ds(34 + half, 1), :]
    put_first(net, pad_ref, w1_ref)
    w2 = jnp.concatenate([rows_ref[pl.ds(36, UNITS, stride=2), :], rows_ref[pl.ds(37, UNITS, stride=2), :]], 1)
    put_square(net, w2, w2f_ref, w2b_ref)
    put_column(b2_ref, net, rows_ref[548:549, :], rows_ref[549:550, :], 0.5)
    flat = jnp.concatenate([rows_ref[550:562, :], jnp.zeros((4, 128), f32)], 0)
    hi, lo = head_of(flat)
    block = jnp.concatenate([hi, hi, lo], 1)
    w3t_ref[net - A] = jnp.concatenate([block, jnp.zeros_like(block)], 0).astype(bf)
    if net == A:
        stacked = jnp.concatenate([hi, hi, lo, jnp.zeros((104, UNITS), f32)], 0)
        w3b_ref[...] = (0.5 * jnp.transpose(stacked)).astype(bf)
    bias = column(rows_ref[562:563, :])
    b3a_ref[net - A] = jnp.zeros((8, 128), f32)
    b3a_ref[net - A, 1 : 1 + ACT, :] = bias[:ACT]


def act(zh):
    u = jnp.tanh(zh) + 1.0
    return u, zh * u


def slope(u, s):
    return u + s * (2.0 - u)


class Step:
    def __init__(self, i, width, x, weights):
        (
            self.w1, self.w2f, self.w2b, self.b2, self.w3, self.b3, self.w3t, self.w3b, self.b3a, self.w1a,
        ) = weights
        self.i, self.width = i, width
        self.lanes = pl.ds(pl.multiple_of(i * width, width), width)
        self.x = x
        self.x3 = three(self.x)
        rows8 = lax.broadcasted_iota(jnp.int32, (8, width), 0)
        self.is_action = (rows8 >= 1) & (rows8 <= ACT)

    def with_action(self, a):
        x = self.x
        return three(jnp.concatenate([x[:16], jnp.where(self.is_action, a, x[16:24]), x[24:]], 0))

    def first(self, net, xx):
        return act(dot(self.w1[net, :, : 3 * FEAT], xx))

    def second(self, net, h3):
        return act(dot(self.w2f[net], h3) + lanes(self.b2[net], self.width))

    def value(self, net, s):
        return jnp.sum(s * lanes(self.w3[net], self.width), 0, keepdims=True) + lanes(self.b3[net], self.width)

    def head(self, net, s3):
        return dot(self.w3t[net - A], s3)[:8] + lanes(self.b3a[net - A], self.width)

    def valid(self, count_ref):
        tiles = self.width // 128
        return jnp.concatenate([((self.i * tiles + t) < count_ref[...]).astype(f32) for t in range(tiles)], 1)

    def grads2(self, net, h1, dz2, g2_ref):
        u = UNITS
        left = jnp.concatenate([h1[:u], h1[u : 2 * u], h1[:u]], 1)
        g2_ref[net] += dot_nt(left, jnp.concatenate([dz2[:u], dz2[:u], dz2[u : 2 * u]], 1))

    def grads1(self, net, dz1, g1_ref):
        xhi, xlo = self.x3[:FEAT], self.x3[FEAT : 2 * FEAT]
        left = jnp.concatenate(
            [jnp.concatenate([xhi, xlo], 0), jnp.concatenate([xhi, jnp.zeros_like(xlo)], 0)], 1
        )
        a, b = split(dz1)
        g1_ref[net] += dot_nt(left, jnp.concatenate([a, b], 1))


def critic_block(i, width, x, nz_ref, count_ref, weights, prio_ref, grads):
    g2_ref, g1_ref, g3a_ref, db2_ref, dw3_ref, st_ref = grads
    st = Step(i, width, x, weights)
    x3 = st.x3

    u, s = st.first(AT, x3)
    u, s = st.second(AT, three(s))
    next_action = jnp.tanh(st.head(AT, three(s)) + nz_ref[:, st.lanes])
    xt = st.with_action(next_action)
    targets = []
    for net in (T0, T1):
        u, s = st.first(net, xt)
        u, s = st.second(net, three(s))
        targets.append(st.value(net, s))
    y = x[23:24] + 0.99 * x[24:25] * jnp.minimum(targets[0], targets[1])
    valid = st.valid(count_ref)
    scaled = valid * SCALE
    st_ref[1:2, :] += fold(valid)

    def top(net, s, d2):
        delta = st.value(net, s) - y
        if net == C0:
            prio = valid * jnp.sqrt(delta * delta + 1.0)
            tiles = width // 128
            for t in range(tiles):
                prio_ref[pl.ds(i * tiles + t, 1), :] = prio[:, 128 * t : 128 * (t + 1)]
        st_ref[0:1, :] += fold(valid * (delta * delta))
        dq = (2.0 * scaled) * delta
        st_ref[2 + net : 3 + net, :] += fold(dq)
        dw3_ref[net] += fold(s * dq)
        dz2 = lanes(st.w3[net], width) * (0.5 * dq) * d2
        db2_ref[net] += fold(dz2)
        return three(dz2)

    u, s = st.first(C0, x3)
    h1, d1 = three(s), slope(u, s)
    u, s = st.second(C0, h1)
    dz2 = top(C0, s, slope(u, s))
    dz1 = dot(st.w2b[C0], dz2) * d1
    u, s = st.first(C1, x3)
    h1b, d1b = three(s), slope(u, s)
    st.grads2(C0, h1, dz2, g2_ref)
    u, s = st.second(C1, h1b)
    st.grads1(C0, dz1, g1_ref)
    dz2 = top(C1, s, slope(u, s))
    dz1 = dot(st.w2b[C1], dz2) * d1b
    st.grads2(C1, h1b, dz2, g2_ref)
    st.grads1(C1, dz1, g1_ref)


def actor_block(i, width, x, count_ref, weights, grads):
    g2_ref, g1_ref, g3a_ref, db2_ref, dw3_ref, st_ref = grads
    st = Step(i, width, x, weights)

    u, s = st.first(A, st.x3)
    h1a, d1a = three(s), slope(u, s)
    u, s = st.second(A, h1a)
    h2a, d2a = three(s), slope(u, s)
    policy = jnp.tanh(st.head(A, h2a))

    u, s = st.first(C0, st.with_action(policy))
    d1f = slope(u, s)
    u, s = st.second(C0, three(s))
    d2f, q_policy = slope(u, s), st.value(C0, s)
    valid = st.valid(count_ref)
    st_ref[0:1, :] -= fold(valid * q_policy)

    dz2 = three(lanes(st.w3[C0], width) * (-0.5 * SCALE * valid) * d2f)
    dz1 = three(dot(st.w2b[C0], dz2) * d1f)
    da = dot(st.w1a[...], dz1)[:8]
    dp = jnp.where(st.is_action, da * (1.0 - policy * policy), 0.0)
    st_ref[8:16, :] += fold(dp)
    hi = dp.astype(bf).astype(f32)
    lo = dp - hi
    zero = jnp.zeros_like(hi)
    stacked = jnp.concatenate([hi, lo, hi, zero], 0).astype(bf)
    left = jnp.concatenate([jnp.concatenate([hi, lo], 0), jnp.concatenate([hi, zero], 0)], 1).astype(bf)
    g3a_ref[...] += dot_nt(left, jnp.concatenate([h2a[:UNITS], h2a[UNITS : 2 * UNITS]], 1))
    dz2 = dot(st.w3b[:, :32], stacked) * d2a
    db2_ref[A] += fold(dz2)
    dz2 = three(dz2)
    dz1 = dot(st.w2b[A], dz2) * d1a
    st.grads2(A, h1a, dz2, g2_ref)
    st.grads1(A, dz1, g1_ref)


def lane_sums(tile):
    return dot_exact(jnp.ones((8, 128), f32), tile, ((1,), (1,)))


def pack_critics(pack_ref, grads):
    g2_ref, g1_ref, g3a_ref, db2_ref, dw3_ref, st_ref = grads
    lane = lax.broadcasted_iota(jnp.int32, (1, 128), 1)
    sums = jnp.sum(st_ref[...], 1, keepdims=True)
    for c in range(2):
        g1 = g1_ref[c, :FEAT, :] + g1_ref[c, FEAT:, :]
        b2 = lane_sums(db2_ref[c])[0:1]
        w3 = lane_sums(dw3_ref[c])[0:1]
        for half in range(2):
            s = slice(128 * half, 128 * (half + 1))
            at = c + 2 * half
            pack_ref[pl.ds(at, OBS + ACT, stride=4), :] = g1[: OBS + ACT, s]
            pack_ref[at + 92 : at + 93, :] = g1[ONE : ONE + 1, s]
            pack_ref[pl.ds(at + 96, UNITS, stride=4), :] = g2_ref[c, :, s]
            pack_ref[at + 1120 : at + 1121, :] = b2[:, s]
            pack_ref[at + 1124 : at + 1125, :] = w3[:, s]
        pack_ref[c + 1128 : c + 1129, :] = jnp.where(lane == 0, sums[2 + c : 3 + c], 0.0)
    pack_ref[STAT : STAT + 1, :] = jnp.where(lane == 0, sums[0:1], jnp.where(lane == 1, sums[1:2], 0.0))
    pack_ref[STAT + 1 : AT_ACTOR, :] = jnp.zeros((AT_ACTOR - STAT - 1, 128), f32)


def pack_actor(pack_ref, grads):
    g2_ref, g1_ref, g3a_ref, db2_ref, dw3_ref, st_ref = grads
    sums = jnp.sum(st_ref[...], 1, keepdims=True)
    g1 = g1_ref[A, :FEAT, :] + g1_ref[A, FEAT:, :]
    b2 = lane_sums(db2_ref[A])[0:1]
    o = AT_ACTOR
    for half in range(2):
        s = slice(128 * half, 128 * (half + 1))
        pack_ref[pl.ds(o + half, OBS, stride=2), :] = g1[:OBS, s]
        pack_ref[o + 34 + half : o + 35 + half, :] = g1[ONE : ONE + 1, s]
        pack_ref[pl.ds(o + 36 + half, UNITS, stride=2), :] = g2_ref[A, :, s]
        pack_ref[o + 548 + half : o + 549 + half, :] = b2[:, s]
    pack_ref[o + 550 : o + 562, :] = head_back(g3a_ref[:8, :] + g3a_ref[8:, :])[:12]
    e = lax.broadcasted_iota(jnp.int32, (8, 128), 1) == lax.broadcasted_iota(jnp.int32, (8, 128), 0) - 1
    pack_ref[o + 562 : o + 563, :] = jnp.sum(jnp.where(e, sums[8:16], 0.0), 0, keepdims=True)
    pack_ref[o + ROWS_A : PACK, :] = jnp.zeros((PACK - o - ROWS_A, 128), f32)


WEIGHTS = [
    pltpu.VMEM((6, UNITS, 256), bf),
    pltpu.VMEM((6, UNITS, 3 * UNITS), bf),
    pltpu.VMEM((3, UNITS, 3 * UNITS), bf),
    pltpu.VMEM((6, UNITS, 128), f32),
    pltpu.VMEM((6, UNITS, 128), f32),
    pltpu.VMEM((6, 1, 128), f32),
    pltpu.VMEM((2, 16, 3 * UNITS), bf),
    pltpu.VMEM((UNITS, 128), bf),
    pltpu.VMEM((2, 8, 128), f32),
    pltpu.VMEM((16, 3 * UNITS), bf),
]
GRADS = [
    pltpu.VMEM((3, UNITS, UNITS), f32),
    pltpu.VMEM((3, 2 * FEAT, UNITS), f32),
    pltpu.VMEM((16, UNITS), f32),
    pltpu.VMEM((3, UNITS, 128), f32),
    pltpu.VMEM((2, UNITS, 128), f32),
    pltpu.VMEM((16, 128), f32),
]


def drain(ref, sem, copies):
    view = ref.at[pl.ds(0, copies)]
    pltpu.make_async_copy(view, view, sem).wait()


class Place:
    def __init__(self):
        group, shard = lax.axis_index("group"), lax.axis_index("shard")
        self.core = lax.rem(shard, 2)
        z, x, y = group // 4, lax.rem(group, 4), shard // 2
        self.chip = group * 4 + y
        self.sibling = (group, shard + 1 - 2 * self.core)
        self.sibling_at = group * 8 + shard + 1 - 2 * self.core
        self.me = group * 8 + shard
        self.zs, self.xs, self.ys = ([lax.rem(v + n, 4) for n in range(4)] for v in (z, x, y))

    def others(self, other_core=False):
        core = 1 - self.core if other_core else self.core
        for dz, dx, dy in STEPS:
            group = self.zs[dz] * 4 + self.xs[dx]
            yield group * 4 + self.ys[dy], (group, self.ys[dy] * 2 + core)


class Sum:
    def __init__(self, place, g, pack_ref, total_ref, buffers, sems):
        self.place, self.chunk = place, CHUNKS[g]
        self.first = (0, AT_ACTOR)[g]
        self.rows = CHIPS * self.chunk
        self.pack_ref, self.total_ref = pack_ref, total_ref
        self.other, self.half, self.parts, self.mine, self.whole = buffers
        self.sems = sems.at[g]

    def remote(self, src, dst, n, to):
        return pltpu.make_async_remote_copy(
            src_ref=src,
            dst_ref=dst,
            send_sem=self.sems.at[2 * n],
            recv_sem=self.sems.at[2 * n + 1],
            device_id=to,
            device_id_type=MESH,
        )

    def swap(self):
        give = pl.multiple_of(self.first + (1 - self.place.core) * self.rows, 8)
        return self.remote(self.pack_ref.at[pl.ds(give, self.rows)], self.other, 0, self.place.sibling)

    def scatter(self):
        keep = pl.multiple_of(self.first + self.place.core * self.rows, 8)
        total = self.pack_ref[pl.ds(keep, self.rows), :] + self.other[...]
        for j in range(self.chunk):
            self.half[:, j, :] = total[CHIPS * j : CHIPS * (j + 1)]
        chip = self.place.chip
        for peer, device in self.place.others():
            self.remote(self.half.at[peer], self.parts.at[chip], 1, device).start()

    def spread(self):
        chip = self.place.chip
        drain(self.half, self.sems.at[2], CHIPS - 1)
        drain(self.parts, self.sems.at[3], CHIPS - 1)
        self.parts[pl.ds(chip, 1)] = self.half[pl.ds(chip, 1)]
        self.mine[...] = jnp.sum(self.parts[...], 0)
        for _, device in self.place.others():
            self.remote(self.mine, self.whole.at[self.place.core, chip], 2, device).start()

    def back_copy(self):
        ref = self.whole.at[self.place.core]
        return self.remote(ref, ref, 3, self.place.sibling)

    def back(self):
        drain(self.parts, self.sems.at[4], CHIPS - 1)
        drain(self.whole.at[0], self.sems.at[5], CHIPS - 1)
        self.whole[pl.ds(self.place.core, 1), pl.ds(self.place.chip, 1)] = self.mine[...][None, None]
        self.back_copy().start()

    def store(self):
        self.back_copy().wait()
        for core in range(2):
            for j in range(self.chunk):
                at = self.first + core * self.rows + CHIPS * j
                self.total_ref[at : at + CHIPS, :] = self.whole[core, :, j, :]


def sum_buffers():
    out = []
    for chunk in CHUNKS:
        out += [
            pltpu.VMEM((CHIPS * chunk, 128), f32),
            pltpu.VMEM((CHIPS, chunk, 128), f32),
            pltpu.VMEM((CHIPS, chunk, 128), f32),
            pltpu.VMEM((chunk, 128), f32),
            pltpu.VMEM((2, CHIPS, chunk, 128), f32),
        ]
    return out


def step_kernel(
    width,
    table_hbm,
    index_hbm,
    noise_hbm,
    count_hbm,
    actor_hbm,
    actor_t_hbm,
    critic_hbm,
    critic_t_hbm,
    prio_ref,
    sum_ref,
    table_ref,
    index_ref,
    noise_ref,
    count_ref,
    actor_ref,
    actor_t_ref,
    critic_ref,
    critic_t_ref,
    in_sems,
    rows_ref,
    picked_ref,
    q_ref,
    nsend,
    nrecv,
    noise_sems,
    x_ref,
    nz_ref,
    flat_ref,
    pad_ref,
    pack_ref,
    sems,
    *scratch,
):
    weights, grads = scratch[: len(WEIGHTS)], scratch[len(WEIGHTS) : len(WEIGHTS) + len(GRADS)]
    buffers = scratch[len(WEIGHTS) + len(GRADS) :]
    w1_ref, w2f_ref, w2b_ref, b2_ref, w3_ref, b3_ref, w3t_ref, w3b_ref, b3a_ref, w1a_ref = weights
    blocks = N // width
    place = Place()
    me = place.me

    loads = [
        pltpu.make_async_copy(src, dst, in_sems.at[n])
        for n, (src, dst) in enumerate(
            (
                (table_hbm, table_ref),
                (index_hbm, index_ref),
                (critic_hbm, critic_ref),
                (actor_hbm, actor_ref),
                (count_hbm, count_ref),
                (noise_hbm, noise_ref),
                (critic_t_hbm, critic_t_ref),
                (actor_t_hbm, actor_t_ref),
            )
        )
    ]
    for load in loads:
        load.start()

    barrier = pltpu.get_barrier_semaphore()

    def all_others():
        for other_core in (False, True):
            for _, device in place.others(other_core):
                yield device[0] * 8 + device[1], device
        yield place.sibling_at, place.sibling

    for _, device in all_others():
        pl.semaphore_signal(barrier, inc=1, device_id=device, device_id_type=MESH)
    for ref in grads:
        ref[...] = jnp.zeros_like(ref)
    loads[0].wait()

    def turn(i, carry):
        turn_table(i, table_ref, rows_ref)
        return carry

    lax.fori_loop(0, R_DEV // TURN, turn, 0)
    loads[1].wait()
    pick_rows(0, width, index_ref, rows_ref, picked_ref)
    loads[2].wait()
    prepare_critics(
        critic_ref, flat_ref, pad_ref, C0, w1_ref, w2f_ref, w2b_ref, b2_ref, w3_ref, b3_ref, w1a_ref
    )
    loads[3].wait()
    prepare_actor(
        A, actor_ref, flat_ref, pad_ref, w1_ref, w2f_ref, w2b_ref, b2_ref, w3t_ref, w3b_ref, b3a_ref
    )
    loads[4].wait()
    loads[5].wait()
    turn_noise(noise_ref, q_ref, nsend)

    def send():
        for peer, device in all_others():
            pltpu.make_async_remote_copy(
                src_ref=nsend.at[peer],
                dst_ref=nrecv.at[me],
                send_sem=noise_sems.at[0],
                recv_sem=noise_sems.at[1],
                device_id=device,
                device_id_type=MESH,
            ).start()

    def actors(i, carry):
        x = turn_rows(width, picked_ref)
        x_ref[:, pl.ds(pl.multiple_of(i * width, width), width)] = x
        actor_block(i, width, x, count_ref, weights, grads)
        pick_rows(lax.rem(i + 1, blocks), width, index_ref, rows_ref, picked_ref)

        @pl.when(i == 0)
        def _():
            pl.semaphore_wait(barrier, DEVS - 1)
            send()

        return carry

    lax.fori_loop(0, blocks, actors, 0)
    pack_actor(pack_ref, grads)
    late, early = (Sum(place, g, pack_ref, sum_ref, buffers[5 * g : 5 * g + 5], sems) for g in range(2))
    early.swap().start()

    loads[6].wait()
    prepare_critics(
        critic_t_ref, flat_ref, pad_ref, T0, w1_ref, w2f_ref, w2b_ref, b2_ref, w3_ref, b3_ref, w1a_ref
    )
    loads[7].wait()
    prepare_actor(
        AT, actor_t_ref, flat_ref, pad_ref, w1_ref, w2f_ref, w2b_ref, b2_ref, w3t_ref, w3b_ref, b3a_ref
    )
    drain(nsend, noise_sems.at[0], DEVS - 1)
    drain(nrecv, noise_sems.at[1], DEVS - 1)
    nrecv[pl.ds(me, 1)] = nsend[pl.ds(me, 1)]
    noise_back(nrecv, nz_ref)

    def critics(i, carry):
        x = x_ref[:, pl.ds(pl.multiple_of(i * width, width), width)]
        critic_block(i, width, x, nz_ref, count_ref, weights, prio_ref, grads)

        @pl.when(i == 0)
        def _():
            early.swap().wait()
            early.scatter()

        @pl.when(i == 1)
        def _():
            early.spread()

        @pl.when(i == 2)
        def _():
            early.back()

        return carry

    lax.fori_loop(0, blocks, critics, 0)
    pack_critics(pack_ref, grads)
    late.swap().start()
    early.store()
    late.swap().wait()
    late.scatter()
    late.spread()
    late.back()
    late.store()


def update(weight, grad, momentum, average, target):
    momentum_new = 0.9 * momentum + grad
    weight_new = weight - 0.1 * (grad + 0.9 * momentum_new)
    average_new = 0.99 * average + 0.01 * weight_new
    target_new = 0.005 * weight_new + 0.995 * target
    return (weight_new, momentum_new, average_new, target_new, weight_new.astype(bf))


STEP = 1024
CUTS = (0, 35 * STEP, PC)


def update_kernel(sum_hbm, prio_hbm, *refs):
    ins_hbm, stat_ref, prio_out, outs_hbm = refs[:8], refs[8], refs[9], refs[10:20]
    sum_ref, ins, outs, grad_ref, in_sems, out_sems = refs[20], refs[21:29], refs[29:39], refs[39], refs[40], refs[41]

    def copies(srcs, dsts, sems, piece):
        out = []
        for n, (src, dst) in enumerate(zip(srcs, dsts)):
            if piece:
                s = pl.ds(CUTS[piece - 1], CUTS[piece] - CUTS[piece - 1])
                src, dst = src.at[:, s], dst.at[:, s]
            out.append(pltpu.make_async_copy(src, dst, sems.at[piece, n]))
        return out

    first = pltpu.make_async_copy(sum_hbm, sum_ref, in_sems.at[3, 0])
    first.start()
    loads = [copies(ins_hbm[min(p, 1) :: 2], ins[min(p, 1) :: 2], in_sems, p) for p in range(3)]
    for piece in loads:
        for load in piece:
            load.start()
    pass_on = pltpu.make_async_copy(prio_hbm, prio_out, in_sems.at[3, 1])
    pass_on.start()
    stores = [copies(outs[min(p, 1) :: 2], outs_hbm[min(p, 1) :: 2], out_sems, p) for p in range(3)]
    first.wait()
    stat = sum_ref[STAT : STAT + 1, :]
    factor = (1.0 / SCALE) / stat[:, 1:2]
    stat_ref[...] = stat[:, :2].reshape(2)

    def actor(s, grad):
        values = update(ins[0][s], grad, ins[2][s], ins[4][s], ins[6][s])
        for ref, value in zip(outs[0::2], values):
            ref[s] = value

    def actors(i, carry):
        r = pl.multiple_of(AT_ACTOR + 8 * i, 8)
        actor(pl.ds(pl.multiple_of(i * STEP, STEP), STEP), (sum_ref[pl.ds(r, 8), :] * factor).reshape(STEP))
        return carry

    for load in loads[0]:
        load.wait()
    lax.fori_loop(0, PA // STEP, actors, 0, unroll=5)
    done = PA // STEP * STEP
    r = AT_ACTOR + done // 128
    more = (PA - done) // 128
    actor(pl.ds(done, 128 * more), (sum_ref[r : r + more, :] * factor).reshape(128 * more))
    done += 128 * more
    actor(pl.ds(done, ACT), (sum_ref[r + more : r + more + 1, :ACT] * factor).reshape(ACT))
    for store in stores[0]:
        store.start()

    def critic(s):
        values = update(ins[1][:, s], grad_ref[:, s], ins[3][:, s], ins[5][:, s], ins[7][:, s])
        for ref, value in zip(outs[1::2], values):
            ref[:, s] = value

    def critics(i, carry):
        critic(pl.ds(pl.multiple_of(i * STEP, STEP), STEP))
        return carry

    for t in range(TILES_C):
        grad_ref[:, 128 * t : 128 * (t + 1)] = sum_ref[2 * t : 2 * t + 2, :] * factor
    for piece in (1, 2):
        for load in loads[piece]:
            load.wait()
        lax.fori_loop(CUTS[piece - 1] // STEP, CUTS[piece] // STEP, critics, 0, unroll=5)
        if piece == 2:
            done = PC // STEP * STEP
            critic(pl.ds(done, PC - done))
        for store in stores[piece]:
            store.start()
    for piece in stores:
        for store in piece:
            store.wait()
    pass_on.wait()


def local(
    replay,
    sample_index,
    pair_count,
    noise,
    actor,
    critic,
    actor_momentum,
    critic_momentum,
    actor_average,
    critic_average,
    actor_target,
    critic_target,
):
    any_ = pl.BlockSpec(memory_space=pl.ANY)
    prio, total = pl.pallas_call(
        functools.partial(step_kernel, WIDTH),
        out_shape=(SDS((CAP, DEVS), f32), SDS((PACK, 128), f32)),
        in_specs=[any_] * 8,
        out_specs=(VM, VM),
        scratch_shapes=[
            pltpu.VMEM((ROW, R_DEV), f32),
            pltpu.SMEM((CAP, DEVS), jnp.int32),
            pltpu.VMEM((ACT, CAP, DEVS), f32),
            pltpu.VMEM((1, DEVS), jnp.int32),
            pltpu.VMEM((PA,), f32),
            pltpu.VMEM((PA,), f32),
            pltpu.VMEM((2, PC), f32),
            pltpu.VMEM((2, PC), f32),
            pltpu.SemaphoreType.DMA((8,)),
            pltpu.VMEM((R_DEV, 128), f32),
            pltpu.VMEM((WIDTH // 128, 128, 128), f32),
            pltpu.VMEM((256, 128), f32),
            pltpu.VMEM((DEVS, 2, 128), f32),
            pltpu.VMEM((DEVS, 2, 128), f32),
            pltpu.SemaphoreType.DMA((2,)),
            pltpu.VMEM((FEAT, N), f32),
            pltpu.VMEM((8, N), f32),
            pltpu.VMEM((2 * TILES_C + 6, 128), f32),
            pltpu.VMEM((FEAT, 256), f32),
            pltpu.VMEM((PACK, 128), f32),
            pltpu.SemaphoreType.DMA((2, 8)),
        ]
        + WEIGHTS
        + GRADS
        + sum_buffers(),
        compiler_params=pltpu.CompilerParams(
            collective_id=0, has_side_effects=True, vmem_limit_bytes=56 << 20
        ),
        name="td3_step",
    )(
        replay.T,
        sample_index[0].T,
        jnp.transpose(noise[0], (2, 1, 0)),
        pair_count,
        actor,
        actor_target,
        critic,
        critic_target,
    )
    shapes = [SDS((2,), f32), SDS((CAP, DEVS), f32)]
    places = [SDS((PA,), f32), SDS((2, PC), f32)] * 4 + [SDS((PA,), bf), SDS((2, PC), bf)]
    stat, prio, *outs = pl.pallas_call(
        update_kernel,
        out_shape=tuple(shapes + places),
        in_specs=[any_] * 10,
        out_specs=(VM,) + (any_,) * 11,
        scratch_shapes=[pltpu.VMEM((PACK, 128), f32)]
        + [pltpu.VMEM(p.shape, p.dtype) for p in places[:8] + places]
        + [pltpu.VMEM((2, TILES_C * 128), f32), pltpu.SemaphoreType.DMA((4, 5)), pltpu.SemaphoreType.DMA((3, 5))],
        compiler_params=pltpu.CompilerParams(vmem_limit_bytes=60 << 20),
        name="update",
    )(
        total,
        prio,
        actor,
        critic,
        actor_momentum,
        critic_momentum,
        actor_average,
        critic_average,
        actor_target,
        critic_target,
    )
    return (stat, prio.T[None], *outs)


def solution(mesh):
    rows = ("group", "shard")
    in_specs = (P(rows, None), P(rows, None, None), P(rows, None), P(rows, None, None, None)) + (P(),) * 8
    out_specs = (P(), P(rows, None, None)) + (P(),) * 10
    return jax.shard_map(local, mesh=mesh, in_specs=in_specs, out_specs=out_specs, check_vma=False)
```

```python
import functools

import jax
import jax.numpy as jnp
from jax import lax
from jax.experimental import pallas as pl
from jax.experimental.pallas import tpu as pltpu
from jax.sharding import PartitionSpec as P

OBS = 17
ACT = 6
UNITS = 256
CAP = 32
DEVS = 128
R_DEV = 8192
ROW = 42
PA = 71942
PC = 72193
N = DEVS * CAP

bf = jnp.bfloat16
f32 = jnp.float32
MESH = pl.DeviceIdType.MESH
VM = pl.BlockSpec(memory_space=pltpu.VMEM)
SDS = jax.ShapeDtypeStruct

SCALE = 2.0**-19
C0, C1, A, AT, T0, T1 = range(6)
FEAT = 48
ONE = 42
NEXT = 25

TILES_C = 565
STAT = 1130
ROWS_A = 563
CHIPS = DEVS // 2
CHUNKS = (9, 5)
AT_ACTOR = 2 * CHIPS * CHUNKS[0]
PACK = AT_ACTOR + 2 * CHIPS * CHUNKS[1]
PLACES = (0, 16)
SUMS = (DEVS + 2, 24, 128)
TURN = 512
WIDTH = 1024
STEPS = sorted(
    ((z, x, y) for z in range(4) for x in range(4) for y in range(4)),
    key=lambda step: -sum(min(n, 4 - n) for n in step),
)[:-1]


def dot(a, b):
    return lax.dot_general(a, b, (((1,), (0,)), ((), ())), preferred_element_type=f32)


def dot_nt(a, b):
    return lax.dot_general(a, b, (((1,), (1,)), ((), ())), preferred_element_type=f32)


def dot_exact(a, b, dims):
    return lax.dot_general(a, b, (dims, ((), ())), precision=lax.Precision.HIGHEST, preferred_element_type=f32)


def split(v):
    hi = v.astype(bf)
    return hi, (v - hi.astype(f32)).astype(bf)


def three(v):
    hi, lo = split(v)
    return jnp.concatenate([hi, lo, hi], 0)


def lanes(tile, width):
    return jnp.concatenate([tile] * (width // 128), 1)


def fold(v):
    out = v[:, :128]
    for i in range(1, v.shape[1] // 128):
        out = out + v[:, 128 * i : 128 * (i + 1)]
    return out


def column(row):
    return jnp.transpose(jnp.broadcast_to(row, (128, 128)))


def turn_noise(noise_ref, q_ref, nsend):
    q_ref[...] = jnp.zeros_like(q_ref)
    for j in range(ACT):
        q_ref[pl.ds(j + 1, CAP, stride=8), :] = 0.5 * jnp.tanh(0.4 * noise_ref[j])
    turned = jnp.transpose(q_ref[...])
    nsend[:, 0, :] = turned[:, :128]
    nsend[:, 1, :] = turned[:, 128:]


def noise_back(nrecv, nz_ref):
    back = jnp.transpose(jnp.concatenate([nrecv[:, 0, :], nrecv[:, 1, :]], 1))
    for c in range(CAP):
        nz_ref[:, 128 * c : 128 * (c + 1)] = back[8 * c : 8 * (c + 1), :]


def turn_table(i, table_ref, rows_ref):
    s = pl.ds(pl.multiple_of(i * TURN, TURN), TURN)
    v = jnp.concatenate([table_ref[:, s], jnp.zeros((128 - ROW, TURN), f32)], 0)
    rows_ref[s, :] = jnp.transpose(v)


def pick_rows(block, width, index_ref, rows_ref, picked_ref):
    tiles = width // 128
    for t in range(tiles):
        for d in range(DEVS):
            picked_ref[t, d : d + 1, :] = rows_ref[pl.ds(index_ref[block * tiles + t, d], 1), :]


def turn_rows(width, picked_ref):
    parts = [jnp.transpose(picked_ref[t])[:FEAT] for t in range(width // 128)]
    x = jnp.concatenate(parts, 1)
    ones = lax.broadcasted_iota(jnp.int32, (8, width), 0) == (ONE - 40)
    return jnp.concatenate([x[:40], jnp.where(ones, 1.0, x[40:])], 0)


def put_square(net, w2, w2f_ref, w2b_ref):
    w2 = 0.5 * w2
    turned = jnp.transpose(w2)
    hi, lo = split(turned)
    w2f_ref[net] = jnp.concatenate([hi, hi, lo], 1)
    if net in (C0, C1, A):
        hi, lo = split(w2)
        w2b_ref[net] = jnp.concatenate([hi, hi, lo], 1)


def put_first(net, pad_ref, w1_ref):
    w1 = 0.5 * pad_ref[...]
    hi = w1.astype(bf).astype(f32)
    lo = w1 - hi
    stacked = jnp.concatenate([hi, hi, lo, jnp.zeros((256 - 3 * FEAT, 256), f32)], 0)
    w1_ref[net] = jnp.transpose(stacked).astype(bf)


def put_column(ref, net, left, right, factor):
    ref[net] = jnp.concatenate([column(left * factor), column(right * factor)], 0)


def prepare_critics(critic_ref, rows_ref, pad_ref, first, w1_ref, w2f_ref, w2b_ref, b2_ref, w3_ref, b3_ref, w1a_ref):
    for t in range(TILES_C - 1):
        rows_ref[2 * t : 2 * t + 2, :] = critic_ref[:, 128 * t : 128 * (t + 1)]
    for c in range(2):
        net = first + c
        start = NEXT if first == T0 else 0
        pad_ref[...] = jnp.zeros_like(pad_ref)
        for half in range(2):
            s = pl.ds(128 * half, 128)
            pad_ref[pl.ds(start, OBS), s] = rows_ref[pl.ds(c + 2 * half, OBS, stride=4), :]
            pad_ref[pl.ds(OBS, ACT), s] = rows_ref[pl.ds(c + 2 * half + 4 * OBS, ACT, stride=4), :]
            pad_ref[pl.ds(ONE, 1), s] = rows_ref[pl.ds(92 + c + 2 * half, 1), :]
        put_first(net, pad_ref, w1_ref)
        if net == C0:
            hi = pad_ref[16:24, :].astype(bf).astype(f32)
            lo = pad_ref[16:24, :] - hi
            block = jnp.concatenate([hi, hi, lo], 1)
            w1a_ref[...] = jnp.concatenate([block, jnp.zeros_like(block)], 0).astype(bf)
        w2 = jnp.concatenate(
            [rows_ref[pl.ds(96 + c, UNITS, stride=4), :], rows_ref[pl.ds(98 + c, UNITS, stride=4), :]], 1
        )
        put_square(net, w2, w2f_ref, w2b_ref)
        put_column(b2_ref, net, rows_ref[1120 + c : 1121 + c, :], rows_ref[1122 + c : 1123 + c, :], 0.5)
        put_column(w3_ref, net, rows_ref[1124 + c : 1125 + c, :], rows_ref[1126 + c : 1127 + c, :], 1.0)
        b3_ref[net] = jnp.broadcast_to(critic_ref[c : c + 1, PC - 1 : PC], (1, 128))


def head_maps(j):
    k = lax.broadcasted_iota(jnp.int32, (UNITS, 16), 0)
    r = lax.broadcasted_iota(jnp.int32, (UNITS, 16), 1)
    row = ((k * ACT + j) >> 7) == r
    k = lax.broadcasted_iota(jnp.int32, (UNITS, 128), 0)
    l = lax.broadcasted_iota(jnp.int32, (UNITS, 128), 1)
    lane = ((k * ACT + j) & 127) == l
    return row.astype(f32), lane


def head_of(flat):
    hi = flat.astype(bf).astype(f32)
    out = []
    for part in (hi, flat - hi):
        part = part.astype(bf)
        spread = []
        for j in range(ACT):
            row, lane = head_maps(j)
            spread.append(jnp.where(lane, dot(row.astype(bf), part), 0.0).astype(bf))
        r = lax.broadcasted_iota(jnp.int32, (16, 128 * ACT), 0)
        l = lax.broadcasted_iota(jnp.int32, (16, 128 * ACT), 1)
        take = ((l >> 7) == (r - 1)).astype(f32).astype(bf)
        out.append(dot_nt(take, jnp.concatenate(spread, 1))[:8])
    return out


def head_back(turned):
    out = jnp.zeros((16, 128), f32)
    for j in range(ACT):
        row, lane = head_maps(j)
        picked = jnp.transpose(row) * turned[j + 1 : j + 2, :]
        out = out + dot_exact(picked, lane.astype(f32), ((1,), (0,)))
    return out


def prepare_actor(net, actor_ref, rows_ref, pad_ref, w1_ref, w2f_ref, w2b_ref, b2_ref, w3t_ref, w3b_ref, b3a_ref):
    whole = PA // 1024
    for t in range(whole):
        rows_ref[8 * t : 8 * t + 8, :] = actor_ref[pl.ds(1024 * t, 1024)].reshape(8, 128)
    rest = (PA - 1024 * whole) // 128
    rows_ref[8 * whole : 8 * whole + rest, :] = actor_ref[pl.ds(1024 * whole, 128 * rest)].reshape(rest, 128)
    rows_ref[562:563, 0:ACT] = actor_ref[pl.ds(562 * 128, ACT)].reshape(1, ACT)
    start = NEXT if net == AT else 0
    pad_ref[...] = jnp.zeros_like(pad_ref)
    for half in range(2):
        s = pl.ds(128 * half, 128)
        pad_ref[pl.ds(start, OBS), s] = rows_ref[pl.ds(half, OBS, stride=2), :]
        pad_ref[pl.ds(ONE, 1), s] = rows_ref[pl.ds(34 + half, 1), :]
    put_first(net, pad_ref, w1_ref)
    w2 = jnp.concatenate([rows_ref[pl.ds(36, UNITS, stride=2), :], rows_ref[pl.ds(37, UNITS, stride=2), :]], 1)
    put_square(net, w2, w2f_ref, w2b_ref)
    put_column(b2_ref, net, rows_ref[548:549, :], rows_ref[549:550, :], 0.5)
    flat = jnp.concatenate([rows_ref[550:562, :], jnp.zeros((4, 128), f32)], 0)
    hi, lo = head_of(flat)
    block = jnp.concatenate([hi, hi, lo], 1)
    w3t_ref[net - A] = jnp.concatenate([block, jnp.zeros_like(block)], 0).astype(bf)
    if net == A:
        stacked = jnp.concatenate([hi, hi, lo, jnp.zeros((104, UNITS), f32)], 0)
        w3b_ref[...] = (0.5 * jnp.transpose(stacked)).astype(bf)
    bias = column(rows_ref[562:563, :])
    b3a_ref[net - A] = jnp.zeros((8, 128), f32)
    b3a_ref[net - A, 1 : 1 + ACT, :] = bias[:ACT]


def act(zh):
    u = jnp.tanh(zh) + 1.0
    return u, zh * u


def slope(u, s):
    return u + s * (2.0 - u)


class Step:
    def __init__(self, i, width, x, weights):
        (
            self.w1, self.w2f, self.w2b, self.b2, self.w3, self.b3, self.w3t, self.w3b, self.b3a, self.w1a,
        ) = weights
        self.i, self.width = i, width
        self.lanes = pl.ds(pl.multiple_of(i * width, width), width)
        self.x = x
        self.x3 = three(self.x)
        rows8 = lax.broadcasted_iota(jnp.int32, (8, width), 0)
        self.is_action = (rows8 >= 1) & (rows8 <= ACT)

    def with_action(self, a):
        x = self.x
        return three(jnp.concatenate([x[:16], jnp.where(self.is_action, a, x[16:24]), x[24:]], 0))

    def first(self, net, xx):
        return act(dot(self.w1[net, :, : 3 * FEAT], xx))

    def second(self, net, h3):
        return act(dot(self.w2f[net], h3) + lanes(self.b2[net], self.width))

    def value(self, net, s):
        return jnp.sum(s * lanes(self.w3[net], self.width), 0, keepdims=True) + lanes(self.b3[net], self.width)

    def head(self, net, s3):
        return dot(self.w3t[net - A], s3)[:8] + lanes(self.b3a[net - A], self.width)

    def valid(self, count_ref):
        tiles = self.width // 128
        return jnp.concatenate([((self.i * tiles + t) < count_ref[...]).astype(f32) for t in range(tiles)], 1)

    def grads2(self, net, h1, dz2, g2_ref):
        u = UNITS
        left = jnp.concatenate([h1[:u], h1[u : 2 * u], h1[:u]], 1)
        g2_ref[net] += dot_nt(left, jnp.concatenate([dz2[:u], dz2[:u], dz2[u : 2 * u]], 1))

    def grads1(self, net, dz1, g1_ref):
        xhi, xlo = self.x3[:FEAT], self.x3[FEAT : 2 * FEAT]
        left = jnp.concatenate(
            [jnp.concatenate([xhi, xlo], 0), jnp.concatenate([xhi, jnp.zeros_like(xlo)], 0)], 1
        )
        a, b = split(dz1)
        g1_ref[net] += dot_nt(left, jnp.concatenate([a, b], 1))


def critic_block(i, width, x, nz_ref, count_ref, weights, prio_ref, grads):
    g2_ref, g1_ref, g3a_ref, db2_ref, dw3_ref, st_ref = grads
    st = Step(i, width, x, weights)
    x3 = st.x3

    u, s = st.first(AT, x3)
    u, s = st.second(AT, three(s))
    next_action = jnp.tanh(st.head(AT, three(s)) + nz_ref[:, st.lanes])
    xt = st.with_action(next_action)
    u, s = st.first(T0, xt)
    h0 = three(s)
    u, s = st.first(T1, xt)
    h1t = three(s)
    u, s = st.second(T0, h0)
    targets = [st.value(T0, s)]
    u0, s0 = st.first(C0, x3)
    h1, d1 = three(s0), slope(u0, s0)
    u, s = st.second(T1, h1t)
    targets.append(st.value(T1, s))
    u0, s0 = st.second(C0, h1)
    y = x[23:24] + 0.99 * x[24:25] * jnp.minimum(targets[0], targets[1])
    valid = st.valid(count_ref)
    scaled = valid * SCALE
    st_ref[1:2, :] += fold(valid)

    def top(net, s, d2):
        delta = st.value(net, s) - y
        if net == C0:
            prio = valid * jnp.sqrt(delta * delta + 1.0)
            tiles = width // 128
            for t in range(tiles):
                prio_ref[pl.ds(i * tiles + t, 1), :] = prio[:, 128 * t : 128 * (t + 1)]
        st_ref[0:1, :] += fold(valid * (delta * delta))
        dq = (2.0 * scaled) * delta
        st_ref[2 + net : 3 + net, :] += fold(dq)
        dw3_ref[net] += fold(s * dq)
        dz2 = lanes(st.w3[net], width) * (0.5 * dq) * d2
        db2_ref[net] += fold(dz2)
        return three(dz2)

    u, s = st.first(C1, x3)
    h1b, d1b = three(s), slope(u, s)
    dz2 = top(C0, s0, slope(u0, s0))
    dz1 = dot(st.w2b[C0], dz2) * d1
    st.grads2(C0, h1, dz2, g2_ref)
    u, s = st.second(C1, h1b)
    st.grads1(C0, dz1, g1_ref)
    dz2 = top(C1, s, slope(u, s))
    dz1 = dot(st.w2b[C1], dz2) * d1b
    st.grads2(C1, h1b, dz2, g2_ref)
    st.grads1(C1, dz1, g1_ref)


def actor_block(i, width, x, count_ref, weights, grads):
    g2_ref, g1_ref, g3a_ref, db2_ref, dw3_ref, st_ref = grads
    st = Step(i, width, x, weights)

    u, s = st.first(A, st.x3)
    h1a, d1a = three(s), slope(u, s)
    u, s = st.second(A, h1a)
    h2a, d2a = three(s), slope(u, s)
    policy = jnp.tanh(st.head(A, h2a))

    u, s = st.first(C0, st.with_action(policy))
    d1f = slope(u, s)
    u, s = st.second(C0, three(s))
    d2f, q_policy = slope(u, s), st.value(C0, s)
    valid = st.valid(count_ref)
    st_ref[0:1, :] -= fold(valid * q_policy)

    dz2 = three(lanes(st.w3[C0], width) * (-0.5 * SCALE * valid) * d2f)
    dz1 = three(dot(st.w2b[C0], dz2) * d1f)
    da = dot(st.w1a[...], dz1)[:8]
    dp = jnp.where(st.is_action, da * (1.0 - policy * policy), 0.0)
    st_ref[8:16, :] += fold(dp)
    hi = dp.astype(bf).astype(f32)
    lo = dp - hi
    zero = jnp.zeros_like(hi)
    stacked = jnp.concatenate([hi, lo, hi, zero], 0).astype(bf)
    left = jnp.concatenate([jnp.concatenate([hi, lo], 0), jnp.concatenate([hi, zero], 0)], 1).astype(bf)
    dz2 = dot(st.w3b[:, :32], stacked) * d2a
    db2_ref[A] += fold(dz2)
    dz2 = three(dz2)
    dz1 = dot(st.w2b[A], dz2) * d1a
    g3a_ref[...] += dot_nt(left, jnp.concatenate([h2a[:UNITS], h2a[UNITS : 2 * UNITS]], 1))
    st.grads2(A, h1a, dz2, g2_ref)
    st.grads1(A, dz1, g1_ref)


def lane_sums(tile):
    return dot_exact(jnp.ones((8, 128), f32), tile, ((1,), (1,)))


def pack_critics(pack_ref, grads):
    g2_ref, g1_ref, g3a_ref, db2_ref, dw3_ref, st_ref = grads
    lane = lax.broadcasted_iota(jnp.int32, (1, 128), 1)
    sums = jnp.sum(st_ref[...], 1, keepdims=True)
    for c in range(2):
        g1 = g1_ref[c, :FEAT, :] + g1_ref[c, FEAT:, :]
        b2 = lane_sums(db2_ref[c])[0:1]
        w3 = lane_sums(dw3_ref[c])[0:1]
        for half in range(2):
            s = slice(128 * half, 128 * (half + 1))
            at = c + 2 * half
            pack_ref[pl.ds(at, OBS + ACT, stride=4), :] = g1[: OBS + ACT, s]
            pack_ref[at + 92 : at + 93, :] = g1[ONE : ONE + 1, s]
            pack_ref[pl.ds(at + 96, UNITS, stride=4), :] = g2_ref[c, :, s]
            pack_ref[at + 1120 : at + 1121, :] = b2[:, s]
            pack_ref[at + 1124 : at + 1125, :] = w3[:, s]
        pack_ref[c + 1128 : c + 1129, :] = jnp.where(lane == 0, sums[2 + c : 3 + c], 0.0)
    pack_ref[STAT : STAT + 1, :] = jnp.where(lane == 0, sums[0:1], jnp.where(lane == 1, sums[1:2], 0.0))
    pack_ref[STAT + 1 : AT_ACTOR, :] = jnp.zeros((AT_ACTOR - STAT - 1, 128), f32)


def pack_actor(pack_ref, grads):
    g2_ref, g1_ref, g3a_ref, db2_ref, dw3_ref, st_ref = grads
    sums = jnp.sum(st_ref[...], 1, keepdims=True)
    g1 = g1_ref[A, :FEAT, :] + g1_ref[A, FEAT:, :]
    b2 = lane_sums(db2_ref[A])[0:1]
    o = AT_ACTOR
    for half in range(2):
        s = slice(128 * half, 128 * (half + 1))
        pack_ref[pl.ds(o + half, OBS, stride=2), :] = g1[:OBS, s]
        pack_ref[o + 34 + half : o + 35 + half, :] = g1[ONE : ONE + 1, s]
        pack_ref[pl.ds(o + 36 + half, UNITS, stride=2), :] = g2_ref[A, :, s]
        pack_ref[o + 548 + half : o + 549 + half, :] = b2[:, s]
    pack_ref[o + 550 : o + 562, :] = head_back(g3a_ref[:8, :] + g3a_ref[8:, :])[:12]
    e = lax.broadcasted_iota(jnp.int32, (8, 128), 1) == lax.broadcasted_iota(jnp.int32, (8, 128), 0) - 1
    pack_ref[o + 562 : o + 563, :] = jnp.sum(jnp.where(e, sums[8:16], 0.0), 0, keepdims=True)
    pack_ref[o + ROWS_A : PACK, :] = jnp.zeros((PACK - o - ROWS_A, 128), f32)


WEIGHTS = [
    pltpu.VMEM((6, UNITS, 256), bf),
    pltpu.VMEM((6, UNITS, 3 * UNITS), bf),
    pltpu.VMEM((3, UNITS, 3 * UNITS), bf),
    pltpu.VMEM((6, UNITS, 128), f32),
    pltpu.VMEM((6, UNITS, 128), f32),
    pltpu.VMEM((6, 1, 128), f32),
    pltpu.VMEM((2, 16, 3 * UNITS), bf),
    pltpu.VMEM((UNITS, 128), bf),
    pltpu.VMEM((2, 8, 128), f32),
    pltpu.VMEM((16, 3 * UNITS), bf),
]
GRADS = [
    pltpu.VMEM((3, UNITS, UNITS), f32),
    pltpu.VMEM((3, 2 * FEAT, UNITS), f32),
    pltpu.VMEM((16, UNITS), f32),
    pltpu.VMEM((3, UNITS, 128), f32),
    pltpu.VMEM((2, UNITS, 128), f32),
    pltpu.VMEM((16, 128), f32),
]


def drain(ref, sem, copies):
    view = ref.at[pl.ds(0, copies)]
    pltpu.make_async_copy(view, view, sem).wait()


class Place:
    def __init__(self):
        group, shard = lax.axis_index("group"), lax.axis_index("shard")
        self.core = lax.rem(shard, 2)
        z, x, y = group // 4, lax.rem(group, 4), shard // 2
        self.chip = group * 4 + y
        self.sibling = (group, shard + 1 - 2 * self.core)
        self.sibling_at = group * 8 + shard + 1 - 2 * self.core
        self.me = group * 8 + shard
        self.zs, self.xs, self.ys = ([lax.rem(v + n, 4) for n in range(4)] for v in (z, x, y))

    def others(self, other_core=False):
        core = 1 - self.core if other_core else self.core
        for dz, dx, dy in STEPS:
            group = self.zs[dz] * 4 + self.xs[dx]
            yield group * 4 + self.ys[dy], (group, self.ys[dy] * 2 + core)


class Sum:
    def __init__(self, place, g, pack_ref, out, buffers, sems):
        self.place, self.chunk = place, CHUNKS[g]
        self.out = out.at[pl.ds(place.core * CHIPS, CHIPS), pl.ds(PLACES[g], self.chunk)]
        self.first = (0, AT_ACTOR)[g]
        self.rows = CHIPS * self.chunk
        self.pack_ref = pack_ref
        self.other, self.half, self.parts, self.mine, self.whole = buffers
        self.sems = sems.at[g]

    def remote(self, src, dst, n, to):
        return pltpu.make_async_remote_copy(
            src_ref=src,
            dst_ref=dst,
            send_sem=self.sems.at[2 * n],
            recv_sem=self.sems.at[2 * n + 1],
            device_id=to,
            device_id_type=MESH,
        )

    def swap(self):
        give = pl.multiple_of(self.first + (1 - self.place.core) * self.rows, 8)
        return self.remote(self.pack_ref.at[pl.ds(give, self.rows)], self.other, 0, self.place.sibling)

    def scatter(self):
        keep = pl.multiple_of(self.first + self.place.core * self.rows, 8)
        total = self.pack_ref[pl.ds(keep, self.rows), :] + self.other[...]
        for j in range(self.chunk):
            self.half[:, j, :] = total[CHIPS * j : CHIPS * (j + 1)]
        chip = self.place.chip
        for peer, device in self.place.others():
            self.remote(self.half.at[peer], self.parts.at[chip], 1, device).start()

    def spread(self):
        chip = self.place.chip
        drain(self.half, self.sems.at[2], CHIPS - 1)
        drain(self.parts, self.sems.at[3], CHIPS - 1)
        self.parts[pl.ds(chip, 1)] = self.half[pl.ds(chip, 1)]
        self.mine[...] = jnp.sum(self.parts[...], 0)
        for _, device in self.place.others():
            self.remote(self.mine, self.whole.at[chip], 2, device).start()

    def back_copies(self):
        return (
            pltpu.make_async_copy(self.whole, self.out, self.sems.at[8]),
            self.remote(self.whole, self.out, 3, self.place.sibling),
        )

    def back(self):
        drain(self.parts, self.sems.at[4], CHIPS - 1)
        drain(self.whole, self.sems.at[5], CHIPS - 1)
        self.whole[pl.ds(self.place.chip, 1)] = self.mine[...][None]
        for copy in self.back_copies():
            copy.start()

    def finish(self):
        for copy in self.back_copies():
            copy.wait()


def sum_buffers():
    out = []
    for chunk in CHUNKS:
        out += [
            pltpu.VMEM((CHIPS * chunk, 128), f32),
            pltpu.VMEM((CHIPS, chunk, 128), f32),
            pltpu.VMEM((CHIPS, chunk, 128), f32),
            pltpu.VMEM((chunk, 128), f32),
            pltpu.VMEM((CHIPS, chunk, 128), f32),
        ]
    return out


def step_kernel(
    width,
    table_hbm,
    index_hbm,
    noise_hbm,
    count_hbm,
    actor_hbm,
    actor_t_hbm,
    critic_hbm,
    critic_t_hbm,
    out_hbm,
    prio_ref,
    table_ref,
    index_ref,
    noise_ref,
    count_ref,
    actor_ref,
    actor_t_ref,
    critic_ref,
    critic_t_ref,
    in_sems,
    rows_ref,
    picked_ref,
    q_ref,
    nsend,
    nrecv,
    noise_sems,
    x_ref,
    nz_ref,
    flat_ref,
    pad_ref,
    pack_ref,
    sems,
    *scratch,
):
    weights, grads = scratch[: len(WEIGHTS)], scratch[len(WEIGHTS) : len(WEIGHTS) + len(GRADS)]
    buffers = scratch[len(WEIGHTS) + len(GRADS) :]
    w1_ref, w2f_ref, w2b_ref, b2_ref, w3_ref, b3_ref, w3t_ref, w3b_ref, b3a_ref, w1a_ref = weights
    blocks = N // width
    place = Place()
    me = place.me

    loads = [
        pltpu.make_async_copy(src, dst, in_sems.at[n])
        for n, (src, dst) in enumerate(
            (
                (critic_hbm, critic_ref),
                (actor_hbm, actor_ref),
                (table_hbm, table_ref),
                (index_hbm, index_ref),
                (count_hbm, count_ref),
                (noise_hbm, noise_ref),
                (critic_t_hbm, critic_t_ref),
                (actor_t_hbm, actor_t_ref),
            )
        )
    ]
    for load in loads:
        load.start()

    barrier = pltpu.get_barrier_semaphore()

    def all_others():
        for other_core in (False, True):
            for _, device in place.others(other_core):
                yield device[0] * 8 + device[1], device
        yield place.sibling_at, place.sibling

    for _, device in all_others():
        pl.semaphore_signal(barrier, inc=1, device_id=device, device_id_type=MESH)
    for ref in grads:
        ref[...] = jnp.zeros_like(ref)
    loads[0].wait()
    prepare_critics(
        critic_ref, flat_ref, pad_ref, C0, w1_ref, w2f_ref, w2b_ref, b2_ref, w3_ref, b3_ref, w1a_ref
    )
    loads[1].wait()
    prepare_actor(
        A, actor_ref, flat_ref, pad_ref, w1_ref, w2f_ref, w2b_ref, b2_ref, w3t_ref, w3b_ref, b3a_ref
    )
    loads[2].wait()

    def turn(i, carry):
        turn_table(i, table_ref, rows_ref)
        return carry

    lax.fori_loop(0, R_DEV // TURN, turn, 0)
    loads[3].wait()
    pick_rows(0, width, index_ref, rows_ref, picked_ref)
    loads[4].wait()
    loads[5].wait()
    turn_noise(noise_ref, q_ref, nsend)

    def send():
        for peer, device in all_others():
            pltpu.make_async_remote_copy(
                src_ref=nsend.at[peer],
                dst_ref=nrecv.at[me],
                send_sem=noise_sems.at[0],
                recv_sem=noise_sems.at[1],
                device_id=device,
                device_id_type=MESH,
            ).start()

    def actors(i, carry):
        x = turn_rows(width, picked_ref)
        x_ref[:, pl.ds(pl.multiple_of(i * width, width), width)] = x
        actor_block(i, width, x, count_ref, weights, grads)
        pick_rows(lax.rem(i + 1, blocks), width, index_ref, rows_ref, picked_ref)

        @pl.when(i == 0)
        def _():
            pl.semaphore_wait(barrier, DEVS - 1)
            send()

        return carry

    lax.fori_loop(0, blocks, actors, 0)
    pack_actor(pack_ref, grads)
    late, early = (Sum(place, g, pack_ref, out_hbm, buffers[5 * g : 5 * g + 5], sems) for g in range(2))
    early.swap().start()

    loads[6].wait()
    prepare_critics(
        critic_t_ref, flat_ref, pad_ref, T0, w1_ref, w2f_ref, w2b_ref, b2_ref, w3_ref, b3_ref, w1a_ref
    )
    loads[7].wait()
    prepare_actor(
        AT, actor_t_ref, flat_ref, pad_ref, w1_ref, w2f_ref, w2b_ref, b2_ref, w3t_ref, w3b_ref, b3a_ref
    )
    drain(nsend, noise_sems.at[0], DEVS - 1)
    drain(nrecv, noise_sems.at[1], DEVS - 1)
    nrecv[pl.ds(me, 1)] = nsend[pl.ds(me, 1)]
    noise_back(nrecv, nz_ref)

    def critics(i, carry):
        x = x_ref[:, pl.ds(pl.multiple_of(i * width, width), width)]
        critic_block(i, width, x, nz_ref, count_ref, weights, prio_ref, grads)

        @pl.when(i == 0)
        def _():
            early.swap().wait()
            early.scatter()

        @pl.when(i == 1)
        def _():
            early.spread()

        @pl.when(i == 2)
        def _():
            early.back()

        return carry

    lax.fori_loop(0, blocks, critics, 0)
    pack_critics(pack_ref, grads)
    late.swap().start()
    prios = [
        pltpu.make_async_copy(
            prio_ref.at[pl.ds(16 * n, 16)], out_hbm.at[DEVS + n, pl.ds(0, 16)], in_sems.at[n]
        )
        for n in range(2)
    ]
    for copy in prios:
        copy.start()
    late.swap().wait()
    late.scatter()
    early.finish()
    for copy in prios:
        copy.wait()
    late.spread()
    late.back()
    late.finish()


def update(weight, grad, momentum, average, target):
    momentum_new = 0.9 * momentum + grad
    weight_new = weight - 0.1 * (grad + 0.9 * momentum_new)
    average_new = 0.99 * average + 0.01 * weight_new
    target_new = 0.005 * weight_new + 0.995 * target
    return (weight_new, momentum_new, average_new, target_new, weight_new.astype(bf))


STEP = 1024
CUTS = (0, 35 * STEP, PC)


def update_kernel(sum_hbm, *refs):
    ins, stat_ref, prio_out, outs_hbm, outs = refs[:8], refs[8], refs[9], refs[10:20], refs[20:30]
    late_ref, early_ref, grad_ref, in_sems, out_sems = refs[30:]
    loads = [
        pltpu.make_async_copy(
            sum_hbm.at[pl.ds(0, DEVS), pl.ds(PLACES[g], CHUNKS[g])], (late_ref, early_ref)[g], in_sems.at[g]
        )
        for g in range(2)
    ]
    for load in loads:
        load.start()
    pass_on = pltpu.make_async_copy(sum_hbm.at[pl.ds(DEVS, 2), pl.ds(0, 16)], prio_out, in_sems.at[2])
    pass_on.start()

    def stores(piece):
        out = []
        for n in range(5):
            src, dst = outs[2 * n + min(piece, 1)], outs_hbm[2 * n + min(piece, 1)]
            if piece:
                s = pl.ds(CUTS[piece - 1], CUTS[piece] - CUTS[piece - 1])
                src, dst = src.at[:, s], dst.at[:, s]
            out.append(pltpu.make_async_copy(src, dst, out_sems.at[piece, n]))
        return out

    for load in loads:
        load.wait()

    def rows(g, r, n):
        core, r = divmod(r, CHIPS * CHUNKS[g])
        j, k = divmod(r, CHIPS)
        return (late_ref, early_ref)[g][core * CHIPS + k : core * CHIPS + k + n, j, :]

    stat = rows(0, STAT, 1)
    factor = (1.0 / SCALE) / stat[:, 1:2]
    stat_ref[...] = stat[:, :2].reshape(2)

    def actor(s, grad):
        values = update(ins[0][s], grad, ins[2][s], ins[4][s], ins[6][s])
        for ref, value in zip(outs[0::2], values):
            ref[s] = value

    for i in range(PA // STEP):
        actor(slice(STEP * i, STEP * (i + 1)), (rows(1, 8 * i, 8) * factor).reshape(STEP))
    done = PA // STEP * STEP
    r = done // 128
    more = (PA - done) // 128
    actor(slice(done, done + 128 * more), (rows(1, r, more) * factor).reshape(128 * more))
    done += 128 * more
    actor(slice(done, PA), (rows(1, r + more, 1)[:, :ACT] * factor).reshape(ACT))
    for store in stores(0):
        store.start()

    def critic(s):
        values = update(ins[1][:, s], grad_ref[:, s], ins[3][:, s], ins[5][:, s], ins[7][:, s])
        for ref, value in zip(outs[1::2], values):
            ref[:, s] = value

    def critics(i, carry):
        critic(pl.ds(pl.multiple_of(i * STEP, STEP), STEP))
        return carry

    for t in range(TILES_C):
        grad_ref[:, 128 * t : 128 * (t + 1)] = rows(0, 2 * t, 2) * factor
    for piece in (1, 2):
        lax.fori_loop(CUTS[piece - 1] // STEP, CUTS[piece] // STEP, critics, 0, unroll=5)
        if piece == 2:
            done = PC // STEP * STEP
            critic(pl.ds(done, PC - done))
        for store in stores(piece):
            store.start()
    for piece in range(3):
        for store in stores(piece):
            store.wait()
    pass_on.wait()


def local(
    replay,
    sample_index,
    pair_count,
    noise,
    actor,
    critic,
    actor_momentum,
    critic_momentum,
    actor_average,
    critic_average,
    actor_target,
    critic_target,
):
    any_ = pl.BlockSpec(memory_space=pl.ANY)
    total = pl.pallas_call(
        functools.partial(step_kernel, WIDTH),
        out_shape=SDS(SUMS, f32),
        in_specs=[any_] * 8,
        out_specs=any_,
        scratch_shapes=[
            pltpu.VMEM((CAP, DEVS), f32),
            pltpu.VMEM((ROW, R_DEV), f32),
            pltpu.SMEM((CAP, DEVS), jnp.int32),
            pltpu.VMEM((ACT, CAP, DEVS), f32),
            pltpu.VMEM((1, DEVS), jnp.int32),
            pltpu.VMEM((PA,), f32),
            pltpu.VMEM((PA,), f32),
            pltpu.VMEM((2, PC), f32),
            pltpu.VMEM((2, PC), f32),
            pltpu.SemaphoreType.DMA((8,)),
            pltpu.VMEM((R_DEV, 128), f32),
            pltpu.VMEM((WIDTH // 128, 128, 128), f32),
            pltpu.VMEM((256, 128), f32),
            pltpu.VMEM((DEVS, 2, 128), f32),
            pltpu.VMEM((DEVS, 2, 128), f32),
            pltpu.SemaphoreType.DMA((2,)),
            pltpu.VMEM((FEAT, N), f32),
            pltpu.VMEM((8, N), f32),
            pltpu.VMEM((2 * TILES_C + 6, 128), f32),
            pltpu.VMEM((FEAT, 256), f32),
            pltpu.VMEM((PACK, 128), f32),
            pltpu.SemaphoreType.DMA((2, 9)),
        ]
        + WEIGHTS
        + GRADS
        + sum_buffers(),
        compiler_params=pltpu.CompilerParams(
            collective_id=0, has_side_effects=True, vmem_limit_bytes=56 << 20
        ),
        name="td3_step",
    )(
        replay.T,
        sample_index[0].T,
        jnp.transpose(noise[0], (2, 1, 0)),
        pair_count,
        actor,
        actor_target,
        critic,
        critic_target,
    )
    shapes = [SDS((2,), f32), SDS((2, CAP // 2, DEVS), f32)]
    places = [SDS((PA,), f32), SDS((2, PC), f32)] * 4 + [SDS((PA,), bf), SDS((2, PC), bf)]
    stat, prio, *outs = pl.pallas_call(
        update_kernel,
        out_shape=tuple(shapes + places),
        in_specs=[any_] + [VM] * 8,
        out_specs=(VM,) + (any_,) * 11,
        scratch_shapes=[pltpu.VMEM(p.shape, p.dtype) for p in places]
        + [
            pltpu.VMEM((DEVS, CHUNKS[0], 128), f32),
            pltpu.VMEM((DEVS, CHUNKS[1], 128), f32),
            pltpu.VMEM((2, TILES_C * 128), f32),
            pltpu.SemaphoreType.DMA((3,)),
            pltpu.SemaphoreType.DMA((3, 5)),
        ],
        compiler_params=pltpu.CompilerParams(vmem_limit_bytes=60 << 20),
        name="update",
    )(
        total,
        actor,
        critic,
        actor_momentum,
        critic_momentum,
        actor_average,
        critic_average,
        actor_target,
        critic_target,
    )
    return (stat, prio.reshape(CAP, DEVS).T[None], *outs)


def solution(mesh):
    rows = ("group", "shard")
    in_specs = (P(rows, None), P(rows, None, None), P(rows, None), P(rows, None, None, None)) + (P(),) * 8
    out_specs = (P(), P(rows, None, None)) + (P(),) * 10
    return jax.shard_map(local, mesh=mesh, in_specs=in_specs, out_specs=out_specs, check_vma=False)
```

```python
import functools

import jax
import jax.numpy as jnp
from jax import lax
from jax.experimental import pallas as pl
from jax.experimental.pallas import tpu as pltpu
from jax.sharding import PartitionSpec as P

OBS = 17
ACT = 6
UNITS = 256
CAP = 32
DEVS = 128
R_DEV = 8192
ROW = 42
PA = 71942
PC = 72193
N = DEVS * CAP

bf = jnp.bfloat16
f32 = jnp.float32
MESH = pl.DeviceIdType.MESH
VM = pl.BlockSpec(memory_space=pltpu.VMEM)
SDS = jax.ShapeDtypeStruct

SCALE = 2.0**-19
C0, C1, A, AT, T0, T1 = range(6)
FEAT = 48
ONE = 42
NEXT = 25

TILES_C = 565
STAT = 1130
ROWS_A = 563
CHIPS = DEVS // 2
CHUNKS = (9, 5)
AT_ACTOR = 2 * CHIPS * CHUNKS[0]
PACK = AT_ACTOR + 2 * CHIPS * CHUNKS[1]
AT_PRIO = DEVS
AT_SUM = DEVS + 2
RESULT = (3700, 16, 128)
TURN = 512
WIDTH = 1024
STEPS = sorted(
    ((z, x, y) for z in range(4) for x in range(4) for y in range(4)),
    key=lambda step: -sum(min(n, 4 - n) for n in step),
)[:-1]


def dot(a, b):
    return lax.dot_general(a, b, (((1,), (0,)), ((), ())), preferred_element_type=f32)


def dot_nt(a, b):
    return lax.dot_general(a, b, (((1,), (1,)), ((), ())), preferred_element_type=f32)


def dot_exact(a, b, dims):
    return lax.dot_general(a, b, (dims, ((), ())), precision=lax.Precision.HIGHEST, preferred_element_type=f32)


def split(v):
    hi = v.astype(bf)
    return hi, (v - hi.astype(f32)).astype(bf)


def three(v):
    hi, lo = split(v)
    return jnp.concatenate([hi, lo, hi], 0)


def lanes(tile, width):
    return jnp.concatenate([tile] * (width // 128), 1)


def fold(v):
    out = v[:, :128]
    for i in range(1, v.shape[1] // 128):
        out = out + v[:, 128 * i : 128 * (i + 1)]
    return out


def column(row):
    return jnp.transpose(jnp.broadcast_to(row, (128, 128)))


def turn_noise(noise_ref, q_ref, nsend):
    q_ref[...] = jnp.zeros_like(q_ref)
    for j in range(ACT):
        q_ref[pl.ds(j + 1, CAP, stride=8), :] = 0.5 * jnp.tanh(0.4 * noise_ref[j])
    turned = jnp.transpose(q_ref[...])
    nsend[:, 0, :] = turned[:, :128]
    nsend[:, 1, :] = turned[:, 128:]


def noise_back(nrecv, nz_ref):
    back = jnp.transpose(jnp.concatenate([nrecv[:, 0, :], nrecv[:, 1, :]], 1))
    for c in range(CAP):
        nz_ref[:, 128 * c : 128 * (c + 1)] = back[8 * c : 8 * (c + 1), :]


def turn_table(i, table_ref, rows_ref):
    s = pl.ds(pl.multiple_of(i * TURN, TURN), TURN)
    v = jnp.concatenate([table_ref[:, s], jnp.zeros((128 - ROW, TURN), f32)], 0)
    rows_ref[s, :] = jnp.transpose(v)


def pick_rows(block, width, index_ref, rows_ref, picked_ref):
    tiles = width // 128
    for t in range(tiles):
        for d in range(DEVS):
            picked_ref[t, d : d + 1, :] = rows_ref[pl.ds(index_ref[block * tiles + t, d], 1), :]


def turn_rows(width, picked_ref):
    parts = [jnp.transpose(picked_ref[t])[:FEAT] for t in range(width // 128)]
    x = jnp.concatenate(parts, 1)
    ones = lax.broadcasted_iota(jnp.int32, (8, width), 0) == (ONE - 40)
    return jnp.concatenate([x[:40], jnp.where(ones, 1.0, x[40:])], 0)


def put_square(net, w2, w2f_ref, w2b_ref):
    w2 = 0.5 * w2
    turned = jnp.transpose(w2)
    hi, lo = split(turned)
    w2f_ref[net] = jnp.concatenate([hi, hi, lo], 1)
    if net in (C0, C1, A):
        hi, lo = split(w2)
        w2b_ref[net] = jnp.concatenate([hi, hi, lo], 1)


def put_first(net, pad_ref, w1_ref):
    w1 = 0.5 * pad_ref[...]
    hi = w1.astype(bf).astype(f32)
    lo = w1 - hi
    stacked = jnp.concatenate([hi, hi, lo, jnp.zeros((256 - 3 * FEAT, 256), f32)], 0)
    w1_ref[net] = jnp.transpose(stacked).astype(bf)


def put_column(ref, net, left, right, factor):
    ref[net] = jnp.concatenate([column(left * factor), column(right * factor)], 0)


def prepare_critics(critic_ref, rows_ref, pad_ref, first, w1_ref, w2f_ref, w2b_ref, b2_ref, w3_ref, b3_ref, w1a_ref):
    for t in range(TILES_C - 1):
        rows_ref[2 * t : 2 * t + 2, :] = critic_ref[:, 128 * t : 128 * (t + 1)]
    for c in range(2):
        net = first + c
        start = NEXT if first == T0 else 0
        pad_ref[...] = jnp.zeros_like(pad_ref)
        for half in range(2):
            s = pl.ds(128 * half, 128)
            pad_ref[pl.ds(start, OBS), s] = rows_ref[pl.ds(c + 2 * half, OBS, stride=4), :]
            pad_ref[pl.ds(OBS, ACT), s] = rows_ref[pl.ds(c + 2 * half + 4 * OBS, ACT, stride=4), :]
            pad_ref[pl.ds(ONE, 1), s] = rows_ref[pl.ds(92 + c + 2 * half, 1), :]
        put_first(net, pad_ref, w1_ref)
        if net == C0:
            hi = pad_ref[16:24, :].astype(bf).astype(f32)
            lo = pad_ref[16:24, :] - hi
            block = jnp.concatenate([hi, hi, lo], 1)
            w1a_ref[...] = jnp.concatenate([block, jnp.zeros_like(block)], 0).astype(bf)
        w2 = jnp.concatenate(
            [rows_ref[pl.ds(96 + c, UNITS, stride=4), :], rows_ref[pl.ds(98 + c, UNITS, stride=4), :]], 1
        )
        put_square(net, w2, w2f_ref, w2b_ref)
        put_column(b2_ref, net, rows_ref[1120 + c : 1121 + c, :], rows_ref[1122 + c : 1123 + c, :], 0.5)
        put_column(w3_ref, net, rows_ref[1124 + c : 1125 + c, :], rows_ref[1126 + c : 1127 + c, :], 1.0)
        b3_ref[net] = jnp.broadcast_to(critic_ref[c : c + 1, PC - 1 : PC], (1, 128))


def head_maps(j):
    k = lax.broadcasted_iota(jnp.int32, (UNITS, 16), 0)
    r = lax.broadcasted_iota(jnp.int32, (UNITS, 16), 1)
    row = ((k * ACT + j) >> 7) == r
    k = lax.broadcasted_iota(jnp.int32, (UNITS, 128), 0)
    l = lax.broadcasted_iota(jnp.int32, (UNITS, 128), 1)
    lane = ((k * ACT + j) & 127) == l
    return row.astype(f32), lane


def head_of(flat):
    hi = flat.astype(bf).astype(f32)
    out = []
    for part in (hi, flat - hi):
        part = part.astype(bf)
        spread = []
        for j in range(ACT):
            row, lane = head_maps(j)
            spread.append(jnp.where(lane, dot(row.astype(bf), part), 0.0).astype(bf))
        r = lax.broadcasted_iota(jnp.int32, (16, 128 * ACT), 0)
        l = lax.broadcasted_iota(jnp.int32, (16, 128 * ACT), 1)
        take = ((l >> 7) == (r - 1)).astype(f32).astype(bf)
        out.append(dot_nt(take, jnp.concatenate(spread, 1))[:8])
    return out


def head_back(turned):
    out = jnp.zeros((16, 128), f32)
    for j in range(ACT):
        row, lane = head_maps(j)
        picked = jnp.transpose(row) * turned[j + 1 : j + 2, :]
        out = out + dot_exact(picked, lane.astype(f32), ((1,), (0,)))
    return out


def prepare_actor(net, actor_ref, rows_ref, pad_ref, w1_ref, w2f_ref, w2b_ref, b2_ref, w3t_ref, w3b_ref, b3a_ref):
    whole = PA // 1024
    for t in range(whole):
        rows_ref[8 * t : 8 * t + 8, :] = actor_ref[pl.ds(1024 * t, 1024)].reshape(8, 128)
    rest = (PA - 1024 * whole) // 128
    rows_ref[8 * whole : 8 * whole + rest, :] = actor_ref[pl.ds(1024 * whole, 128 * rest)].reshape(rest, 128)
    rows_ref[562:563, 0:ACT] = actor_ref[pl.ds(562 * 128, ACT)].reshape(1, ACT)
    start = NEXT if net == AT else 0
    pad_ref[...] = jnp.zeros_like(pad_ref)
    for half in range(2):
        s = pl.ds(128 * half, 128)
        pad_ref[pl.ds(start, OBS), s] = rows_ref[pl.ds(half, OBS, stride=2), :]
        pad_ref[pl.ds(ONE, 1), s] = rows_ref[pl.ds(34 + half, 1), :]
    put_first(net, pad_ref, w1_ref)
    w2 = jnp.concatenate([rows_ref[pl.ds(36, UNITS, stride=2), :], rows_ref[pl.ds(37, UNITS, stride=2), :]], 1)
    put_square(net, w2, w2f_ref, w2b_ref)
    put_column(b2_ref, net, rows_ref[548:549, :], rows_ref[549:550, :], 0.5)
    flat = jnp.concatenate([rows_ref[550:562, :], jnp.zeros((4, 128), f32)], 0)
    hi, lo = head_of(flat)
    block = jnp.concatenate([hi, hi, lo], 1)
    w3t_ref[net - A] = jnp.concatenate([block, jnp.zeros_like(block)], 0).astype(bf)
    if net == A:
        stacked = jnp.concatenate([hi, hi, lo, jnp.zeros((104, UNITS), f32)], 0)
        w3b_ref[...] = (0.5 * jnp.transpose(stacked)).astype(bf)
    bias = column(rows_ref[562:563, :])
    b3a_ref[net - A] = jnp.zeros((8, 128), f32)
    b3a_ref[net - A, 1 : 1 + ACT, :] = bias[:ACT]


def act(zh):
    u = jnp.tanh(zh) + 1.0
    return u, zh * u


def slope(u, s):
    return u + s * (2.0 - u)


class Step:
    def __init__(self, i, width, x, weights):
        (
            self.w1, self.w2f, self.w2b, self.b2, self.w3, self.b3, self.w3t, self.w3b, self.b3a, self.w1a,
        ) = weights
        self.i, self.width = i, width
        self.lanes = pl.ds(pl.multiple_of(i * width, width), width)
        self.x = x
        self.x3 = three(self.x)
        rows8 = lax.broadcasted_iota(jnp.int32, (8, width), 0)
        self.is_action = (rows8 >= 1) & (rows8 <= ACT)

    def with_action(self, a):
        x = self.x
        return three(jnp.concatenate([x[:16], jnp.where(self.is_action, a, x[16:24]), x[24:]], 0))

    def first(self, net, xx):
        return act(dot(self.w1[net, :, : 3 * FEAT], xx))

    def second(self, net, h3):
        return act(dot(self.w2f[net], h3) + lanes(self.b2[net], self.width))

    def value(self, net, s):
        return jnp.sum(s * lanes(self.w3[net], self.width), 0, keepdims=True) + lanes(self.b3[net], self.width)

    def head(self, net, s3):
        return dot(self.w3t[net - A], s3)[:8] + lanes(self.b3a[net - A], self.width)

    def valid(self, count_ref):
        tiles = self.width // 128
        return jnp.concatenate([((self.i * tiles + t) < count_ref[...]).astype(f32) for t in range(tiles)], 1)

    def grads2(self, net, h1, dz2, g2_ref):
        u = UNITS
        left = jnp.concatenate([h1[:u], h1[u : 2 * u], h1[:u]], 1)
        g2_ref[net] += dot_nt(left, jnp.concatenate([dz2[:u], dz2[:u], dz2[u : 2 * u]], 1))

    def grads1(self, net, dz1, g1_ref):
        xhi, xlo = self.x3[:FEAT], self.x3[FEAT : 2 * FEAT]
        left = jnp.concatenate(
            [jnp.concatenate([xhi, xlo], 0), jnp.concatenate([xhi, jnp.zeros_like(xlo)], 0)], 1
        )
        a, b = split(dz1)
        g1_ref[net] += dot_nt(left, jnp.concatenate([a, b], 1))


def critic_block(i, width, x, nz_ref, count_ref, weights, prio_ref, grads):
    g2_ref, g1_ref, g3a_ref, db2_ref, dw3_ref, st_ref = grads
    st = Step(i, width, x, weights)
    x3 = st.x3

    u, s = st.first(AT, x3)
    u, s = st.second(AT, three(s))
    next_action = jnp.tanh(st.head(AT, three(s)) + nz_ref[:, st.lanes])
    xt = st.with_action(next_action)
    u, s = st.first(T0, xt)
    h0 = three(s)
    u, s = st.first(T1, xt)
    h1t = three(s)
    u, s = st.second(T0, h0)
    targets = [st.value(T0, s)]
    u0, s0 = st.first(C0, x3)
    h1, d1 = three(s0), slope(u0, s0)
    u, s = st.second(T1, h1t)
    targets.append(st.value(T1, s))
    u0, s0 = st.second(C0, h1)
    y = x[23:24] + 0.99 * x[24:25] * jnp.minimum(targets[0], targets[1])
    valid = st.valid(count_ref)
    scaled = valid * SCALE
    st_ref[1:2, :] += fold(valid)

    def top(net, s, d2):
        delta = st.value(net, s) - y
        if net == C0:
            prio = valid * jnp.sqrt(delta * delta + 1.0)
            tiles = width // 128
            for t in range(tiles):
                prio_ref[(i * tiles) // 16, pl.ds(lax.rem(i * tiles, 16) + t, 1), :] = prio[:, 128 * t : 128 * (t + 1)]
        st_ref[0:1, :] += fold(valid * (delta * delta))
        dq = (2.0 * scaled) * delta
        st_ref[2 + net : 3 + net, :] += fold(dq)
        dw3_ref[net] += fold(s * dq)
        dz2 = lanes(st.w3[net], width) * (0.5 * dq) * d2
        db2_ref[net] += fold(dz2)
        return three(dz2)

    u, s = st.first(C1, x3)
    h1b, d1b = three(s), slope(u, s)
    dz2 = top(C0, s0, slope(u0, s0))
    dz1 = dot(st.w2b[C0], dz2) * d1
    st.grads2(C0, h1, dz2, g2_ref)
    u, s = st.second(C1, h1b)
    st.grads1(C0, dz1, g1_ref)
    dz2 = top(C1, s, slope(u, s))
    dz1 = dot(st.w2b[C1], dz2) * d1b
    st.grads2(C1, h1b, dz2, g2_ref)
    st.grads1(C1, dz1, g1_ref)


def actor_block(i, width, x, count_ref, weights, grads):
    g2_ref, g1_ref, g3a_ref, db2_ref, dw3_ref, st_ref = grads
    st = Step(i, width, x, weights)

    u, s = st.first(A, st.x3)
    h1a, d1a = three(s), slope(u, s)
    u, s = st.second(A, h1a)
    h2a, d2a = three(s), slope(u, s)
    policy = jnp.tanh(st.head(A, h2a))

    u, s = st.first(C0, st.with_action(policy))
    d1f = slope(u, s)
    u, s = st.second(C0, three(s))
    d2f, q_policy = slope(u, s), st.value(C0, s)
    valid = st.valid(count_ref)
    st_ref[0:1, :] -= fold(valid * q_policy)

    dz2 = three(lanes(st.w3[C0], width) * (-0.5 * SCALE * valid) * d2f)
    dz1 = three(dot(st.w2b[C0], dz2) * d1f)
    da = dot(st.w1a[...], dz1)[:8]
    dp = jnp.where(st.is_action, da * (1.0 - policy * policy), 0.0)
    st_ref[8:16, :] += fold(dp)
    hi = dp.astype(bf).astype(f32)
    lo = dp - hi
    zero = jnp.zeros_like(hi)
    stacked = jnp.concatenate([hi, lo, hi, zero], 0).astype(bf)
    left = jnp.concatenate([jnp.concatenate([hi, lo], 0), jnp.concatenate([hi, zero], 0)], 1).astype(bf)
    dz2 = dot(st.w3b[:, :32], stacked) * d2a
    db2_ref[A] += fold(dz2)
    dz2 = three(dz2)
    dz1 = dot(st.w2b[A], dz2) * d1a
    g3a_ref[...] += dot_nt(left, jnp.concatenate([h2a[:UNITS], h2a[UNITS : 2 * UNITS]], 1))
    st.grads2(A, h1a, dz2, g2_ref)
    st.grads1(A, dz1, g1_ref)


def lane_sums(tile):
    return dot_exact(jnp.ones((8, 128), f32), tile, ((1,), (1,)))


def pack_critics(pack_ref, grads):
    g2_ref, g1_ref, g3a_ref, db2_ref, dw3_ref, st_ref = grads
    lane = lax.broadcasted_iota(jnp.int32, (1, 128), 1)
    sums = jnp.sum(st_ref[...], 1, keepdims=True)
    for c in range(2):
        g1 = g1_ref[c, :FEAT, :] + g1_ref[c, FEAT:, :]
        b2 = lane_sums(db2_ref[c])[0:1]
        w3 = lane_sums(dw3_ref[c])[0:1]
        for half in range(2):
            s = slice(128 * half, 128 * (half + 1))
            at = c + 2 * half
            pack_ref[pl.ds(at, OBS + ACT, stride=4), :] = g1[: OBS + ACT, s]
            pack_ref[at + 92 : at + 93, :] = g1[ONE : ONE + 1, s]
            pack_ref[pl.ds(at + 96, UNITS, stride=4), :] = g2_ref[c, :, s]
            pack_ref[at + 1120 : at + 1121, :] = b2[:, s]
            pack_ref[at + 1124 : at + 1125, :] = w3[:, s]
        pack_ref[c + 1128 : c + 1129, :] = jnp.where(lane == 0, sums[2 + c : 3 + c], 0.0)
    pack_ref[STAT : STAT + 1, :] = jnp.where(lane == 0, sums[0:1], jnp.where(lane == 1, sums[1:2], 0.0))
    pack_ref[STAT + 1 : AT_ACTOR, :] = jnp.zeros((AT_ACTOR - STAT - 1, 128), f32)


def pack_actor(pack_ref, grads):
    g2_ref, g1_ref, g3a_ref, db2_ref, dw3_ref, st_ref = grads
    sums = jnp.sum(st_ref[...], 1, keepdims=True)
    g1 = g1_ref[A, :FEAT, :] + g1_ref[A, FEAT:, :]
    b2 = lane_sums(db2_ref[A])[0:1]
    o = AT_ACTOR
    for half in range(2):
        s = slice(128 * half, 128 * (half + 1))
        pack_ref[pl.ds(o + half, OBS, stride=2), :] = g1[:OBS, s]
        pack_ref[o + 34 + half : o + 35 + half, :] = g1[ONE : ONE + 1, s]
        pack_ref[pl.ds(o + 36 + half, UNITS, stride=2), :] = g2_ref[A, :, s]
        pack_ref[o + 548 + half : o + 549 + half, :] = b2[:, s]
    pack_ref[o + 550 : o + 562, :] = head_back(g3a_ref[:8, :] + g3a_ref[8:, :])[:12]
    e = lax.broadcasted_iota(jnp.int32, (8, 128), 1) == lax.broadcasted_iota(jnp.int32, (8, 128), 0) - 1
    pack_ref[o + 562 : o + 563, :] = jnp.sum(jnp.where(e, sums[8:16], 0.0), 0, keepdims=True)
    pack_ref[o + ROWS_A : PACK, :] = jnp.zeros((PACK - o - ROWS_A, 128), f32)


WEIGHTS = [
    pltpu.VMEM((6, UNITS, 256), bf),
    pltpu.VMEM((6, UNITS, 3 * UNITS), bf),
    pltpu.VMEM((3, UNITS, 3 * UNITS), bf),
    pltpu.VMEM((6, UNITS, 128), f32),
    pltpu.VMEM((6, UNITS, 128), f32),
    pltpu.VMEM((6, 1, 128), f32),
    pltpu.VMEM((2, 16, 3 * UNITS), bf),
    pltpu.VMEM((UNITS, 128), bf),
    pltpu.VMEM((2, 8, 128), f32),
    pltpu.VMEM((16, 3 * UNITS), bf),
]
GRADS = [
    pltpu.VMEM((3, UNITS, UNITS), f32),
    pltpu.VMEM((3, 2 * FEAT, UNITS), f32),
    pltpu.VMEM((16, UNITS), f32),
    pltpu.VMEM((3, UNITS, 128), f32),
    pltpu.VMEM((2, UNITS, 128), f32),
    pltpu.VMEM((16, 128), f32),
]


def drain(ref, sem, copies):
    view = ref.at[pl.ds(0, copies)]
    pltpu.make_async_copy(view, view, sem).wait()


class Place:
    def __init__(self):
        group, shard = lax.axis_index("group"), lax.axis_index("shard")
        self.core = lax.rem(shard, 2)
        z, x, y = group // 4, lax.rem(group, 4), shard // 2
        self.chip = group * 4 + y
        self.sibling = (group, shard + 1 - 2 * self.core)
        self.sibling_at = group * 8 + shard + 1 - 2 * self.core
        self.me = group * 8 + shard
        self.zs, self.xs, self.ys = ([lax.rem(v + n, 4) for n in range(4)] for v in (z, x, y))

    def others(self, other_core=False):
        core = 1 - self.core if other_core else self.core
        for dz, dx, dy in STEPS:
            group = self.zs[dz] * 4 + self.xs[dx]
            yield group * 4 + self.ys[dy], (group, self.ys[dy] * 2 + core)


class Sum:
    def __init__(self, place, g, pack_ref, out, buffers, sems):
        self.place, self.chunk = place, CHUNKS[g]
        self.late = g == 0
        self.first = (0, AT_ACTOR)[g]
        self.rows = CHIPS * self.chunk
        self.pack_ref = pack_ref
        self.other, self.half, self.parts, self.mine, self.both = buffers
        self.whole = self.both.at[place.core]
        if self.late:
            self.out = out.at[pl.ds(place.core * CHIPS, CHIPS), pl.ds(0, self.chunk)]
        else:
            self.out = self.whole
        self.sems = sems.at[g]

    def remote(self, src, dst, n, to):
        return pltpu.make_async_remote_copy(
            src_ref=src,
            dst_ref=dst,
            send_sem=self.sems.at[2 * n],
            recv_sem=self.sems.at[2 * n + 1],
            device_id=to,
            device_id_type=MESH,
        )

    def swap(self):
        give = pl.multiple_of(self.first + (1 - self.place.core) * self.rows, 8)
        return self.remote(self.pack_ref.at[pl.ds(give, self.rows)], self.other, 0, self.place.sibling)

    def scatter(self):
        keep = pl.multiple_of(self.first + self.place.core * self.rows, 8)
        total = self.pack_ref[pl.ds(keep, self.rows), :] + self.other[...]
        for j in range(self.chunk):
            self.half[:, j, :] = total[CHIPS * j : CHIPS * (j + 1)]
        chip = self.place.chip
        for peer, device in self.place.others():
            self.remote(self.half.at[peer], self.parts.at[chip], 1, device).start()

    def spread(self):
        chip = self.place.chip
        drain(self.half, self.sems.at[2], CHIPS - 1)
        drain(self.parts, self.sems.at[3], CHIPS - 1)
        self.parts[pl.ds(chip, 1)] = self.half[pl.ds(chip, 1)]
        self.mine[...] = jnp.sum(self.parts[...], 0)
        for _, device in self.place.others():
            self.remote(self.mine, self.whole.at[chip], 2, device).start()

    def back_copies(self):
        copies = [self.remote(self.whole, self.out, 3, self.place.sibling)]
        if self.late:
            copies.append(pltpu.make_async_copy(self.whole, self.out, self.sems.at[8]))
        return copies

    def back(self):
        drain(self.parts, self.sems.at[4], CHIPS - 1)
        drain(self.whole, self.sems.at[5], CHIPS - 1)
        self.whole[pl.ds(self.place.chip, 1)] = self.mine[...][None]
        for copy in self.back_copies():
            copy.start()

    def finish(self):
        for copy in self.back_copies():
            copy.wait()

    def in_order(self, flat_ref):
        for core in range(2):
            for j in range(self.chunk):
                at = (core * self.chunk + j) * CHIPS
                flat_ref[at // 16 : (at + CHIPS) // 16] = self.both[core, :, j, :].reshape(CHIPS // 16, 16, 128)


def sum_buffers():
    out = []
    for chunk in CHUNKS:
        out += [
            pltpu.VMEM((CHIPS * chunk, 128), f32),
            pltpu.VMEM((CHIPS, chunk, 128), f32),
            pltpu.VMEM((CHIPS, chunk, 128), f32),
            pltpu.VMEM((chunk, 128), f32),
            pltpu.VMEM((2, CHIPS, chunk, 128), f32),
        ]
    return out


def step_kernel(
    width,
    table_hbm,
    index_hbm,
    noise_hbm,
    count_hbm,
    actor_hbm,
    actor_t_hbm,
    critic_hbm,
    critic_t_hbm,
    out_hbm,
    prio_ref,
    order_ref,
    table_ref,
    index_ref,
    noise_ref,
    count_ref,
    actor_ref,
    actor_t_ref,
    critic_ref,
    critic_t_ref,
    in_sems,
    rows_ref,
    picked_ref,
    q_ref,
    nsend,
    nrecv,
    noise_sems,
    x_ref,
    nz_ref,
    flat_ref,
    pad_ref,
    pack_ref,
    sems,
    *scratch,
):
    weights, grads = scratch[: len(WEIGHTS)], scratch[len(WEIGHTS) : len(WEIGHTS) + len(GRADS)]
    buffers = scratch[len(WEIGHTS) + len(GRADS) :]
    w1_ref, w2f_ref, w2b_ref, b2_ref, w3_ref, b3_ref, w3t_ref, w3b_ref, b3a_ref, w1a_ref = weights
    blocks = N // width
    place = Place()
    me = place.me

    loads = [
        pltpu.make_async_copy(src, dst, in_sems.at[n])
        for n, (src, dst) in enumerate(
            (
                (critic_hbm, critic_ref),
                (actor_hbm, actor_ref),
                (table_hbm, table_ref),
                (index_hbm, index_ref),
                (count_hbm, count_ref),
                (noise_hbm, noise_ref),
                (critic_t_hbm, critic_t_ref),
                (actor_t_hbm, actor_t_ref),
            )
        )
    ]
    for load in loads:
        load.start()

    barrier = pltpu.get_barrier_semaphore()

    def all_others():
        for other_core in (False, True):
            for _, device in place.others(other_core):
                yield device[0] * 8 + device[1], device
        yield place.sibling_at, place.sibling

    for ref in grads:
        ref[...] = jnp.zeros_like(ref)
    loads[0].wait()
    loads[1].wait()
    for _, device in all_others():
        pl.semaphore_signal(barrier, inc=1, device_id=device, device_id_type=MESH)
    prepare_critics(
        critic_ref, flat_ref, pad_ref, C0, w1_ref, w2f_ref, w2b_ref, b2_ref, w3_ref, b3_ref, w1a_ref
    )
    prepare_actor(
        A, actor_ref, flat_ref, pad_ref, w1_ref, w2f_ref, w2b_ref, b2_ref, w3t_ref, w3b_ref, b3a_ref
    )
    loads[2].wait()

    def turn(i, carry):
        turn_table(i, table_ref, rows_ref)
        return carry

    lax.fori_loop(0, R_DEV // TURN, turn, 0)
    loads[3].wait()
    pick_rows(0, width, index_ref, rows_ref, picked_ref)
    loads[4].wait()
    loads[5].wait()
    turn_noise(noise_ref, q_ref, nsend)

    def send():
        for peer, device in all_others():
            pltpu.make_async_remote_copy(
                src_ref=nsend.at[peer],
                dst_ref=nrecv.at[me],
                send_sem=noise_sems.at[0],
                recv_sem=noise_sems.at[1],
                device_id=device,
                device_id_type=MESH,
            ).start()

    def actors(i, carry):
        x = turn_rows(width, picked_ref)
        x_ref[:, pl.ds(pl.multiple_of(i * width, width), width)] = x
        actor_block(i, width, x, count_ref, weights, grads)
        pick_rows(lax.rem(i + 1, blocks), width, index_ref, rows_ref, picked_ref)

        @pl.when(i == 0)
        def _():
            loads[6].wait()
            loads[7].wait()
            pl.semaphore_wait(barrier, DEVS - 1)
            send()
            prepare_critics(
                critic_t_ref, flat_ref, pad_ref, T0, w1_ref, w2f_ref, w2b_ref, b2_ref, w3_ref, b3_ref, w1a_ref
            )
            prepare_actor(
                AT, actor_t_ref, flat_ref, pad_ref, w1_ref, w2f_ref, w2b_ref, b2_ref, w3t_ref, w3b_ref, b3a_ref
            )

        return carry

    lax.fori_loop(0, blocks, actors, 0)
    pack_actor(pack_ref, grads)
    late, early = (Sum(place, g, pack_ref, out_hbm, buffers[5 * g : 5 * g + 5], sems) for g in range(2))
    early.swap().start()

    drain(nsend, noise_sems.at[0], DEVS - 1)
    drain(nrecv, noise_sems.at[1], DEVS - 1)
    nrecv[pl.ds(me, 1)] = nsend[pl.ds(me, 1)]
    noise_back(nrecv, nz_ref)

    def critics(i, carry):
        x = x_ref[:, pl.ds(pl.multiple_of(i * width, width), width)]
        critic_block(i, width, x, nz_ref, count_ref, weights, prio_ref, grads)

        @pl.when(i == 0)
        def _():
            early.swap().wait()
            early.scatter()

        @pl.when(i == 1)
        def _():
            early.spread()

        @pl.when(i == 2)
        def _():
            early.back()

        return carry

    lax.fori_loop(0, blocks, critics, 0)
    pack_critics(pack_ref, grads)
    late.swap().start()
    prios = pltpu.make_async_copy(prio_ref, out_hbm.at[pl.ds(AT_PRIO, 2)], in_sems.at[0])
    prios.start()
    early.finish()
    late.swap().wait()
    late.scatter()
    early.in_order(order_ref)
    order = pltpu.make_async_copy(order_ref, out_hbm.at[pl.ds(AT_SUM, order_ref.shape[0])], in_sems.at[1])
    order.start()
    prios.wait()
    late.spread()
    order.wait()
    late.back()
    late.finish()


def update(weight, grad, momentum, average, target):
    momentum_new = 0.9 * momentum + grad
    weight_new = weight - 0.1 * (grad + 0.9 * momentum_new)
    average_new = 0.99 * average + 0.01 * weight_new
    target_new = 0.005 * weight_new + 0.995 * target
    return (weight_new, momentum_new, average_new, target_new, weight_new.astype(bf))


STEP = 1024
CUTS = (0, 35 * STEP, PC)


def update_kernel(sum_hbm, *refs):
    ins, stat_ref, prio_out, outs_hbm, outs = refs[:8], refs[8], refs[9], refs[10:20], refs[20:30]
    late_ref, early_ref, count_ref, grad_ref, in_sems, out_sems = refs[30:]
    early = pltpu.make_async_copy(sum_hbm.at[pl.ds(AT_SUM, early_ref.shape[0])], early_ref, in_sems.at[0])
    late = pltpu.make_async_copy(sum_hbm.at[pl.ds(0, DEVS), pl.ds(0, CHUNKS[0])], late_ref, in_sems.at[1])
    stat_core, stat_row = divmod(STAT, CHIPS * CHUNKS[0])
    stat_at = stat_core * CHIPS + stat_row % CHIPS
    count = pltpu.make_async_copy(sum_hbm.at[pl.ds(stat_at, 1), pl.ds(0, CHUNKS[0])], count_ref, in_sems.at[3])
    for load in (count, early, late):
        load.start()
    pass_on = pltpu.make_async_copy(sum_hbm.at[pl.ds(AT_PRIO, 2)], prio_out, in_sems.at[2])
    pass_on.start()

    def stores(piece):
        out = []
        for n in range(5):
            src, dst = outs[2 * n + min(piece, 1)], outs_hbm[2 * n + min(piece, 1)]
            if piece:
                s = pl.ds(CUTS[piece - 1], CUTS[piece] - CUTS[piece - 1])
                src, dst = src.at[:, s], dst.at[:, s]
            out.append(pltpu.make_async_copy(src, dst, out_sems.at[piece, n]))
        return out

    count.wait()
    stat = count_ref[0, stat_row // CHIPS : stat_row // CHIPS + 1, :]
    factor = (1.0 / SCALE) / stat[:, 1:2]
    stat_ref[...] = stat[:, :2].reshape(2)
    early.wait()

    def actor(s, grad):
        values = update(ins[0][s], grad, ins[2][s], ins[4][s], ins[6][s])
        for ref, value in zip(outs[0::2], values):
            ref[s] = value

    for i in range(PA // STEP):
        actor(slice(STEP * i, STEP * (i + 1)), (early_ref[i // 2, 8 * (i % 2) : 8 * (i % 2) + 8, :] * factor).reshape(STEP))
    done = PA // STEP * STEP
    last = early_ref[done // 2048, done // 128 % 16 : done // 128 % 16 + 8, :] * factor
    more = (PA - done) // 128
    actor(slice(done, done + 128 * more), last[:more].reshape(128 * more))
    done += 128 * more
    actor(slice(done, PA), last[more : more + 1, :ACT].reshape(ACT))
    for store in stores(0):
        store.start()

    def critic(s):
        values = update(ins[1][:, s], grad_ref[:, s] * factor, ins[3][:, s], ins[5][:, s], ins[7][:, s])
        for ref, value in zip(outs[1::2], values):
            ref[:, s] = value

    def critics(i, carry):
        critic(pl.ds(pl.multiple_of(i * STEP, STEP), STEP))
        return carry

    late.wait()
    for t in range(TILES_C):
        core, r = divmod(2 * t, CHIPS * CHUNKS[0])
        j, k = divmod(r, CHIPS)
        k += core * CHIPS
        grad_ref[:, 128 * t : 128 * (t + 1)] = late_ref[k : k + 2, j, :]
    for piece in (1, 2):
        lax.fori_loop(CUTS[piece - 1] // STEP, CUTS[piece] // STEP, critics, 0, unroll=5)
        if piece == 2:
            done = PC // STEP * STEP
            critic(pl.ds(done, PC - done))
        for store in stores(piece):
            store.start()
    for piece in range(3):
        for store in stores(piece):
            store.wait()
    pass_on.wait()


def local(
    replay,
    sample_index,
    pair_count,
    noise,
    actor,
    critic,
    actor_momentum,
    critic_momentum,
    actor_average,
    critic_average,
    actor_target,
    critic_target,
):
    any_ = pl.BlockSpec(memory_space=pl.ANY)
    total = pl.pallas_call(
        functools.partial(step_kernel, WIDTH),
        out_shape=SDS(RESULT, f32),
        in_specs=[any_] * 8,
        out_specs=any_,
        scratch_shapes=[
            pltpu.VMEM((2, 16, DEVS), f32),
            pltpu.VMEM((2 * CHIPS * CHUNKS[1] // 16, 16, 128), f32),
            pltpu.VMEM((ROW, R_DEV), f32),
            pltpu.SMEM((CAP, DEVS), jnp.int32),
            pltpu.VMEM((ACT, CAP, DEVS), f32),
            pltpu.VMEM((1, DEVS), jnp.int32),
            pltpu.VMEM((PA,), f32),
            pltpu.VMEM((PA,), f32),
            pltpu.VMEM((2, PC), f32),
            pltpu.VMEM((2, PC), f32),
            pltpu.SemaphoreType.DMA((8,)),
            pltpu.VMEM((R_DEV, 128), f32),
            pltpu.VMEM((WIDTH // 128, 128, 128), f32),
            pltpu.VMEM((256, 128), f32),
            pltpu.VMEM((DEVS, 2, 128), f32),
            pltpu.VMEM((DEVS, 2, 128), f32),
            pltpu.SemaphoreType.DMA((2,)),
            pltpu.VMEM((FEAT, N), f32),
            pltpu.VMEM((8, N), f32),
            pltpu.VMEM((2 * TILES_C + 6, 128), f32),
            pltpu.VMEM((FEAT, 256), f32),
            pltpu.VMEM((PACK, 128), f32),
            pltpu.SemaphoreType.DMA((2, 9)),
        ]
        + WEIGHTS
        + GRADS
        + sum_buffers(),
        compiler_params=pltpu.CompilerParams(
            collective_id=0, has_side_effects=True, vmem_limit_bytes=56 << 20
        ),
        name="td3_step",
    )(
        replay.T,
        sample_index[0].T,
        jnp.transpose(noise[0], (2, 1, 0)),
        pair_count,
        actor,
        actor_target,
        critic,
        critic_target,
    )
    shapes = [SDS((2,), f32), SDS((2, CAP // 2, DEVS), f32)]
    places = [SDS((PA,), f32), SDS((2, PC), f32)] * 4 + [SDS((PA,), bf), SDS((2, PC), bf)]
    stat, prio, *outs = pl.pallas_call(
        update_kernel,
        out_shape=tuple(shapes + places),
        in_specs=[any_] + [VM] * 8,
        out_specs=(VM,) + (any_,) * 11,
        scratch_shapes=[pltpu.VMEM(p.shape, p.dtype) for p in places]
        + [
            pltpu.VMEM((DEVS, CHUNKS[0], 128), f32),
            pltpu.VMEM((2 * CHIPS * CHUNKS[1] // 16, 16, 128), f32),
            pltpu.VMEM((1, CHUNKS[0], 128), f32),
            pltpu.VMEM((2, TILES_C * 128), f32),
            pltpu.SemaphoreType.DMA((4,)),
            pltpu.SemaphoreType.DMA((3, 5)),
        ],
        compiler_params=pltpu.CompilerParams(vmem_limit_bytes=24 << 20),
        name="update",
    )(
        total,
        actor,
        critic,
        actor_momentum,
        critic_momentum,
        actor_average,
        critic_average,
        actor_target,
        critic_target,
    )
    return (stat, prio.reshape(CAP, DEVS).T[None], *outs)


def solution(mesh):
    rows = ("group", "shard")
    in_specs = (P(rows, None), P(rows, None, None), P(rows, None), P(rows, None, None, None)) + (P(),) * 8
    out_specs = (P(), P(rows, None, None)) + (P(),) * 10
    return jax.shard_map(local, mesh=mesh, in_specs=in_specs, out_specs=out_specs, check_vma=False)
```

```python
import functools

import jax
import jax.numpy as jnp
from jax import lax
from jax.experimental import pallas as pl
from jax.experimental.pallas import tpu as pltpu
from jax.sharding import PartitionSpec as P

OBS = 17
ACT = 6
UNITS = 256
CAP = 32
DEVS = 128
R_DEV = 8192
ROW = 42
PA = 71942
PC = 72193
N = DEVS * CAP

bf = jnp.bfloat16
f32 = jnp.float32
MESH = pl.DeviceIdType.MESH
VM = pl.BlockSpec(memory_space=pltpu.VMEM)
SDS = jax.ShapeDtypeStruct

SCALE = 2.0**-19
C0, C1, A, AT, T0, T1 = range(6)
FEAT = 48
ONE = 42
NEXT = 25

TILES_C = 565
STAT = 1130
ROWS_A = 563
CHIPS = DEVS // 2
CHUNKS = (9, 5)
AT_ACTOR = 2 * CHIPS * CHUNKS[0]
PACK = AT_ACTOR + 2 * CHIPS * CHUNKS[1]
AT_PRIO = DEVS
AT_SUM = DEVS + 2
RESULT = (3700, 16, 128)
TURN = 512
WIDTH = 1024
STEPS = sorted(
    ((z, x, y) for z in range(4) for x in range(4) for y in range(4)),
    key=lambda step: -sum(min(n, 4 - n) for n in step),
)[:-1]


def dot(a, b):
    return lax.dot_general(a, b, (((1,), (0,)), ((), ())), preferred_element_type=f32)


def dot_nt(a, b):
    return lax.dot_general(a, b, (((1,), (1,)), ((), ())), preferred_element_type=f32)


def dot_exact(a, b, dims):
    return lax.dot_general(a, b, (dims, ((), ())), precision=lax.Precision.HIGHEST, preferred_element_type=f32)


def split(v):
    hi = v.astype(bf)
    return hi, (v - hi.astype(f32)).astype(bf)


def three(v):
    hi, lo = split(v)
    return jnp.concatenate([hi, lo, hi], 0)


def lanes(tile, width):
    return jnp.concatenate([tile] * (width // 128), 1)


def fold(v):
    out = v[:, :128]
    for i in range(1, v.shape[1] // 128):
        out = out + v[:, 128 * i : 128 * (i + 1)]
    return out


def column(row):
    return jnp.transpose(jnp.broadcast_to(row, (128, 128)))


def turn_noise(noise_ref, q_ref, nsend):
    q_ref[...] = jnp.zeros_like(q_ref)
    for j in range(ACT):
        q_ref[pl.ds(j + 1, CAP, stride=8), :] = 0.5 * jnp.tanh(0.4 * noise_ref[j])
    turned = jnp.transpose(q_ref[...])
    nsend[:, 0, :] = turned[:, :128]
    nsend[:, 1, :] = turned[:, 128:]


def noise_back(nrecv, nz_ref):
    back = jnp.transpose(jnp.concatenate([nrecv[:, 0, :], nrecv[:, 1, :]], 1))
    for c in range(CAP):
        nz_ref[:, 128 * c : 128 * (c + 1)] = back[8 * c : 8 * (c + 1), :]


def turn_table(i, table_ref, rows_ref):
    s = pl.ds(pl.multiple_of(i * TURN, TURN), TURN)
    v = jnp.concatenate([table_ref[:, s], jnp.zeros((128 - ROW, TURN), f32)], 0)
    rows_ref[s, :] = jnp.transpose(v)


def pick_rows(block, width, index_ref, rows_ref, picked_ref):
    tiles = width // 128
    for t in range(tiles):
        for d in range(DEVS):
            picked_ref[t, d : d + 1, :] = rows_ref[pl.ds(index_ref[block * tiles + t, d], 1), :]


def turn_rows(width, picked_ref):
    parts = [jnp.transpose(picked_ref[t])[:FEAT] for t in range(width // 128)]
    x = jnp.concatenate(parts, 1)
    ones = lax.broadcasted_iota(jnp.int32, (8, width), 0) == (ONE - 40)
    return jnp.concatenate([x[:40], jnp.where(ones, 1.0, x[40:])], 0)


def put_square(net, w2, w2f_ref, w2b_ref):
    w2 = 0.5 * w2
    turned = jnp.transpose(w2)
    hi, lo = split(turned)
    w2f_ref[net] = jnp.concatenate([hi, hi, lo], 1)
    if net in (C0, C1, A):
        hi, lo = split(w2)
        w2b_ref[net] = jnp.concatenate([hi, hi, lo], 1)


def put_first(net, pad_ref, w1_ref):
    w1 = 0.5 * pad_ref[...]
    hi = w1.astype(bf).astype(f32)
    lo = w1 - hi
    stacked = jnp.concatenate([hi, hi, lo, jnp.zeros((256 - 3 * FEAT, 256), f32)], 0)
    w1_ref[net] = jnp.transpose(stacked).astype(bf)


def put_column(ref, net, left, right, factor):
    ref[net] = jnp.concatenate([column(left * factor), column(right * factor)], 0)


def prepare_critics(critic_ref, rows_ref, pad_ref, first, w1_ref, w2f_ref, w2b_ref, b2_ref, w3_ref, b3_ref, w1a_ref):
    for t in range(TILES_C - 1):
        rows_ref[2 * t : 2 * t + 2, :] = critic_ref[:, 128 * t : 128 * (t + 1)]
    for c in range(2):
        net = first + c
        start = NEXT if first == T0 else 0
        pad_ref[...] = jnp.zeros_like(pad_ref)
        for half in range(2):
            s = pl.ds(128 * half, 128)
            pad_ref[pl.ds(start, OBS), s] = rows_ref[pl.ds(c + 2 * half, OBS, stride=4), :]
            pad_ref[pl.ds(OBS, ACT), s] = rows_ref[pl.ds(c + 2 * half + 4 * OBS, ACT, stride=4), :]
            pad_ref[pl.ds(ONE, 1), s] = rows_ref[pl.ds(92 + c + 2 * half, 1), :]
        put_first(net, pad_ref, w1_ref)
        if net == C0:
            hi = pad_ref[16:24, :].astype(bf).astype(f32)
            lo = pad_ref[16:24, :] - hi
            block = jnp.concatenate([hi, hi, lo], 1)
            w1a_ref[...] = jnp.concatenate([block, jnp.zeros_like(block)], 0).astype(bf)
        w2 = jnp.concatenate(
            [rows_ref[pl.ds(96 + c, UNITS, stride=4), :], rows_ref[pl.ds(98 + c, UNITS, stride=4), :]], 1
        )
        put_square(net, w2, w2f_ref, w2b_ref)
        put_column(b2_ref, net, rows_ref[1120 + c : 1121 + c, :], rows_ref[1122 + c : 1123 + c, :], 0.5)
        put_column(w3_ref, net, rows_ref[1124 + c : 1125 + c, :], rows_ref[1126 + c : 1127 + c, :], 1.0)
        b3_ref[net] = jnp.broadcast_to(critic_ref[c : c + 1, PC - 1 : PC], (1, 128))


def head_maps(j):
    k = lax.broadcasted_iota(jnp.int32, (UNITS, 16), 0)
    r = lax.broadcasted_iota(jnp.int32, (UNITS, 16), 1)
    row = ((k * ACT + j) >> 7) == r
    k = lax.broadcasted_iota(jnp.int32, (UNITS, 128), 0)
    l = lax.broadcasted_iota(jnp.int32, (UNITS, 128), 1)
    lane = ((k * ACT + j) & 127) == l
    return row.astype(f32), lane


def head_of(flat):
    hi = flat.astype(bf).astype(f32)
    out = []
    for part in (hi, flat - hi):
        part = part.astype(bf)
        spread = []
        for j in range(ACT):
            row, lane = head_maps(j)
            spread.append(jnp.where(lane, dot(row.astype(bf), part), 0.0).astype(bf))
        r = lax.broadcasted_iota(jnp.int32, (16, 128 * ACT), 0)
        l = lax.broadcasted_iota(jnp.int32, (16, 128 * ACT), 1)
        take = ((l >> 7) == (r - 1)).astype(f32).astype(bf)
        out.append(dot_nt(take, jnp.concatenate(spread, 1))[:8])
    return out


def head_back(turned):
    out = jnp.zeros((16, 128), f32)
    for j in range(ACT):
        row, lane = head_maps(j)
        picked = jnp.transpose(row) * turned[j + 1 : j + 2, :]
        out = out + dot_exact(picked, lane.astype(f32), ((1,), (0,)))
    return out


def prepare_actor(net, actor_ref, rows_ref, pad_ref, w1_ref, w2f_ref, w2b_ref, b2_ref, w3t_ref, w3b_ref, b3a_ref):
    whole = PA // 1024
    for t in range(whole):
        rows_ref[8 * t : 8 * t + 8, :] = actor_ref[pl.ds(1024 * t, 1024)].reshape(8, 128)
    rest = (PA - 1024 * whole) // 128
    rows_ref[8 * whole : 8 * whole + rest, :] = actor_ref[pl.ds(1024 * whole, 128 * rest)].reshape(rest, 128)
    rows_ref[562:563, 0:ACT] = actor_ref[pl.ds(562 * 128, ACT)].reshape(1, ACT)
    start = NEXT if net == AT else 0
    pad_ref[...] = jnp.zeros_like(pad_ref)
    for half in range(2):
        s = pl.ds(128 * half, 128)
        pad_ref[pl.ds(start, OBS), s] = rows_ref[pl.ds(half, OBS, stride=2), :]
        pad_ref[pl.ds(ONE, 1), s] = rows_ref[pl.ds(34 + half, 1), :]
    put_first(net, pad_ref, w1_ref)
    w2 = jnp.concatenate([rows_ref[pl.ds(36, UNITS, stride=2), :], rows_ref[pl.ds(37, UNITS, stride=2), :]], 1)
    put_square(net, w2, w2f_ref, w2b_ref)
    put_column(b2_ref, net, rows_ref[548:549, :], rows_ref[549:550, :], 0.5)
    flat = jnp.concatenate([rows_ref[550:562, :], jnp.zeros((4, 128), f32)], 0)
    hi, lo = head_of(flat)
    block = jnp.concatenate([hi, hi, lo], 1)
    w3t_ref[net - A] = jnp.concatenate([block, jnp.zeros_like(block)], 0).astype(bf)
    if net == A:
        stacked = jnp.concatenate([hi, hi, lo, jnp.zeros((104, UNITS), f32)], 0)
        w3b_ref[...] = (0.5 * jnp.transpose(stacked)).astype(bf)
    bias = column(rows_ref[562:563, :])
    b3a_ref[net - A] = jnp.zeros((8, 128), f32)
    b3a_ref[net - A, 1 : 1 + ACT, :] = bias[:ACT]


def act(zh):
    u = jnp.tanh(zh) + 1.0
    return u, zh * u


def slope(u, s):
    return u + s * (2.0 - u)


class Step:
    def __init__(self, i, width, x, weights):
        (
            self.w1, self.w2f, self.w2b, self.b2, self.w3, self.b3, self.w3t, self.w3b, self.b3a, self.w1a,
        ) = weights
        self.i, self.width = i, width
        self.lanes = pl.ds(pl.multiple_of(i * width, width), width)
        self.x = x
        self.x3 = three(self.x)
        rows8 = lax.broadcasted_iota(jnp.int32, (8, width), 0)
        self.is_action = (rows8 >= 1) & (rows8 <= ACT)

    def with_action(self, a):
        x = self.x
        return three(jnp.concatenate([x[:16], jnp.where(self.is_action, a, x[16:24]), x[24:]], 0))

    def first(self, net, xx):
        return act(dot(self.w1[net, :, : 3 * FEAT], xx))

    def second(self, net, h3):
        return act(dot(self.w2f[net], h3) + lanes(self.b2[net], self.width))

    def value(self, net, s):
        return jnp.sum(s * lanes(self.w3[net], self.width), 0, keepdims=True) + lanes(self.b3[net], self.width)

    def head(self, net, s3):
        return dot(self.w3t[net - A], s3)[:8] + lanes(self.b3a[net - A], self.width)

    def valid(self, count_ref):
        tiles = self.width // 128
        return jnp.concatenate([((self.i * tiles + t) < count_ref[...]).astype(f32) for t in range(tiles)], 1)

    def grads2(self, net, h1, dz2, g2_ref):
        u = UNITS
        right = jnp.concatenate([dz2[:u], dz2[:u], dz2[u : 2 * u]], 1)
        hi, lo = h1[:u], h1[u : 2 * u]
        if net == A:
            g2_ref[net, :u, :] += dot_nt(jnp.concatenate([hi, lo, hi], 1), right)
        else:
            hi = jnp.concatenate([hi, jnp.ones((16, self.width), bf)], 0)
            lo = jnp.concatenate([lo, jnp.zeros((16, self.width), bf)], 0)
            g2_ref[net] += dot_nt(jnp.concatenate([hi, lo, hi], 1), right)

    def grads1(self, net, dz1, g1_ref):
        xhi, xlo = self.x3[:FEAT], self.x3[FEAT : 2 * FEAT]
        left = jnp.concatenate(
            [jnp.concatenate([xhi, xlo], 0), jnp.concatenate([xhi, jnp.zeros_like(xlo)], 0)], 1
        )
        a, b = split(dz1)
        g1_ref[net] += dot_nt(left, jnp.concatenate([a, b], 1))


def critic_block(i, width, x, nz_ref, count_ref, weights, prio_ref, grads):
    g2_ref, g1_ref, g3a_ref, db2_ref, dw3_ref, st_ref = grads
    st = Step(i, width, x, weights)
    x3 = st.x3

    u, s = st.first(AT, x3)
    u, s = st.second(AT, three(s))
    next_action = jnp.tanh(st.head(AT, three(s)) + nz_ref[:, st.lanes])
    xt = st.with_action(next_action)
    u, s = st.first(T0, xt)
    h0 = three(s)
    u, s = st.first(T1, xt)
    h1t = three(s)
    u, s = st.second(T0, h0)
    targets = [st.value(T0, s)]
    u0, s0 = st.first(C0, x3)
    h1, d1 = three(s0), slope(u0, s0)
    u, s = st.second(T1, h1t)
    targets.append(st.value(T1, s))
    u0, s0 = st.second(C0, h1)
    y = x[23:24] + 0.99 * x[24:25] * jnp.minimum(targets[0], targets[1])
    valid = st.valid(count_ref)
    scaled = valid * SCALE
    st_ref[1:2, :] += fold(valid)

    def top(net, s, d2):
        delta = st.value(net, s) - y
        if net == C0:
            prio = valid * jnp.sqrt(delta * delta + 1.0)
            tiles = width // 128
            for t in range(tiles):
                prio_ref[(i * tiles) // 16, pl.ds(lax.rem(i * tiles, 16) + t, 1), :] = prio[:, 128 * t : 128 * (t + 1)]
        st_ref[0:1, :] += fold(valid * (delta * delta))
        dq = (2.0 * scaled) * delta
        st_ref[2 + net : 3 + net, :] += fold(dq)
        dw3_ref[net] += fold(s * dq)
        dz2 = lanes(st.w3[net], width) * (0.5 * dq) * d2
        return three(dz2)

    u, s = st.first(C1, x3)
    h1b, d1b = three(s), slope(u, s)
    dz2 = top(C0, s0, slope(u0, s0))
    dz1 = dot(st.w2b[C0], dz2) * d1
    st.grads2(C0, h1, dz2, g2_ref)
    u, s = st.second(C1, h1b)
    st.grads1(C0, dz1, g1_ref)
    dz2 = top(C1, s, slope(u, s))
    dz1 = dot(st.w2b[C1], dz2) * d1b
    st.grads2(C1, h1b, dz2, g2_ref)
    st.grads1(C1, dz1, g1_ref)


def actor_block(i, width, x, count_ref, weights, grads):
    g2_ref, g1_ref, g3a_ref, db2_ref, dw3_ref, st_ref = grads
    st = Step(i, width, x, weights)

    u, s = st.first(A, st.x3)
    h1a, d1a = three(s), slope(u, s)
    u, s = st.second(A, h1a)
    h2a, d2a = three(s), slope(u, s)
    policy = jnp.tanh(st.head(A, h2a))

    u, s = st.first(C0, st.with_action(policy))
    d1f = slope(u, s)
    u, s = st.second(C0, three(s))
    d2f, q_policy = slope(u, s), st.value(C0, s)
    valid = st.valid(count_ref)
    st_ref[0:1, :] -= fold(valid * q_policy)

    dz2 = three(lanes(st.w3[C0], width) * (-0.5 * SCALE * valid) * d2f)
    dz1 = three(dot(st.w2b[C0], dz2) * d1f)
    da = dot(st.w1a[...], dz1)[:8]
    dp = jnp.where(st.is_action, da * (1.0 - policy * policy), 0.0)
    st_ref[8:16, :] += fold(dp)
    hi = dp.astype(bf).astype(f32)
    lo = dp - hi
    zero = jnp.zeros_like(hi)
    stacked = jnp.concatenate([hi, lo, hi, zero], 0).astype(bf)
    left = jnp.concatenate([jnp.concatenate([hi, lo], 0), jnp.concatenate([hi, zero], 0)], 1).astype(bf)
    dz2 = dot(st.w3b[:, :32], stacked) * d2a
    db2_ref[...] += fold(dz2)
    dz2 = three(dz2)
    dz1 = dot(st.w2b[A], dz2) * d1a
    g3a_ref[...] += dot_nt(left, jnp.concatenate([h2a[:UNITS], h2a[UNITS : 2 * UNITS]], 1))
    st.grads2(A, h1a, dz2, g2_ref)
    st.grads1(A, dz1, g1_ref)


def lane_sums(tile):
    return dot_exact(jnp.ones((8, 128), f32), tile, ((1,), (1,)))


def pack_critics(pack_ref, grads):
    g2_ref, g1_ref, g3a_ref, db2_ref, dw3_ref, st_ref = grads
    lane = lax.broadcasted_iota(jnp.int32, (1, 128), 1)
    sums = jnp.sum(st_ref[...], 1, keepdims=True)
    for c in range(2):
        g1 = g1_ref[c, :FEAT, :] + g1_ref[c, FEAT:, :]
        b2 = g2_ref[c, UNITS : UNITS + 1, :]
        w3 = lane_sums(dw3_ref[c])[0:1]
        for half in range(2):
            s = slice(128 * half, 128 * (half + 1))
            at = c + 2 * half
            pack_ref[pl.ds(at, OBS + ACT, stride=4), :] = g1[: OBS + ACT, s]
            pack_ref[at + 92 : at + 93, :] = g1[ONE : ONE + 1, s]
            pack_ref[pl.ds(at + 96, UNITS, stride=4), :] = g2_ref[c, :UNITS, s]
            pack_ref[at + 1120 : at + 1121, :] = b2[:, s]
            pack_ref[at + 1124 : at + 1125, :] = w3[:, s]
        pack_ref[c + 1128 : c + 1129, :] = jnp.where(lane == 0, sums[2 + c : 3 + c], 0.0)
    pack_ref[STAT : STAT + 1, :] = jnp.where(lane == 0, sums[0:1], jnp.where(lane == 1, sums[1:2], 0.0))
    pack_ref[STAT + 1 : AT_ACTOR, :] = jnp.zeros((AT_ACTOR - STAT - 1, 128), f32)


def pack_actor(pack_ref, grads):
    g2_ref, g1_ref, g3a_ref, db2_ref, dw3_ref, st_ref = grads
    sums = jnp.sum(st_ref[...], 1, keepdims=True)
    g1 = g1_ref[A, :FEAT, :] + g1_ref[A, FEAT:, :]
    b2 = lane_sums(db2_ref[...])[0:1]
    o = AT_ACTOR
    for half in range(2):
        s = slice(128 * half, 128 * (half + 1))
        pack_ref[pl.ds(o + half, OBS, stride=2), :] = g1[:OBS, s]
        pack_ref[o + 34 + half : o + 35 + half, :] = g1[ONE : ONE + 1, s]
        pack_ref[pl.ds(o + 36 + half, UNITS, stride=2), :] = g2_ref[A, :UNITS, s]
        pack_ref[o + 548 + half : o + 549 + half, :] = b2[:, s]
    pack_ref[o + 550 : o + 562, :] = head_back(g3a_ref[:8, :] + g3a_ref[8:, :])[:12]
    e = lax.broadcasted_iota(jnp.int32, (8, 128), 1) == lax.broadcasted_iota(jnp.int32, (8, 128), 0) - 1
    pack_ref[o + 562 : o + 563, :] = jnp.sum(jnp.where(e, sums[8:16], 0.0), 0, keepdims=True)
    pack_ref[o + ROWS_A : PACK, :] = jnp.zeros((PACK - o - ROWS_A, 128), f32)


WEIGHTS = [
    pltpu.VMEM((6, UNITS, 256), bf),
    pltpu.VMEM((6, UNITS, 3 * UNITS), bf),
    pltpu.VMEM((3, UNITS, 3 * UNITS), bf),
    pltpu.VMEM((6, UNITS, 128), f32),
    pltpu.VMEM((6, UNITS, 128), f32),
    pltpu.VMEM((6, 1, 128), f32),
    pltpu.VMEM((2, 16, 3 * UNITS), bf),
    pltpu.VMEM((UNITS, 128), bf),
    pltpu.VMEM((2, 8, 128), f32),
    pltpu.VMEM((16, 3 * UNITS), bf),
]
GRADS = [
    pltpu.VMEM((3, UNITS + 16, UNITS), f32),
    pltpu.VMEM((3, 2 * FEAT, UNITS), f32),
    pltpu.VMEM((16, UNITS), f32),
    pltpu.VMEM((UNITS, 128), f32),
    pltpu.VMEM((2, UNITS, 128), f32),
    pltpu.VMEM((16, 128), f32),
]


def drain(ref, sem, copies):
    view = ref.at[pl.ds(0, copies)]
    pltpu.make_async_copy(view, view, sem).wait()


class Place:
    def __init__(self):
        group, shard = lax.axis_index("group"), lax.axis_index("shard")
        self.core = lax.rem(shard, 2)
        z, x, y = group // 4, lax.rem(group, 4), shard // 2
        self.chip = group * 4 + y
        self.sibling = (group, shard + 1 - 2 * self.core)
        self.sibling_at = group * 8 + shard + 1 - 2 * self.core
        self.me = group * 8 + shard
        self.zs, self.xs, self.ys = ([lax.rem(v + n, 4) for n in range(4)] for v in (z, x, y))

    def others(self, other_core=False):
        core = 1 - self.core if other_core else self.core
        for dz, dx, dy in STEPS:
            group = self.zs[dz] * 4 + self.xs[dx]
            yield group * 4 + self.ys[dy], (group, self.ys[dy] * 2 + core)


class Sum:
    def __init__(self, place, g, pack_ref, out, buffers, sems):
        self.place, self.chunk = place, CHUNKS[g]
        self.late = g == 0
        self.first = (0, AT_ACTOR)[g]
        self.rows = CHIPS * self.chunk
        self.pack_ref = pack_ref
        self.other, self.half, self.parts, self.mine, self.both = buffers
        self.whole = self.both.at[place.core]
        if self.late:
            self.out = out.at[pl.ds(place.core * CHIPS, CHIPS), pl.ds(0, self.chunk)]
        else:
            self.out = self.whole
        self.sems = sems.at[g]

    def remote(self, src, dst, n, to):
        return pltpu.make_async_remote_copy(
            src_ref=src,
            dst_ref=dst,
            send_sem=self.sems.at[2 * n],
            recv_sem=self.sems.at[2 * n + 1],
            device_id=to,
            device_id_type=MESH,
        )

    def swap(self):
        give = pl.multiple_of(self.first + (1 - self.place.core) * self.rows, 8)
        return self.remote(self.pack_ref.at[pl.ds(give, self.rows)], self.other, 0, self.place.sibling)

    def scatter(self):
        keep = pl.multiple_of(self.first + self.place.core * self.rows, 8)
        total = self.pack_ref[pl.ds(keep, self.rows), :] + self.other[...]
        for j in range(self.chunk):
            self.half[:, j, :] = total[CHIPS * j : CHIPS * (j + 1)]
        chip = self.place.chip
        for peer, device in self.place.others():
            self.remote(self.half.at[peer], self.parts.at[chip], 1, device).start()

    def spread(self):
        chip = self.place.chip
        drain(self.half, self.sems.at[2], CHIPS - 1)
        drain(self.parts, self.sems.at[3], CHIPS - 1)
        self.parts[pl.ds(chip, 1)] = self.half[pl.ds(chip, 1)]
        self.mine[...] = jnp.sum(self.parts[...], 0)
        for _, device in self.place.others():
            self.remote(self.mine, self.whole.at[chip], 2, device).start()

    def back_copies(self):
        copies = [self.remote(self.whole, self.out, 3, self.place.sibling)]
        if self.late:
            copies.append(pltpu.make_async_copy(self.whole, self.out, self.sems.at[8]))
        return copies

    def back(self):
        drain(self.parts, self.sems.at[4], CHIPS - 1)
        drain(self.whole, self.sems.at[5], CHIPS - 1)
        self.whole[pl.ds(self.place.chip, 1)] = self.mine[...][None]
        for copy in self.back_copies():
            copy.start()

    def finish(self):
        for copy in self.back_copies():
            copy.wait()

    def in_order(self, flat_ref):
        for core in range(2):
            for j in range(self.chunk):
                at = (core * self.chunk + j) * CHIPS
                flat_ref[at // 16 : (at + CHIPS) // 16] = self.both[core, :, j, :].reshape(CHIPS // 16, 16, 128)


def sum_buffers():
    out = []
    for chunk in CHUNKS:
        out += [
            pltpu.VMEM((CHIPS * chunk, 128), f32),
            pltpu.VMEM((CHIPS, chunk, 128), f32),
            pltpu.VMEM((CHIPS, chunk, 128), f32),
            pltpu.VMEM((chunk, 128), f32),
            pltpu.VMEM((2, CHIPS, chunk, 128), f32),
        ]
    return out


def step_kernel(
    width,
    table_hbm,
    index_hbm,
    noise_hbm,
    count_hbm,
    actor_hbm,
    actor_t_hbm,
    critic_hbm,
    critic_t_hbm,
    out_hbm,
    prio_ref,
    order_ref,
    table_ref,
    index_ref,
    noise_ref,
    count_ref,
    actor_ref,
    actor_t_ref,
    critic_ref,
    critic_t_ref,
    in_sems,
    rows_ref,
    picked_ref,
    q_ref,
    nsend,
    nrecv,
    noise_sems,
    x_ref,
    nz_ref,
    flat_ref,
    pad_ref,
    pack_ref,
    sems,
    *scratch,
):
    weights, grads = scratch[: len(WEIGHTS)], scratch[len(WEIGHTS) : len(WEIGHTS) + len(GRADS)]
    buffers = scratch[len(WEIGHTS) + len(GRADS) :]
    w1_ref, w2f_ref, w2b_ref, b2_ref, w3_ref, b3_ref, w3t_ref, w3b_ref, b3a_ref, w1a_ref = weights
    blocks = N // width
    place = Place()
    me = place.me

    loads = [
        pltpu.make_async_copy(src, dst, in_sems.at[n])
        for n, (src, dst) in enumerate(
            (
                (critic_hbm, critic_ref),
                (actor_hbm, actor_ref),
                (table_hbm, table_ref),
                (index_hbm, index_ref),
                (count_hbm, count_ref),
                (noise_hbm, noise_ref),
                (critic_t_hbm, critic_t_ref),
                (actor_t_hbm, actor_t_ref),
            )
        )
    ]
    for load in loads:
        load.start()

    barrier = pltpu.get_barrier_semaphore()

    def all_others():
        for other_core in (False, True):
            for _, device in place.others(other_core):
                yield device[0] * 8 + device[1], device
        yield place.sibling_at, place.sibling

    def greet(devices):
        for _, device in devices:
            pl.semaphore_signal(barrier, inc=1, device_id=device, device_id_type=MESH)

    names = list(all_others())
    greet(names[:80])
    for ref in grads:
        ref[...] = jnp.zeros_like(ref)
    loads[0].wait()
    loads[1].wait()
    greet(names[80:])
    prepare_critics(
        critic_ref, flat_ref, pad_ref, C0, w1_ref, w2f_ref, w2b_ref, b2_ref, w3_ref, b3_ref, w1a_ref
    )
    prepare_actor(
        A, actor_ref, flat_ref, pad_ref, w1_ref, w2f_ref, w2b_ref, b2_ref, w3t_ref, w3b_ref, b3a_ref
    )
    loads[2].wait()

    def turn(i, carry):
        turn_table(i, table_ref, rows_ref)
        return carry

    lax.fori_loop(0, R_DEV // TURN, turn, 0)
    loads[3].wait()
    pick_rows(0, width, index_ref, rows_ref, picked_ref)
    loads[4].wait()
    loads[5].wait()
    turn_noise(noise_ref, q_ref, nsend)

    def send():
        for peer, device in names:
            pltpu.make_async_remote_copy(
                src_ref=nsend.at[peer],
                dst_ref=nrecv.at[me],
                send_sem=noise_sems.at[0],
                recv_sem=noise_sems.at[1],
                device_id=device,
                device_id_type=MESH,
            ).start()

    def actors(i, carry):
        x = turn_rows(width, picked_ref)
        x_ref[:, pl.ds(pl.multiple_of(i * width, width), width)] = x
        actor_block(i, width, x, count_ref, weights, grads)
        pick_rows(lax.rem(i + 1, blocks), width, index_ref, rows_ref, picked_ref)

        @pl.when(i == 0)
        def _():
            loads[6].wait()
            loads[7].wait()
            pl.semaphore_wait(barrier, DEVS - 1)
            send()
            prepare_critics(
                critic_t_ref, flat_ref, pad_ref, T0, w1_ref, w2f_ref, w2b_ref, b2_ref, w3_ref, b3_ref, w1a_ref
            )
            prepare_actor(
                AT, actor_t_ref, flat_ref, pad_ref, w1_ref, w2f_ref, w2b_ref, b2_ref, w3t_ref, w3b_ref, b3a_ref
            )

        return carry

    lax.fori_loop(0, blocks, actors, 0)
    pack_actor(pack_ref, grads)
    late, early = (Sum(place, g, pack_ref, out_hbm, buffers[5 * g : 5 * g + 5], sems) for g in range(2))
    early.swap().start()

    drain(nsend, noise_sems.at[0], DEVS - 1)
    drain(nrecv, noise_sems.at[1], DEVS - 1)
    nrecv[pl.ds(me, 1)] = nsend[pl.ds(me, 1)]
    noise_back(nrecv, nz_ref)

    def critics(i, carry):
        x = x_ref[:, pl.ds(pl.multiple_of(i * width, width), width)]
        critic_block(i, width, x, nz_ref, count_ref, weights, prio_ref, grads)

        @pl.when(i == 0)
        def _():
            early.swap().wait()
            early.scatter()

        @pl.when(i == 1)
        def _():
            early.spread()

        @pl.when(i == 2)
        def _():
            early.back()

        return carry

    lax.fori_loop(0, blocks, critics, 0)
    pack_critics(pack_ref, grads)
    late.swap().start()
    prios = pltpu.make_async_copy(prio_ref, out_hbm.at[pl.ds(AT_PRIO, 2)], in_sems.at[0])
    prios.start()
    early.finish()
    late.swap().wait()
    late.scatter()
    early.in_order(order_ref)
    order = pltpu.make_async_copy(order_ref, out_hbm.at[pl.ds(AT_SUM, order_ref.shape[0])], in_sems.at[1])
    order.start()
    prios.wait()
    late.spread()
    order.wait()
    late.back()
    late.finish()


def update(weight, grad, momentum, average, target):
    momentum_new = 0.9 * momentum + grad
    weight_new = weight - 0.1 * (grad + 0.9 * momentum_new)
    average_new = 0.99 * average + 0.01 * weight_new
    target_new = 0.005 * weight_new + 0.995 * target
    return (weight_new, momentum_new, average_new, target_new, weight_new.astype(bf))


STEP = 1024
CUTS = (0, 24 * STEP, 44 * STEP, 60 * STEP, PC)
LAST = len(CUTS) - 1


def update_kernel(sum_hbm, *refs):
    ins, stat_ref, prio_out, outs_hbm, outs = refs[:8], refs[8], refs[9], refs[10:20], refs[20:30]
    late_ref, early_ref, count_ref, grad_ref, in_sems, out_sems = refs[30:]
    early = pltpu.make_async_copy(sum_hbm.at[pl.ds(AT_SUM, early_ref.shape[0])], early_ref, in_sems.at[0])
    late = pltpu.make_async_copy(sum_hbm.at[pl.ds(0, DEVS), pl.ds(0, CHUNKS[0])], late_ref, in_sems.at[1])
    stat_core, stat_row = divmod(STAT, CHIPS * CHUNKS[0])
    stat_at = stat_core * CHIPS + stat_row % CHIPS
    count = pltpu.make_async_copy(sum_hbm.at[pl.ds(stat_at, 1), pl.ds(0, CHUNKS[0])], count_ref, in_sems.at[3])
    for load in (count, early, late):
        load.start()
    pass_on = pltpu.make_async_copy(sum_hbm.at[pl.ds(AT_PRIO, 2)], prio_out, in_sems.at[2])
    pass_on.start()

    def stores(piece):
        out = []
        for n in range(5):
            src, dst = outs[2 * n + min(piece, 1)], outs_hbm[2 * n + min(piece, 1)]
            if piece:
                s = pl.ds(CUTS[piece - 1], CUTS[piece] - CUTS[piece - 1])
                src, dst = src.at[:, s], dst.at[:, s]
            out.append(pltpu.make_async_copy(src, dst, out_sems.at[piece, n]))
        return out

    count.wait()
    stat = count_ref[0, stat_row // CHIPS : stat_row // CHIPS + 1, :]
    factor = (1.0 / SCALE) / stat[:, 1:2]
    stat_ref[...] = stat[:, :2].reshape(2)
    early.wait()

    def actor(s, grad):
        values = update(ins[0][s], grad, ins[2][s], ins[4][s], ins[6][s])
        for ref, value in zip(outs[0::2], values):
            ref[s] = value

    for i in range(PA // STEP):
        actor(slice(STEP * i, STEP * (i + 1)), (early_ref[i // 2, 8 * (i % 2) : 8 * (i % 2) + 8, :] * factor).reshape(STEP))
    done = PA // STEP * STEP
    last = early_ref[done // 2048, done // 128 % 16 : done // 128 % 16 + 8, :] * factor
    more = (PA - done) // 128
    actor(slice(done, done + 128 * more), last[:more].reshape(128 * more))
    done += 128 * more
    actor(slice(done, PA), last[more : more + 1, :ACT].reshape(ACT))
    for store in stores(0):
        store.start()

    def critic(s):
        values = update(ins[1][:, s], grad_ref[:, s] * factor, ins[3][:, s], ins[5][:, s], ins[7][:, s])
        for ref, value in zip(outs[1::2], values):
            ref[:, s] = value

    def critics(i, carry):
        critic(pl.ds(pl.multiple_of(i * STEP, STEP), STEP))
        return carry

    late.wait()
    for piece in range(1, LAST + 1):
        for t in range(CUTS[piece - 1] // 128, -(-CUTS[piece] // 128)):
            core, r = divmod(2 * t, CHIPS * CHUNKS[0])
            j, k = divmod(r, CHIPS)
            k += core * CHIPS
            grad_ref[:, 128 * t : 128 * (t + 1)] = late_ref[k : k + 2, j, :]
        lax.fori_loop(CUTS[piece - 1] // STEP, CUTS[piece] // STEP, critics, 0, unroll=4)
        if piece == LAST:
            done = PC // STEP * STEP
            critic(pl.ds(done, PC - done))
        for store in stores(piece):
            store.start()
    for piece in range(LAST + 1):
        for store in stores(piece):
            store.wait()
    pass_on.wait()


def local(
    replay,
    sample_index,
    pair_count,
    noise,
    actor,
    critic,
    actor_momentum,
    critic_momentum,
    actor_average,
    critic_average,
    actor_target,
    critic_target,
):
    any_ = pl.BlockSpec(memory_space=pl.ANY)
    total = pl.pallas_call(
        functools.partial(step_kernel, WIDTH),
        out_shape=SDS(RESULT, f32),
        in_specs=[any_] * 8,
        out_specs=any_,
        scratch_shapes=[
            pltpu.VMEM((2, 16, DEVS), f32),
            pltpu.VMEM((2 * CHIPS * CHUNKS[1] // 16, 16, 128), f32),
            pltpu.VMEM((ROW, R_DEV), f32),
            pltpu.SMEM((CAP, DEVS), jnp.int32),
            pltpu.VMEM((ACT, CAP, DEVS), f32),
            pltpu.VMEM((1, DEVS), jnp.int32),
            pltpu.VMEM((PA,), f32),
            pltpu.VMEM((PA,), f32),
            pltpu.VMEM((2, PC), f32),
            pltpu.VMEM((2, PC), f32),
            pltpu.SemaphoreType.DMA((8,)),
            pltpu.VMEM((R_DEV, 128), f32),
            pltpu.VMEM((WIDTH // 128, 128, 128), f32),
            pltpu.VMEM((256, 128), f32),
            pltpu.VMEM((DEVS, 2, 128), f32),
            pltpu.VMEM((DEVS, 2, 128), f32),
            pltpu.SemaphoreType.DMA((2,)),
            pltpu.VMEM((FEAT, N), f32),
            pltpu.VMEM((8, N), f32),
            pltpu.VMEM((2 * TILES_C + 6, 128), f32),
            pltpu.VMEM((FEAT, 256), f32),
            pltpu.VMEM((PACK, 128), f32),
            pltpu.SemaphoreType.DMA((2, 9)),
        ]
        + WEIGHTS
        + GRADS
        + sum_buffers(),
        compiler_params=pltpu.CompilerParams(
            collective_id=0, has_side_effects=True, vmem_limit_bytes=56 << 20
        ),
        name="td3_step",
    )(
        replay.T,
        sample_index[0].T,
        jnp.transpose(noise[0], (2, 1, 0)),
        pair_count,
        actor,
        actor_target,
        critic,
        critic_target,
    )
    shapes = [SDS((2,), f32), SDS((2, CAP // 2, DEVS), f32)]
    places = [SDS((PA,), f32), SDS((2, PC), f32)] * 4 + [SDS((PA,), bf), SDS((2, PC), bf)]
    stat, prio, *outs = pl.pallas_call(
        update_kernel,
        out_shape=tuple(shapes + places),
        in_specs=[any_] + [VM] * 8,
        out_specs=(VM,) + (any_,) * 11,
        scratch_shapes=[pltpu.VMEM(p.shape, p.dtype) for p in places]
        + [
            pltpu.VMEM((DEVS, CHUNKS[0], 128), f32),
            pltpu.VMEM((2 * CHIPS * CHUNKS[1] // 16, 16, 128), f32),
            pltpu.VMEM((1, CHUNKS[0], 128), f32),
            pltpu.VMEM((2, TILES_C * 128), f32),
            pltpu.SemaphoreType.DMA((4,)),
            pltpu.SemaphoreType.DMA((LAST + 1, 5)),
        ],
        compiler_params=pltpu.CompilerParams(vmem_limit_bytes=24 << 20),
        name="update",
    )(
        total,
        actor,
        critic,
        actor_momentum,
        critic_momentum,
        actor_average,
        critic_average,
        actor_target,
        critic_target,
    )
    return (stat, prio.reshape(CAP, DEVS).T[None], *outs)


def solution(mesh):
    rows = ("group", "shard")
    in_specs = (P(rows, None), P(rows, None, None), P(rows, None), P(rows, None, None, None)) + (P(),) * 8
    out_specs = (P(), P(rows, None, None)) + (P(),) * 10
    return jax.shard_map(local, mesh=mesh, in_specs=in_specs, out_specs=out_specs, check_vma=False)
```

```python
import functools

import jax
import jax.numpy as jnp
from jax import lax
from jax.experimental import pallas as pl
from jax.experimental.pallas import tpu as pltpu
from jax.sharding import PartitionSpec as P

OBS = 17
ACT = 6
UNITS = 256
CAP = 32
DEVS = 128
R_DEV = 8192
ROW = 42
PA = 71942
PC = 72193
N = DEVS * CAP

bf = jnp.bfloat16
f32 = jnp.float32
MESH = pl.DeviceIdType.MESH
VM = pl.BlockSpec(memory_space=pltpu.VMEM)
SDS = jax.ShapeDtypeStruct

SCALE = 2.0**-19
C0, C1, A, AT, T0, T1 = range(6)
FEAT = 48
ONE = 42
NEXT = 25

TILES_C = 565
STAT = 1130
ROWS_A = 563
CHIPS = DEVS // 2
PLANE = 16
CHUNK = 9
CHUNK_A = 20
AT_ACTOR = 2 * CHIPS * CHUNK
PACK = AT_ACTOR + 2 * PLANE * CHUNK_A
AT_PRIO = DEVS
AT_SUM = DEVS + 2
RESULT = (3700, 16, 128)
TURN = 512
WIDTH = 1024
STEPS = sorted(
    ((z, x, y) for z in range(4) for x in range(4) for y in range(4)),
    key=lambda step: -sum(min(n, 4 - n) for n in step),
)[:-1]


def dot(a, b):
    return lax.dot_general(a, b, (((1,), (0,)), ((), ())), preferred_element_type=f32)


def dot_nt(a, b):
    return lax.dot_general(a, b, (((1,), (1,)), ((), ())), preferred_element_type=f32)


def dot_exact(a, b, dims):
    return lax.dot_general(a, b, (dims, ((), ())), precision=lax.Precision.HIGHEST, preferred_element_type=f32)


def split(v):
    hi = v.astype(bf)
    return hi, (v - hi.astype(f32)).astype(bf)


def three(v):
    hi, lo = split(v)
    return jnp.concatenate([hi, lo, hi], 0)


def lanes(tile, width):
    return jnp.concatenate([tile] * (width // 128), 1)


def fold(v):
    out = v[:, :128]
    for i in range(1, v.shape[1] // 128):
        out = out + v[:, 128 * i : 128 * (i + 1)]
    return out


def column(row):
    return jnp.transpose(jnp.broadcast_to(row, (128, 128)))


def turn_noise(noise_ref, q_ref, nsend):
    q_ref[...] = jnp.zeros_like(q_ref)
    for j in range(ACT):
        q_ref[pl.ds(j + 1, CAP, stride=8), :] = 0.5 * jnp.tanh(0.4 * noise_ref[j])
    turned = jnp.transpose(q_ref[...])
    nsend[:, :, :, :, 0, :] = turned[:, :128].reshape(4, 4, 4, 2, 128)
    nsend[:, :, :, :, 1, :] = turned[:, 128:].reshape(4, 4, 4, 2, 128)


def noise_back(nrecv, turned_ref, nz_ref):
    for d in range(DEVS):
        core, y, x, z = d % 2, d // 2 % 4, d // 8 % 4, d // 32
        for half in range(2):
            turned_ref[d : d + 1, 128 * half : 128 * (half + 1)] = nrecv[core, y, x, z, half : half + 1, :]
    back = jnp.transpose(turned_ref[...])
    for c in range(CAP):
        nz_ref[:, 128 * c : 128 * (c + 1)] = back[8 * c : 8 * (c + 1), :]


class Exchange:
    def __init__(self, place, buffers, sems):
        self.place, self.sems = place, sems
        self.buffers = buffers

    def slab(self, stage, n):
        p, (send, by_z, by_x, by_y, by_core) = self.place, self.buffers
        if stage == 0:
            return send.at[p.zs[n]], by_z.at[p.zs[0]], (p.zs[n] * 4 + p.xs[0], p.shard)
        if stage == 1:
            return by_z.at[:, p.xs[n]], by_x.at[p.xs[0]], (p.zs[0] * 4 + p.xs[n], p.shard)
        if stage == 2:
            return by_x.at[:, :, p.ys[n]], by_y.at[p.ys[0]], (p.group, p.ys[n] * 2 + p.core)
        return by_y.at[:, :, :, (1 - p.core) if n else p.core], by_core.at[p.core], p.sibling

    def start(self, stage):
        for n in range(1, 2 if stage == 3 else 4):
            src, dst, device = self.slab(stage, n)
            pltpu.make_async_remote_copy(
                src_ref=src,
                dst_ref=dst,
                send_sem=self.sems.at[2 * stage],
                recv_sem=self.sems.at[2 * stage + 1],
                device_id=device,
                device_id_type=MESH,
            ).start()
        src, dst, _ = self.slab(stage, 0)
        dst[...] = src[...]

    def wait(self, stage):
        if stage == 3:
            view = self.buffers[4].at[0]
        else:
            view = self.buffers[stage + 1].at[pl.ds(0, 3)]
        for n in range(2):
            pltpu.make_async_copy(view, view, self.sems.at[2 * stage + n]).wait()


def turn_table(i, table_ref, rows_ref):
    s = pl.ds(pl.multiple_of(i * TURN, TURN), TURN)
    v = jnp.concatenate([table_ref[:, s], jnp.zeros((128 - ROW, TURN), f32)], 0)
    rows_ref[s, :] = jnp.transpose(v)


def pick_rows(block, width, index_ref, rows_ref, picked_ref):
    tiles = width // 128
    for t in range(tiles):
        for d in range(DEVS):
            picked_ref[t, d : d + 1, :] = rows_ref[pl.ds(index_ref[block * tiles + t, d], 1), :]


def turn_rows(width, picked_ref):
    parts = [jnp.transpose(picked_ref[t])[:FEAT] for t in range(width // 128)]
    x = jnp.concatenate(parts, 1)
    ones = lax.broadcasted_iota(jnp.int32, (8, width), 0) == (ONE - 40)
    return jnp.concatenate([x[:40], jnp.where(ones, 1.0, x[40:])], 0)


def put_square(net, w2, w2f_ref, w2b_ref):
    w2 = 0.5 * w2
    turned = jnp.transpose(w2)
    hi, lo = split(turned)
    w2f_ref[net] = jnp.concatenate([hi, hi, lo], 1)
    if net in (C0, C1, A):
        hi, lo = split(w2)
        w2b_ref[net] = jnp.concatenate([hi, hi, lo], 1)


def put_first(net, pad_ref, w1_ref):
    w1 = 0.5 * pad_ref[...]
    hi = w1.astype(bf).astype(f32)
    lo = w1 - hi
    stacked = jnp.concatenate([hi, hi, lo, jnp.zeros((256 - 3 * FEAT, 256), f32)], 0)
    w1_ref[net] = jnp.transpose(stacked).astype(bf)


def put_column(ref, net, left, right, factor):
    ref[net] = jnp.concatenate([column(left * factor), column(right * factor)], 0)


def prepare_critics(critic_ref, rows_ref, pad_ref, first, w1_ref, w2f_ref, w2b_ref, b2_ref, w3_ref, b3_ref, w1a_ref):
    for t in range(TILES_C - 1):
        rows_ref[2 * t : 2 * t + 2, :] = critic_ref[:, 128 * t : 128 * (t + 1)]
    for c in range(2):
        net = first + c
        start = NEXT if first == T0 else 0
        pad_ref[...] = jnp.zeros_like(pad_ref)
        for half in range(2):
            s = pl.ds(128 * half, 128)
            pad_ref[pl.ds(start, OBS), s] = rows_ref[pl.ds(c + 2 * half, OBS, stride=4), :]
            pad_ref[pl.ds(OBS, ACT), s] = rows_ref[pl.ds(c + 2 * half + 4 * OBS, ACT, stride=4), :]
            pad_ref[pl.ds(ONE, 1), s] = rows_ref[pl.ds(92 + c + 2 * half, 1), :]
        put_first(net, pad_ref, w1_ref)
        if net == C0:
            hi = pad_ref[16:24, :].astype(bf).astype(f32)
            lo = pad_ref[16:24, :] - hi
            block = jnp.concatenate([hi, hi, lo], 1)
            w1a_ref[...] = jnp.concatenate([block, jnp.zeros_like(block)], 0).astype(bf)
        w2 = jnp.concatenate(
            [rows_ref[pl.ds(96 + c, UNITS, stride=4), :], rows_ref[pl.ds(98 + c, UNITS, stride=4), :]], 1
        )
        put_square(net, w2, w2f_ref, w2b_ref)
        put_column(b2_ref, net, rows_ref[1120 + c : 1121 + c, :], rows_ref[1122 + c : 1123 + c, :], 0.5)
        put_column(w3_ref, net, rows_ref[1124 + c : 1125 + c, :], rows_ref[1126 + c : 1127 + c, :], 1.0)
        b3_ref[net] = jnp.broadcast_to(critic_ref[c : c + 1, PC - 1 : PC], (1, 128))


def head_maps(j):
    k = lax.broadcasted_iota(jnp.int32, (UNITS, 16), 0)
    r = lax.broadcasted_iota(jnp.int32, (UNITS, 16), 1)
    row = ((k * ACT + j) >> 7) == r
    k = lax.broadcasted_iota(jnp.int32, (UNITS, 128), 0)
    l = lax.broadcasted_iota(jnp.int32, (UNITS, 128), 1)
    lane = ((k * ACT + j) & 127) == l
    return row.astype(f32), lane


def head_of(flat):
    hi = flat.astype(bf).astype(f32)
    out = []
    for part in (hi, flat - hi):
        part = part.astype(bf)
        spread = []
        for j in range(ACT):
            row, lane = head_maps(j)
            spread.append(jnp.where(lane, dot(row.astype(bf), part), 0.0).astype(bf))
        r = lax.broadcasted_iota(jnp.int32, (16, 128 * ACT), 0)
        l = lax.broadcasted_iota(jnp.int32, (16, 128 * ACT), 1)
        take = ((l >> 7) == (r - 1)).astype(f32).astype(bf)
        out.append(dot_nt(take, jnp.concatenate(spread, 1))[:8])
    return out


def head_back(turned):
    out = jnp.zeros((16, 128), f32)
    for j in range(ACT):
        row, lane = head_maps(j)
        picked = jnp.transpose(row) * turned[j + 1 : j + 2, :]
        out = out + dot_exact(picked, lane.astype(f32), ((1,), (0,)))
    return out


def prepare_actor(net, actor_ref, rows_ref, pad_ref, w1_ref, w2f_ref, w2b_ref, b2_ref, w3t_ref, w3b_ref, b3a_ref):
    whole = PA // 1024
    for t in range(whole):
        rows_ref[8 * t : 8 * t + 8, :] = actor_ref[pl.ds(1024 * t, 1024)].reshape(8, 128)
    rest = (PA - 1024 * whole) // 128
    rows_ref[8 * whole : 8 * whole + rest, :] = actor_ref[pl.ds(1024 * whole, 128 * rest)].reshape(rest, 128)
    rows_ref[562:563, 0:ACT] = actor_ref[pl.ds(562 * 128, ACT)].reshape(1, ACT)
    start = NEXT if net == AT else 0
    pad_ref[...] = jnp.zeros_like(pad_ref)
    for half in range(2):
        s = pl.ds(128 * half, 128)
        pad_ref[pl.ds(start, OBS), s] = rows_ref[pl.ds(half, OBS, stride=2), :]
        pad_ref[pl.ds(ONE, 1), s] = rows_ref[pl.ds(34 + half, 1), :]
    put_first(net, pad_ref, w1_ref)
    w2 = jnp.concatenate([rows_ref[pl.ds(36, UNITS, stride=2), :], rows_ref[pl.ds(37, UNITS, stride=2), :]], 1)
    put_square(net, w2, w2f_ref, w2b_ref)
    put_column(b2_ref, net, rows_ref[548:549, :], rows_ref[549:550, :], 0.5)
    flat = jnp.concatenate([rows_ref[550:562, :], jnp.zeros((4, 128), f32)], 0)
    hi, lo = head_of(flat)
    block = jnp.concatenate([hi, hi, lo], 1)
    w3t_ref[net - A] = jnp.concatenate([block, jnp.zeros_like(block)], 0).astype(bf)
    if net == A:
        stacked = jnp.concatenate([hi, hi, lo, jnp.zeros((104, UNITS), f32)], 0)
        w3b_ref[...] = (0.5 * jnp.transpose(stacked)).astype(bf)
    bias = column(rows_ref[562:563, :])
    b3a_ref[net - A] = jnp.zeros((8, 128), f32)
    b3a_ref[net - A, 1 : 1 + ACT, :] = bias[:ACT]


def act(zh):
    u = jnp.tanh(zh) + 1.0
    return u, zh * u


def slope(u, s):
    return u + s * (2.0 - u)


class Step:
    def __init__(self, i, width, x, weights):
        (
            self.w1, self.w2f, self.w2b, self.b2, self.w3, self.b3, self.w3t, self.w3b, self.b3a, self.w1a,
        ) = weights
        self.i, self.width = i, width
        self.lanes = pl.ds(pl.multiple_of(i * width, width), width)
        self.x = x
        self.x3 = three(self.x)
        rows8 = lax.broadcasted_iota(jnp.int32, (8, width), 0)
        self.is_action = (rows8 >= 1) & (rows8 <= ACT)

    def with_action(self, a):
        x = self.x
        return three(jnp.concatenate([x[:16], jnp.where(self.is_action, a, x[16:24]), x[24:]], 0))

    def first(self, net, xx):
        return act(dot(self.w1[net, :, : 3 * FEAT], xx))

    def second(self, net, h3):
        return act(dot(self.w2f[net], h3) + lanes(self.b2[net], self.width))

    def value(self, net, s):
        return jnp.sum(s * lanes(self.w3[net], self.width), 0, keepdims=True) + lanes(self.b3[net], self.width)

    def head(self, net, s3):
        return dot(self.w3t[net - A], s3)[:8] + lanes(self.b3a[net - A], self.width)

    def valid(self, count_ref):
        tiles = self.width // 128
        return jnp.concatenate([((self.i * tiles + t) < count_ref[...]).astype(f32) for t in range(tiles)], 1)

    def grads2(self, net, h1, dz2, g2_ref):
        u = UNITS
        right = jnp.concatenate([dz2[:u], dz2[:u], dz2[u : 2 * u]], 1)
        hi, lo = h1[:u], h1[u : 2 * u]
        if net == A:
            g2_ref[net, :u, :] += dot_nt(jnp.concatenate([hi, lo, hi], 1), right)
        else:
            hi = jnp.concatenate([hi, jnp.ones((16, self.width), bf)], 0)
            lo = jnp.concatenate([lo, jnp.zeros((16, self.width), bf)], 0)
            g2_ref[net] += dot_nt(jnp.concatenate([hi, lo, hi], 1), right)

    def grads1(self, net, dz1, g1_ref):
        xhi, xlo = self.x3[:FEAT], self.x3[FEAT : 2 * FEAT]
        left = jnp.concatenate(
            [jnp.concatenate([xhi, xlo], 0), jnp.concatenate([xhi, jnp.zeros_like(xlo)], 0)], 1
        )
        a, b = split(dz1)
        g1_ref[net] += dot_nt(left, jnp.concatenate([a, b], 1))


def critic_block(i, width, x, nz_ref, count_ref, weights, prio_ref, grads):
    g2_ref, g1_ref, g3a_ref, db2_ref, dw3_ref, st_ref = grads
    st = Step(i, width, x, weights)
    x3 = st.x3

    u, s = st.first(AT, x3)
    u, s = st.second(AT, three(s))
    next_action = jnp.tanh(st.head(AT, three(s)) + nz_ref[:, st.lanes])
    xt = st.with_action(next_action)
    u, s = st.first(T0, xt)
    h0 = three(s)
    u, s = st.first(T1, xt)
    h1t = three(s)
    u, s = st.second(T0, h0)
    targets = [st.value(T0, s)]
    u0, s0 = st.first(C0, x3)
    h1, d1 = three(s0), slope(u0, s0)
    u, s = st.second(T1, h1t)
    targets.append(st.value(T1, s))
    u0, s0 = st.second(C0, h1)
    y = x[23:24] + 0.99 * x[24:25] * jnp.minimum(targets[0], targets[1])
    valid = st.valid(count_ref)
    scaled = valid * SCALE
    st_ref[1:2, :] += fold(valid)

    def top(net, s, d2):
        delta = st.value(net, s) - y
        if net == C0:
            prio = valid * jnp.sqrt(delta * delta + 1.0)
            tiles = width // 128
            for t in range(tiles):
                prio_ref[(i * tiles) // 16, pl.ds(lax.rem(i * tiles, 16) + t, 1), :] = prio[:, 128 * t : 128 * (t + 1)]
        st_ref[0:1, :] += fold(valid * (delta * delta))
        dq = (2.0 * scaled) * delta
        st_ref[2 + net : 3 + net, :] += fold(dq)
        dw3_ref[net] += fold(s * dq)
        dz2 = lanes(st.w3[net], width) * (0.5 * dq) * d2
        return three(dz2)

    u, s = st.first(C1, x3)
    h1b, d1b = three(s), slope(u, s)
    dz2 = top(C0, s0, slope(u0, s0))
    dz1 = dot(st.w2b[C0], dz2) * d1
    st.grads2(C0, h1, dz2, g2_ref)
    u, s = st.second(C1, h1b)
    st.grads1(C0, dz1, g1_ref)
    dz2 = top(C1, s, slope(u, s))
    dz1 = dot(st.w2b[C1], dz2) * d1b
    st.grads2(C1, h1b, dz2, g2_ref)
    st.grads1(C1, dz1, g1_ref)


def actor_block(i, width, x, count_ref, weights, grads):
    g2_ref, g1_ref, g3a_ref, db2_ref, dw3_ref, st_ref = grads
    st = Step(i, width, x, weights)

    u, s = st.first(A, st.x3)
    h1a, d1a = three(s), slope(u, s)
    u, s = st.second(A, h1a)
    h2a, d2a = three(s), slope(u, s)
    policy = jnp.tanh(st.head(A, h2a))

    u, s = st.first(C0, st.with_action(policy))
    d1f = slope(u, s)
    u, s = st.second(C0, three(s))
    d2f, q_policy = slope(u, s), st.value(C0, s)
    valid = st.valid(count_ref)
    st_ref[0:1, :] -= fold(valid * q_policy)

    dz2 = three(lanes(st.w3[C0], width) * (-0.5 * SCALE * valid) * d2f)
    dz1 = three(dot(st.w2b[C0], dz2) * d1f)
    da = dot(st.w1a[...], dz1)[:8]
    dp = jnp.where(st.is_action, da * (1.0 - policy * policy), 0.0)
    st_ref[8:16, :] += fold(dp)
    hi = dp.astype(bf).astype(f32)
    lo = dp - hi
    zero = jnp.zeros_like(hi)
    stacked = jnp.concatenate([hi, lo, hi, zero], 0).astype(bf)
    left = jnp.concatenate([jnp.concatenate([hi, lo], 0), jnp.concatenate([hi, zero], 0)], 1).astype(bf)
    dz2 = dot(st.w3b[:, :32], stacked) * d2a
    db2_ref[...] += fold(dz2)
    dz2 = three(dz2)
    dz1 = dot(st.w2b[A], dz2) * d1a
    g3a_ref[...] += dot_nt(left, jnp.concatenate([h2a[:UNITS], h2a[UNITS : 2 * UNITS]], 1))
    st.grads2(A, h1a, dz2, g2_ref)
    st.grads1(A, dz1, g1_ref)


def lane_sums(tile):
    return dot_exact(jnp.ones((8, 128), f32), tile, ((1,), (1,)))


def pack_critics(pack_ref, grads):
    g2_ref, g1_ref, g3a_ref, db2_ref, dw3_ref, st_ref = grads
    lane = lax.broadcasted_iota(jnp.int32, (1, 128), 1)
    sums = jnp.sum(st_ref[...], 1, keepdims=True)
    for c in range(2):
        g1 = g1_ref[c, :FEAT, :] + g1_ref[c, FEAT:, :]
        b2 = g2_ref[c, UNITS : UNITS + 1, :]
        w3 = lane_sums(dw3_ref[c])[0:1]
        for half in range(2):
            s = slice(128 * half, 128 * (half + 1))
            at = c + 2 * half
            pack_ref[pl.ds(at, OBS + ACT, stride=4), :] = g1[: OBS + ACT, s]
            pack_ref[at + 92 : at + 93, :] = g1[ONE : ONE + 1, s]
            pack_ref[pl.ds(at + 96, UNITS, stride=4), :] = g2_ref[c, :UNITS, s]
            pack_ref[at + 1120 : at + 1121, :] = b2[:, s]
            pack_ref[at + 1124 : at + 1125, :] = w3[:, s]
        pack_ref[c + 1128 : c + 1129, :] = jnp.where(lane == 0, sums[2 + c : 3 + c], 0.0)
    pack_ref[STAT : STAT + 1, :] = jnp.where(lane == 0, sums[0:1], jnp.where(lane == 1, sums[1:2], 0.0))
    pack_ref[STAT + 1 : AT_ACTOR, :] = jnp.zeros((AT_ACTOR - STAT - 1, 128), f32)


def pack_actor(pack_ref, grads):
    g2_ref, g1_ref, g3a_ref, db2_ref, dw3_ref, st_ref = grads
    sums = jnp.sum(st_ref[...], 1, keepdims=True)
    g1 = g1_ref[A, :FEAT, :] + g1_ref[A, FEAT:, :]
    b2 = lane_sums(db2_ref[...])[0:1]
    o = AT_ACTOR
    for half in range(2):
        s = slice(128 * half, 128 * (half + 1))
        pack_ref[pl.ds(o + half, OBS, stride=2), :] = g1[:OBS, s]
        pack_ref[o + 34 + half : o + 35 + half, :] = g1[ONE : ONE + 1, s]
        pack_ref[pl.ds(o + 36 + half, UNITS, stride=2), :] = g2_ref[A, :UNITS, s]
        pack_ref[o + 548 + half : o + 549 + half, :] = b2[:, s]
    pack_ref[o + 550 : o + 562, :] = head_back(g3a_ref[:8, :] + g3a_ref[8:, :])[:12]
    e = lax.broadcasted_iota(jnp.int32, (8, 128), 1) == lax.broadcasted_iota(jnp.int32, (8, 128), 0) - 1
    pack_ref[o + 562 : o + 563, :] = jnp.sum(jnp.where(e, sums[8:16], 0.0), 0, keepdims=True)
    pack_ref[o + ROWS_A : PACK, :] = jnp.zeros((PACK - o - ROWS_A, 128), f32)


WEIGHTS = [
    pltpu.VMEM((6, UNITS, 256), bf),
    pltpu.VMEM((6, UNITS, 3 * UNITS), bf),
    pltpu.VMEM((3, UNITS, 3 * UNITS), bf),
    pltpu.VMEM((6, UNITS, 128), f32),
    pltpu.VMEM((6, UNITS, 128), f32),
    pltpu.VMEM((6, 1, 128), f32),
    pltpu.VMEM((2, 16, 3 * UNITS), bf),
    pltpu.VMEM((UNITS, 128), bf),
    pltpu.VMEM((2, 8, 128), f32),
    pltpu.VMEM((16, 3 * UNITS), bf),
]
GRADS = [
    pltpu.VMEM((3, UNITS + 16, UNITS), f32),
    pltpu.VMEM((3, 2 * FEAT, UNITS), f32),
    pltpu.VMEM((16, UNITS), f32),
    pltpu.VMEM((UNITS, 128), f32),
    pltpu.VMEM((2, UNITS, 128), f32),
    pltpu.VMEM((16, 128), f32),
]


def drain(ref, sem, copies):
    view = ref.at[pl.ds(0, copies)]
    pltpu.make_async_copy(view, view, sem).wait()


class Place:
    def __init__(self):
        group, shard = lax.axis_index("group"), lax.axis_index("shard")
        self.group, self.shard = group, shard
        self.core = lax.rem(shard, 2)
        z, x, y = group // 4, lax.rem(group, 4), shard // 2
        self.chip = group * 4 + y
        self.sibling = (group, shard + 1 - 2 * self.core)
        self.zs, self.xs, self.ys = ([lax.rem(v + n, 4) for n in range(4)] for v in (z, x, y))

    def others(self):
        for dz, dx, dy in STEPS:
            group = self.zs[dz] * 4 + self.xs[dx]
            yield group * 4 + self.ys[dy], (group, self.ys[dy] * 2 + self.core)

    def plane(self):
        for dz, dx, dy in STEPS:
            if not dy:
                group = self.zs[dz] * 4 + self.xs[dx]
                yield group, (group, self.shard)

    def column(self):
        for y in (self.ys[2], self.ys[1], self.ys[3]):
            yield (self.group, y * 2 + self.core)


def remote(src, dst, sems, n, device):
    return pltpu.make_async_remote_copy(
        src_ref=src,
        dst_ref=dst,
        send_sem=sems.at[2 * n],
        recv_sem=sems.at[2 * n + 1],
        device_id=device,
        device_id_type=MESH,
    )


def halves(place, first, rows):
    return tuple(pl.multiple_of(first + core * rows, 8) for core in (place.core, 1 - place.core))


class CriticSum:
    def __init__(self, place, pack_ref, out, buffers, sems):
        self.place, self.pack_ref, self.sems = place, pack_ref, sems
        self.rows = CHIPS * CHUNK
        self.keep, self.give = halves(place, 0, self.rows)
        self.other, self.half, self.parts, self.mine, self.whole = buffers
        self.out = out.at[pl.ds(place.core * CHIPS, CHIPS), pl.ds(0, CHUNK)]

    def swap(self):
        return remote(self.pack_ref.at[pl.ds(self.give, self.rows)], self.other, self.sems, 0, self.place.sibling)

    def scatter(self):
        total = self.pack_ref[pl.ds(self.keep, self.rows), :] + self.other[...]
        for j in range(CHUNK):
            self.half[:, j, :] = total[CHIPS * j : CHIPS * (j + 1)]
        for peer, device in self.place.others():
            remote(self.half.at[peer], self.parts.at[self.place.chip], self.sems, 1, device).start()

    def spread(self):
        chip = self.place.chip
        drain(self.half, self.sems.at[2], CHIPS - 1)
        drain(self.parts, self.sems.at[3], CHIPS - 1)
        self.parts[pl.ds(chip, 1)] = self.half[pl.ds(chip, 1)]
        self.mine[...] = jnp.sum(self.parts[...], 0)
        for _, device in self.place.others():
            remote(self.mine, self.whole.at[chip], self.sems, 2, device).start()

    def back(self):
        drain(self.parts, self.sems.at[4], CHIPS - 1)
        drain(self.whole, self.sems.at[5], CHIPS - 1)
        self.whole[pl.ds(self.place.chip, 1)] = self.mine[...][None]
        copies = (
            remote(self.whole, self.out, self.sems, 3, self.place.sibling),
            pltpu.make_async_copy(self.whole, self.out, self.sems.at[8]),
        )
        for copy in copies:
            copy.start()
        for copy in copies:
            copy.wait()


class ActorSum:
    def __init__(self, place, pack_ref, buffers, sems):
        self.place, self.pack_ref, self.sems = place, pack_ref, sems
        self.rows = PLANE * CHUNK_A
        self.keep, self.give = halves(place, AT_ACTOR, self.rows)
        self.other, self.half, self.parts, self.columns, self.mine, self.both = buffers
        self.whole = self.both.at[place.core]

    def swap(self):
        return remote(self.pack_ref.at[pl.ds(self.give, self.rows)], self.other, self.sems, 0, self.place.sibling)

    def scatter(self):
        total = self.pack_ref[pl.ds(self.keep, self.rows), :] + self.other[...]
        for j in range(CHUNK_A):
            self.half[:, j, :] = total[PLANE * j : PLANE * (j + 1)]
        for peer, device in self.place.plane():
            remote(self.half.at[peer], self.parts.at[self.place.group], self.sems, 1, device).start()

    def along(self):
        group, y = self.place.group, self.place.ys[0]
        drain(self.half, self.sems.at[2], PLANE - 1)
        drain(self.parts, self.sems.at[3], PLANE - 1)
        self.parts[pl.ds(group, 1)] = self.half[pl.ds(group, 1)]
        self.mine[0] = jnp.sum(self.parts[...], 0)
        self.columns[pl.ds(y, 1)] = self.mine[0:1]
        for device in self.place.column():
            remote(self.mine.at[0], self.columns.at[y], self.sems, 2, device).start()

    def spread(self):
        drain(self.columns, self.sems.at[4], 3)
        drain(self.columns, self.sems.at[5], 3)
        self.mine[1] = jnp.sum(self.columns[...], 0)
        for _, device in self.place.plane():
            remote(self.mine.at[1], self.whole.at[self.place.group], self.sems, 3, device).start()

    def back_copy(self):
        return remote(self.whole, self.whole, self.sems, 4, self.place.sibling)

    def back(self):
        drain(self.parts, self.sems.at[6], PLANE - 1)
        drain(self.whole, self.sems.at[7], PLANE - 1)
        self.whole[pl.ds(self.place.group, 1)] = self.mine[1:2]
        self.back_copy().start()

    def in_order(self, flat_ref):
        for core in range(2):
            for j in range(CHUNK_A):
                flat_ref[core * CHUNK_A + j] = self.both[core, :, j, :]


SUM_BUFFERS = [
    pltpu.VMEM((CHIPS * CHUNK, 128), f32),
    pltpu.VMEM((CHIPS, CHUNK, 128), f32),
    pltpu.VMEM((CHIPS, CHUNK, 128), f32),
    pltpu.VMEM((CHUNK, 128), f32),
    pltpu.VMEM((CHIPS, CHUNK, 128), f32),
    pltpu.VMEM((PLANE * CHUNK_A, 128), f32),
    pltpu.VMEM((PLANE, CHUNK_A, 128), f32),
    pltpu.VMEM((PLANE, CHUNK_A, 128), f32),
    pltpu.VMEM((4, CHUNK_A, 128), f32),
    pltpu.VMEM((2, CHUNK_A, 128), f32),
    pltpu.VMEM((2, PLANE, CHUNK_A, 128), f32),
]
NOISE_BUFFERS = [
    pltpu.VMEM((4, 4, 4, 2, 2, 128), f32),
    pltpu.VMEM((4, 4, 4, 2, 2, 128), f32),
    pltpu.VMEM((4, 4, 4, 2, 2, 128), f32),
    pltpu.VMEM((4, 4, 4, 2, 2, 128), f32),
    pltpu.VMEM((2, 4, 4, 4, 2, 128), f32),
]


def step_kernel(
    width,
    table_hbm,
    index_hbm,
    noise_hbm,
    count_hbm,
    actor_hbm,
    actor_t_hbm,
    critic_hbm,
    critic_t_hbm,
    out_hbm,
    prio_ref,
    order_ref,
    table_ref,
    index_ref,
    noise_ref,
    count_ref,
    actor_ref,
    actor_t_ref,
    critic_ref,
    critic_t_ref,
    in_sems,
    rows_ref,
    picked_ref,
    q_ref,
    turned_ref,
    noise_sems,
    x_ref,
    nz_ref,
    flat_ref,
    pad_ref,
    pack_ref,
    sems,
    *scratch,
):
    weights, grads = scratch[: len(WEIGHTS)], scratch[len(WEIGHTS) : len(WEIGHTS) + len(GRADS)]
    buffers = scratch[len(WEIGHTS) + len(GRADS) :]
    noise = Exchange(place := Place(), buffers[len(SUM_BUFFERS) :], noise_sems)
    w1_ref, w2f_ref, w2b_ref, b2_ref, w3_ref, b3_ref, w3t_ref, w3b_ref, b3a_ref, w1a_ref = weights
    blocks = N // width
    loads = [
        pltpu.make_async_copy(src, dst, in_sems.at[n])
        for n, (src, dst) in enumerate(
            (
                (critic_hbm, critic_ref),
                (actor_hbm, actor_ref),
                (table_hbm, table_ref),
                (index_hbm, index_ref),
                (count_hbm, count_ref),
                (noise_hbm, noise_ref),
                (critic_t_hbm, critic_t_ref),
                (actor_t_hbm, actor_t_ref),
            )
        )
    ]
    for load in loads:
        load.start()

    barrier = pltpu.get_barrier_semaphore()

    for device in [place.sibling] + [device for _, device in place.others()]:
        pl.semaphore_signal(barrier, inc=1, device_id=device, device_id_type=MESH)
    for ref in grads:
        ref[...] = jnp.zeros_like(ref)
    loads[0].wait()
    loads[1].wait()
    prepare_critics(
        critic_ref, flat_ref, pad_ref, C0, w1_ref, w2f_ref, w2b_ref, b2_ref, w3_ref, b3_ref, w1a_ref
    )
    prepare_actor(
        A, actor_ref, flat_ref, pad_ref, w1_ref, w2f_ref, w2b_ref, b2_ref, w3t_ref, w3b_ref, b3a_ref
    )
    loads[2].wait()

    def turn(i, carry):
        turn_table(i, table_ref, rows_ref)
        return carry

    lax.fori_loop(0, R_DEV // TURN, turn, 0)
    loads[3].wait()
    pick_rows(0, width, index_ref, rows_ref, picked_ref)
    loads[4].wait()
    loads[5].wait()
    turn_noise(noise_ref, q_ref, noise.buffers[0])

    def actors(i, carry):
        x = turn_rows(width, picked_ref)
        x_ref[:, pl.ds(pl.multiple_of(i * width, width), width)] = x
        actor_block(i, width, x, count_ref, weights, grads)
        pick_rows(lax.rem(i + 1, blocks), width, index_ref, rows_ref, picked_ref)

        @pl.when(i == 0)
        def _():
            loads[6].wait()
            loads[7].wait()
            pl.semaphore_wait(barrier, CHIPS)
            noise.start(0)
            prepare_critics(
                critic_t_ref, flat_ref, pad_ref, T0, w1_ref, w2f_ref, w2b_ref, b2_ref, w3_ref, b3_ref, w1a_ref
            )
            prepare_actor(
                AT, actor_t_ref, flat_ref, pad_ref, w1_ref, w2f_ref, w2b_ref, b2_ref, w3t_ref, w3b_ref, b3a_ref
            )

        for stage in range(1, 4):

            @pl.when(i == stage)
            def _():
                noise.wait(stage - 1)
                noise.start(stage)

        return carry

    lax.fori_loop(0, blocks, actors, 0)
    pack_actor(pack_ref, grads)
    late = CriticSum(place, pack_ref, out_hbm, buffers[:5], sems.at[0])
    early = ActorSum(place, pack_ref, buffers[5 : len(SUM_BUFFERS)], sems.at[1])
    early.swap().start()

    noise.wait(3)
    noise_back(noise.buffers[4], turned_ref, nz_ref)

    def critics(i, carry):
        x = x_ref[:, pl.ds(pl.multiple_of(i * width, width), width)]
        critic_block(i, width, x, nz_ref, count_ref, weights, prio_ref, grads)

        @pl.when(i == 0)
        def _():
            early.swap().wait()
            early.scatter()

        @pl.when(i == 1)
        def _():
            early.along()

        @pl.when(i == 2)
        def _():
            early.spread()

        @pl.when(i == 3)
        def _():
            early.back()

        return carry

    lax.fori_loop(0, blocks, critics, 0)
    pack_critics(pack_ref, grads)
    late.swap().start()
    prios = pltpu.make_async_copy(prio_ref, out_hbm.at[pl.ds(AT_PRIO, 2)], in_sems.at[0])
    prios.start()
    late.swap().wait()
    late.scatter()
    early.back_copy().wait()
    early.in_order(order_ref)
    order = pltpu.make_async_copy(order_ref, out_hbm.at[pl.ds(AT_SUM, order_ref.shape[0])], in_sems.at[1])
    order.start()
    prios.wait()
    late.spread()
    order.wait()
    late.back()


def update(weight, grad, momentum, average, target):
    momentum_new = 0.9 * momentum + grad
    weight_new = weight - 0.1 * (grad + 0.9 * momentum_new)
    average_new = 0.99 * average + 0.01 * weight_new
    target_new = 0.005 * weight_new + 0.995 * target
    return (weight_new, momentum_new, average_new, target_new, weight_new.astype(bf))


STEP = 1024
CUTS = (0, 24 * STEP, 44 * STEP, 60 * STEP, PC)
LAST = len(CUTS) - 1


def update_kernel(sum_hbm, *refs):
    ins, stat_ref, prio_out, outs_hbm, outs = refs[:8], refs[8], refs[9], refs[10:20], refs[20:30]
    late_ref, early_ref, count_ref, grad_ref, in_sems, out_sems = refs[30:]
    early = pltpu.make_async_copy(sum_hbm.at[pl.ds(AT_SUM, early_ref.shape[0])], early_ref, in_sems.at[0])
    late = pltpu.make_async_copy(sum_hbm.at[pl.ds(0, DEVS), pl.ds(0, CHUNK)], late_ref, in_sems.at[1])
    stat_core, stat_row = divmod(STAT, CHIPS * CHUNK)
    stat_at = stat_core * CHIPS + stat_row % CHIPS
    count = pltpu.make_async_copy(sum_hbm.at[pl.ds(stat_at, 1), pl.ds(0, CHUNK)], count_ref, in_sems.at[3])
    for load in (count, early, late):
        load.start()
    pass_on = pltpu.make_async_copy(sum_hbm.at[pl.ds(AT_PRIO, 2)], prio_out, in_sems.at[2])
    pass_on.start()

    def stores(piece):
        out = []
        for n in range(5):
            src, dst = outs[2 * n + min(piece, 1)], outs_hbm[2 * n + min(piece, 1)]
            if piece:
                s = pl.ds(CUTS[piece - 1], CUTS[piece] - CUTS[piece - 1])
                src, dst = src.at[:, s], dst.at[:, s]
            out.append(pltpu.make_async_copy(src, dst, out_sems.at[piece, n]))
        return out

    count.wait()
    stat = count_ref[0, stat_row // CHIPS : stat_row // CHIPS + 1, :]
    factor = (1.0 / SCALE) / stat[:, 1:2]
    stat_ref[...] = stat[:, :2].reshape(2)
    early.wait()

    def actor(s, grad):
        values = update(ins[0][s], grad, ins[2][s], ins[4][s], ins[6][s])
        for ref, value in zip(outs[0::2], values):
            ref[s] = value

    for i in range(PA // STEP):
        actor(slice(STEP * i, STEP * (i + 1)), (early_ref[i // 2, 8 * (i % 2) : 8 * (i % 2) + 8, :] * factor).reshape(STEP))
    done = PA // STEP * STEP
    last = early_ref[done // 2048, done // 128 % 16 : done // 128 % 16 + 8, :] * factor
    more = (PA - done) // 128
    actor(slice(done, done + 128 * more), last[:more].reshape(128 * more))
    done += 128 * more
    actor(slice(done, PA), last[more : more + 1, :ACT].reshape(ACT))
    for store in stores(0):
        store.start()

    def critic(s):
        values = update(ins[1][:, s], grad_ref[:, s] * factor, ins[3][:, s], ins[5][:, s], ins[7][:, s])
        for ref, value in zip(outs[1::2], values):
            ref[:, s] = value

    def critics(i, carry):
        critic(pl.ds(pl.multiple_of(i * STEP, STEP), STEP))
        return carry

    late.wait()
    for piece in range(1, LAST + 1):
        for t in range(CUTS[piece - 1] // 128, -(-CUTS[piece] // 128)):
            core, r = divmod(2 * t, CHIPS * CHUNK)
            j, k = divmod(r, CHIPS)
            k += core * CHIPS
            grad_ref[:, 128 * t : 128 * (t + 1)] = late_ref[k : k + 2, j, :]
        lax.fori_loop(CUTS[piece - 1] // STEP, CUTS[piece] // STEP, critics, 0, unroll=4)
        if piece == LAST:
            done = PC // STEP * STEP
            critic(pl.ds(done, PC - done))
        for store in stores(piece):
            store.start()
    for piece in range(LAST + 1):
        for store in stores(piece):
            store.wait()
    pass_on.wait()


def local(
    replay,
    sample_index,
    pair_count,
    noise,
    actor,
    critic,
    actor_momentum,
    critic_momentum,
    actor_average,
    critic_average,
    actor_target,
    critic_target,
):
    any_ = pl.BlockSpec(memory_space=pl.ANY)
    total = pl.pallas_call(
        functools.partial(step_kernel, WIDTH),
        out_shape=SDS(RESULT, f32),
        in_specs=[any_] * 8,
        out_specs=any_,
        scratch_shapes=[
            pltpu.VMEM((2, 16, DEVS), f32),
            pltpu.VMEM((2 * CHUNK_A, PLANE, 128), f32),
            pltpu.VMEM((ROW, R_DEV), f32),
            pltpu.SMEM((CAP, DEVS), jnp.int32),
            pltpu.VMEM((ACT, CAP, DEVS), f32),
            pltpu.VMEM((1, DEVS), jnp.int32),
            pltpu.VMEM((PA,), f32),
            pltpu.VMEM((PA,), f32),
            pltpu.VMEM((2, PC), f32),
            pltpu.VMEM((2, PC), f32),
            pltpu.SemaphoreType.DMA((8,)),
            pltpu.VMEM((R_DEV, 128), f32),
            pltpu.VMEM((WIDTH // 128, 128, 128), f32),
            pltpu.VMEM((256, 128), f32),
            pltpu.VMEM((DEVS, 256), f32),
            pltpu.SemaphoreType.DMA((8,)),
            pltpu.VMEM((FEAT, N), f32),
            pltpu.VMEM((8, N), f32),
            pltpu.VMEM((2 * TILES_C + 6, 128), f32),
            pltpu.VMEM((FEAT, 256), f32),
            pltpu.VMEM((PACK, 128), f32),
            pltpu.SemaphoreType.DMA((2, 10)),
        ]
        + WEIGHTS
        + GRADS
        + SUM_BUFFERS
        + NOISE_BUFFERS,
        compiler_params=pltpu.CompilerParams(
            collective_id=0, has_side_effects=True, vmem_limit_bytes=56 << 20
        ),
        name="td3_step",
    )(
        replay.T,
        sample_index[0].T,
        jnp.transpose(noise[0], (2, 1, 0)),
        pair_count,
        actor,
        actor_target,
        critic,
        critic_target,
    )
    shapes = [SDS((2,), f32), SDS((2, CAP // 2, DEVS), f32)]
    places = [SDS((PA,), f32), SDS((2, PC), f32)] * 4 + [SDS((PA,), bf), SDS((2, PC), bf)]
    stat, prio, *outs = pl.pallas_call(
        update_kernel,
        out_shape=tuple(shapes + places),
        in_specs=[any_] + [VM] * 8,
        out_specs=(VM,) + (any_,) * 11,
        scratch_shapes=[pltpu.VMEM(p.shape, p.dtype) for p in places]
        + [
            pltpu.VMEM((DEVS, CHUNK, 128), f32),
            pltpu.VMEM((2 * CHUNK_A, PLANE, 128), f32),
            pltpu.VMEM((1, CHUNK, 128), f32),
            pltpu.VMEM((2, TILES_C * 128), f32),
            pltpu.SemaphoreType.DMA((4,)),
            pltpu.SemaphoreType.DMA((LAST + 1, 5)),
        ],
        compiler_params=pltpu.CompilerParams(vmem_limit_bytes=24 << 20),
        name="update",
    )(
        total,
        actor,
        critic,
        actor_momentum,
        critic_momentum,
        actor_average,
        critic_average,
        actor_target,
        critic_target,
    )
    return (stat, prio.reshape(CAP, DEVS).T[None], *outs)


def solution(mesh):
    rows = ("group", "shard")
    in_specs = (P(rows, None), P(rows, None, None), P(rows, None), P(rows, None, None, None)) + (P(),) * 8
    out_specs = (P(), P(rows, None, None)) + (P(),) * 10
    return jax.shard_map(local, mesh=mesh, in_specs=in_specs, out_specs=out_specs, check_vma=False)
```

```python
import functools

import jax
import jax.numpy as jnp
from jax import lax
from jax.experimental import pallas as pl
from jax.experimental.pallas import tpu as pltpu
from jax.sharding import PartitionSpec as P

OBS = 17
ACT = 6
UNITS = 256
CAP = 32
DEVS = 128
R_DEV = 8192
ROW = 42
PA = 71942
PC = 72193
N = DEVS * CAP

bf = jnp.bfloat16
f32 = jnp.float32
MESH = pl.DeviceIdType.MESH
VM = pl.BlockSpec(memory_space=pltpu.VMEM)
SDS = jax.ShapeDtypeStruct

SCALE = 2.0**-19
C0, C1, A, AT, T0, T1 = range(6)
FEAT = 48
ONE = 42
NEXT = 25

TILES_C = 565
W2_ROW, W2_END = 96, 1120
REST = 1024
STAT = 1130
ROWS_A = 563
CHIPS = DEVS // 2
PLANE = 16
CHUNK = 9
CHUNK_A = 20
AT_ACTOR = 2 * CHIPS * CHUNK
PACK = AT_ACTOR + 2 * PLANE * CHUNK_A
AT_PRIO = DEVS
AT_SUM = DEVS + 2
RESULT = (3700, 16, 128)
TURN = 512
WIDTH = 1024
STEPS = sorted(
    ((z, x, y) for z in range(4) for x in range(4) for y in range(4)),
    key=lambda step: -sum(min(n, 4 - n) for n in step),
)[:-1]


def dot(a, b):
    return lax.dot_general(a, b, (((1,), (0,)), ((), ())), preferred_element_type=f32)


def dot_nt(a, b):
    return lax.dot_general(a, b, (((1,), (1,)), ((), ())), preferred_element_type=f32)


def split(v):
    hi = v.astype(bf)
    return hi, (v - hi.astype(f32)).astype(bf)


def three(v):
    hi, lo = split(v)
    return jnp.concatenate([hi, lo, hi], 0)


def lanes(tile, width):
    return jnp.concatenate([tile] * (width // 128), 1)


def fold(v):
    out = v[:, :128]
    for i in range(1, v.shape[1] // 128):
        out = out + v[:, 128 * i : 128 * (i + 1)]
    return out


def column(row):
    return jnp.transpose(jnp.broadcast_to(row, (128, 128)))


def turn_noise(noise_ref, q_ref, nsend):
    q_ref[...] = jnp.zeros_like(q_ref)
    for j in range(ACT):
        q_ref[pl.ds(j + 1, CAP, stride=8), :] = 0.5 * jnp.tanh(0.4 * noise_ref[j])
    turned = jnp.transpose(q_ref[...])
    nsend[:, :, :, :, 0, :] = turned[:, :128].reshape(4, 4, 4, 2, 128)
    nsend[:, :, :, :, 1, :] = turned[:, 128:].reshape(4, 4, 4, 2, 128)


def noise_back(nrecv, turned_ref, nz_ref):
    for d in range(DEVS):
        core, y, x, z = d % 2, d // 2 % 4, d // 8 % 4, d // 32
        for half in range(2):
            turned_ref[d : d + 1, 128 * half : 128 * (half + 1)] = nrecv[core, y, x, z, half : half + 1, :]
    back = jnp.transpose(turned_ref[...])
    for c in range(CAP):
        nz_ref[:, 128 * c : 128 * (c + 1)] = back[8 * c : 8 * (c + 1), :]


class Exchange:
    def __init__(self, place, buffers, sems):
        self.place, self.sems = place, sems
        self.buffers = buffers

    def slab(self, stage, n):
        p, (send, by_z, by_x, by_y, by_core) = self.place, self.buffers
        if stage == 0:
            return send.at[p.zs[n]], by_z.at[p.zs[0]], (p.zs[n] * 4 + p.xs[0], p.shard)
        if stage == 1:
            return by_z.at[:, p.xs[n]], by_x.at[p.xs[0]], (p.zs[0] * 4 + p.xs[n], p.shard)
        if stage == 2:
            return by_x.at[:, :, p.ys[n]], by_y.at[p.ys[0]], (p.group, p.ys[n] * 2 + p.core)
        return by_y.at[:, :, :, (1 - p.core) if n else p.core], by_core.at[p.core], p.sibling

    def start(self, stage):
        for n in range(1, 2 if stage == 3 else 4):
            src, dst, device = self.slab(stage, n)
            pltpu.make_async_remote_copy(
                src_ref=src,
                dst_ref=dst,
                send_sem=self.sems.at[2 * stage],
                recv_sem=self.sems.at[2 * stage + 1],
                device_id=device,
                device_id_type=MESH,
            ).start()
        src, dst, _ = self.slab(stage, 0)
        dst[...] = src[...]

    def wait(self, stage):
        if stage == 3:
            view = self.buffers[4].at[0]
        else:
            view = self.buffers[stage + 1].at[pl.ds(0, 3)]
        for n in range(2):
            pltpu.make_async_copy(view, view, self.sems.at[2 * stage + n]).wait()


def turn_table(i, table_ref, rows_ref):
    s = pl.ds(pl.multiple_of(i * TURN, TURN), TURN)
    v = jnp.concatenate([table_ref[:, s], jnp.zeros((FEAT - ROW, TURN), f32)], 0)
    rows_ref[s, :FEAT] = jnp.transpose(v)


def pick_rows(block, width, index_ref, rows_ref, picked_ref):
    tiles = width // 128
    for t in range(tiles):
        for d in range(DEVS):
            picked_ref[t, d : d + 1, :] = rows_ref[pl.ds(index_ref[block * tiles + t, d], 1), :]


def turn_rows(width, picked_ref):
    parts = [jnp.transpose(picked_ref[t, :, :FEAT]) for t in range(width // 128)]
    x = jnp.concatenate(parts, 1)
    ones = lax.broadcasted_iota(jnp.int32, (8, width), 0) == (ONE - 40)
    return jnp.concatenate([x[:40], jnp.where(ones, 1.0, x[40:])], 0)


def put_square(net, w2, w2f_ref, w2b_ref):
    w2 = 0.5 * w2
    turned = jnp.transpose(w2)
    hi, lo = split(turned)
    w2f_ref[net] = jnp.concatenate([hi, hi, lo], 1)
    if net in (C0, C1, A):
        hi, lo = split(w2)
        w2b_ref[net] = jnp.concatenate([hi, hi, lo], 1)


def put_first(net, pad_ref, w1_ref):
    w1 = 0.5 * pad_ref[...]
    hi = w1.astype(bf).astype(f32)
    lo = w1 - hi
    stacked = jnp.concatenate([hi, hi, lo, jnp.zeros((256 - 3 * FEAT, 256), f32)], 0)
    w1_ref[net] = jnp.transpose(stacked).astype(bf)


def put_column(ref, net, left, right, factor):
    ref[net] = jnp.concatenate([column(left * factor), column(right * factor)], 0)


def prepare_critics(critic_ref, rows_ref, pad_ref, first, w1_ref, w2f_ref, w2b_ref, b2_ref, w3_ref, b3_ref, w1a_ref):
    for t in range(TILES_C - 1):
        rows_ref[2 * t : 2 * t + 2, :] = critic_ref[:, 128 * t : 128 * (t + 1)]
    for c in range(2):
        net = first + c
        start = NEXT if first == T0 else 0
        pad_ref[...] = jnp.zeros_like(pad_ref)
        for half in range(2):
            s = pl.ds(128 * half, 128)
            pad_ref[pl.ds(start, OBS), s] = rows_ref[pl.ds(c + 2 * half, OBS, stride=4), :]
            pad_ref[pl.ds(OBS, ACT), s] = rows_ref[pl.ds(c + 2 * half + 4 * OBS, ACT, stride=4), :]
            pad_ref[pl.ds(ONE, 1), s] = rows_ref[pl.ds(92 + c + 2 * half, 1), :]
        put_first(net, pad_ref, w1_ref)
        if net == C0:
            hi = pad_ref[16:24, :].astype(bf).astype(f32)
            lo = pad_ref[16:24, :] - hi
            block = jnp.concatenate([hi, hi, lo], 1)
            w1a_ref[...] = jnp.concatenate([block, jnp.zeros_like(block)], 0).astype(bf)
        w2 = jnp.concatenate(
            [rows_ref[pl.ds(96 + c, UNITS, stride=4), :], rows_ref[pl.ds(98 + c, UNITS, stride=4), :]], 1
        )
        put_square(net, w2, w2f_ref, w2b_ref)
        put_column(b2_ref, net, rows_ref[1120 + c : 1121 + c, :], rows_ref[1122 + c : 1123 + c, :], 0.5)
        put_column(w3_ref, net, rows_ref[1124 + c : 1125 + c, :], rows_ref[1126 + c : 1127 + c, :], 1.0)
        b3_ref[net] = jnp.broadcast_to(critic_ref[c : c + 1, PC - 1 : PC], (1, 128))


def head_maps(j):
    k = lax.broadcasted_iota(jnp.int32, (UNITS, 16), 0)
    r = lax.broadcasted_iota(jnp.int32, (UNITS, 16), 1)
    row = ((k * ACT + j) >> 7) == r
    k = lax.broadcasted_iota(jnp.int32, (UNITS, 128), 0)
    l = lax.broadcasted_iota(jnp.int32, (UNITS, 128), 1)
    lane = ((k * ACT + j) & 127) == l
    return row.astype(f32), lane


def head_of(flat):
    hi = flat.astype(bf).astype(f32)
    out = []
    for part in (hi, flat - hi):
        part = part.astype(bf)
        spread = []
        for j in range(ACT):
            row, lane = head_maps(j)
            spread.append(jnp.where(lane, dot(row.astype(bf), part), 0.0).astype(bf))
        r = lax.broadcasted_iota(jnp.int32, (16, 128 * ACT), 0)
        l = lax.broadcasted_iota(jnp.int32, (16, 128 * ACT), 1)
        take = ((l >> 7) == (r - 1)).astype(f32).astype(bf)
        out.append(dot_nt(take, jnp.concatenate(spread, 1))[:8])
    return out


def head_back(turned):
    out = jnp.zeros((16, 128), f32)
    for j in range(ACT):
        row, lane = head_maps(j)
        picked = jnp.transpose(row) * turned[j + 1 : j + 2, :]
        hi, lo = split(picked)
        lane = lane.astype(f32).astype(bf)
        out = out + dot(hi, lane) + dot(lo, lane)
    return out


def prepare_actor(net, actor_ref, rows_ref, pad_ref, w1_ref, w2f_ref, w2b_ref, b2_ref, w3t_ref, w3b_ref, b3a_ref):
    whole = PA // 1024
    for t in range(whole):
        rows_ref[8 * t : 8 * t + 8, :] = actor_ref[pl.ds(1024 * t, 1024)].reshape(8, 128)
    rest = (PA - 1024 * whole) // 128
    rows_ref[8 * whole : 8 * whole + rest, :] = actor_ref[pl.ds(1024 * whole, 128 * rest)].reshape(rest, 128)
    rows_ref[562:563, 0:ACT] = actor_ref[pl.ds(562 * 128, ACT)].reshape(1, ACT)
    start = NEXT if net == AT else 0
    pad_ref[...] = jnp.zeros_like(pad_ref)
    for half in range(2):
        s = pl.ds(128 * half, 128)
        pad_ref[pl.ds(start, OBS), s] = rows_ref[pl.ds(half, OBS, stride=2), :]
        pad_ref[pl.ds(ONE, 1), s] = rows_ref[pl.ds(34 + half, 1), :]
    put_first(net, pad_ref, w1_ref)
    w2 = jnp.concatenate([rows_ref[pl.ds(36, UNITS, stride=2), :], rows_ref[pl.ds(37, UNITS, stride=2), :]], 1)
    put_square(net, w2, w2f_ref, w2b_ref)
    put_column(b2_ref, net, rows_ref[548:549, :], rows_ref[549:550, :], 0.5)
    flat = jnp.concatenate([rows_ref[550:562, :], jnp.zeros((4, 128), f32)], 0)
    hi, lo = head_of(flat)
    block = jnp.concatenate([hi, hi, lo], 1)
    w3t_ref[net - A] = jnp.concatenate([block, jnp.zeros_like(block)], 0).astype(bf)
    if net == A:
        stacked = jnp.concatenate([hi, hi, lo, jnp.zeros((104, UNITS), f32)], 0)
        w3b_ref[...] = (0.5 * jnp.transpose(stacked)).astype(bf)
    bias = column(rows_ref[562:563, :])
    b3a_ref[net - A] = jnp.zeros((8, 128), f32)
    b3a_ref[net - A, 1 : 1 + ACT, :] = bias[:ACT]


def act(zh):
    u = jnp.tanh(zh) + 1.0
    return u, zh * u


def slope(u, s):
    return u + s * (2.0 - u)


class Step:
    def __init__(self, i, width, x, weights):
        (
            self.w1, self.w2f, self.w2b, self.b2, self.w3, self.b3, self.w3t, self.w3b, self.b3a, self.w1a,
        ) = weights
        self.i, self.width = i, width
        self.lanes = pl.ds(pl.multiple_of(i * width, width), width)
        self.x = x
        self.x3 = three(self.x)
        rows8 = lax.broadcasted_iota(jnp.int32, (8, width), 0)
        self.is_action = (rows8 >= 1) & (rows8 <= ACT)

    def with_action(self, a):
        x = self.x
        return three(jnp.concatenate([x[:16], jnp.where(self.is_action, a, x[16:24]), x[24:]], 0))

    def first(self, net, xx):
        return act(dot(self.w1[net, :, : 3 * FEAT], xx))

    def second(self, net, h3):
        return act(dot(self.w2f[net], h3) + lanes(self.b2[net], self.width))

    def value(self, net, s):
        return jnp.sum(s * lanes(self.w3[net], self.width), 0, keepdims=True) + lanes(self.b3[net], self.width)

    def head(self, net, s3):
        return dot(self.w3t[net - A], s3)[:8] + lanes(self.b3a[net - A], self.width)

    def valid(self, count_ref):
        tiles = self.width // 128
        return jnp.concatenate([((self.i * tiles + t) < count_ref[...]).astype(f32) for t in range(tiles)], 1)

    def grads2(self, net, h1, dz2, g2_ref):
        u = UNITS
        right = jnp.concatenate([dz2[:u], dz2[:u], dz2[u : 2 * u]], 1)
        hi, lo = h1[:u], h1[u : 2 * u]
        if net == A:
            g2_ref[net, :u, :] += dot_nt(jnp.concatenate([hi, lo, hi], 1), right)
        else:
            hi = jnp.concatenate([hi, jnp.ones((16, self.width), bf)], 0)
            lo = jnp.concatenate([lo, jnp.zeros((16, self.width), bf)], 0)
            g2_ref[net] += dot_nt(jnp.concatenate([hi, lo, hi], 1), right)

    def grads1(self, net, dz1, g1_ref):
        xhi, xlo = self.x3[:FEAT], self.x3[FEAT : 2 * FEAT]
        left = jnp.concatenate(
            [jnp.concatenate([xhi, xlo], 0), jnp.concatenate([xhi, jnp.zeros_like(xlo)], 0)], 1
        )
        a, b = split(dz1)
        g1_ref[net] += dot_nt(left, jnp.concatenate([a, b], 1))


def critic_block(i, width, x, nz_ref, count_ref, weights, prio_ref, grads):
    g2_ref, g1_ref, g3a_ref, db2_ref, dw3_ref, st_ref = grads
    st = Step(i, width, x, weights)
    x3 = st.x3

    u, s = st.first(AT, x3)
    u, s = st.second(AT, three(s))
    next_action = jnp.tanh(st.head(AT, three(s)) + nz_ref[:, st.lanes])
    xt = st.with_action(next_action)
    u, s = st.first(T0, xt)
    h0 = three(s)
    u, s = st.first(T1, xt)
    h1t = three(s)
    u, s = st.second(T0, h0)
    targets = [st.value(T0, s)]
    u0, s0 = st.first(C0, x3)
    h1, d1 = three(s0), slope(u0, s0)
    u, s = st.second(T1, h1t)
    targets.append(st.value(T1, s))
    u0, s0 = st.second(C0, h1)
    y = x[23:24] + 0.99 * x[24:25] * jnp.minimum(targets[0], targets[1])
    valid = st.valid(count_ref)
    scaled = valid * SCALE
    st_ref[1:2, :] += fold(valid)

    def top(net, s, d2):
        delta = st.value(net, s) - y
        if net == C0:
            prio = valid * jnp.sqrt(delta * delta + 1.0)
            tiles = width // 128
            for t in range(tiles):
                prio_ref[(i * tiles) // 16, pl.ds(lax.rem(i * tiles, 16) + t, 1), :] = prio[:, 128 * t : 128 * (t + 1)]
        st_ref[0:1, :] += fold(valid * (delta * delta))
        dq = (2.0 * scaled) * delta
        st_ref[2 + net : 3 + net, :] += fold(dq)
        dw3_ref[net] += fold(s * dq)
        dz2 = lanes(st.w3[net], width) * (0.5 * dq) * d2
        return three(dz2)

    u, s = st.first(C1, x3)
    h1b, d1b = three(s), slope(u, s)
    dz2 = top(C0, s0, slope(u0, s0))
    dz1 = dot(st.w2b[C0], dz2) * d1
    st.grads2(C0, h1, dz2, g2_ref)
    u, s = st.second(C1, h1b)
    st.grads1(C0, dz1, g1_ref)
    dz2 = top(C1, s, slope(u, s))
    dz1 = dot(st.w2b[C1], dz2) * d1b
    st.grads2(C1, h1b, dz2, g2_ref)
    st.grads1(C1, dz1, g1_ref)


def actor_block(i, width, x, count_ref, weights, grads):
    g2_ref, g1_ref, g3a_ref, db2_ref, dw3_ref, st_ref = grads
    st = Step(i, width, x, weights)

    u, s = st.first(A, st.x3)
    h1a, d1a = three(s), slope(u, s)
    u, s = st.second(A, h1a)
    h2a, d2a = three(s), slope(u, s)
    policy = jnp.tanh(st.head(A, h2a))

    u, s = st.first(C0, st.with_action(policy))
    d1f = slope(u, s)
    u, s = st.second(C0, three(s))
    d2f, q_policy = slope(u, s), st.value(C0, s)
    valid = st.valid(count_ref)
    st_ref[0:1, :] -= fold(valid * q_policy)

    dz2 = three(lanes(st.w3[C0], width) * (-0.5 * SCALE * valid) * d2f)
    dz1 = three(dot(st.w2b[C0], dz2) * d1f)
    da = dot(st.w1a[...], dz1)[:8]
    dp = jnp.where(st.is_action, da * (1.0 - policy * policy), 0.0)
    st_ref[8:16, :] += fold(dp)
    hi = dp.astype(bf).astype(f32)
    lo = dp - hi
    zero = jnp.zeros_like(hi)
    stacked = jnp.concatenate([hi, lo, hi, zero], 0).astype(bf)
    left = jnp.concatenate([jnp.concatenate([hi, lo], 0), jnp.concatenate([hi, zero], 0)], 1).astype(bf)
    dz2 = dot(st.w3b[:, :32], stacked) * d2a
    db2_ref[...] += fold(dz2)
    dz2 = three(dz2)
    dz1 = dot(st.w2b[A], dz2) * d1a
    g3a_ref[...] += dot_nt(left, jnp.concatenate([h2a[:UNITS], h2a[UNITS : 2 * UNITS]], 1))
    st.grads2(A, h1a, dz2, g2_ref)
    st.grads1(A, dz1, g1_ref)


def lane_sums(tile):
    hi, lo = split(tile)
    ones = jnp.ones((16, 128), bf)
    return (dot_nt(ones, hi) + dot_nt(ones, lo))[:8]


def pack_critics(pack_ref, grads):
    g2_ref, g1_ref, g3a_ref, db2_ref, dw3_ref, st_ref = grads
    lane = lax.broadcasted_iota(jnp.int32, (1, 128), 1)
    sums = jnp.sum(st_ref[...], 1, keepdims=True)
    for c in range(2):
        g1 = g1_ref[c, :FEAT, :] + g1_ref[c, FEAT:, :]
        b2 = g2_ref[c, UNITS : UNITS + 1, :]
        w3 = lane_sums(dw3_ref[c])[0:1]
        for half in range(2):
            s = slice(128 * half, 128 * (half + 1))
            at = c + 2 * half
            pack_ref[pl.ds(REST + at, OBS + ACT, stride=4), :] = g1[: OBS + ACT, s]
            pack_ref[REST + at + 92 : REST + at + 93, :] = g1[ONE : ONE + 1, s]
            pack_ref[pl.ds(at, UNITS, stride=4), :] = g2_ref[c, :UNITS, s]
            pack_ref[at + 1120 : at + 1121, :] = b2[:, s]
            pack_ref[at + 1124 : at + 1125, :] = w3[:, s]
        pack_ref[c + 1128 : c + 1129, :] = jnp.where(lane == 0, sums[2 + c : 3 + c], 0.0)
    pack_ref[STAT : STAT + 1, :] = jnp.where(lane == 0, sums[0:1], jnp.where(lane == 1, sums[1:2], 0.0))
    pack_ref[STAT + 1 : AT_ACTOR, :] = jnp.zeros((AT_ACTOR - STAT - 1, 128), f32)


def pack_actor(pack_ref, grads):
    g2_ref, g1_ref, g3a_ref, db2_ref, dw3_ref, st_ref = grads
    sums = jnp.sum(st_ref[...], 1, keepdims=True)
    g1 = g1_ref[A, :FEAT, :] + g1_ref[A, FEAT:, :]
    b2 = lane_sums(db2_ref[...])[0:1]
    o = AT_ACTOR
    for half in range(2):
        s = slice(128 * half, 128 * (half + 1))
        pack_ref[pl.ds(o + half, OBS, stride=2), :] = g1[:OBS, s]
        pack_ref[o + 34 + half : o + 35 + half, :] = g1[ONE : ONE + 1, s]
        pack_ref[pl.ds(o + 36 + half, UNITS, stride=2), :] = g2_ref[A, :UNITS, s]
        pack_ref[o + 548 + half : o + 549 + half, :] = b2[:, s]
    pack_ref[o + 550 : o + 562, :] = head_back(g3a_ref[:8, :] + g3a_ref[8:, :])[:12]
    e = lax.broadcasted_iota(jnp.int32, (8, 128), 1) == lax.broadcasted_iota(jnp.int32, (8, 128), 0) - 1
    pack_ref[o + 562 : o + 563, :] = jnp.sum(jnp.where(e, sums[8:16], 0.0), 0, keepdims=True)
    pack_ref[o + ROWS_A : PACK, :] = jnp.zeros((PACK - o - ROWS_A, 128), f32)


WEIGHTS = [
    pltpu.VMEM((6, UNITS, 256), bf),
    pltpu.VMEM((6, UNITS, 3 * UNITS), bf),
    pltpu.VMEM((3, UNITS, 3 * UNITS), bf),
    pltpu.VMEM((6, UNITS, 128), f32),
    pltpu.VMEM((6, UNITS, 128), f32),
    pltpu.VMEM((6, 1, 128), f32),
    pltpu.VMEM((2, 16, 3 * UNITS), bf),
    pltpu.VMEM((UNITS, 128), bf),
    pltpu.VMEM((2, 8, 128), f32),
    pltpu.VMEM((16, 3 * UNITS), bf),
]
GRADS = [
    pltpu.VMEM((3, UNITS + 16, UNITS), f32),
    pltpu.VMEM((3, 2 * FEAT, UNITS), f32),
    pltpu.VMEM((16, UNITS), f32),
    pltpu.VMEM((UNITS, 128), f32),
    pltpu.VMEM((2, UNITS, 128), f32),
    pltpu.VMEM((16, 128), f32),
]


def drain(ref, sem, copies):
    view = ref.at[pl.ds(0, copies)]
    pltpu.make_async_copy(view, view, sem).wait()


class Place:
    def __init__(self):
        group, shard = lax.axis_index("group"), lax.axis_index("shard")
        self.group, self.shard = group, shard
        self.core = lax.rem(shard, 2)
        z, x, y = group // 4, lax.rem(group, 4), shard // 2
        self.chip = group * 4 + y
        self.sibling = (group, shard + 1 - 2 * self.core)
        self.zs, self.xs, self.ys = ([lax.rem(v + n, 4) for n in range(4)] for v in (z, x, y))

    def others(self):
        for dz, dx, dy in STEPS:
            group = self.zs[dz] * 4 + self.xs[dx]
            yield group * 4 + self.ys[dy], (group, self.ys[dy] * 2 + self.core)

    def plane(self):
        for dz, dx, dy in STEPS:
            if not dy:
                group = self.zs[dz] * 4 + self.xs[dx]
                yield group, (group, self.shard)

    def column(self):
        for y in (self.ys[2], self.ys[1], self.ys[3]):
            yield (self.group, y * 2 + self.core)


def remote(src, dst, sems, n, device):
    return pltpu.make_async_remote_copy(
        src_ref=src,
        dst_ref=dst,
        send_sem=sems.at[2 * n],
        recv_sem=sems.at[2 * n + 1],
        device_id=device,
        device_id_type=MESH,
    )


def halves(place, first, rows):
    return tuple(pl.multiple_of(first + core * rows, 8) for core in (place.core, 1 - place.core))


class CriticSum:
    def __init__(self, place, pack_ref, out, buffers, sems):
        self.place, self.pack_ref, self.sems = place, pack_ref, sems
        self.wide = CHIPS * (CHUNK - 1)
        self.pieces = (halves(place, 0, self.wide), halves(place, REST, CHIPS))
        self.other, self.half, self.parts, self.mine, self.whole = buffers
        self.out = out.at[pl.ds(place.core * CHIPS, CHIPS), pl.ds(0, CHUNK)]

    def swap(self):
        at = 0
        for (_, give), rows in zip(self.pieces, (self.wide, CHIPS)):
            src, dst = self.pack_ref.at[pl.ds(give, rows)], self.other.at[pl.ds(at, rows)]
            remote(src, dst, self.sems, 0, self.place.sibling).start()
            at += rows

    def scatter(self):
        drain(self.other, self.sems.at[0], CHIPS * CHUNK)
        drain(self.other, self.sems.at[1], CHIPS * CHUNK)
        (wide, _), (more, _) = self.pieces
        total = self.pack_ref[pl.ds(wide, self.wide), :] + self.other[: self.wide, :]
        self.half[:, : CHUNK - 1, :] = total.reshape(CHIPS, CHUNK - 1, 128)
        self.half[:, CHUNK - 1, :] = self.pack_ref[pl.ds(more, CHIPS), :] + self.other[self.wide :, :]
        for peer, device in self.place.others():
            remote(self.half.at[peer], self.parts.at[self.place.chip], self.sems, 1, device).start()

    def spread(self):
        chip = self.place.chip
        drain(self.half, self.sems.at[2], CHIPS - 1)
        drain(self.parts, self.sems.at[3], CHIPS - 1)
        self.parts[pl.ds(chip, 1)] = self.half[pl.ds(chip, 1)]
        self.mine[...] = jnp.sum(self.parts[...], 0)
        for _, device in self.place.others():
            remote(self.mine, self.whole.at[chip], self.sems, 2, device).start()

    def back(self):
        drain(self.parts, self.sems.at[4], CHIPS - 1)
        drain(self.whole, self.sems.at[5], CHIPS - 1)
        self.whole[pl.ds(self.place.chip, 1)] = self.mine[...][None]
        copies = (
            remote(self.whole, self.out, self.sems, 3, self.place.sibling),
            pltpu.make_async_copy(self.whole, self.out, self.sems.at[8]),
        )
        for copy in copies:
            copy.start()
        for copy in copies:
            copy.wait()


class ActorSum:
    def __init__(self, place, pack_ref, buffers, sems):
        self.place, self.pack_ref, self.sems = place, pack_ref, sems
        self.rows = PLANE * CHUNK_A
        self.keep, self.give = halves(place, AT_ACTOR, self.rows)
        self.other, self.half, self.parts, self.columns, self.mine, self.both = buffers
        self.whole = self.both.at[place.core]

    def swap(self):
        return remote(self.pack_ref.at[pl.ds(self.give, self.rows)], self.other, self.sems, 0, self.place.sibling)

    def scatter(self):
        total = self.pack_ref[pl.ds(self.keep, self.rows), :] + self.other[...]
        for j in range(CHUNK_A):
            self.half[:, j, :] = total[PLANE * j : PLANE * (j + 1)]
        for peer, device in self.place.plane():
            remote(self.half.at[peer], self.parts.at[self.place.group], self.sems, 1, device).start()

    def along(self):
        group, y = self.place.group, self.place.ys[0]
        drain(self.half, self.sems.at[2], PLANE - 1)
        drain(self.parts, self.sems.at[3], PLANE - 1)
        self.parts[pl.ds(group, 1)] = self.half[pl.ds(group, 1)]
        self.mine[0] = jnp.sum(self.parts[...], 0)
        self.columns[pl.ds(y, 1)] = self.mine[0:1]
        for device in self.place.column():
            remote(self.mine.at[0], self.columns.at[y], self.sems, 2, device).start()

    def spread(self):
        drain(self.columns, self.sems.at[4], 3)
        drain(self.columns, self.sems.at[5], 3)
        self.mine[1] = jnp.sum(self.columns[...], 0)
        for _, device in self.place.plane():
            remote(self.mine.at[1], self.whole.at[self.place.group], self.sems, 3, device).start()

    def back_copy(self):
        return remote(self.whole, self.whole, self.sems, 4, self.place.sibling)

    def back(self):
        drain(self.parts, self.sems.at[6], PLANE - 1)
        drain(self.whole, self.sems.at[7], PLANE - 1)
        self.whole[pl.ds(self.place.group, 1)] = self.mine[1:2]
        self.back_copy().start()

    def in_order(self, flat_ref):
        for core in range(2):
            for j in range(CHUNK_A):
                flat_ref[core * CHUNK_A + j] = self.both[core, :, j, :]


SUM_BUFFERS = [
    pltpu.VMEM((CHIPS * CHUNK, 128), f32),
    pltpu.VMEM((CHIPS, CHUNK, 128), f32),
    pltpu.VMEM((CHIPS, CHUNK, 128), f32),
    pltpu.VMEM((CHUNK, 128), f32),
    pltpu.VMEM((CHIPS, CHUNK, 128), f32),
    pltpu.VMEM((PLANE * CHUNK_A, 128), f32),
    pltpu.VMEM((PLANE, CHUNK_A, 128), f32),
    pltpu.VMEM((PLANE, CHUNK_A, 128), f32),
    pltpu.VMEM((4, CHUNK_A, 128), f32),
    pltpu.VMEM((2, CHUNK_A, 128), f32),
    pltpu.VMEM((2, PLANE, CHUNK_A, 128), f32),
]
NOISE_BUFFERS = [
    pltpu.VMEM((4, 4, 4, 2, 2, 128), f32),
    pltpu.VMEM((4, 4, 4, 2, 2, 128), f32),
    pltpu.VMEM((4, 4, 4, 2, 2, 128), f32),
    pltpu.VMEM((4, 4, 4, 2, 2, 128), f32),
    pltpu.VMEM((2, 4, 4, 4, 2, 128), f32),
]


def step_kernel(
    width,
    table_hbm,
    index_hbm,
    noise_hbm,
    count_hbm,
    actor_hbm,
    actor_t_hbm,
    critic_hbm,
    critic_t_hbm,
    out_hbm,
    prio_ref,
    order_ref,
    table_ref,
    index_ref,
    noise_ref,
    count_ref,
    actor_ref,
    actor_t_ref,
    critic_ref,
    critic_t_ref,
    in_sems,
    rows_ref,
    picked_ref,
    q_ref,
    turned_ref,
    noise_sems,
    x_ref,
    nz_ref,
    flat_ref,
    pad_ref,
    pack_ref,
    sems,
    *scratch,
):
    weights, grads = scratch[: len(WEIGHTS)], scratch[len(WEIGHTS) : len(WEIGHTS) + len(GRADS)]
    buffers = scratch[len(WEIGHTS) + len(GRADS) :]
    noise = Exchange(place := Place(), buffers[len(SUM_BUFFERS) :], noise_sems)
    w1_ref, w2f_ref, w2b_ref, b2_ref, w3_ref, b3_ref, w3t_ref, w3b_ref, b3a_ref, w1a_ref = weights
    blocks = N // width
    loads = [
        pltpu.make_async_copy(src, dst, in_sems.at[n])
        for n, (src, dst) in enumerate(
            (
                (critic_hbm, critic_ref),
                (actor_hbm, actor_ref),
                (table_hbm, table_ref),
                (index_hbm, index_ref),
                (count_hbm, count_ref),
                (noise_hbm, noise_ref),
                (critic_t_hbm, critic_t_ref),
                (actor_t_hbm, actor_t_ref),
            )
        )
    ]
    for load in loads:
        load.start()

    barrier = pltpu.get_barrier_semaphore()

    for device in [place.sibling] + [device for _, device in place.others()]:
        pl.semaphore_signal(barrier, inc=1, device_id=device, device_id_type=MESH)
    for ref in grads:
        ref[...] = jnp.zeros_like(ref)
    loads[0].wait()
    loads[1].wait()
    prepare_critics(
        critic_ref, flat_ref, pad_ref, C0, w1_ref, w2f_ref, w2b_ref, b2_ref, w3_ref, b3_ref, w1a_ref
    )
    prepare_actor(
        A, actor_ref, flat_ref, pad_ref, w1_ref, w2f_ref, w2b_ref, b2_ref, w3t_ref, w3b_ref, b3a_ref
    )
    loads[2].wait()

    def turn(i, carry):
        turn_table(i, table_ref, rows_ref)
        return carry

    lax.fori_loop(0, R_DEV // TURN, turn, 0)
    loads[3].wait()
    pick_rows(0, width, index_ref, rows_ref, picked_ref)
    loads[4].wait()
    loads[5].wait()
    turn_noise(noise_ref, q_ref, noise.buffers[0])

    def actors(i, carry):
        x = turn_rows(width, picked_ref)
        x_ref[:, pl.ds(pl.multiple_of(i * width, width), width)] = x
        actor_block(i, width, x, count_ref, weights, grads)
        pick_rows(lax.rem(i + 1, blocks), width, index_ref, rows_ref, picked_ref)

        @pl.when(i == 0)
        def _():
            loads[6].wait()
            loads[7].wait()
            pl.semaphore_wait(barrier, CHIPS)
            noise.start(0)
            prepare_critics(
                critic_t_ref, flat_ref, pad_ref, T0, w1_ref, w2f_ref, w2b_ref, b2_ref, w3_ref, b3_ref, w1a_ref
            )
            prepare_actor(
                AT, actor_t_ref, flat_ref, pad_ref, w1_ref, w2f_ref, w2b_ref, b2_ref, w3t_ref, w3b_ref, b3a_ref
            )

        for stage in range(1, 4):

            @pl.when(i == stage)
            def _():
                noise.wait(stage - 1)
                noise.start(stage)

        return carry

    lax.fori_loop(0, blocks, actors, 0)
    pack_actor(pack_ref, grads)
    late = CriticSum(place, pack_ref, out_hbm, buffers[:5], sems.at[0])
    early = ActorSum(place, pack_ref, buffers[5 : len(SUM_BUFFERS)], sems.at[1])
    early.swap().start()

    noise.wait(3)
    noise_back(noise.buffers[4], turned_ref, nz_ref)

    def critics(i, carry):
        x = x_ref[:, pl.ds(pl.multiple_of(i * width, width), width)]
        critic_block(i, width, x, nz_ref, count_ref, weights, prio_ref, grads)

        @pl.when(i == 0)
        def _():
            early.swap().wait()
            early.scatter()

        @pl.when(i == 1)
        def _():
            early.along()

        @pl.when(i == 2)
        def _():
            early.spread()

        @pl.when(i == 3)
        def _():
            early.back()

        return carry

    lax.fori_loop(0, blocks, critics, 0)
    pack_critics(pack_ref, grads)
    late.swap()
    prios = pltpu.make_async_copy(prio_ref, out_hbm.at[pl.ds(AT_PRIO, 2)], in_sems.at[0])
    prios.start()
    late.scatter()
    early.back_copy().wait()
    early.in_order(order_ref)
    order = pltpu.make_async_copy(order_ref, out_hbm.at[pl.ds(AT_SUM, order_ref.shape[0])], in_sems.at[1])
    order.start()
    prios.wait()
    late.spread()
    order.wait()
    late.back()


def update(weight, grad, momentum, average, target):
    momentum_new = 0.9 * momentum + grad
    weight_new = weight - 0.1 * (grad + 0.9 * momentum_new)
    average_new = 0.99 * average + 0.01 * weight_new
    target_new = 0.005 * weight_new + 0.995 * target
    return (weight_new, momentum_new, average_new, target_new, weight_new.astype(bf))


STEP = 1024
CUTS = (0, 24 * STEP, 44 * STEP, 60 * STEP, PC)
LAST = len(CUTS) - 1


def update_kernel(sum_hbm, *refs):
    ins, stat_ref, prio_out, outs_hbm, outs = refs[:8], refs[8], refs[9], refs[10:20], refs[20:30]
    late_ref, early_ref, count_ref, grad_ref, in_sems, out_sems = refs[30:]
    early = pltpu.make_async_copy(sum_hbm.at[pl.ds(AT_SUM, early_ref.shape[0])], early_ref, in_sems.at[0])
    late = pltpu.make_async_copy(sum_hbm.at[pl.ds(0, DEVS), pl.ds(0, CHUNK)], late_ref, in_sems.at[1])
    stat_at = STAT - REST
    count = pltpu.make_async_copy(sum_hbm.at[pl.ds(stat_at, 1), pl.ds(0, CHUNK)], count_ref, in_sems.at[3])
    for load in (count, early, late):
        load.start()
    pass_on = pltpu.make_async_copy(sum_hbm.at[pl.ds(AT_PRIO, 2)], prio_out, in_sems.at[2])
    pass_on.start()

    def stores(piece):
        out = []
        for n in range(5):
            src, dst = outs[2 * n + min(piece, 1)], outs_hbm[2 * n + min(piece, 1)]
            if piece:
                s = pl.ds(CUTS[piece - 1], CUTS[piece] - CUTS[piece - 1])
                src, dst = src.at[:, s], dst.at[:, s]
            out.append(pltpu.make_async_copy(src, dst, out_sems.at[piece, n]))
        return out

    count.wait()
    stat = count_ref[0, CHUNK - 1 : CHUNK, :]
    factor = (1.0 / SCALE) / stat[:, 1:2]
    stat_ref[...] = stat[:, :2].reshape(2)
    early.wait()

    def actor(s, grad):
        values = update(ins[0][s], grad, ins[2][s], ins[4][s], ins[6][s])
        for ref, value in zip(outs[0::2], values):
            ref[s] = value

    for i in range(PA // STEP):
        actor(slice(STEP * i, STEP * (i + 1)), (early_ref[i // 2, 8 * (i % 2) : 8 * (i % 2) + 8, :] * factor).reshape(STEP))
    done = PA // STEP * STEP
    last = early_ref[done // 2048, done // 128 % 16 : done // 128 % 16 + 8, :] * factor
    more = (PA - done) // 128
    actor(slice(done, done + 128 * more), last[:more].reshape(128 * more))
    done += 128 * more
    actor(slice(done, PA), last[more : more + 1, :ACT].reshape(ACT))
    for store in stores(0):
        store.start()

    def critic(s):
        values = update(ins[1][:, s], grad_ref[:, s] * factor, ins[3][:, s], ins[5][:, s], ins[7][:, s])
        for ref, value in zip(outs[1::2], values):
            ref[:, s] = value

    def critics(i, carry):
        critic(pl.ds(pl.multiple_of(i * STEP, STEP), STEP))
        return carry

    late.wait()
    for piece in range(1, LAST + 1):
        for t in range(CUTS[piece - 1] // 128, -(-CUTS[piece] // 128)):
            r = 2 * t
            if W2_ROW <= r < W2_END:
                k, j = divmod(r - W2_ROW, CHUNK - 1)
                pair = late_ref[k, j : j + 2, :]
            else:
                k = r % REST
                pair = late_ref[k : k + 2, CHUNK - 1, :]
            grad_ref[:, 128 * t : 128 * (t + 1)] = pair
        lax.fori_loop(CUTS[piece - 1] // STEP, CUTS[piece] // STEP, critics, 0, unroll=4)
        if piece == LAST:
            done = PC // STEP * STEP
            critic(pl.ds(done, PC - done))
        for store in stores(piece):
            store.start()
    for piece in range(LAST + 1):
        for store in stores(piece):
            store.wait()
    pass_on.wait()


def local(
    replay,
    sample_index,
    pair_count,
    noise,
    actor,
    critic,
    actor_momentum,
    critic_momentum,
    actor_average,
    critic_average,
    actor_target,
    critic_target,
):
    any_ = pl.BlockSpec(memory_space=pl.ANY)
    total = pl.pallas_call(
        functools.partial(step_kernel, WIDTH),
        out_shape=SDS(RESULT, f32),
        in_specs=[any_] * 8,
        out_specs=any_,
        scratch_shapes=[
            pltpu.VMEM((2, 16, DEVS), f32),
            pltpu.VMEM((2 * CHUNK_A, PLANE, 128), f32),
            pltpu.VMEM((ROW, R_DEV), f32),
            pltpu.SMEM((CAP, DEVS), jnp.int32),
            pltpu.VMEM((ACT, CAP, DEVS), f32),
            pltpu.VMEM((1, DEVS), jnp.int32),
            pltpu.VMEM((PA,), f32),
            pltpu.VMEM((PA,), f32),
            pltpu.VMEM((2, PC), f32),
            pltpu.VMEM((2, PC), f32),
            pltpu.SemaphoreType.DMA((8,)),
            pltpu.VMEM((R_DEV, 128), f32),
            pltpu.VMEM((WIDTH // 128, 128, 128), f32),
            pltpu.VMEM((256, 128), f32),
            pltpu.VMEM((DEVS, 256), f32),
            pltpu.SemaphoreType.DMA((8,)),
            pltpu.VMEM((FEAT, N), f32),
            pltpu.VMEM((8, N), f32),
            pltpu.VMEM((2 * TILES_C + 6, 128), f32),
            pltpu.VMEM((FEAT, 256), f32),
            pltpu.VMEM((PACK, 128), f32),
            pltpu.SemaphoreType.DMA((2, 10)),
        ]
        + WEIGHTS
        + GRADS
        + SUM_BUFFERS
        + NOISE_BUFFERS,
        compiler_params=pltpu.CompilerParams(
            collective_id=0, has_side_effects=True, vmem_limit_bytes=56 << 20
        ),
        name="td3_step",
    )(
        replay.T,
        sample_index[0].T,
        jnp.transpose(noise[0], (2, 1, 0)),
        pair_count,
        actor,
        actor_target,
        critic,
        critic_target,
    )
    shapes = [SDS((2,), f32), SDS((2, CAP // 2, DEVS), f32)]
    places = [SDS((PA,), f32), SDS((2, PC), f32)] * 4 + [SDS((PA,), bf), SDS((2, PC), bf)]
    stat, prio, *outs = pl.pallas_call(
        update_kernel,
        out_shape=tuple(shapes + places),
        in_specs=[any_] + [VM] * 8,
        out_specs=(VM,) + (any_,) * 11,
        scratch_shapes=[pltpu.VMEM(p.shape, p.dtype) for p in places]
        + [
            pltpu.VMEM((DEVS, CHUNK, 128), f32),
            pltpu.VMEM((2 * CHUNK_A, PLANE, 128), f32),
            pltpu.VMEM((1, CHUNK, 128), f32),
            pltpu.VMEM((2, TILES_C * 128), f32),
            pltpu.SemaphoreType.DMA((4,)),
            pltpu.SemaphoreType.DMA((LAST + 1, 5)),
        ],
        compiler_params=pltpu.CompilerParams(vmem_limit_bytes=24 << 20),
        name="update",
    )(
        total,
        actor,
        critic,
        actor_momentum,
        critic_momentum,
        actor_average,
        critic_average,
        actor_target,
        critic_target,
    )
    return (stat, prio.reshape(CAP, DEVS).T[None], *outs)


def solution(mesh):
    rows = ("group", "shard")
    in_specs = (P(rows, None), P(rows, None, None), P(rows, None), P(rows, None, None, None)) + (P(),) * 8
    out_specs = (P(), P(rows, None, None)) + (P(),) * 10
    return jax.shard_map(local, mesh=mesh, in_specs=in_specs, out_specs=out_specs, check_vma=False)
```

```python
import functools

import jax
import jax.numpy as jnp
from jax import lax
from jax.experimental import pallas as pl
from jax.experimental.pallas import tpu as pltpu
from jax.sharding import PartitionSpec as P

OBS = 17
ACT = 6
UNITS = 256
CAP = 32
DEVS = 128
R_DEV = 8192
ROW = 42
PA = 71942
PC = 72193
N = DEVS * CAP

bf = jnp.bfloat16
f32 = jnp.float32
MESH = pl.DeviceIdType.MESH
VM = pl.BlockSpec(memory_space=pltpu.VMEM)
SDS = jax.ShapeDtypeStruct

SCALE = 2.0**-19
C0, C1, A, AT, T0, T1 = range(6)
FEAT = 48
ONE = 42
NEXT = 25

TILES_C = 565
W2_ROW, W2_END = 96, 1120
REST = 1024
STAT = 1130
ROWS_A = 563
CHIPS = DEVS // 2
PLANE = 16
CHUNK = 9
CHUNK_A = 20
AT_ACTOR = 2 * CHIPS * CHUNK
PACK = AT_ACTOR + 2 * PLANE * CHUNK_A
AT_PRIO = DEVS
AT_SUM = DEVS + 2
RESULT = (3700, 16, 128)
TURN = 512
WIDTH = 1024
STEPS = sorted(
    ((z, x, y) for z in range(4) for x in range(4) for y in range(4)),
    key=lambda step: -sum(min(n, 4 - n) for n in step),
)[:-1]


def dot(a, b):
    return lax.dot_general(a, b, (((1,), (0,)), ((), ())), preferred_element_type=f32)


def dot_nt(a, b):
    return lax.dot_general(a, b, (((1,), (1,)), ((), ())), preferred_element_type=f32)


def split(v):
    hi = v.astype(bf)
    return hi, (v - hi.astype(f32)).astype(bf)


def three(v):
    hi, lo = split(v)
    return jnp.concatenate([hi, lo, hi], 0)


def lanes(tile, width):
    return jnp.concatenate([tile] * (width // 128), 1)


def fold(v):
    out = v[:, :128]
    for i in range(1, v.shape[1] // 128):
        out = out + v[:, 128 * i : 128 * (i + 1)]
    return out


def column(row):
    return jnp.transpose(jnp.broadcast_to(row, (128, 128)))


def turn_noise(noise_ref, q_ref, nsend):
    q_ref[...] = jnp.zeros_like(q_ref)
    for j in range(ACT):
        q_ref[pl.ds(j + 1, CAP, stride=8), :] = 0.5 * jnp.tanh(0.4 * noise_ref[j])
    turned = jnp.transpose(q_ref[...])
    nsend[:, :, :, :, 0, :] = turned[:, :128].reshape(4, 4, 4, 2, 128)
    nsend[:, :, :, :, 1, :] = turned[:, 128:].reshape(4, 4, 4, 2, 128)


def noise_back(nrecv, turned_ref, nz_ref):
    for d in range(DEVS):
        core, y, x, z = d % 2, d // 2 % 4, d // 8 % 4, d // 32
        for half in range(2):
            turned_ref[d : d + 1, 128 * half : 128 * (half + 1)] = nrecv[core, y, x, z, half : half + 1, :]
    back = jnp.transpose(turned_ref[...])
    for c in range(CAP):
        nz_ref[:, 128 * c : 128 * (c + 1)] = back[8 * c : 8 * (c + 1), :]


class Exchange:
    def __init__(self, place, buffers, sems):
        self.place, self.sems = place, sems
        self.buffers = buffers

    def slab(self, stage, n):
        p, (send, by_z, by_x, by_y, by_core) = self.place, self.buffers
        if stage == 0:
            return send.at[p.zs[n]], by_z.at[p.zs[0]], (p.zs[n] * 4 + p.xs[0], p.shard)
        if stage == 1:
            return by_z.at[:, p.xs[n]], by_x.at[p.xs[0]], (p.zs[0] * 4 + p.xs[n], p.shard)
        if stage == 2:
            return by_x.at[:, :, p.ys[n]], by_y.at[p.ys[0]], (p.group, p.ys[n] * 2 + p.core)
        return by_y.at[:, :, :, (1 - p.core) if n else p.core], by_core.at[p.core], p.sibling

    def start(self, stage):
        for n in range(1, 2 if stage == 3 else 4):
            src, dst, device = self.slab(stage, n)
            pltpu.make_async_remote_copy(
                src_ref=src,
                dst_ref=dst,
                send_sem=self.sems.at[2 * stage],
                recv_sem=self.sems.at[2 * stage + 1],
                device_id=device,
                device_id_type=MESH,
            ).start()
        src, dst, _ = self.slab(stage, 0)
        dst[...] = src[...]

    def wait(self, stage):
        if stage == 3:
            view = self.buffers[4].at[0]
        else:
            view = self.buffers[stage + 1].at[pl.ds(0, 3)]
        for n in range(2):
            pltpu.make_async_copy(view, view, self.sems.at[2 * stage + n]).wait()


def turn_table(i, table_ref, rows_ref):
    s = pl.ds(pl.multiple_of(i * TURN, TURN), TURN)
    v = jnp.concatenate([table_ref[:, s], jnp.zeros((FEAT - ROW, TURN), f32)], 0)
    rows_ref[s, :FEAT] = jnp.transpose(v)


def pick_rows(block, width, index_ref, rows_ref, picked_ref):
    tiles = width // 128
    for t in range(tiles):
        for d in range(DEVS):
            picked_ref[t, d : d + 1, :] = rows_ref[pl.ds(index_ref[block * tiles + t, d], 1), :]


def turn_rows(width, picked_ref):
    parts = [jnp.transpose(picked_ref[t, :, :FEAT]) for t in range(width // 128)]
    x = jnp.concatenate(parts, 1)
    ones = lax.broadcasted_iota(jnp.int32, (8, width), 0) == (ONE - 40)
    return jnp.concatenate([x[:40], jnp.where(ones, 1.0, x[40:])], 0)


def put_square(net, w2, w2f_ref, w2b_ref):
    w2 = 0.5 * w2
    turned = jnp.transpose(w2)
    hi, lo = split(turned)
    w2f_ref[net] = jnp.concatenate([hi, hi, lo], 1)
    if net in (C0, C1, A):
        hi, lo = split(w2)
        w2b_ref[net] = jnp.concatenate([hi, hi, lo], 1)


def put_first(net, pad_ref, w1_ref):
    w1 = 0.5 * pad_ref[...]
    hi = w1.astype(bf).astype(f32)
    lo = w1 - hi
    stacked = jnp.concatenate([hi, hi, lo, jnp.zeros((256 - 3 * FEAT, 256), f32)], 0)
    w1_ref[net] = jnp.transpose(stacked).astype(bf)


def put_column(ref, net, left, right, factor):
    ref[net] = jnp.concatenate([column(left * factor), column(right * factor)], 0)


def prepare_critics(critic_ref, rows_ref, pad_ref, first, w1_ref, w2f_ref, w2b_ref, b2_ref, w3_ref, b3_ref, w1a_ref):
    for t in range(TILES_C - 1):
        rows_ref[2 * t : 2 * t + 2, :] = critic_ref[:, 128 * t : 128 * (t + 1)]
    for c in range(2):
        net = first + c
        start = NEXT if first == T0 else 0
        pad_ref[...] = jnp.zeros_like(pad_ref)
        for half in range(2):
            s = pl.ds(128 * half, 128)
            pad_ref[pl.ds(start, OBS), s] = rows_ref[pl.ds(c + 2 * half, OBS, stride=4), :]
            pad_ref[pl.ds(OBS, ACT), s] = rows_ref[pl.ds(c + 2 * half + 4 * OBS, ACT, stride=4), :]
            pad_ref[pl.ds(ONE, 1), s] = rows_ref[pl.ds(92 + c + 2 * half, 1), :]
        put_first(net, pad_ref, w1_ref)
        if net == C0:
            hi = pad_ref[16:24, :].astype(bf).astype(f32)
            lo = pad_ref[16:24, :] - hi
            block = jnp.concatenate([hi, hi, lo], 1)
            w1a_ref[...] = jnp.concatenate([block, jnp.zeros_like(block)], 0).astype(bf)
        w2 = jnp.concatenate(
            [rows_ref[pl.ds(96 + c, UNITS, stride=4), :], rows_ref[pl.ds(98 + c, UNITS, stride=4), :]], 1
        )
        put_square(net, w2, w2f_ref, w2b_ref)
        put_column(b2_ref, net, rows_ref[1120 + c : 1121 + c, :], rows_ref[1122 + c : 1123 + c, :], 0.5)
        put_column(w3_ref, net, rows_ref[1124 + c : 1125 + c, :], rows_ref[1126 + c : 1127 + c, :], 1.0)
        b3_ref[net] = jnp.broadcast_to(critic_ref[c : c + 1, PC - 1 : PC], (1, 128))


def make_maps(row_ref, turned_ref, lane_ref):
    def entry(shape, axis, j):
        return lax.broadcasted_iota(jnp.int32, shape, axis) * ACT + j

    for j in range(ACT):
        r = lax.broadcasted_iota(jnp.int32, (UNITS, 16), 1)
        row_ref[j] = ((entry((UNITS, 16), 0, j) >> 7) == r).astype(f32).astype(bf)
        r = lax.broadcasted_iota(jnp.int32, (16, UNITS), 0)
        turned_ref[j] = ((entry((16, UNITS), 1, j) >> 7) == r).astype(f32)
        l = lax.broadcasted_iota(jnp.int32, (UNITS, 128), 1)
        lane_ref[j] = ((entry((UNITS, 128), 0, j) & 127) == l).astype(f32).astype(bf)


def head_of(flat, maps):
    row_ref, _, lane_ref = maps
    hi = flat.astype(bf).astype(f32)
    r = lax.broadcasted_iota(jnp.int32, (16, 128 * ACT), 0)
    l = lax.broadcasted_iota(jnp.int32, (16, 128 * ACT), 1)
    take = ((l >> 7) == (r - 1)).astype(f32).astype(bf)
    out = []
    for part in (hi, flat - hi):
        part = part.astype(bf)
        spread = [dot(row_ref[j], part).astype(bf) * lane_ref[j] for j in range(ACT)]
        out.append(dot_nt(take, jnp.concatenate(spread, 1))[:8])
    return out


def head_back(turned, maps):
    _, turned_ref, lane_ref = maps
    out = jnp.zeros((16, 128), f32)
    for j in range(ACT):
        hi, lo = split(turned_ref[j] * turned[j + 1 : j + 2, :])
        out = out + dot(hi, lane_ref[j]) + dot(lo, lane_ref[j])
    return out


def prepare_actor(net, maps, actor_ref, rows_ref, pad_ref, w1_ref, w2f_ref, w2b_ref, b2_ref, w3t_ref, w3b_ref, b3a_ref):
    whole = PA // 1024
    for t in range(whole):
        rows_ref[8 * t : 8 * t + 8, :] = actor_ref[pl.ds(1024 * t, 1024)].reshape(8, 128)
    rest = (PA - 1024 * whole) // 128
    rows_ref[8 * whole : 8 * whole + rest, :] = actor_ref[pl.ds(1024 * whole, 128 * rest)].reshape(rest, 128)
    rows_ref[562:563, 0:ACT] = actor_ref[pl.ds(562 * 128, ACT)].reshape(1, ACT)
    start = NEXT if net == AT else 0
    pad_ref[...] = jnp.zeros_like(pad_ref)
    for half in range(2):
        s = pl.ds(128 * half, 128)
        pad_ref[pl.ds(start, OBS), s] = rows_ref[pl.ds(half, OBS, stride=2), :]
        pad_ref[pl.ds(ONE, 1), s] = rows_ref[pl.ds(34 + half, 1), :]
    put_first(net, pad_ref, w1_ref)
    w2 = jnp.concatenate([rows_ref[pl.ds(36, UNITS, stride=2), :], rows_ref[pl.ds(37, UNITS, stride=2), :]], 1)
    put_square(net, w2, w2f_ref, w2b_ref)
    put_column(b2_ref, net, rows_ref[548:549, :], rows_ref[549:550, :], 0.5)
    flat = jnp.concatenate([rows_ref[550:562, :], jnp.zeros((4, 128), f32)], 0)
    hi, lo = head_of(flat, maps)
    block = jnp.concatenate([hi, hi, lo], 1)
    w3t_ref[net - A] = jnp.concatenate([block, jnp.zeros_like(block)], 0).astype(bf)
    if net == A:
        stacked = jnp.concatenate([hi, hi, lo, jnp.zeros((104, UNITS), f32)], 0)
        w3b_ref[...] = (0.5 * jnp.transpose(stacked)).astype(bf)
    bias = column(rows_ref[562:563, :])
    b3a_ref[net - A] = jnp.zeros((8, 128), f32)
    b3a_ref[net - A, 1 : 1 + ACT, :] = bias[:ACT]


def act(zh):
    u = jnp.tanh(zh) + 1.0
    return u, zh * u


def slope(u, s):
    return u + s * (2.0 - u)


class Step:
    def __init__(self, i, width, x, weights):
        (
            self.w1, self.w2f, self.w2b, self.b2, self.w3, self.b3, self.w3t, self.w3b, self.b3a, self.w1a,
        ) = weights
        self.i, self.width = i, width
        self.lanes = pl.ds(pl.multiple_of(i * width, width), width)
        self.x = x
        self.x3 = three(self.x)
        rows8 = lax.broadcasted_iota(jnp.int32, (8, width), 0)
        self.is_action = (rows8 >= 1) & (rows8 <= ACT)

    def with_action(self, a):
        x = self.x
        return three(jnp.concatenate([x[:16], jnp.where(self.is_action, a, x[16:24]), x[24:]], 0))

    def first(self, net, xx):
        return act(dot(self.w1[net, :, : 3 * FEAT], xx))

    def second(self, net, h3):
        return act(dot(self.w2f[net], h3) + lanes(self.b2[net], self.width))

    def value(self, net, s):
        return jnp.sum(s * lanes(self.w3[net], self.width), 0, keepdims=True) + lanes(self.b3[net], self.width)

    def head(self, net, s3):
        return dot(self.w3t[net - A], s3)[:8] + lanes(self.b3a[net - A], self.width)

    def valid(self, count_ref):
        tiles = self.width // 128
        return jnp.concatenate([((self.i * tiles + t) < count_ref[...]).astype(f32) for t in range(tiles)], 1)

    def grads2(self, net, h1, dz2, g2_ref):
        u = UNITS
        right = jnp.concatenate([dz2[:u], dz2[:u], dz2[u : 2 * u]], 1)
        hi, lo = h1[:u], h1[u : 2 * u]
        if net == A:
            g2_ref[net, :u, :] += dot_nt(jnp.concatenate([hi, lo, hi], 1), right)
        else:
            hi = jnp.concatenate([hi, jnp.ones((16, self.width), bf)], 0)
            lo = jnp.concatenate([lo, jnp.zeros((16, self.width), bf)], 0)
            g2_ref[net] += dot_nt(jnp.concatenate([hi, lo, hi], 1), right)

    def grads1(self, net, dz1, g1_ref):
        xhi, xlo = self.x3[:FEAT], self.x3[FEAT : 2 * FEAT]
        left = jnp.concatenate(
            [jnp.concatenate([xhi, xlo], 0), jnp.concatenate([xhi, jnp.zeros_like(xlo)], 0)], 1
        )
        a, b = split(dz1)
        g1_ref[net] += dot_nt(left, jnp.concatenate([a, b], 1))


def critic_block(i, width, x, nz_ref, count_ref, weights, prio_ref, grads):
    g2_ref, g1_ref, g3a_ref, db2_ref, dw3_ref, st_ref = grads
    st = Step(i, width, x, weights)
    x3 = st.x3

    u, s = st.first(AT, x3)
    u, s = st.second(AT, three(s))
    next_action = jnp.tanh(st.head(AT, three(s)) + nz_ref[:, st.lanes])
    xt = st.with_action(next_action)
    u, s = st.first(T0, xt)
    h0 = three(s)
    u, s = st.first(T1, xt)
    h1t = three(s)
    u, s = st.second(T0, h0)
    targets = [st.value(T0, s)]
    u0, s0 = st.first(C0, x3)
    h1, d1 = three(s0), slope(u0, s0)
    u, s = st.second(T1, h1t)
    targets.append(st.value(T1, s))
    u0, s0 = st.second(C0, h1)
    y = x[23:24] + 0.99 * x[24:25] * jnp.minimum(targets[0], targets[1])
    valid = st.valid(count_ref)
    scaled = valid * SCALE
    st_ref[1:2, :] += fold(valid)

    def top(net, s, d2):
        delta = st.value(net, s) - y
        if net == C0:
            prio = valid * jnp.sqrt(delta * delta + 1.0)
            tiles = width // 128
            for t in range(tiles):
                prio_ref[(i * tiles) // 16, pl.ds(lax.rem(i * tiles, 16) + t, 1), :] = prio[:, 128 * t : 128 * (t + 1)]
        st_ref[0:1, :] += fold(valid * (delta * delta))
        dq = (2.0 * scaled) * delta
        st_ref[2 + net : 3 + net, :] += fold(dq)
        dw3_ref[net] += fold(s * dq)
        dz2 = lanes(st.w3[net], width) * (0.5 * dq) * d2
        return three(dz2)

    u, s = st.first(C1, x3)
    h1b, d1b = three(s), slope(u, s)
    dz2 = top(C0, s0, slope(u0, s0))
    dz1 = dot(st.w2b[C0], dz2) * d1
    st.grads2(C0, h1, dz2, g2_ref)
    u, s = st.second(C1, h1b)
    st.grads1(C0, dz1, g1_ref)
    dz2 = top(C1, s, slope(u, s))
    dz1 = dot(st.w2b[C1], dz2) * d1b
    st.grads2(C1, h1b, dz2, g2_ref)
    st.grads1(C1, dz1, g1_ref)


def actor_block(i, width, x, count_ref, weights, grads):
    g2_ref, g1_ref, g3a_ref, db2_ref, dw3_ref, st_ref = grads
    st = Step(i, width, x, weights)

    u, s = st.first(A, st.x3)
    h1a, d1a = three(s), slope(u, s)
    u, s = st.second(A, h1a)
    h2a, d2a = three(s), slope(u, s)
    policy = jnp.tanh(st.head(A, h2a))

    u, s = st.first(C0, st.with_action(policy))
    d1f = slope(u, s)
    u, s = st.second(C0, three(s))
    d2f, q_policy = slope(u, s), st.value(C0, s)
    valid = st.valid(count_ref)
    st_ref[0:1, :] -= fold(valid * q_policy)

    dz2 = three(lanes(st.w3[C0], width) * (-0.5 * SCALE * valid) * d2f)
    dz1 = three(dot(st.w2b[C0], dz2) * d1f)
    da = dot(st.w1a[...], dz1)[:8]
    dp = jnp.where(st.is_action, da * (1.0 - policy * policy), 0.0)
    st_ref[8:16, :] += fold(dp)
    hi = dp.astype(bf).astype(f32)
    lo = dp - hi
    zero = jnp.zeros_like(hi)
    stacked = jnp.concatenate([hi, lo, hi, zero], 0).astype(bf)
    left = jnp.concatenate([jnp.concatenate([hi, lo], 0), jnp.concatenate([hi, zero], 0)], 1).astype(bf)
    dz2 = dot(st.w3b[:, :32], stacked) * d2a
    db2_ref[...] += fold(dz2)
    dz2 = three(dz2)
    dz1 = dot(st.w2b[A], dz2) * d1a
    g3a_ref[...] += dot_nt(left, jnp.concatenate([h2a[:UNITS], h2a[UNITS : 2 * UNITS]], 1))
    st.grads2(A, h1a, dz2, g2_ref)
    st.grads1(A, dz1, g1_ref)


def lane_sums(tile):
    hi, lo = split(tile)
    ones = jnp.ones((16, 128), bf)
    return (dot_nt(ones, hi) + dot_nt(ones, lo))[:8]


def pack_w2(pack_ref, grads):
    for c in range(2):
        for half in range(2):
            s = slice(128 * half, 128 * (half + 1))
            pack_ref[pl.ds(c + 2 * half, UNITS, stride=4), :] = grads[0][c, :UNITS, s]


def pack_rest(pack_ref, grads):
    g2_ref, g1_ref, g3a_ref, db2_ref, dw3_ref, st_ref = grads
    lane = lax.broadcasted_iota(jnp.int32, (1, 128), 1)
    sums = jnp.sum(st_ref[...], 1, keepdims=True)
    for c in range(2):
        g1 = g1_ref[c, :FEAT, :] + g1_ref[c, FEAT:, :]
        b2 = g2_ref[c, UNITS : UNITS + 1, :]
        w3 = lane_sums(dw3_ref[c])[0:1]
        for half in range(2):
            s = slice(128 * half, 128 * (half + 1))
            at = c + 2 * half
            pack_ref[pl.ds(REST + at, OBS + ACT, stride=4), :] = g1[: OBS + ACT, s]
            pack_ref[REST + at + 92 : REST + at + 93, :] = g1[ONE : ONE + 1, s]
            pack_ref[at + 1120 : at + 1121, :] = b2[:, s]
            pack_ref[at + 1124 : at + 1125, :] = w3[:, s]
        pack_ref[c + 1128 : c + 1129, :] = jnp.where(lane == 0, sums[2 + c : 3 + c], 0.0)
    pack_ref[STAT : STAT + 1, :] = jnp.where(lane == 0, sums[0:1], jnp.where(lane == 1, sums[1:2], 0.0))
    pack_ref[STAT + 1 : AT_ACTOR, :] = jnp.zeros((AT_ACTOR - STAT - 1, 128), f32)


def pack_actor(pack_ref, maps, grads):
    g2_ref, g1_ref, g3a_ref, db2_ref, dw3_ref, st_ref = grads
    sums = jnp.sum(st_ref[...], 1, keepdims=True)
    g1 = g1_ref[A, :FEAT, :] + g1_ref[A, FEAT:, :]
    b2 = lane_sums(db2_ref[...])[0:1]
    o = AT_ACTOR
    for half in range(2):
        s = slice(128 * half, 128 * (half + 1))
        pack_ref[pl.ds(o + half, OBS, stride=2), :] = g1[:OBS, s]
        pack_ref[o + 34 + half : o + 35 + half, :] = g1[ONE : ONE + 1, s]
        pack_ref[pl.ds(o + 36 + half, UNITS, stride=2), :] = g2_ref[A, :UNITS, s]
        pack_ref[o + 548 + half : o + 549 + half, :] = b2[:, s]
    pack_ref[o + 550 : o + 562, :] = head_back(g3a_ref[:8, :] + g3a_ref[8:, :], maps)[:12]
    e = lax.broadcasted_iota(jnp.int32, (8, 128), 1) == lax.broadcasted_iota(jnp.int32, (8, 128), 0) - 1
    pack_ref[o + 562 : o + 563, :] = jnp.sum(jnp.where(e, sums[8:16], 0.0), 0, keepdims=True)
    pack_ref[o + ROWS_A : PACK, :] = jnp.zeros((PACK - o - ROWS_A, 128), f32)


WEIGHTS = [
    pltpu.VMEM((6, UNITS, 256), bf),
    pltpu.VMEM((6, UNITS, 3 * UNITS), bf),
    pltpu.VMEM((3, UNITS, 3 * UNITS), bf),
    pltpu.VMEM((6, UNITS, 128), f32),
    pltpu.VMEM((6, UNITS, 128), f32),
    pltpu.VMEM((6, 1, 128), f32),
    pltpu.VMEM((2, 16, 3 * UNITS), bf),
    pltpu.VMEM((UNITS, 128), bf),
    pltpu.VMEM((2, 8, 128), f32),
    pltpu.VMEM((16, 3 * UNITS), bf),
]
GRADS = [
    pltpu.VMEM((3, UNITS + 16, UNITS), f32),
    pltpu.VMEM((3, 2 * FEAT, UNITS), f32),
    pltpu.VMEM((16, UNITS), f32),
    pltpu.VMEM((UNITS, 128), f32),
    pltpu.VMEM((2, UNITS, 128), f32),
    pltpu.VMEM((16, 128), f32),
]


def drain(ref, sem, copies):
    view = ref.at[pl.ds(0, copies)]
    pltpu.make_async_copy(view, view, sem).wait()


class Place:
    def __init__(self):
        group, shard = lax.axis_index("group"), lax.axis_index("shard")
        self.group, self.shard = group, shard
        self.core = lax.rem(shard, 2)
        z, x, y = group // 4, lax.rem(group, 4), shard // 2
        self.chip = group * 4 + y
        self.sibling = (group, shard + 1 - 2 * self.core)
        self.zs, self.xs, self.ys = ([lax.rem(v + n, 4) for n in range(4)] for v in (z, x, y))

    def others(self):
        for dz, dx, dy in STEPS:
            group = self.zs[dz] * 4 + self.xs[dx]
            yield group * 4 + self.ys[dy], (group, self.ys[dy] * 2 + self.core)

    def plane(self):
        for dz, dx, dy in STEPS:
            if not dy:
                group = self.zs[dz] * 4 + self.xs[dx]
                yield group, (group, self.shard)

    def column(self):
        for y in (self.ys[2], self.ys[1], self.ys[3]):
            yield (self.group, y * 2 + self.core)


def remote(src, dst, sems, n, device):
    return pltpu.make_async_remote_copy(
        src_ref=src,
        dst_ref=dst,
        send_sem=sems.at[2 * n],
        recv_sem=sems.at[2 * n + 1],
        device_id=device,
        device_id_type=MESH,
    )


def halves(place, first, rows):
    return tuple(pl.multiple_of(first + core * rows, 8) for core in (place.core, 1 - place.core))


class CriticSum:
    def __init__(self, place, pack_ref, out, buffers, sems):
        self.place, self.pack_ref, self.sems = place, pack_ref, sems
        self.wide = CHIPS * (CHUNK - 1)
        self.pieces = (halves(place, 0, self.wide), halves(place, REST, CHIPS))
        self.other, self.half, self.parts, self.mine, self.whole = buffers
        self.out = out.at[pl.ds(place.core * CHIPS, CHIPS), pl.ds(0, CHUNK)]

    def swap(self, piece):
        at, rows = ((0, self.wide), (self.wide, CHIPS))[piece]
        src = self.pack_ref.at[pl.ds(self.pieces[piece][1], rows)]
        remote(src, self.other.at[pl.ds(at, rows)], self.sems, 0, self.place.sibling).start()

    def scatter(self):
        drain(self.other, self.sems.at[0], CHIPS * CHUNK)
        drain(self.other, self.sems.at[1], CHIPS * CHUNK)
        (wide, _), (more, _) = self.pieces
        total = self.pack_ref[pl.ds(wide, self.wide), :] + self.other[: self.wide, :]
        self.half[:, : CHUNK - 1, :] = total.reshape(CHIPS, CHUNK - 1, 128)
        self.half[:, CHUNK - 1, :] = self.pack_ref[pl.ds(more, CHIPS), :] + self.other[self.wide :, :]
        for peer, device in self.place.others():
            remote(self.half.at[peer], self.parts.at[self.place.chip], self.sems, 1, device).start()

    def spread(self):
        chip = self.place.chip
        drain(self.half, self.sems.at[2], CHIPS - 1)
        drain(self.parts, self.sems.at[3], CHIPS - 1)
        self.parts[pl.ds(chip, 1)] = self.half[pl.ds(chip, 1)]
        self.mine[...] = jnp.sum(self.parts[...], 0)
        for _, device in self.place.others():
            remote(self.mine, self.whole.at[chip], self.sems, 2, device).start()

    def back(self):
        drain(self.parts, self.sems.at[4], CHIPS - 1)
        drain(self.whole, self.sems.at[5], CHIPS - 1)
        self.whole[pl.ds(self.place.chip, 1)] = self.mine[...][None]
        copies = (
            remote(self.whole, self.out, self.sems, 3, self.place.sibling),
            pltpu.make_async_copy(self.whole, self.out, self.sems.at[8]),
        )
        for copy in copies:
            copy.start()
        for copy in copies:
            copy.wait()


class ActorSum:
    def __init__(self, place, pack_ref, buffers, sems):
        self.place, self.pack_ref, self.sems = place, pack_ref, sems
        self.rows = PLANE * CHUNK_A
        self.keep, self.give = halves(place, AT_ACTOR, self.rows)
        self.other, self.half, self.parts, self.columns, self.mine, self.both = buffers
        self.whole = self.both.at[place.core]

    def swap(self):
        return remote(self.pack_ref.at[pl.ds(self.give, self.rows)], self.other, self.sems, 0, self.place.sibling)

    def scatter(self):
        total = self.pack_ref[pl.ds(self.keep, self.rows), :] + self.other[...]
        for j in range(CHUNK_A):
            self.half[:, j, :] = total[PLANE * j : PLANE * (j + 1)]
        for peer, device in self.place.plane():
            remote(self.half.at[peer], self.parts.at[self.place.group], self.sems, 1, device).start()

    def along(self):
        group, y = self.place.group, self.place.ys[0]
        drain(self.half, self.sems.at[2], PLANE - 1)
        drain(self.parts, self.sems.at[3], PLANE - 1)
        self.parts[pl.ds(group, 1)] = self.half[pl.ds(group, 1)]
        self.mine[0] = jnp.sum(self.parts[...], 0)
        self.columns[pl.ds(y, 1)] = self.mine[0:1]
        for device in self.place.column():
            remote(self.mine.at[0], self.columns.at[y], self.sems, 2, device).start()

    def spread(self):
        drain(self.columns, self.sems.at[4], 3)
        drain(self.columns, self.sems.at[5], 3)
        self.mine[1] = jnp.sum(self.columns[...], 0)
        for _, device in self.place.plane():
            remote(self.mine.at[1], self.whole.at[self.place.group], self.sems, 3, device).start()

    def back_copy(self):
        return remote(self.whole, self.whole, self.sems, 4, self.place.sibling)

    def back(self):
        drain(self.parts, self.sems.at[6], PLANE - 1)
        drain(self.whole, self.sems.at[7], PLANE - 1)
        self.whole[pl.ds(self.place.group, 1)] = self.mine[1:2]
        self.back_copy().start()

    def in_order(self, flat_ref):
        for core in range(2):
            for j in range(CHUNK_A):
                flat_ref[core * CHUNK_A + j] = self.both[core, :, j, :]


MAPS = [
    pltpu.VMEM((ACT, UNITS, 16), bf),
    pltpu.VMEM((ACT, 16, UNITS), f32),
    pltpu.VMEM((ACT, UNITS, 128), bf),
]
SUM_BUFFERS = [
    pltpu.VMEM((CHIPS * CHUNK, 128), f32),
    pltpu.VMEM((CHIPS, CHUNK, 128), f32),
    pltpu.VMEM((CHIPS, CHUNK, 128), f32),
    pltpu.VMEM((CHUNK, 128), f32),
    pltpu.VMEM((CHIPS, CHUNK, 128), f32),
    pltpu.VMEM((PLANE * CHUNK_A, 128), f32),
    pltpu.VMEM((PLANE, CHUNK_A, 128), f32),
    pltpu.VMEM((PLANE, CHUNK_A, 128), f32),
    pltpu.VMEM((4, CHUNK_A, 128), f32),
    pltpu.VMEM((2, CHUNK_A, 128), f32),
    pltpu.VMEM((2, PLANE, CHUNK_A, 128), f32),
]
NOISE_BUFFERS = [
    pltpu.VMEM((4, 4, 4, 2, 2, 128), f32),
    pltpu.VMEM((4, 4, 4, 2, 2, 128), f32),
    pltpu.VMEM((4, 4, 4, 2, 2, 128), f32),
    pltpu.VMEM((4, 4, 4, 2, 2, 128), f32),
    pltpu.VMEM((2, 4, 4, 4, 2, 128), f32),
]


def step_kernel(
    width,
    table_hbm,
    index_hbm,
    noise_hbm,
    count_hbm,
    actor_hbm,
    actor_t_hbm,
    critic_hbm,
    critic_t_hbm,
    out_hbm,
    prio_ref,
    order_ref,
    table_ref,
    index_ref,
    noise_ref,
    count_ref,
    actor_ref,
    actor_t_ref,
    critic_ref,
    critic_t_ref,
    in_sems,
    rows_ref,
    picked_ref,
    q_ref,
    turned_ref,
    noise_sems,
    x_ref,
    nz_ref,
    flat_ref,
    pad_ref,
    pack_ref,
    sems,
    *scratch,
):
    weights, grads = scratch[: len(WEIGHTS)], scratch[len(WEIGHTS) : len(WEIGHTS) + len(GRADS)]
    buffers = scratch[len(WEIGHTS) + len(GRADS) : -len(MAPS)]
    maps = scratch[-len(MAPS) :]
    noise = Exchange(place := Place(), buffers[len(SUM_BUFFERS) :], noise_sems)
    w1_ref, w2f_ref, w2b_ref, b2_ref, w3_ref, b3_ref, w3t_ref, w3b_ref, b3a_ref, w1a_ref = weights
    blocks = N // width
    loads = [
        pltpu.make_async_copy(src, dst, in_sems.at[n])
        for n, (src, dst) in enumerate(
            (
                (critic_hbm, critic_ref),
                (actor_hbm, actor_ref),
                (table_hbm, table_ref),
                (index_hbm, index_ref),
                (count_hbm, count_ref),
                (noise_hbm, noise_ref),
                (critic_t_hbm, critic_t_ref),
                (actor_t_hbm, actor_t_ref),
            )
        )
    ]
    for load in loads:
        load.start()

    barrier = pltpu.get_barrier_semaphore()

    for device in [place.sibling] + [device for _, device in place.others()]:
        pl.semaphore_signal(barrier, inc=1, device_id=device, device_id_type=MESH)
    for ref in grads:
        ref[...] = jnp.zeros_like(ref)
    make_maps(*maps)
    loads[0].wait()
    loads[1].wait()
    prepare_critics(
        critic_ref, flat_ref, pad_ref, C0, w1_ref, w2f_ref, w2b_ref, b2_ref, w3_ref, b3_ref, w1a_ref
    )
    prepare_actor(
        A, maps, actor_ref, flat_ref, pad_ref, w1_ref, w2f_ref, w2b_ref, b2_ref, w3t_ref, w3b_ref, b3a_ref
    )
    loads[2].wait()

    def turn(i, carry):
        turn_table(i, table_ref, rows_ref)
        return carry

    lax.fori_loop(0, R_DEV // TURN, turn, 0)
    loads[3].wait()
    pick_rows(0, width, index_ref, rows_ref, picked_ref)
    loads[4].wait()
    loads[5].wait()
    turn_noise(noise_ref, q_ref, noise.buffers[0])

    def actors(i, carry):
        x = turn_rows(width, picked_ref)
        x_ref[:, pl.ds(pl.multiple_of(i * width, width), width)] = x
        actor_block(i, width, x, count_ref, weights, grads)
        pick_rows(lax.rem(i + 1, blocks), width, index_ref, rows_ref, picked_ref)

        @pl.when(i == 0)
        def _():
            loads[6].wait()
            loads[7].wait()
            pl.semaphore_wait(barrier, CHIPS)
            noise.start(0)
            prepare_critics(
                critic_t_ref, flat_ref, pad_ref, T0, w1_ref, w2f_ref, w2b_ref, b2_ref, w3_ref, b3_ref, w1a_ref
            )
            prepare_actor(
                AT, maps, actor_t_ref, flat_ref, pad_ref, w1_ref, w2f_ref, w2b_ref, b2_ref, w3t_ref, w3b_ref, b3a_ref
            )

        for stage in range(1, 4):

            @pl.when(i == stage)
            def _():
                noise.wait(stage - 1)
                noise.start(stage)

        return carry

    lax.fori_loop(0, blocks, actors, 0)
    pack_actor(pack_ref, maps, grads)
    late = CriticSum(place, pack_ref, out_hbm, buffers[:5], sems.at[0])
    early = ActorSum(place, pack_ref, buffers[5 : len(SUM_BUFFERS)], sems.at[1])
    early.swap().start()

    noise.wait(3)
    noise_back(noise.buffers[4], turned_ref, nz_ref)

    def critics(i, carry):
        x = x_ref[:, pl.ds(pl.multiple_of(i * width, width), width)]
        critic_block(i, width, x, nz_ref, count_ref, weights, prio_ref, grads)

        @pl.when(i == 0)
        def _():
            early.swap().wait()
            early.scatter()

        @pl.when(i == 1)
        def _():
            early.along()

        @pl.when(i == 2)
        def _():
            early.spread()

        @pl.when(i == 3)
        def _():
            early.back()

        return carry

    lax.fori_loop(0, blocks, critics, 0)
    pack_w2(pack_ref, grads)
    late.swap(0)
    pack_rest(pack_ref, grads)
    late.swap(1)
    prios = pltpu.make_async_copy(prio_ref, out_hbm.at[pl.ds(AT_PRIO, 2)], in_sems.at[0])
    prios.start()
    late.scatter()
    early.back_copy().wait()
    early.in_order(order_ref)
    order = pltpu.make_async_copy(order_ref, out_hbm.at[pl.ds(AT_SUM, order_ref.shape[0])], in_sems.at[1])
    order.start()
    prios.wait()
    late.spread()
    order.wait()
    late.back()


def update(weight, grad, momentum, average, target):
    momentum_new = 0.9 * momentum + grad
    weight_new = weight - 0.1 * (grad + 0.9 * momentum_new)
    average_new = 0.99 * average + 0.01 * weight_new
    target_new = 0.005 * weight_new + 0.995 * target
    return (weight_new, momentum_new, average_new, target_new, weight_new.astype(bf))


STEP = 1024
CUTS = (0, 24 * STEP, 44 * STEP, 60 * STEP, PC)
LAST = len(CUTS) - 1


def update_kernel(sum_hbm, *refs):
    ins, stat_ref, prio_out, outs_hbm, outs = refs[:8], refs[8], refs[9], refs[10:20], refs[20:30]
    late_ref, early_ref, count_ref, grad_ref, in_sems, out_sems = refs[30:]
    early = pltpu.make_async_copy(sum_hbm.at[pl.ds(AT_SUM, early_ref.shape[0])], early_ref, in_sems.at[0])
    late = pltpu.make_async_copy(sum_hbm.at[pl.ds(0, DEVS), pl.ds(0, CHUNK)], late_ref, in_sems.at[1])
    stat_at = STAT - REST
    count = pltpu.make_async_copy(sum_hbm.at[pl.ds(stat_at, 1), pl.ds(0, CHUNK)], count_ref, in_sems.at[3])
    for load in (count, early, late):
        load.start()
    pass_on = pltpu.make_async_copy(sum_hbm.at[pl.ds(AT_PRIO, 2)], prio_out, in_sems.at[2])
    pass_on.start()

    def stores(piece):
        out = []
        for n in range(5):
            src, dst = outs[2 * n + min(piece, 1)], outs_hbm[2 * n + min(piece, 1)]
            if piece:
                s = pl.ds(CUTS[piece - 1], CUTS[piece] - CUTS[piece - 1])
                src, dst = src.at[:, s], dst.at[:, s]
            out.append(pltpu.make_async_copy(src, dst, out_sems.at[piece, n]))
        return out

    count.wait()
    stat = count_ref[0, CHUNK - 1 : CHUNK, :]
    factor = (1.0 / SCALE) / stat[:, 1:2]
    stat_ref[...] = stat[:, :2].reshape(2)
    early.wait()

    def actor(s, grad):
        values = update(ins[0][s], grad, ins[2][s], ins[4][s], ins[6][s])
        for ref, value in zip(outs[0::2], values):
            ref[s] = value

    for i in range(PA // STEP):
        actor(slice(STEP * i, STEP * (i + 1)), (early_ref[i // 2, 8 * (i % 2) : 8 * (i % 2) + 8, :] * factor).reshape(STEP))
    done = PA // STEP * STEP
    last = early_ref[done // 2048, done // 128 % 16 : done // 128 % 16 + 8, :] * factor
    more = (PA - done) // 128
    actor(slice(done, done + 128 * more), last[:more].reshape(128 * more))
    done += 128 * more
    actor(slice(done, PA), last[more : more + 1, :ACT].reshape(ACT))
    for store in stores(0):
        store.start()

    def critic(s):
        values = update(ins[1][:, s], grad_ref[:, s] * factor, ins[3][:, s], ins[5][:, s], ins[7][:, s])
        for ref, value in zip(outs[1::2], values):
            ref[:, s] = value

    def critics(i, carry):
        critic(pl.ds(pl.multiple_of(i * STEP, STEP), STEP))
        return carry

    late.wait()
    for piece in range(1, LAST + 1):
        for t in range(CUTS[piece - 1] // 128, -(-CUTS[piece] // 128)):
            r = 2 * t
            if W2_ROW <= r < W2_END:
                k, j = divmod(r - W2_ROW, CHUNK - 1)
                pair = late_ref[k, j : j + 2, :]
            else:
                k = r % REST
                pair = late_ref[k : k + 2, CHUNK - 1, :]
            grad_ref[:, 128 * t : 128 * (t + 1)] = pair
        lax.fori_loop(CUTS[piece - 1] // STEP, CUTS[piece] // STEP, critics, 0, unroll=4)
        if piece == LAST:
            done = PC // STEP * STEP
            critic(pl.ds(done, PC - done))
        for store in stores(piece):
            store.start()
    for piece in range(LAST + 1):
        for store in stores(piece):
            store.wait()
    pass_on.wait()


def local(
    replay,
    sample_index,
    pair_count,
    noise,
    actor,
    critic,
    actor_momentum,
    critic_momentum,
    actor_average,
    critic_average,
    actor_target,
    critic_target,
):
    any_ = pl.BlockSpec(memory_space=pl.ANY)
    total = pl.pallas_call(
        functools.partial(step_kernel, WIDTH),
        out_shape=SDS(RESULT, f32),
        in_specs=[any_] * 8,
        out_specs=any_,
        scratch_shapes=[
            pltpu.VMEM((2, 16, DEVS), f32),
            pltpu.VMEM((2 * CHUNK_A, PLANE, 128), f32),
            pltpu.VMEM((ROW, R_DEV), f32),
            pltpu.SMEM((CAP, DEVS), jnp.int32),
            pltpu.VMEM((ACT, CAP, DEVS), f32),
            pltpu.VMEM((1, DEVS), jnp.int32),
            pltpu.VMEM((PA,), f32),
            pltpu.VMEM((PA,), f32),
            pltpu.VMEM((2, PC), f32),
            pltpu.VMEM((2, PC), f32),
            pltpu.SemaphoreType.DMA((8,)),
            pltpu.VMEM((R_DEV, 128), f32),
            pltpu.VMEM((WIDTH // 128, 128, 128), f32),
            pltpu.VMEM((256, 128), f32),
            pltpu.VMEM((DEVS, 256), f32),
            pltpu.SemaphoreType.DMA((8,)),
            pltpu.VMEM((FEAT, N), f32),
            pltpu.VMEM((8, N), f32),
            pltpu.VMEM((2 * TILES_C + 6, 128), f32),
            pltpu.VMEM((FEAT, 256), f32),
            pltpu.VMEM((PACK, 128), f32),
            pltpu.SemaphoreType.DMA((2, 10)),
        ]
        + WEIGHTS
        + GRADS
        + SUM_BUFFERS
        + NOISE_BUFFERS
        + MAPS,
        compiler_params=pltpu.CompilerParams(
            collective_id=0, has_side_effects=True, vmem_limit_bytes=56 << 20
        ),
        name="td3_step",
    )(
        replay.T,
        sample_index[0].T,
        jnp.transpose(noise[0], (2, 1, 0)),
        pair_count,
        actor,
        actor_target,
        critic,
        critic_target,
    )
    shapes = [SDS((2,), f32), SDS((2, CAP // 2, DEVS), f32)]
    places = [SDS((PA,), f32), SDS((2, PC), f32)] * 4 + [SDS((PA,), bf), SDS((2, PC), bf)]
    stat, prio, *outs = pl.pallas_call(
        update_kernel,
        out_shape=tuple(shapes + places),
        in_specs=[any_] + [VM] * 8,
        out_specs=(VM,) + (any_,) * 11,
        scratch_shapes=[pltpu.VMEM(p.shape, p.dtype) for p in places]
        + [
            pltpu.VMEM((DEVS, CHUNK, 128), f32),
            pltpu.VMEM((2 * CHUNK_A, PLANE, 128), f32),
            pltpu.VMEM((1, CHUNK, 128), f32),
            pltpu.VMEM((2, TILES_C * 128), f32),
            pltpu.SemaphoreType.DMA((4,)),
            pltpu.SemaphoreType.DMA((LAST + 1, 5)),
        ],
        compiler_params=pltpu.CompilerParams(vmem_limit_bytes=24 << 20),
        name="update",
    )(
        total,
        actor,
        critic,
        actor_momentum,
        critic_momentum,
        actor_average,
        critic_average,
        actor_target,
        critic_target,
    )
    return (stat, prio.reshape(CAP, DEVS).T[None], *outs)


def solution(mesh):
    rows = ("group", "shard")
    in_specs = (P(rows, None), P(rows, None, None), P(rows, None), P(rows, None, None, None)) + (P(),) * 8
    out_specs = (P(), P(rows, None, None)) + (P(),) * 10
    return jax.shard_map(local, mesh=mesh, in_specs=in_specs, out_specs=out_specs, check_vma=False)
```

```python
import functools

import jax
import jax.numpy as jnp
from jax import lax
from jax.experimental import pallas as pl
from jax.experimental.pallas import tpu as pltpu
from jax.sharding import PartitionSpec as P

OBS = 17
ACT = 6
UNITS = 256
CAP = 32
DEVS = 128
R_DEV = 8192
ROW = 42
PA = 71942
PC = 72193
N = DEVS * CAP

bf = jnp.bfloat16
f32 = jnp.float32
MESH = pl.DeviceIdType.MESH
VM = pl.BlockSpec(memory_space=pltpu.VMEM)
SDS = jax.ShapeDtypeStruct

SCALE = 2.0**-19
C0, C1, A, AT, T0, T1 = range(6)
FEAT = 48
ONE = 42
NEXT = 25

TILES_C = 565
W2_ROW, W2_END = 96, 1120
REST = 1024
STAT = 1130
ROWS_A = 563
CHIPS = DEVS // 2
PLANE = 16
CHUNK = 9
CHUNK_A = 20
AT_ACTOR = 2 * CHIPS * CHUNK
PACK = AT_ACTOR + 2 * PLANE * CHUNK_A
AT_PRIO = DEVS
AT_SUM = DEVS + 2
RESULT = (3700, 16, 128)
TURN = 512
WIDTH = 1024
STEPS = sorted(
    ((z, x, y) for z in range(4) for x in range(4) for y in range(4)),
    key=lambda step: -sum(min(n, 4 - n) for n in step),
)[:-1]


def dot(a, b):
    return lax.dot_general(a, b, (((1,), (0,)), ((), ())), preferred_element_type=f32)


def dot_nt(a, b):
    return lax.dot_general(a, b, (((1,), (1,)), ((), ())), preferred_element_type=f32)


def split(v):
    hi = v.astype(bf)
    return hi, (v - hi.astype(f32)).astype(bf)


def three(v):
    hi, lo = split(v)
    return jnp.concatenate([hi, lo, hi], 0)


def lanes(tile, width):
    return jnp.concatenate([tile] * (width // 128), 1)


def fold(v):
    out = v[:, :128]
    for i in range(1, v.shape[1] // 128):
        out = out + v[:, 128 * i : 128 * (i + 1)]
    return out


def column(row):
    return jnp.transpose(jnp.broadcast_to(row, (128, 128)))


def turn_noise(noise_ref, q_ref, nsend):
    q_ref[...] = jnp.zeros_like(q_ref)
    for j in range(ACT):
        q_ref[pl.ds(j + 1, CAP, stride=8), :] = 0.5 * jnp.tanh(0.4 * noise_ref[j])
    turned = jnp.transpose(q_ref[...])
    nsend[:, :, :, :, 0, :] = turned[:, :128].reshape(4, 4, 4, 2, 128)
    nsend[:, :, :, :, 1, :] = turned[:, 128:].reshape(4, 4, 4, 2, 128)


def noise_back(nrecv, turned_ref, nz_ref):
    for d in range(DEVS):
        core, y, x, z = d % 2, d // 2 % 4, d // 8 % 4, d // 32
        for half in range(2):
            turned_ref[d : d + 1, 128 * half : 128 * (half + 1)] = nrecv[core, y, x, z, half : half + 1, :]
    back = jnp.transpose(turned_ref[...])
    for c in range(CAP):
        nz_ref[:, 128 * c : 128 * (c + 1)] = back[8 * c : 8 * (c + 1), :]


class Exchange:
    def __init__(self, place, buffers, sems):
        self.place, self.sems = place, sems
        self.buffers = buffers

    def slab(self, stage, n):
        p, (send, by_z, by_x, by_y, by_core) = self.place, self.buffers
        if stage == 0:
            return send.at[p.zs[n]], by_z.at[p.zs[0]], (p.zs[n] * 4 + p.xs[0], p.shard)
        if stage == 1:
            return by_z.at[:, p.xs[n]], by_x.at[p.xs[0]], (p.zs[0] * 4 + p.xs[n], p.shard)
        if stage == 2:
            return by_x.at[:, :, p.ys[n]], by_y.at[p.ys[0]], (p.group, p.ys[n] * 2 + p.core)
        return by_y.at[:, :, :, (1 - p.core) if n else p.core], by_core.at[p.core], p.sibling

    def start(self, stage):
        for n in range(1, 2 if stage == 3 else 4):
            src, dst, device = self.slab(stage, n)
            pltpu.make_async_remote_copy(
                src_ref=src,
                dst_ref=dst,
                send_sem=self.sems.at[2 * stage],
                recv_sem=self.sems.at[2 * stage + 1],
                device_id=device,
                device_id_type=MESH,
            ).start()
        src, dst, _ = self.slab(stage, 0)
        dst[...] = src[...]

    def wait(self, stage):
        if stage == 3:
            view = self.buffers[4].at[0]
        else:
            view = self.buffers[stage + 1].at[pl.ds(0, 3)]
        for n in range(2):
            pltpu.make_async_copy(view, view, self.sems.at[2 * stage + n]).wait()


def turn_table(i, table_ref, rows_ref):
    s = pl.ds(pl.multiple_of(i * TURN, TURN), TURN)
    v = jnp.concatenate([table_ref[:, s], jnp.zeros((FEAT - ROW, TURN), f32)], 0)
    rows_ref[s, :FEAT] = jnp.transpose(v)


def pick_rows(block, width, index_ref, rows_ref, picked_ref):
    tiles = width // 128
    for t in range(tiles):
        for d in range(DEVS):
            picked_ref[t, d : d + 1, :] = rows_ref[pl.ds(index_ref[block * tiles + t, d], 1), :]


def turn_rows(width, picked_ref):
    parts = [jnp.transpose(picked_ref[t, :, :FEAT]) for t in range(width // 128)]
    x = jnp.concatenate(parts, 1)
    ones = lax.broadcasted_iota(jnp.int32, (8, width), 0) == (ONE - 40)
    return jnp.concatenate([x[:40], jnp.where(ones, 1.0, x[40:])], 0)


def put_square(net, w2, w2f_ref, w2b_ref):
    w2 = 0.5 * w2
    turned = jnp.transpose(w2)
    hi, lo = split(turned)
    w2f_ref[net] = jnp.concatenate([hi, hi, lo], 1)
    if net in (C0, C1, A):
        hi, lo = split(w2)
        w2b_ref[net] = jnp.concatenate([hi, hi, lo], 1)


def put_first(net, pad_ref, w1_ref):
    w1 = 0.5 * pad_ref[...]
    hi = w1.astype(bf).astype(f32)
    lo = w1 - hi
    stacked = jnp.concatenate([hi, hi, lo, jnp.zeros((256 - 3 * FEAT, 256), f32)], 0)
    w1_ref[net] = jnp.transpose(stacked).astype(bf)


def put_column(ref, net, left, right, factor):
    ref[net] = jnp.concatenate([column(left * factor), column(right * factor)], 0)


def prepare_critics(critic_ref, rows_ref, pad_ref, first, w1_ref, w2f_ref, w2b_ref, b2_ref, w3_ref, b3_ref, w1a_ref):
    for t in range(TILES_C - 1):
        rows_ref[2 * t : 2 * t + 2, :] = critic_ref[:, 128 * t : 128 * (t + 1)]
    for c in range(2):
        net = first + c
        start = NEXT if first == T0 else 0
        pad_ref[...] = jnp.zeros_like(pad_ref)
        for half in range(2):
            s = pl.ds(128 * half, 128)
            pad_ref[pl.ds(start, OBS), s] = rows_ref[pl.ds(c + 2 * half, OBS, stride=4), :]
            pad_ref[pl.ds(OBS, ACT), s] = rows_ref[pl.ds(c + 2 * half + 4 * OBS, ACT, stride=4), :]
            pad_ref[pl.ds(ONE, 1), s] = rows_ref[pl.ds(92 + c + 2 * half, 1), :]
        put_first(net, pad_ref, w1_ref)
        if net == C0:
            hi = pad_ref[16:24, :].astype(bf).astype(f32)
            lo = pad_ref[16:24, :] - hi
            block = jnp.concatenate([hi, hi, lo], 1)
            w1a_ref[...] = jnp.concatenate([block, jnp.zeros_like(block)], 0).astype(bf)
        w2 = jnp.concatenate(
            [rows_ref[pl.ds(96 + c, UNITS, stride=4), :], rows_ref[pl.ds(98 + c, UNITS, stride=4), :]], 1
        )
        put_square(net, w2, w2f_ref, w2b_ref)
        put_column(b2_ref, net, rows_ref[1120 + c : 1121 + c, :], rows_ref[1122 + c : 1123 + c, :], 0.5)
        put_column(w3_ref, net, rows_ref[1124 + c : 1125 + c, :], rows_ref[1126 + c : 1127 + c, :], 1.0)
        b3_ref[net] = jnp.broadcast_to(critic_ref[c : c + 1, PC - 1 : PC], (1, 128))


def make_maps(row_ref, turned_ref, lane_ref):
    def entry(shape, axis, j):
        return lax.broadcasted_iota(jnp.int32, shape, axis) * ACT + j

    for j in range(ACT):
        r = lax.broadcasted_iota(jnp.int32, (UNITS, 16), 1)
        row_ref[j] = ((entry((UNITS, 16), 0, j) >> 7) == r).astype(f32).astype(bf)
        r = lax.broadcasted_iota(jnp.int32, (16, UNITS), 0)
        turned_ref[j] = ((entry((16, UNITS), 1, j) >> 7) == r).astype(f32)
        l = lax.broadcasted_iota(jnp.int32, (UNITS, 128), 1)
        lane_ref[j] = ((entry((UNITS, 128), 0, j) & 127) == l).astype(f32).astype(bf)


def head_of(flat, maps):
    row_ref, _, lane_ref = maps
    hi = flat.astype(bf).astype(f32)
    r = lax.broadcasted_iota(jnp.int32, (16, 128 * ACT), 0)
    l = lax.broadcasted_iota(jnp.int32, (16, 128 * ACT), 1)
    take = ((l >> 7) == (r - 1)).astype(f32).astype(bf)
    out = []
    for part in (hi, flat - hi):
        part = part.astype(bf)
        spread = [dot(row_ref[j], part).astype(bf) * lane_ref[j] for j in range(ACT)]
        out.append(dot_nt(take, jnp.concatenate(spread, 1))[:8])
    return out


def head_back(turned, maps):
    _, turned_ref, lane_ref = maps
    out = jnp.zeros((16, 128), f32)
    for j in range(ACT):
        hi, lo = split(turned_ref[j] * turned[j + 1 : j + 2, :])
        out = out + dot(hi, lane_ref[j]) + dot(lo, lane_ref[j])
    return out


def prepare_actor(net, maps, actor_ref, rows_ref, pad_ref, w1_ref, w2f_ref, w2b_ref, b2_ref, w3t_ref, w3b_ref, b3a_ref):
    whole = PA // 1024
    for t in range(whole):
        rows_ref[8 * t : 8 * t + 8, :] = actor_ref[pl.ds(1024 * t, 1024)].reshape(8, 128)
    rest = (PA - 1024 * whole) // 128
    rows_ref[8 * whole : 8 * whole + rest, :] = actor_ref[pl.ds(1024 * whole, 128 * rest)].reshape(rest, 128)
    rows_ref[562:563, 0:ACT] = actor_ref[pl.ds(562 * 128, ACT)].reshape(1, ACT)
    start = NEXT if net == AT else 0
    pad_ref[...] = jnp.zeros_like(pad_ref)
    for half in range(2):
        s = pl.ds(128 * half, 128)
        pad_ref[pl.ds(start, OBS), s] = rows_ref[pl.ds(half, OBS, stride=2), :]
        pad_ref[pl.ds(ONE, 1), s] = rows_ref[pl.ds(34 + half, 1), :]
    put_first(net, pad_ref, w1_ref)
    w2 = jnp.concatenate([rows_ref[pl.ds(36, UNITS, stride=2), :], rows_ref[pl.ds(37, UNITS, stride=2), :]], 1)
    put_square(net, w2, w2f_ref, w2b_ref)
    put_column(b2_ref, net, rows_ref[548:549, :], rows_ref[549:550, :], 0.5)
    flat = jnp.concatenate([rows_ref[550:562, :], jnp.zeros((4, 128), f32)], 0)
    hi, lo = head_of(flat, maps)
    block = jnp.concatenate([hi, hi, lo], 1)
    w3t_ref[net - A] = jnp.concatenate([block, jnp.zeros_like(block)], 0).astype(bf)
    if net == A:
        stacked = jnp.concatenate([hi, hi, lo, jnp.zeros((104, UNITS), f32)], 0)
        w3b_ref[...] = (0.5 * jnp.transpose(stacked)).astype(bf)
    bias = column(rows_ref[562:563, :])
    b3a_ref[net - A] = jnp.zeros((8, 128), f32)
    b3a_ref[net - A, 1 : 1 + ACT, :] = bias[:ACT]


def act(zh):
    u = jnp.tanh(zh) + 1.0
    return u, zh * u


def slope(u, s):
    return u + s * (2.0 - u)


class Step:
    def __init__(self, i, width, x, weights):
        (
            self.w1, self.w2f, self.w2b, self.b2, self.w3, self.b3, self.w3t, self.w3b, self.b3a, self.w1a,
        ) = weights
        self.i, self.width = i, width
        self.lanes = pl.ds(pl.multiple_of(i * width, width), width)
        self.x = x
        self.x3 = three(self.x)
        rows8 = lax.broadcasted_iota(jnp.int32, (8, width), 0)
        self.is_action = (rows8 >= 1) & (rows8 <= ACT)

    def with_action(self, a):
        x = self.x
        return three(jnp.concatenate([x[:16], jnp.where(self.is_action, a, x[16:24]), x[24:]], 0))

    def first(self, net, xx):
        return act(dot(self.w1[net, :, : 3 * FEAT], xx))

    def second(self, net, h3):
        return act(dot(self.w2f[net], h3) + lanes(self.b2[net], self.width))

    def value(self, net, s):
        return jnp.sum(s * lanes(self.w3[net], self.width), 0, keepdims=True) + lanes(self.b3[net], self.width)

    def head(self, net, s3):
        return dot(self.w3t[net - A], s3)[:8] + lanes(self.b3a[net - A], self.width)

    def valid(self, count_ref):
        tiles = self.width // 128
        return jnp.concatenate([((self.i * tiles + t) < count_ref[...]).astype(f32) for t in range(tiles)], 1)

    def grads2(self, net, h1, dz2, g2_ref):
        u = UNITS
        right = jnp.concatenate([dz2[:u], dz2[:u], dz2[u : 2 * u]], 1)
        hi, lo = h1[:u], h1[u : 2 * u]
        if net == A:
            g2_ref[net, :u, :] += dot_nt(jnp.concatenate([hi, lo, hi], 1), right)
        else:
            hi = jnp.concatenate([hi, jnp.ones((16, self.width), bf)], 0)
            lo = jnp.concatenate([lo, jnp.zeros((16, self.width), bf)], 0)
            g2_ref[net] += dot_nt(jnp.concatenate([hi, lo, hi], 1), right)

    def grads1(self, net, dz1, g1_ref):
        xhi, xlo = self.x3[:FEAT], self.x3[FEAT : 2 * FEAT]
        left = jnp.concatenate(
            [jnp.concatenate([xhi, xlo], 0), jnp.concatenate([xhi, jnp.zeros_like(xlo)], 0)], 1
        )
        a, b = split(dz1)
        g1_ref[net] += dot_nt(left, jnp.concatenate([a, b], 1))


def critic_block(i, width, x, nz_ref, count_ref, weights, prio_ref, grads):
    g2_ref, g1_ref, g3a_ref, db2_ref, dw3_ref, st_ref = grads
    st = Step(i, width, x, weights)
    x3 = st.x3

    u, s = st.first(AT, x3)
    u, s = st.second(AT, three(s))
    next_action = jnp.tanh(st.head(AT, three(s)) + nz_ref[:, st.lanes])
    xt = st.with_action(next_action)
    u, s = st.first(T0, xt)
    h0 = three(s)
    u, s = st.first(T1, xt)
    h1t = three(s)
    u, s = st.second(T0, h0)
    targets = [st.value(T0, s)]
    u0, s0 = st.first(C0, x3)
    h1, d1 = three(s0), slope(u0, s0)
    u, s = st.second(T1, h1t)
    targets.append(st.value(T1, s))
    u0, s0 = st.second(C0, h1)
    y = x[23:24] + 0.99 * x[24:25] * jnp.minimum(targets[0], targets[1])
    valid = st.valid(count_ref)
    scaled = valid * SCALE
    st_ref[1:2, :] += fold(valid)

    def top(net, s, d2):
        delta = st.value(net, s) - y
        if net == C0:
            prio = valid * jnp.sqrt(delta * delta + 1.0)
            tiles = width // 128
            for t in range(tiles):
                prio_ref[(i * tiles) // 16, pl.ds(lax.rem(i * tiles, 16) + t, 1), :] = prio[:, 128 * t : 128 * (t + 1)]
        st_ref[0:1, :] += fold(valid * (delta * delta))
        dq = (2.0 * scaled) * delta
        st_ref[2 + net : 3 + net, :] += fold(dq)
        dw3_ref[net] += fold(s * dq)
        dz2 = lanes(st.w3[net], width) * (0.5 * dq) * d2
        return three(dz2)

    u, s = st.first(C1, x3)
    h1b, d1b = three(s), slope(u, s)
    dz2 = top(C0, s0, slope(u0, s0))
    dz1 = dot(st.w2b[C0], dz2) * d1
    st.grads2(C0, h1, dz2, g2_ref)
    u, s = st.second(C1, h1b)
    st.grads1(C0, dz1, g1_ref)
    dz2 = top(C1, s, slope(u, s))
    dz1 = dot(st.w2b[C1], dz2) * d1b
    st.grads2(C1, h1b, dz2, g2_ref)
    st.grads1(C1, dz1, g1_ref)


def actor_block(i, width, x, count_ref, weights, grads):
    g2_ref, g1_ref, g3a_ref, db2_ref, dw3_ref, st_ref = grads
    st = Step(i, width, x, weights)

    u, s = st.first(A, st.x3)
    h1a, d1a = three(s), slope(u, s)
    u, s = st.second(A, h1a)
    h2a, d2a = three(s), slope(u, s)
    policy = jnp.tanh(st.head(A, h2a))

    u, s = st.first(C0, st.with_action(policy))
    d1f = slope(u, s)
    u, s = st.second(C0, three(s))
    d2f, q_policy = slope(u, s), st.value(C0, s)
    valid = st.valid(count_ref)
    st_ref[0:1, :] -= fold(valid * q_policy)

    dz2 = three(lanes(st.w3[C0], width) * (-0.5 * SCALE * valid) * d2f)
    dz1 = three(dot(st.w2b[C0], dz2) * d1f)
    da = dot(st.w1a[...], dz1)[:8]
    dp = jnp.where(st.is_action, da * (1.0 - policy * policy), 0.0)
    st_ref[8:16, :] += fold(dp)
    hi = dp.astype(bf).astype(f32)
    lo = dp - hi
    zero = jnp.zeros_like(hi)
    stacked = jnp.concatenate([hi, lo, hi, zero], 0).astype(bf)
    left = jnp.concatenate([jnp.concatenate([hi, lo], 0), jnp.concatenate([hi, zero], 0)], 1).astype(bf)
    dz2 = dot(st.w3b[:, :32], stacked) * d2a
    db2_ref[...] += fold(dz2)
    dz2 = three(dz2)
    dz1 = dot(st.w2b[A], dz2) * d1a
    g3a_ref[...] += dot_nt(left, jnp.concatenate([h2a[:UNITS], h2a[UNITS : 2 * UNITS]], 1))
    st.grads2(A, h1a, dz2, g2_ref)
    st.grads1(A, dz1, g1_ref)


def lane_sums(tile):
    hi, lo = split(tile)
    ones = jnp.ones((16, 128), bf)
    return (dot_nt(ones, hi) + dot_nt(ones, lo))[:8]


def pack_w2(pack_ref, grads):
    for c in range(2):
        for half in range(2):
            s = slice(128 * half, 128 * (half + 1))
            pack_ref[pl.ds(c + 2 * half, UNITS, stride=4), :] = grads[0][c, :UNITS, s]


def pack_rest(pack_ref, grads):
    g2_ref, g1_ref, g3a_ref, db2_ref, dw3_ref, st_ref = grads
    lane = lax.broadcasted_iota(jnp.int32, (1, 128), 1)
    sums = jnp.sum(st_ref[...], 1, keepdims=True)
    for c in range(2):
        g1 = g1_ref[c, :FEAT, :] + g1_ref[c, FEAT:, :]
        b2 = g2_ref[c, UNITS : UNITS + 1, :]
        w3 = lane_sums(dw3_ref[c])[0:1]
        for half in range(2):
            s = slice(128 * half, 128 * (half + 1))
            at = c + 2 * half
            pack_ref[pl.ds(REST + at, OBS + ACT, stride=4), :] = g1[: OBS + ACT, s]
            pack_ref[REST + at + 92 : REST + at + 93, :] = g1[ONE : ONE + 1, s]
            pack_ref[at + 1120 : at + 1121, :] = b2[:, s]
            pack_ref[at + 1124 : at + 1125, :] = w3[:, s]
        pack_ref[c + 1128 : c + 1129, :] = jnp.where(lane == 0, sums[2 + c : 3 + c], 0.0)
    pack_ref[STAT : STAT + 1, :] = jnp.where(lane == 0, sums[0:1], jnp.where(lane == 1, sums[1:2], 0.0))
    pack_ref[STAT + 1 : AT_ACTOR, :] = jnp.zeros((AT_ACTOR - STAT - 1, 128), f32)


def pack_actor(pack_ref, maps, grads):
    g2_ref, g1_ref, g3a_ref, db2_ref, dw3_ref, st_ref = grads
    sums = jnp.sum(st_ref[...], 1, keepdims=True)
    g1 = g1_ref[A, :FEAT, :] + g1_ref[A, FEAT:, :]
    b2 = lane_sums(db2_ref[...])[0:1]
    o = AT_ACTOR
    for half in range(2):
        s = slice(128 * half, 128 * (half + 1))
        pack_ref[pl.ds(o + half, OBS, stride=2), :] = g1[:OBS, s]
        pack_ref[o + 34 + half : o + 35 + half, :] = g1[ONE : ONE + 1, s]
        pack_ref[pl.ds(o + 36 + half, UNITS, stride=2), :] = g2_ref[A, :UNITS, s]
        pack_ref[o + 548 + half : o + 549 + half, :] = b2[:, s]
    pack_ref[o + 550 : o + 562, :] = head_back(g3a_ref[:8, :] + g3a_ref[8:, :], maps)[:12]
    e = lax.broadcasted_iota(jnp.int32, (8, 128), 1) == lax.broadcasted_iota(jnp.int32, (8, 128), 0) - 1
    pack_ref[o + 562 : o + 563, :] = jnp.sum(jnp.where(e, sums[8:16], 0.0), 0, keepdims=True)
    pack_ref[o + ROWS_A : PACK, :] = jnp.zeros((PACK - o - ROWS_A, 128), f32)


WEIGHTS = [
    pltpu.VMEM((6, UNITS, 256), bf),
    pltpu.VMEM((6, UNITS, 3 * UNITS), bf),
    pltpu.VMEM((3, UNITS, 3 * UNITS), bf),
    pltpu.VMEM((6, UNITS, 128), f32),
    pltpu.VMEM((6, UNITS, 128), f32),
    pltpu.VMEM((6, 1, 128), f32),
    pltpu.VMEM((2, 16, 3 * UNITS), bf),
    pltpu.VMEM((UNITS, 128), bf),
    pltpu.VMEM((2, 8, 128), f32),
    pltpu.VMEM((16, 3 * UNITS), bf),
]
GRADS = [
    pltpu.VMEM((3, UNITS + 16, UNITS), f32),
    pltpu.VMEM((3, 2 * FEAT, UNITS), f32),
    pltpu.VMEM((16, UNITS), f32),
    pltpu.VMEM((UNITS, 128), f32),
    pltpu.VMEM((2, UNITS, 128), f32),
    pltpu.VMEM((16, 128), f32),
]


def drain(ref, sem, copies):
    view = ref.at[pl.ds(0, copies)]
    pltpu.make_async_copy(view, view, sem).wait()


class Place:
    def __init__(self):
        group, shard = lax.axis_index("group"), lax.axis_index("shard")
        self.group, self.shard = group, shard
        self.core = lax.rem(shard, 2)
        z, x, y = group // 4, lax.rem(group, 4), shard // 2
        self.chip = group * 4 + y
        self.sibling = (group, shard + 1 - 2 * self.core)
        self.zs, self.xs, self.ys = ([lax.rem(v + n, 4) for n in range(4)] for v in (z, x, y))

    def others(self):
        for dz, dx, dy in STEPS:
            group = self.zs[dz] * 4 + self.xs[dx]
            yield group * 4 + self.ys[dy], (group, self.ys[dy] * 2 + self.core)

    def plane(self):
        for dz, dx, dy in STEPS:
            if not dy:
                group = self.zs[dz] * 4 + self.xs[dx]
                yield group, (group, self.shard)

    def column(self):
        for y in (self.ys[2], self.ys[1], self.ys[3]):
            yield (self.group, y * 2 + self.core)


def remote(src, dst, sems, n, device):
    return pltpu.make_async_remote_copy(
        src_ref=src,
        dst_ref=dst,
        send_sem=sems.at[2 * n],
        recv_sem=sems.at[2 * n + 1],
        device_id=device,
        device_id_type=MESH,
    )


def halves(place, first, rows):
    return tuple(pl.multiple_of(first + core * rows, 8) for core in (place.core, 1 - place.core))


class CriticSum:
    def __init__(self, place, pack_ref, out, buffers, sems):
        self.place, self.pack_ref, self.sems = place, pack_ref, sems
        self.wide = CHIPS * (CHUNK - 1)
        self.pieces = (halves(place, 0, self.wide), halves(place, REST, CHIPS))
        self.other, self.half, self.parts, self.mine, self.whole = buffers
        self.out = out.at[pl.ds(place.core * CHIPS, CHIPS), pl.ds(0, CHUNK)]

    def swap(self, piece):
        at, rows = ((0, self.wide), (self.wide, CHIPS))[piece]
        src = self.pack_ref.at[pl.ds(self.pieces[piece][1], rows)]
        remote(src, self.other.at[pl.ds(at, rows)], self.sems, 0, self.place.sibling).start()

    def scatter(self):
        drain(self.other, self.sems.at[0], CHIPS * CHUNK)
        drain(self.other, self.sems.at[1], CHIPS * CHUNK)
        (wide, _), (more, _) = self.pieces
        total = self.pack_ref[pl.ds(wide, self.wide), :] + self.other[: self.wide, :]
        self.half[:, : CHUNK - 1, :] = total.reshape(CHIPS, CHUNK - 1, 128)
        self.half[:, CHUNK - 1, :] = self.pack_ref[pl.ds(more, CHIPS), :] + self.other[self.wide :, :]
        for peer, device in self.place.others():
            remote(self.half.at[peer], self.parts.at[self.place.chip], self.sems, 1, device).start()

    def spread(self):
        chip = self.place.chip
        drain(self.half, self.sems.at[2], CHIPS - 1)
        drain(self.parts, self.sems.at[3], CHIPS - 1)
        self.parts[pl.ds(chip, 1)] = self.half[pl.ds(chip, 1)]
        self.mine[...] = jnp.sum(self.parts[...], 0)
        for _, device in self.place.others():
            remote(self.mine, self.whole.at[chip], self.sems, 2, device).start()

    def back(self):
        drain(self.parts, self.sems.at[4], CHIPS - 1)
        drain(self.whole, self.sems.at[5], CHIPS - 1)
        self.whole[pl.ds(self.place.chip, 1)] = self.mine[...][None]
        copies = (
            remote(self.whole, self.out, self.sems, 3, self.place.sibling),
            pltpu.make_async_copy(self.whole, self.out, self.sems.at[8]),
        )
        for copy in copies:
            copy.start()
        for copy in copies:
            copy.wait()


class ActorSum:
    def __init__(self, place, pack_ref, buffers, sems):
        self.place, self.pack_ref, self.sems = place, pack_ref, sems
        self.rows = PLANE * CHUNK_A
        self.keep, self.give = halves(place, AT_ACTOR, self.rows)
        self.other, self.half, self.parts, self.columns, self.mine, self.both = buffers
        self.whole = self.both.at[place.core]

    def swap(self):
        return remote(self.pack_ref.at[pl.ds(self.give, self.rows)], self.other, self.sems, 0, self.place.sibling)

    def scatter(self):
        total = self.pack_ref[pl.ds(self.keep, self.rows), :] + self.other[...]
        for j in range(CHUNK_A):
            self.half[:, j, :] = total[PLANE * j : PLANE * (j + 1)]
        for peer, device in self.place.plane():
            remote(self.half.at[peer], self.parts.at[self.place.group], self.sems, 1, device).start()

    def along(self):
        group, y = self.place.group, self.place.ys[0]
        drain(self.half, self.sems.at[2], PLANE - 1)
        drain(self.parts, self.sems.at[3], PLANE - 1)
        self.parts[pl.ds(group, 1)] = self.half[pl.ds(group, 1)]
        self.mine[0] = jnp.sum(self.parts[...], 0)
        self.columns[pl.ds(y, 1)] = self.mine[0:1]
        for device in self.place.column():
            remote(self.mine.at[0], self.columns.at[y], self.sems, 2, device).start()

    def spread(self):
        drain(self.columns, self.sems.at[4], 3)
        drain(self.columns, self.sems.at[5], 3)
        self.mine[1] = jnp.sum(self.columns[...], 0)
        for _, device in self.place.plane():
            remote(self.mine.at[1], self.whole.at[self.place.group], self.sems, 3, device).start()

    def back_copy(self):
        return remote(self.whole, self.whole, self.sems, 4, self.place.sibling)

    def back(self):
        drain(self.parts, self.sems.at[6], PLANE - 1)
        drain(self.whole, self.sems.at[7], PLANE - 1)
        self.whole[pl.ds(self.place.group, 1)] = self.mine[1:2]
        self.back_copy().start()

    def in_order(self, flat_ref):
        for core in range(2):
            for j in range(CHUNK_A):
                flat_ref[core * CHUNK_A + j] = self.both[core, :, j, :]


MAPS = [
    pltpu.VMEM((ACT, UNITS, 16), bf),
    pltpu.VMEM((ACT, 16, UNITS), f32),
    pltpu.VMEM((ACT, UNITS, 128), bf),
]
SUM_BUFFERS = [
    pltpu.VMEM((CHIPS * CHUNK, 128), f32),
    pltpu.VMEM((CHIPS, CHUNK, 128), f32),
    pltpu.VMEM((CHIPS, CHUNK, 128), f32),
    pltpu.VMEM((CHUNK, 128), f32),
    pltpu.VMEM((CHIPS, CHUNK, 128), f32),
    pltpu.VMEM((PLANE * CHUNK_A, 128), f32),
    pltpu.VMEM((PLANE, CHUNK_A, 128), f32),
    pltpu.VMEM((PLANE, CHUNK_A, 128), f32),
    pltpu.VMEM((4, CHUNK_A, 128), f32),
    pltpu.VMEM((2, CHUNK_A, 128), f32),
    pltpu.VMEM((2, PLANE, CHUNK_A, 128), f32),
]
NOISE_BUFFERS = [
    pltpu.VMEM((4, 4, 4, 2, 2, 128), f32),
    pltpu.VMEM((4, 4, 4, 2, 2, 128), f32),
    pltpu.VMEM((4, 4, 4, 2, 2, 128), f32),
    pltpu.VMEM((4, 4, 4, 2, 2, 128), f32),
    pltpu.VMEM((2, 4, 4, 4, 2, 128), f32),
]


def step_kernel(
    width,
    table_hbm,
    index_hbm,
    noise_hbm,
    count_hbm,
    actor_hbm,
    actor_t_hbm,
    critic_hbm,
    critic_t_hbm,
    out_hbm,
    prio_ref,
    order_ref,
    table_ref,
    index_ref,
    noise_ref,
    count_ref,
    actor_ref,
    actor_t_ref,
    critic_ref,
    critic_t_ref,
    in_sems,
    rows_ref,
    picked_ref,
    q_ref,
    turned_ref,
    noise_sems,
    x_ref,
    nz_ref,
    flat_ref,
    pad_ref,
    pack_ref,
    sems,
    *scratch,
):
    weights, grads = scratch[: len(WEIGHTS)], scratch[len(WEIGHTS) : len(WEIGHTS) + len(GRADS)]
    buffers = scratch[len(WEIGHTS) + len(GRADS) : -len(MAPS)]
    maps = scratch[-len(MAPS) :]
    noise = Exchange(place := Place(), buffers[len(SUM_BUFFERS) :], noise_sems)
    w1_ref, w2f_ref, w2b_ref, b2_ref, w3_ref, b3_ref, w3t_ref, w3b_ref, b3a_ref, w1a_ref = weights
    blocks = N // width
    loads = [
        pltpu.make_async_copy(src, dst, in_sems.at[n])
        for n, (src, dst) in enumerate(
            (
                (critic_hbm, critic_ref),
                (actor_hbm, actor_ref),
                (table_hbm, table_ref),
                (index_hbm, index_ref),
                (count_hbm, count_ref),
                (noise_hbm, noise_ref),
                (critic_t_hbm, critic_t_ref),
                (actor_t_hbm, actor_t_ref),
            )
        )
    ]
    for load in loads:
        load.start()

    barrier = pltpu.get_barrier_semaphore()

    for device in [place.sibling] + [device for _, device in place.others()]:
        pl.semaphore_signal(barrier, inc=1, device_id=device, device_id_type=MESH)
    for ref in grads:
        ref[...] = jnp.zeros_like(ref)
    make_maps(*maps)
    loads[0].wait()
    loads[1].wait()
    prepare_critics(
        critic_ref, flat_ref, pad_ref, C0, w1_ref, w2f_ref, w2b_ref, b2_ref, w3_ref, b3_ref, w1a_ref
    )
    prepare_actor(
        A, maps, actor_ref, flat_ref, pad_ref, w1_ref, w2f_ref, w2b_ref, b2_ref, w3t_ref, w3b_ref, b3a_ref
    )
    loads[2].wait()

    def turn(i, carry):
        turn_table(i, table_ref, rows_ref)
        return carry

    lax.fori_loop(0, R_DEV // TURN, turn, 0)
    loads[3].wait()
    pick_rows(0, width, index_ref, rows_ref, picked_ref)
    loads[4].wait()
    loads[5].wait()
    turn_noise(noise_ref, q_ref, noise.buffers[0])

    def actors(i):
        x = turn_rows(width, picked_ref)
        x_ref[:, pl.ds(pl.multiple_of(i * width, width), width)] = x
        actor_block(i, width, x, count_ref, weights, grads)

    def actors_and_pick(i, carry):
        actors(i)
        pick_rows(i + 1, width, index_ref, rows_ref, picked_ref)

        @pl.when(i == 0)
        def _():
            loads[6].wait()
            loads[7].wait()
            pl.semaphore_wait(barrier, CHIPS)
            noise.start(0)
            prepare_critics(
                critic_t_ref, flat_ref, pad_ref, T0, w1_ref, w2f_ref, w2b_ref, b2_ref, w3_ref, b3_ref, w1a_ref
            )
            prepare_actor(
                AT, maps, actor_t_ref, flat_ref, pad_ref, w1_ref, w2f_ref, w2b_ref, b2_ref, w3t_ref, w3b_ref, b3a_ref
            )

        for stage in range(1, blocks - 1):

            @pl.when(i == stage)
            def _():
                noise.wait(stage - 1)
                noise.start(stage)

        return carry

    lax.fori_loop(0, blocks - 1, actors_and_pick, 0)
    actors(blocks - 1)
    noise.wait(2)
    noise.start(3)
    pack_actor(pack_ref, maps, grads)
    late = CriticSum(place, pack_ref, out_hbm, buffers[:5], sems.at[0])
    early = ActorSum(place, pack_ref, buffers[5 : len(SUM_BUFFERS)], sems.at[1])
    early.swap().start()

    noise.wait(3)
    noise_back(noise.buffers[4], turned_ref, nz_ref)

    def critics(i, carry):
        x = x_ref[:, pl.ds(pl.multiple_of(i * width, width), width)]
        critic_block(i, width, x, nz_ref, count_ref, weights, prio_ref, grads)

        @pl.when(i == 0)
        def _():
            early.swap().wait()
            early.scatter()

        @pl.when(i == 1)
        def _():
            early.along()

        @pl.when(i == 2)
        def _():
            early.spread()

        @pl.when(i == 3)
        def _():
            early.back()

        return carry

    lax.fori_loop(0, blocks, critics, 0)
    pack_w2(pack_ref, grads)
    late.swap(0)
    pack_rest(pack_ref, grads)
    late.swap(1)
    prios = pltpu.make_async_copy(prio_ref, out_hbm.at[pl.ds(AT_PRIO, 2)], in_sems.at[0])
    prios.start()
    late.scatter()
    early.back_copy().wait()
    early.in_order(order_ref)
    order = pltpu.make_async_copy(order_ref, out_hbm.at[pl.ds(AT_SUM, order_ref.shape[0])], in_sems.at[1])
    order.start()
    prios.wait()
    late.spread()
    order.wait()
    late.back()


def update(weight, grad, momentum, average, target):
    momentum_new = 0.9 * momentum + grad
    weight_new = weight - 0.1 * (grad + 0.9 * momentum_new)
    average_new = 0.99 * average + 0.01 * weight_new
    target_new = 0.005 * weight_new + 0.995 * target
    return (weight_new, momentum_new, average_new, target_new, weight_new.astype(bf))


STEP = 1024
CUTS = (0, 24 * STEP, 44 * STEP, 60 * STEP, PC)
LAST = len(CUTS) - 1


def update_kernel(sum_hbm, *refs):
    ins, stat_ref, prio_out, outs_hbm, outs = refs[:8], refs[8], refs[9], refs[10:20], refs[20:30]
    late_ref, early_ref, count_ref, grad_ref, in_sems, out_sems = refs[30:]
    early = pltpu.make_async_copy(sum_hbm.at[pl.ds(AT_SUM, early_ref.shape[0])], early_ref, in_sems.at[0])
    late = pltpu.make_async_copy(sum_hbm.at[pl.ds(0, DEVS), pl.ds(0, CHUNK)], late_ref, in_sems.at[1])
    stat_at = STAT - REST
    count = pltpu.make_async_copy(sum_hbm.at[pl.ds(stat_at, 1), pl.ds(0, CHUNK)], count_ref, in_sems.at[3])
    for load in (count, early, late):
        load.start()
    pass_on = pltpu.make_async_copy(sum_hbm.at[pl.ds(AT_PRIO, 2)], prio_out, in_sems.at[2])
    pass_on.start()

    def stores(piece):
        out = []
        for n in range(5):
            src, dst = outs[2 * n + min(piece, 1)], outs_hbm[2 * n + min(piece, 1)]
            if piece:
                s = pl.ds(CUTS[piece - 1], CUTS[piece] - CUTS[piece - 1])
                src, dst = src.at[:, s], dst.at[:, s]
            out.append(pltpu.make_async_copy(src, dst, out_sems.at[piece, n]))
        return out

    count.wait()
    stat = count_ref[0, CHUNK - 1 : CHUNK, :]
    factor = (1.0 / SCALE) / stat[:, 1:2]
    stat_ref[...] = stat[:, :2].reshape(2)
    early.wait()

    def actor(s, grad):
        values = update(ins[0][s], grad, ins[2][s], ins[4][s], ins[6][s])
        for ref, value in zip(outs[0::2], values):
            ref[s] = value

    for i in range(PA // STEP):
        actor(slice(STEP * i, STEP * (i + 1)), (early_ref[i // 2, 8 * (i % 2) : 8 * (i % 2) + 8, :] * factor).reshape(STEP))
    done = PA // STEP * STEP
    last = early_ref[done // 2048, done // 128 % 16 : done // 128 % 16 + 8, :] * factor
    more = (PA - done) // 128
    actor(slice(done, done + 128 * more), last[:more].reshape(128 * more))
    done += 128 * more
    actor(slice(done, PA), last[more : more + 1, :ACT].reshape(ACT))
    for store in stores(0):
        store.start()

    def critic(s):
        values = update(ins[1][:, s], grad_ref[:, s] * factor, ins[3][:, s], ins[5][:, s], ins[7][:, s])
        for ref, value in zip(outs[1::2], values):
            ref[:, s] = value

    def critics(i, carry):
        critic(pl.ds(pl.multiple_of(i * STEP, STEP), STEP))
        return carry

    late.wait()
    for piece in range(1, LAST + 1):
        for t in range(CUTS[piece - 1] // 128, -(-CUTS[piece] // 128)):
            r = 2 * t
            if W2_ROW <= r < W2_END:
                k, j = divmod(r - W2_ROW, CHUNK - 1)
                pair = late_ref[k, j : j + 2, :]
            else:
                k = r % REST
                pair = late_ref[k : k + 2, CHUNK - 1, :]
            grad_ref[:, 128 * t : 128 * (t + 1)] = pair
        lax.fori_loop(CUTS[piece - 1] // STEP, CUTS[piece] // STEP, critics, 0, unroll=4)
        if piece == LAST:
            done = PC // STEP * STEP
            critic(pl.ds(done, PC - done))
        for store in stores(piece):
            store.start()
    for piece in range(LAST + 1):
        for store in stores(piece):
            store.wait()
    pass_on.wait()


def local(
    replay,
    sample_index,
    pair_count,
    noise,
    actor,
    critic,
    actor_momentum,
    critic_momentum,
    actor_average,
    critic_average,
    actor_target,
    critic_target,
):
    any_ = pl.BlockSpec(memory_space=pl.ANY)
    total = pl.pallas_call(
        functools.partial(step_kernel, WIDTH),
        out_shape=SDS(RESULT, f32),
        in_specs=[any_] * 8,
        out_specs=any_,
        scratch_shapes=[
            pltpu.VMEM((2, 16, DEVS), f32),
            pltpu.VMEM((2 * CHUNK_A, PLANE, 128), f32),
            pltpu.VMEM((ROW, R_DEV), f32),
            pltpu.SMEM((CAP, DEVS), jnp.int32),
            pltpu.VMEM((ACT, CAP, DEVS), f32),
            pltpu.VMEM((1, DEVS), jnp.int32),
            pltpu.VMEM((PA,), f32),
            pltpu.VMEM((PA,), f32),
            pltpu.VMEM((2, PC), f32),
            pltpu.VMEM((2, PC), f32),
            pltpu.SemaphoreType.DMA((8,)),
            pltpu.VMEM((R_DEV, 128), f32),
            pltpu.VMEM((WIDTH // 128, 128, 128), f32),
            pltpu.VMEM((256, 128), f32),
            pltpu.VMEM((DEVS, 256), f32),
            pltpu.SemaphoreType.DMA((8,)),
            pltpu.VMEM((FEAT, N), f32),
            pltpu.VMEM((8, N), f32),
            pltpu.VMEM((2 * TILES_C + 6, 128), f32),
            pltpu.VMEM((FEAT, 256), f32),
            pltpu.VMEM((PACK, 128), f32),
            pltpu.SemaphoreType.DMA((2, 10)),
        ]
        + WEIGHTS
        + GRADS
        + SUM_BUFFERS
        + NOISE_BUFFERS
        + MAPS,
        compiler_params=pltpu.CompilerParams(
            collective_id=0, has_side_effects=True, vmem_limit_bytes=56 << 20
        ),
        name="td3_step",
    )(
        replay.T,
        sample_index[0].T,
        jnp.transpose(noise[0], (2, 1, 0)),
        pair_count,
        actor,
        actor_target,
        critic,
        critic_target,
    )
    shapes = [SDS((2,), f32), SDS((2, CAP // 2, DEVS), f32)]
    places = [SDS((PA,), f32), SDS((2, PC), f32)] * 4 + [SDS((PA,), bf), SDS((2, PC), bf)]
    stat, prio, *outs = pl.pallas_call(
        update_kernel,
        out_shape=tuple(shapes + places),
        in_specs=[any_] + [VM] * 8,
        out_specs=(VM,) + (any_,) * 11,
        scratch_shapes=[pltpu.VMEM(p.shape, p.dtype) for p in places]
        + [
            pltpu.VMEM((DEVS, CHUNK, 128), f32),
            pltpu.VMEM((2 * CHUNK_A, PLANE, 128), f32),
            pltpu.VMEM((1, CHUNK, 128), f32),
            pltpu.VMEM((2, TILES_C * 128), f32),
            pltpu.SemaphoreType.DMA((4,)),
            pltpu.SemaphoreType.DMA((LAST + 1, 5)),
        ],
        compiler_params=pltpu.CompilerParams(vmem_limit_bytes=24 << 20),
        name="update",
    )(
        total,
        actor,
        critic,
        actor_momentum,
        critic_momentum,
        actor_average,
        critic_average,
        actor_target,
        critic_target,
    )
    return (stat, prio.reshape(CAP, DEVS).T[None], *outs)


def solution(mesh):
    rows = ("group", "shard")
    in_specs = (P(rows, None), P(rows, None, None), P(rows, None), P(rows, None, None, None)) + (P(),) * 8
    out_specs = (P(), P(rows, None, None)) + (P(),) * 10
    return jax.shard_map(local, mesh=mesh, in_specs=in_specs, out_specs=out_specs, check_vma=False)
```
